32 devices in a mesh: prompt: 4 (over y, x), tile: 8 (over z, core).
Axes of the slice: x: 2, y: 2, z: 4, core: 2. Of those that a mesh axis runs over, the one named last changes fastest.
Arguments:
- latent: bfloat16 [128, 160, 16], P(('prompt', 'tile')), parts along dimension 0, may hold values from -6 to 6
- cached_latent: bfloat16 [2, 128, 160, 16], P(None, ('prompt', 'tile')), parts along dimension 1, may hold values from -6 to 6
- cached_features: bfloat16 [2, 128, 160, 384], P(None, ('prompt', 'tile')), parts along dimension 1, may hold values from -5 to 5
- reward_grad: bfloat16 [256, 320, 192], P(('prompt', 'tile')), parts along dimension 0, may hold values from -6 to 6
- conv_in_weight: bfloat16 [3, 3, 3, 16, 384], replicated, may hold values from -0.3125 to 0.3125
- conv_mid_weight: bfloat16 [3, 3, 3, 384, 384], replicated, may hold values from -0.0625 to 0.0625
- conv_up_weight: bfloat16 [3, 3, 384, 192], replicated, may hold values from -0.109375 to 0.109375
- norm_gain: float32 [384], replicated, may hold values from 0.5 to 1.5
- out_gain: float32 [192], replicated, may hold values from 0.5 to 1.5
- shard_order: int32 [32], P('prompt'), parts along dimension 0, may hold values from 0 to 7, each once
Outputs:
- token_grad: float32 [5120, 64], P(('prompt', 'tile')), parts along dimension 0
The draws below stay inside these ranges and needn't reach their ends.
There are 4 independent parts, one for each index of `prompt`. The reference program is written for one: setup_inputs(seed, part) draws one part's arguments, and reference() takes and returns one part's arrays. A program takes and returns all parts, laid end to end along the dimension named above; an argument that names none is the same for every part. Nothing has to cross between parts.
Inputs may be any that keep to these rules, and one draw needn't show every extreme that they name: shard_order is a permutation: each of 0 to 7 once.
All inputs are finite; a program needn't handle non-finite values.
Results may differ from the reference program's by a relative error of at most 0.0095.
Values may be sent and summed in bfloat16 or wider, within the bound.
No kernel may reach another device: no remote copies, remote signals or barrier semaphores. Data moves between devices by JAX's collectives and lax.ppermute only.
A program may use at most 64 MiB of HBM per device.

```python
import jax
import jax.numpy as jnp
from jax import lax

LAT = 16
C_MID = 384
C_OUT = 192
COLS = 160
HEIGHT = 32
TOKENS = 1280
PIECE = 20
N_TILE = 8


def shard_levels(own_key, extent, pieces, least, largest):
    def one(dim, blocks):
        heights = jax.random.uniform(jax.random.fold_in(jax.random.fold_in(own_key, 6), dim), (blocks,), jnp.float32, least / len(pieces), largest / len(pieces))
        return jnp.repeat(jnp.exp(heights), extent[dim] // blocks).reshape((-1,) + (1,) * (len(extent) - dim - 1))

    gain = one(*pieces[0])
    for cut in pieces[1:]:
        gain = gain * one(*cut)
    return gain


def noise(rng, dims, scale, limit, cuts=(), kind=jnp.bfloat16):
    level = shard_levels(rng, dims, cuts, -0.22, 0.18) if cuts else 1.0
    drawn = jax.random.normal(rng, dims, jnp.float32) * scale * level
    return jnp.minimum(jnp.maximum(drawn, -limit), limit).astype(kind)


def setup_inputs(seed: int = 0, part: int = 0) -> dict:
    key_of = jax.random.split(jax.random.key(seed), 11)
    part_splits = jax.random.split(jax.random.fold_in(key_of[10], part), 11)
    latent = noise(part_splits[0], (HEIGHT, COLS, LAT), 1.0, 6.0, ((0, 8),))
    cached_latent = noise(part_splits[1], (2, HEIGHT, COLS, LAT), 1.0, 6.0, ((1, 8),))
    cached_features = noise(part_splits[2], (2, HEIGHT, COLS, C_MID), 0.8, 5.0, ((1, 8),))
    reward_grad = noise(part_splits[3], (2 * HEIGHT, 2 * COLS, C_OUT), 1.0, 6.0, ((0, 8),))
    conv_in_weight = noise(key_of[4], (3, 3, 3, LAT, C_MID), (27 * LAT) ** -0.5, 0.3125)
    conv_mid_weight = noise(key_of[5], (3, 3, 3, C_MID, C_MID), (27 * C_MID) ** -0.5, 0.0625)
    conv_up_weight = noise(key_of[6], (3, 3, C_MID, C_OUT), (9 * C_MID) ** -0.5, 0.109375)
    norm_gain = jnp.clip(jax.random.uniform(key_of[7], (C_MID,), jnp.float32, 0.5, 1.5), 0.5, 1.5)
    out_gain = jnp.clip(jax.random.uniform(key_of[8], (C_OUT,), jnp.float32, 0.5, 1.5), 0.5, 1.5)
    shard_order = jax.random.permutation(part_splits[9], N_TILE).astype(jnp.int32)
    return dict(latent=latent, cached_latent=cached_latent, cached_features=cached_features, reward_grad=reward_grad, conv_in_weight=conv_in_weight, conv_mid_weight=conv_mid_weight, conv_up_weight=conv_up_weight, norm_gain=norm_gain, out_gain=out_gain, shard_order=shard_order)


epsilon = 1e-06
highest = lax.Precision.HIGHEST

def norm_silu(values, gain_vector):
    scaled = values * lax.rsqrt(lax.optimization_barrier(jnp.mean(values * values, axis=-1, keepdims=True)) + epsilon)
    return jax.nn.silu(scaled * gain_vector)

def causal_conv(frames, kernel):
    result = lax.conv_general_dilated(frames.astype(jnp.float32)[None], kernel.astype(jnp.float32), (1, 1, 1), ((0, 0), (1, 1), (1, 1)), dimension_numbers=('NDHWC', 'DHWIO', 'NDHWC'), precision=highest)
    return result[0, 0]

def plane_conv(plane_in, kernel):
    result = lax.conv_general_dilated(plane_in.astype(jnp.float32)[None], kernel.astype(jnp.float32), (1, 1), ((1, 1), (1, 1)), dimension_numbers=('NHWC', 'HWIO', 'NHWC'), precision=highest)
    return result[0]

def plane_back(grad_in, kernel):
    flipped = kernel[::-1, ::-1].astype(jnp.float32)
    result = lax.conv_general_dilated(grad_in.astype(jnp.float32)[None], flipped, (1, 1), ((1, 1), (1, 1)), dimension_numbers=('NHWC', 'HWOI', 'NHWC'), precision=highest)
    return result[0]

def reference(latent, cached_latent, cached_features, reward_grad, conv_in_weight, conv_mid_weight, conv_up_weight, norm_gain, out_gain, shard_order):
    latent_frames = jnp.concatenate([cached_latent, latent[None]], axis=0)
    hidden = lax.optimization_barrier(causal_conv(latent_frames, conv_in_weight).astype(jnp.bfloat16))
    hidden_wide = hidden.astype(jnp.float32)
    activated = norm_silu(hidden_wide, norm_gain).astype(jnp.bfloat16)
    feature_frames = jnp.concatenate([cached_features, activated[None]], axis=0)
    block_state = (hidden_wide + causal_conv(feature_frames, conv_mid_weight)).astype(jnp.bfloat16)
    doubled = jnp.repeat(jnp.repeat(block_state, 2, axis=0), 2, axis=1)
    upper_plane = lax.optimization_barrier(plane_conv(doubled, conv_up_weight).astype(jnp.bfloat16))
    upper_wide = upper_plane.astype(jnp.float32)
    outcome, pullback = jax.vjp(lambda values: norm_silu(values, out_gain), upper_wide)
    upper_grad = pullback(reward_grad.astype(jnp.float32))[0].astype(jnp.bfloat16)
    doubled_grad = plane_back(upper_grad, conv_up_weight)
    block_grad = lax.optimization_barrier(doubled_grad.reshape(HEIGHT, 2, COLS, 2, C_MID).sum(axis=(1, 3)).astype(jnp.bfloat16))
    activated_grad = plane_back(block_grad, conv_mid_weight[2])
    ignored, hidden_pull = jax.vjp(lambda values: norm_silu(values, norm_gain), hidden_wide)
    hidden_grad = (block_grad.astype(jnp.float32) + hidden_pull(activated_grad)[0]).astype(jnp.bfloat16)
    latent_grad = plane_back(hidden_grad, conv_in_weight[2])
    patches = latent_grad.reshape(HEIGHT // 2, 2, COLS // 2, 2, LAT).transpose(0, 2, 1, 3, 4)
    patches = patches.reshape(N_TILE, N_TILE, PIECE, 4 * LAT)
    swapped = jnp.transpose(patches, (1, 0, 2, 3))
    placed = jnp.zeros_like(swapped).at[:, shard_order].set(swapped)
    return placed.reshape(TOKENS, 4 * LAT)
```

```python
import jax
import jax.numpy as jnp
from jax import lax
from jax.experimental import pallas as pl
from jax.experimental.pallas import tpu as pltpu
from jax.sharding import PartitionSpec as P

EPS = 1e-06
F32 = jnp.float32
BF16 = jnp.bfloat16
VM = pl.BlockSpec(memory_space=pltpu.VMEM)
SM = pl.BlockSpec(memory_space=pltpu.SMEM)


def call(body, outs, n_smem, n_vmem, scratch, flops, limit):
    specs = [SM] * n_smem + [VM] * n_vmem
    return pl.pallas_call(
        body,
        out_shape=[jax.ShapeDtypeStruct(s, d) for s, d in outs],
        in_specs=specs,
        out_specs=[VM] * len(outs),
        scratch_shapes=scratch,
        cost_estimate=pl.CostEstimate(flops=int(flops), bytes_accessed=2**20, transcendentals=0),
        compiler_params=pltpu.CompilerParams(vmem_limit_bytes=limit << 20),
    )


def mm(a, b):
    return jnp.dot(a, b, preferred_element_type=F32)


def mm_t(a, b):
    return lax.dot_general(a, b, (((1,), (1,)), ((), ())), preferred_element_type=F32)


def flag(info, k):
    return info[k].astype(F32)


def col_index(cols, lanes):
    return lax.broadcasted_iota(jnp.int32, (cols, lanes), 0)


def from_left(x):
    col = col_index(*x.shape)
    return jnp.where(col == 0, 0.0, pltpu.roll(x, 1, 0))


def from_right(x):
    cols = x.shape[0]
    col = col_index(*x.shape)
    return jnp.where(col == cols - 1, 0.0, pltpu.roll(x, cols - 1, 0))


def pack_body(rows, cols, o, chan):
    half = o - 128

    def body(info, reward, latent, cached, own, send_even, send_odd):
        x_index = lax.broadcasted_iota(jnp.int32, (cols, 2 * cols), 1)
        w_index = lax.broadcasted_iota(jnp.int32, (cols, 2 * cols), 0)
        pick = [(x_index == 2 * w_index + b).astype(F32).astype(BF16) for b in (0, 1)]
        zeros = jnp.zeros((128 - half, 2 * cols), BF16)
        for f in range(2 * rows):
            r = reward[f]
            first, rest = r[:128], r[128:]
            low = jnp.concatenate([first, rest, zeros], axis=0)
            high = jnp.concatenate([first, zeros, rest], axis=0)
            sides = (low, high) if f % 2 else (high, low)
            d0, d1 = mm_t(pick[0], sides[0]), mm_t(pick[1], sides[1])
            own[f, :, 0:128] = d0[:, :128].astype(BF16)
            own[f, :, 128:256] = d1[:, :128].astype(BF16)
            own[f, :, 256:384] = (d0[:, 128:] + d1[:, 128:]).astype(BF16)
        base = 3 * cols
        per = chan * rows
        for send, last in ((send_even, 1 - info[0]), (send_odd, info[0])):
            begin = last * (2 * rows - 3)
            for k in range(3):
                send[k * cols : (k + 1) * cols] = own[begin + k]
            for t in range(3):
                src = cached[t] if t < 2 else latent[...]
                lat = src.reshape(per, cols)
                send[base : base + per, t * 128 : t * 128 + 128] = lat[:, :128]
                send[base + per : base + 2 * per, t * 128 : t * 128 + cols - 128] = lat[:, 128:]

    return body


def taps_body(up, fwd, back_odd, back_even):
    def rows_of(q, j):
        parts = ((2,), (1, 2), (0, 1), (0,))[q]
        total = up[parts[0], j].astype(F32)
        for i in parts[1:]:
            total = total + up[i, j].astype(F32)
        return total

    for q in range(4):
        c0, c1, c2 = (rows_of(q, j) for j in range(3))
        tap = [t.astype(BF16) for t in (c2, c1 + c2, c0 + c1, c0)]
        for b, order in ((0, (3, 1)), (1, (2, 0))):
            place = q if b == 0 else (1, 0, 3, 2)[q]
            for side, p in enumerate(order):
                lanes = slice(side * 384, side * 384 + 384)
                fwd[b, q * 128 : q * 128 + 128, lanes] = tap[p][:128]
                fwd[b, 512 + place * 64 : 576 + place * 64, lanes] = tap[p][128:]
        target, side = ((back_odd, 1), (back_even, 0), (back_odd, 0), (back_even, 1))[q]
        lanes = slice(side * 384, side * 384 + 384)
        for block, (p0, p1) in enumerate(((1, 2), (3, 0))):
            base = block * 384
            target[base : base + 128, lanes] = tap[p0][:128]
            target[base + 128 : base + 256, lanes] = tap[p1][:128]
            low, high = (p0, p1) if q % 2 == 0 else (p1, p0)
            target[base + 256 : base + 320, lanes] = tap[low][128:]
            target[base + 320 : base + 384, lanes] = tap[high][128:]


def cached_body(rows, cols):
    size = rows * cols

    def body(info, features, mid, acc, send_even, send_odd, wide):
        for t in range(2):
            for r in range(rows):
                at = slice(r * cols, (r + 1) * cols)
                x = features[t, r]
                x32 = x.astype(F32)
                base = t * 1152
                wide[at, base : base + 384] = from_left(x32).astype(BF16)
                wide[at, base + 384 : base + 768] = x
                wide[at, base + 768 : base + 1152] = from_right(x32).astype(BF16)
        lhs = wide[...]
        kernels = [jnp.concatenate([mid[0, i], mid[1, i]], axis=0) for i in range(3)]
        pair = mm(lhs, jnp.concatenate([kernels[0], kernels[1]], axis=1))
        zero = jnp.zeros((cols, 384), F32)
        acc[0:cols] = zero
        acc[cols : 2 * cols] = zero
        acc[2 * cols :] = pair[:, :384]
        acc[cols : cols + size] += pair[:, 384:]
        acc[0:size] += mm(lhs, kernels[2])
        for send, last in ((send_even, 1 - info[0]), (send_odd, info[0])):
            send[...] = acc[pl.ds(pl.multiple_of(last * 3 * cols, 3 * cols), 3 * cols)].astype(BF16)

    return body


def current_body(rows, cols, chan):
    per = chan * rows
    base = 3 * cols

    def body(info, latent, cached, got_even, got_odd, w_in, mid, gain, hidden, conv, lat, tall, wide, w_order):
        even = info[0] == 0
        lat[...] = jnp.zeros_like(lat)

        def fill(first_row, got, ok):
            scale = ok.astype(F32)
            for t in range(3):
                x = got[base : base + per, t * 128 : t * 128 + 128].astype(F32) * scale
                y = got[base + per : base + 2 * per, t * 128 : t * 128 + cols - 128].astype(F32) * scale
                for r in range(rows):
                    at = pl.ds((first_row + r) * 3 * chan + t * chan, chan)
                    lat[at, 0:128] = x[r * chan : (r + 1) * chan]
                    lat[at, 128:cols] = y[r * chan : (r + 1) * chan]

        @pl.when(even)
        def _():
            fill(0, got_odd, info[1])
            fill(2 * rows, got_even, info[2])

        @pl.when(jnp.logical_not(even))
        def _():
            fill(0, got_even, info[1])
            fill(2 * rows, got_odd, info[2])

        for t in range(3):
            for r in range(rows):
                at = pl.ds((rows + r) * 3 * chan + t * chan, chan)
                lat[at, 0:cols] = (cached[t, r] if t < 2 else latent[r]).astype(F32)

        for r in range(3 * rows):
            for t in range(3):
                x = lat[pl.ds((r * 3 + t) * chan, chan), :]
                at = (r * 3 + t) * 3 * chan
                tall[at : at + chan] = pltpu.roll(x, 1, 1).astype(BF16)
                tall[at + chan : at + 2 * chan] = x.astype(BF16)
                tall[at + 2 * chan : at + 3 * chan] = pltpu.roll(x, 255, 1).astype(BF16)
        for i in range(3):
            for t in range(3):
                at = (i * 3 + t) * 3 * chan
                w_order[at : at + 3 * chan] = w_in[t, i]

        deep = 27 * chan
        for k in range(rows + 6):
            lhs = tall[k * 9 * chan : k * 9 * chan + deep, 0:cols]
            h = lax.dot_general(lhs, w_order[...], (((0,), (0,)), ((), ())), preferred_element_type=F32)
            h = h.astype(BF16)
            if 1 <= k <= rows + 4:
                hidden[k - 1] = h
            v = h.astype(F32)
            inv = lax.rsqrt(jnp.mean(v * v, axis=1, keepdims=True) + EPS)
            y = v * inv * gain[...]
            act = y * (0.5 * jnp.tanh(0.5 * y) + 0.5)
            if k < 3:
                act = act * flag(info, 1)
            if k >= rows + 3:
                act = act * flag(info, 2)
            at = slice(k * cols, (k + 1) * cols)
            wide[at, 0:384] = from_left(act).astype(BF16)
            wide[at, 384:768] = act.astype(BF16)
            wide[at, 768:1152] = from_right(act).astype(BF16)

        size = rows * cols
        for part in range(2):
            start = part * size
            total = mm(wide[start : start + size], mid[2, 0])
            total += mm(wide[start + cols : start + cols + size], mid[2, 1])
            total += mm(wide[start + 2 * cols : start + 2 * cols + size], mid[2, 2])
            conv[start : start + size] = total

    return body


def pull_scale(y):
    sig = 0.5 * jnp.tanh(0.5 * y) + 0.5
    return sig * (1.0 + y * (1.0 - sig))


def back_body(rows, cols, chan, count, o):
    deep_rows = rows + 4
    size = rows * cols
    width = 2 * cols // count

    def body(
        info, hidden, conv, acc, got_even, got_odd, packed_even, packed_odd, own, fwd, back_odd, back_even, mid, w_in, gain,
        out_gain, payload, reward, edge, p0, p1, g_odd, g_even, wide, lines,
    ):
        even = info[0] == 0
        top, bottom = flag(info, 1), flag(info, 2)

        def take(got, packed, before):
            ok = top if before else bottom
            place = 0 if before else 3
            for k in range(3):
                at = slice(k * cols, (k + 1) * cols)
                edge[(place + k) * cols : (place + k + 1) * cols] = got[at].astype(F32) * ok
                reward[k if before else 2 * rows + 3 + k] = (packed[at].astype(F32) * ok).astype(BF16)

        @pl.when(even)
        def _():
            take(got_odd, packed_odd, True)
            take(got_even, packed_even, False)

        @pl.when(jnp.logical_not(even))
        def _():
            take(got_even, packed_even, True)
            take(got_odd, packed_odd, False)

        reward[3 : 2 * rows + 3] = own[...]

        def row(ref, k):
            return ref[k * cols : (k + 1) * cols]

        state_rows = []
        for k in range(deep_rows):
            x = hidden[k].astype(F32) + row(conv, k)
            if 1 <= k <= rows + 2:
                x = x + row(acc, k - 1)
            if k < 3:
                x = x + row(edge, k)
            if k >= rows + 1:
                x = x + row(edge, k - rows + 2)
            if k < 2:
                x = x * top
            if k >= rows + 2:
                x = x * bottom
            x = x.astype(BF16)
            x32 = x.astype(F32)
            at = slice(k * cols, (k + 1) * cols)
            wide[at, 0:384] = from_left(x32).astype(BF16)
            wide[at, 384:768] = x
            wide[at, 768:1152] = from_right(x32).astype(BF16)

        for part in range(2):
            at = slice(part * size, (part + 1) * size)
            p0[at] = mm_t(wide[at, 0:768], fwd[0])
            p1[at] = mm_t(wide[at, 384:1152], fwd[1])

        lane = lax.broadcasted_iota(jnp.int32, (cols, 128), 1)
        low = lane < 64
        gains = [out_gain[:, 0:128], out_gain[:, 128:256]]

        def pull(v0, v1, vm, r, zero_low):
            mine = low if zero_low else jnp.logical_not(low)
            v0, v1, vm = (v.astype(BF16).astype(F32) for v in (v0, v1, vm))

            def both(a0, a1, am):
                s0 = jnp.sum(a0 + jnp.where(mine, am, 0.0), axis=1, keepdims=True)
                s1 = jnp.sum(a1 + jnp.where(mine, 0.0, am), axis=1, keepdims=True)
                return s0 * (1.0 / o), s1 * (1.0 / o)

            q0, q1 = both(v0 * v0, v1 * v1, vm * vm)
            i0, i1 = lax.rsqrt(q0 + EPS), lax.rsqrt(q1 + EPS)
            im = jnp.where(mine, i0, i1)
            out = []
            for v, i, g, k in ((v0, i0, gains[0], 0), (v1, i1, gains[0], 1), (vm, im, gains[1], 2)):
                s = v * i
                y = s * g
                d = r[:, k * 128 : k * 128 + 128].astype(F32) * pull_scale(y) * g
                out.append((s, d))
            m0, m1 = both(*(s * d for s, d in out))
            mm_ = jnp.where(mine, m0, m1)
            return [i * (d - s * m) for (s, d), i, m in zip(out, (i0, i1, im), (m0, m1, mm_))], mine

        def store(g, target, k):
            (a0, a1, am), mine = g
            at = slice(k * cols, (k + 1) * cols)
            target[at, 0:128] = a0.astype(BF16)
            target[at, 128:256] = a1.astype(BF16)
            target[at, 256:384] = am.astype(BF16)
            target[at, 384:512] = from_right(a0).astype(BF16)
            target[at, 512:640] = from_left(a1).astype(BF16)
            target[at, 640:768] = jnp.where(mine, from_right(am), from_left(am)).astype(BF16)

        fine = rows + 3
        for k in range(fine):
            a, b = slice(k * cols, (k + 1) * cols), slice((k + 1) * cols, (k + 2) * cols)
            v0 = p0[a, 256:384] + p0[b, 0:128]
            v1 = p1[a, 256:384] + p1[b, 0:128]
            vm = jnp.where(low, p0[a, 640:768] + p0[b, 512:640], p1[a, 640:768] + p1[b, 512:640])
            store(pull(v0, v1, vm, reward[2 * k], True), g_odd, k)
            v0 = p0[b, 128:256] + p0[a, 384:512]
            v1 = p1[b, 128:256] + p1[a, 384:512]
            vm = jnp.where(low, p1[b, 512:640] + p1[a, 640:768], p0[b, 512:640] + p0[a, 640:768])
            store(pull(v0, v1, vm, reward[2 * k + 1], False), g_even, k)

        span = fine * cols
        p0[0:span] = mm(g_odd[...], back_odd[...])
        p1[0:span] = mm(g_even[...], back_even[...])
        for k in range(rows + 2):
            a, b = slice(k * cols, (k + 1) * cols), slice((k + 1) * cols, (k + 2) * cols)
            x = p0[b, 0:384] + p0[a, 384:768] + p1[a, 0:384] + p1[b, 384:768]
            if k == 0:
                x = x * top
            if k == rows + 1:
                x = x * bottom
            x = x.astype(BF16)
            x32 = x.astype(F32)
            wide[a, 0:384] = from_right(x32).astype(BF16)
            wide[a, 384:768] = x
            wide[a, 768:1152] = from_left(x32).astype(BF16)

        total = None
        for i in range(3):
            kernel = jnp.concatenate([mid[2, i, j * 384 : (j + 1) * 384] for j in range(3)], axis=1)
            term = mm_t(wide[(2 - i) * cols : (2 - i) * cols + size], kernel)
            total = term if total is None else total + term
        p0[0:size, 0:384] = total
        g = gain[...]
        for k in range(rows):
            at = slice(k * cols, (k + 1) * cols)
            v = hidden[k + 2].astype(F32)
            inv = lax.rsqrt(jnp.mean(v * v, axis=1, keepdims=True) + EPS)
            s = v * inv
            d = p0[at, 0:384] * pull_scale(s * g) * g
            dv = inv * (d - s * jnp.mean(d * s, axis=1, keepdims=True))
            block = wide[(k + 1) * cols : (k + 2) * cols, 384:768].astype(F32)
            g_odd[at, 0:384] = (block + dv).astype(BF16)

        z = mm_t(w_in[...], g_odd[0:size, 0:384])
        place = lax.broadcasted_iota(jnp.int32, (chan, size), 1)
        col = lax.rem(place, cols)
        sums = []
        for i in range(3):
            z0, z1, z2 = (z[(i * 3 + j) * chan : (i * 3 + j + 1) * chan] for j in range(3))
            left = jnp.where(col == cols - 1, 0.0, pltpu.roll(z0, size - 1, 1))
            right = jnp.where(col == 0, 0.0, pltpu.roll(z2, 1, 1))
            sums.append(left + z1 + right)
        inner = sums[1]
        inner = inner + jnp.where(place < size - cols, pltpu.roll(sums[0], size - cols, 1), 0.0)
        inner = inner + jnp.where(place >= cols, pltpu.roll(sums[2], cols, 1), 0.0)
        lines[0:chan] = inner
        lines[chan : 2 * chan] = sums[0]
        lines[2 * chan : 3 * chan] = sums[2]
        per_row = count // 2
        for u in range(count):
            pair, piece = u // per_row, u % per_row
            for a in range(2):
                at = (2 * pair + a) * cols + piece * width
                payload[u, a * chan : (a + 1) * chan] = lines[0:chan, at : at + width].astype(BF16)
            if pair == 0:
                at = (rows - 1) * cols + piece * width
                payload[u, 2 * chan : 3 * chan] = lines[2 * chan : 3 * chan, at : at + width].astype(BF16)
            else:
                at = piece * width
                payload[u, 2 * chan : 3 * chan] = lines[chan : 2 * chan, at : at + width].astype(BF16)

    return body


def place_body(count, chan, width, tokens):
    piece = width // 2

    def body(info, order, got, out):
        pair = info[3]
        w = lax.broadcasted_iota(jnp.int32, (width, tokens), 0)
        pos = lax.broadcasted_iota(jnp.int32, (width, tokens), 1)
        inner, outer = [None, None], [None, None]
        for t in range(count):
            step = t + 1 - 2 * pair
            valid = jnp.logical_and(step >= 0, step < count)
            beside = order[jnp.clip(step, 0, count - 1)]
            for b in range(2):
                want = 2 * pos + b - w
                sel = (want == 2 * piece * order[t]).astype(F32).astype(BF16)
                sel_e = (want == jnp.where(valid, 2 * piece * beside, -99999)).astype(F32).astype(BF16)
                x = mm(got[t, 0 : 2 * chan], sel)
                e = mm(got[t, 2 * chan : 3 * chan], sel_e)
                inner[b] = x if inner[b] is None else inner[b] + x
                outer[b] = e if outer[b] is None else outer[b] + e
        for a in range(2):
            mine = (pair == a).astype(F32)
            for b in range(2):
                at = (2 * a + b) * chan
                out[at : at + chan] = inner[b][a * chan : (a + 1) * chan] + outer[b] * mine

    return body


def swaps(count):
    within = [(i, i ^ 1) for i in range(count)]
    across = [(0, 0), (count - 1, count - 1)]
    for i in range(1, count - 1, 2):
        across += [(i, i + 1), (i + 1, i)]
    return within, sorted(across)


def shards(
    latent, cached_latent, cached_features, reward_grad, conv_in_weight, conv_mid_weight, conv_up_weight, norm_gain, out_gain, shard_order
):
    count = lax.axis_size("tile")
    rows, cols, chan = latent.shape
    mid_chan = norm_gain.shape[0]
    o = out_gain.shape[0]
    tile = lax.axis_index("tile")
    info = jnp.stack(
        [tile % 2, (tile > 0).astype(jnp.int32), (tile < count - 1).astype(jnp.int32), (tile >= count // 2).astype(jnp.int32)]
    ).astype(jnp.int32)
    lat = jnp.transpose(latent, (0, 2, 1))
    lat_cached = jnp.transpose(cached_latent, (0, 1, 3, 2))
    reward_t = jnp.transpose(reward_grad, (0, 2, 1))
    up_t = jnp.transpose(conv_up_weight, (0, 1, 3, 2))
    mid = conv_mid_weight.reshape(3, 3, 3 * mid_chan, mid_chan)
    w_in = conv_in_weight.reshape(3, 3, 3 * chan, mid_chan)
    gain = norm_gain.reshape(1, mid_chan)
    gain_out = jnp.concatenate([out_gain, out_gain[128:]]).reshape(1, 256)
    within, across = swaps(count)
    size = rows * cols
    edge_rows = 3 * cols + 2 * chan * rows

    own, send_even, send_odd = call(
        pack_body(rows, cols, o, chan),
        [((2 * rows, cols, 384), BF16), ((edge_rows, 384), BF16), ((edge_rows, 384), BF16)],
        1, 3, [], 2e9, 16,
    )(info, reward_t, lat, lat_cached)
    packed_even = lax.ppermute(send_even, "tile", within)
    packed_odd = lax.ppermute(send_odd, "tile", across)

    fwd, back_odd, back_even = call(
        taps_body, [((2, 768, 768), BF16), ((768, 768), BF16), ((768, 768), BF16)], 0, 1, [], 1e9, 16
    )(up_t)

    acc, part_even, part_odd = call(
        cached_body(rows, cols),
        [((6 * cols, 384), F32), ((3 * cols, 384), BF16), ((3 * cols, 384), BF16)],
        1, 2, [pltpu.VMEM((size, 2304), BF16)], 4e9, 24,
    )(info, cached_features, mid)
    got_even = lax.ppermute(part_even, "tile", within)
    got_odd = lax.ppermute(part_odd, "tile", across)

    hidden, conv = call(
        current_body(rows, cols, chan),
        [((rows + 4, cols, 384), BF16), ((2 * size, 384), F32)],
        1, 7,
        [
            pltpu.VMEM((9 * rows * chan, 256), F32),
            pltpu.VMEM((27 * rows * chan, 256), BF16),
            pltpu.VMEM(((rows + 6) * cols, 1152), BF16),
            pltpu.VMEM((27 * chan, 384), BF16),
        ],
        5e9, 24,
    )(info, lat, lat_cached, packed_even, packed_odd, w_in, mid, gain)

    width = 2 * cols // count
    (payload,) = call(
        back_body(rows, cols, chan, count, o),
        [((count, 3 * chan, width), BF16)],
        1, 15,
        [
            pltpu.VMEM((2 * rows + 6, cols, 384), BF16),
            pltpu.VMEM((6 * cols, 384), F32),
            pltpu.VMEM(((rows + 4) * cols, 768), F32),
            pltpu.VMEM(((rows + 4) * cols, 768), F32),
            pltpu.VMEM(((rows + 3) * cols, 768), BF16),
            pltpu.VMEM(((rows + 3) * cols, 768), BF16),
            pltpu.VMEM(((rows + 4) * cols, 1152), BF16),
            pltpu.VMEM((3 * chan, size), F32),
        ],
        8e9, 32,
    )(
        info, hidden, conv, acc, got_even, got_odd, packed_even, packed_odd, own, fwd, back_odd, back_even, mid,
        w_in[2].reshape(9 * chan, mid_chan), gain, gain_out,
    )
    received = lax.all_to_all(payload, "tile", split_axis=0, concat_axis=0, tiled=True)
    tokens = size // 4
    (placed,) = call(place_body(count, chan, width, tokens), [((4 * chan, tokens), F32)], 2, 1, [], 1e7, 16)(
        info, shard_order, received
    )
    return placed.T


def solution(mesh):
    return jax.shard_map(
        shards,
        mesh=mesh,
        in_specs=(
            P(("prompt", "tile"), None, None),
            P(None, ("prompt", "tile"), None, None),
            P(None, ("prompt", "tile"), None, None),
            P(("prompt", "tile"), None, None),
            P(),
            P(),
            P(),
            P(),
            P(),
            P("prompt"),
        ),
        out_specs=P(("prompt", "tile"), None),
        check_vma=False,
    )
```

```python
import jax
import jax.numpy as jnp
from jax import lax
from jax.experimental import pallas as pl
from jax.experimental.pallas import tpu as pltpu
from jax.sharding import PartitionSpec as P

EPS = 1e-06
F32 = jnp.float32
BF16 = jnp.bfloat16
VM = pl.BlockSpec(memory_space=pltpu.VMEM)
SM = pl.BlockSpec(memory_space=pltpu.SMEM)


def call(body, outs, n_smem, n_vmem, scratch, flops, limit):
    specs = [SM] * n_smem + [VM] * n_vmem
    return pl.pallas_call(
        body,
        out_shape=[jax.ShapeDtypeStruct(s, d) for s, d in outs],
        in_specs=specs,
        out_specs=[VM] * len(outs),
        scratch_shapes=scratch,
        cost_estimate=pl.CostEstimate(flops=int(flops), bytes_accessed=2**20, transcendentals=0),
        compiler_params=pltpu.CompilerParams(vmem_limit_bytes=limit << 20),
    )


def mm(a, b):
    return jnp.dot(a, b, preferred_element_type=F32)


def mm_t(a, b):
    return lax.dot_general(a, b, (((1,), (1,)), ((), ())), preferred_element_type=F32)


def flag(info, k):
    return info[k].astype(F32)


def col_index(cols, lanes):
    return lax.broadcasted_iota(jnp.int32, (cols, lanes), 0)


def from_left(x):
    col = col_index(*x.shape)
    return jnp.where(col == 0, 0.0, pltpu.roll(x, 1, 0))


def from_right(x):
    cols = x.shape[0]
    col = col_index(*x.shape)
    return jnp.where(col == cols - 1, 0.0, pltpu.roll(x, cols - 1, 0))


def pack_body(rows, cols, o, chan):
    half = o - 128

    def body(info, reward, latent, cached, own, send_even, send_odd):
        x_index = lax.broadcasted_iota(jnp.int32, (cols, 2 * cols), 1)
        w_index = lax.broadcasted_iota(jnp.int32, (cols, 2 * cols), 0)
        pick = [(x_index == 2 * w_index + b).astype(F32).astype(BF16) for b in (0, 1)]
        zeros = jnp.zeros((128 - half, 2 * cols), BF16)
        for f in range(2 * rows):
            r = reward[f]
            first, rest = r[:128], r[128:]
            low = jnp.concatenate([first, rest, zeros], axis=0)
            high = jnp.concatenate([first, zeros, rest], axis=0)
            sides = (low, high) if f % 2 else (high, low)
            d0, d1 = mm_t(pick[0], sides[0]), mm_t(pick[1], sides[1])
            own[f, :, 0:128] = d0[:, :128].astype(BF16)
            own[f, :, 128:256] = d1[:, :128].astype(BF16)
            own[f, :, 256:384] = (d0[:, 128:] + d1[:, 128:]).astype(BF16)
        base = 3 * cols
        per = chan * rows
        for send, last in ((send_even, 1 - info[0]), (send_odd, info[0])):
            begin = last * (2 * rows - 3)
            for k in range(3):
                send[k * cols : (k + 1) * cols] = own[begin + k]
            for t in range(3):
                src = cached[t] if t < 2 else latent[...]
                lat = src.reshape(per, cols)
                send[base : base + per, t * 128 : t * 128 + 128] = lat[:, :128]
                send[base + per : base + 2 * per, t * 128 : t * 128 + cols - 128] = lat[:, 128:]

    return body


def taps_body(up, fwd, back_odd, back_even):
    def rows_of(q, j):
        parts = ((2,), (1, 2), (0, 1), (0,))[q]
        total = up[parts[0], j].astype(F32)
        for i in parts[1:]:
            total = total + up[i, j].astype(F32)
        return total

    for q in range(4):
        c0, c1, c2 = (rows_of(q, j) for j in range(3))
        tap = [t.astype(BF16) for t in (c2, c1 + c2, c0 + c1, c0)]
        for b, order in ((0, (3, 1)), (1, (2, 0))):
            place = q if b == 0 else (1, 0, 3, 2)[q]
            for side, p in enumerate(order):
                lanes = slice(side * 384, side * 384 + 384)
                fwd[b, q * 128 : q * 128 + 128, lanes] = tap[p][:128]
                fwd[b, 512 + place * 64 : 576 + place * 64, lanes] = tap[p][128:]
        target, side = ((back_odd, 1), (back_even, 0), (back_odd, 0), (back_even, 1))[q]
        lanes = slice(side * 384, side * 384 + 384)
        for block, (p0, p1) in enumerate(((1, 2), (3, 0))):
            base = block * 384
            target[base : base + 128, lanes] = tap[p0][:128]
            target[base + 128 : base + 256, lanes] = tap[p1][:128]
            low, high = (p0, p1) if q % 2 == 0 else (p1, p0)
            target[base + 256 : base + 320, lanes] = tap[low][128:]
            target[base + 320 : base + 384, lanes] = tap[high][128:]


def cached_body(rows, cols):
    size = rows * cols

    def body(info, features, mid, acc, send_even, send_odd, wide):
        for t in range(2):
            for r in range(rows):
                at = slice(r * cols, (r + 1) * cols)
                x = features[t, r]
                x32 = x.astype(F32)
                base = t * 1152
                wide[at, base : base + 384] = from_left(x32).astype(BF16)
                wide[at, base + 384 : base + 768] = x
                wide[at, base + 768 : base + 1152] = from_right(x32).astype(BF16)
        lhs = wide[...]
        kernels = [jnp.concatenate([mid[0, i], mid[1, i]], axis=0) for i in range(3)]
        pair = mm(lhs, jnp.concatenate([kernels[0], kernels[1]], axis=1))
        zero = jnp.zeros((cols, 384), F32)
        acc[0:cols] = zero
        acc[cols : 2 * cols] = zero
        acc[2 * cols :] = pair[:, :384]
        acc[cols : cols + size] += pair[:, 384:]
        acc[0:size] += mm(lhs, kernels[2])
        for send, last in ((send_even, 1 - info[0]), (send_odd, info[0])):
            send[...] = acc[pl.ds(pl.multiple_of(last * 3 * cols, 3 * cols), 3 * cols)].astype(BF16)

    return body


def current_body(rows, cols, chan):
    per = chan * rows
    base = 3 * cols

    def body(info, latent, cached, got_even, got_odd, w_in, mid, gain, hidden, conv, lat, tall, wide, w_order):
        even = info[0] == 0
        lat[...] = jnp.zeros_like(lat)

        def fill(first_row, got, ok):
            scale = ok.astype(F32)
            for t in range(3):
                x = got[base : base + per, t * 128 : t * 128 + 128].astype(F32) * scale
                y = got[base + per : base + 2 * per, t * 128 : t * 128 + cols - 128].astype(F32) * scale
                for r in range(rows):
                    at = pl.ds((first_row + r) * 3 * chan + t * chan, chan)
                    lat[at, 0:128] = x[r * chan : (r + 1) * chan]
                    lat[at, 128:cols] = y[r * chan : (r + 1) * chan]

        @pl.when(even)
        def _():
            fill(0, got_odd, info[1])
            fill(2 * rows, got_even, info[2])

        @pl.when(jnp.logical_not(even))
        def _():
            fill(0, got_even, info[1])
            fill(2 * rows, got_odd, info[2])

        for t in range(3):
            for r in range(rows):
                at = pl.ds((rows + r) * 3 * chan + t * chan, chan)
                lat[at, 0:cols] = (cached[t, r] if t < 2 else latent[r]).astype(F32)

        for r in range(3 * rows):
            for t in range(3):
                x = lat[pl.ds((r * 3 + t) * chan, chan), :]
                at = (r * 3 + t) * 3 * chan
                tall[at : at + chan] = pltpu.roll(x, 1, 1).astype(BF16)
                tall[at + chan : at + 2 * chan] = x.astype(BF16)
                tall[at + 2 * chan : at + 3 * chan] = pltpu.roll(x, 255, 1).astype(BF16)
        for i in range(3):
            for t in range(3):
                at = (i * 3 + t) * 3 * chan
                w_order[at : at + 3 * chan] = w_in[t, i]

        deep = 27 * chan
        for k in range(rows + 6):
            lhs = tall[k * 9 * chan : k * 9 * chan + deep, 0:cols]
            h = lax.dot_general(lhs, w_order[...], (((0,), (0,)), ((), ())), preferred_element_type=F32)
            h = h.astype(BF16)
            if 1 <= k <= rows + 4:
                hidden[k - 1] = h
            v = h.astype(F32)
            inv = lax.rsqrt(jnp.mean(v * v, axis=1, keepdims=True) + EPS)
            y = v * inv * gain[...]
            act = y * (0.5 * jnp.tanh(0.5 * y) + 0.5)
            if k < 3:
                act = act * flag(info, 1)
            if k >= rows + 3:
                act = act * flag(info, 2)
            at = slice(k * cols, (k + 1) * cols)
            wide[at, 0:384] = from_left(act).astype(BF16)
            wide[at, 384:768] = act.astype(BF16)
            wide[at, 768:1152] = from_right(act).astype(BF16)

        size = rows * cols
        for part in range(2):
            start = part * size
            total = mm(wide[start : start + size], mid[2, 0])
            total += mm(wide[start + cols : start + cols + size], mid[2, 1])
            total += mm(wide[start + 2 * cols : start + 2 * cols + size], mid[2, 2])
            conv[start : start + size] = total

    return body


def pull_scale(y):
    sig = 0.5 * jnp.tanh(0.5 * y) + 0.5
    return sig * (1.0 + y * (1.0 - sig))


def back_body(rows, cols, chan, count, o):
    deep_rows = rows + 4
    size = rows * cols
    width = 2 * cols // count

    def body(
        info, hidden, conv, acc, got_even, got_odd, packed_even, packed_odd, own, fwd, back_odd, back_even, mid, w_in, gain,
        out_gain, payload, reward, edge, p0, p1, g_odd, g_even, wide, lines,
    ):
        even = info[0] == 0
        top, bottom = flag(info, 1), flag(info, 2)

        def take(got, packed, before, slot):
            ok = top if before else bottom
            place = 0 if before else 3
            for k in range(3):
                at = slice(k * cols, (k + 1) * cols)
                edge[(place + k) * cols : (place + k + 1) * cols] = got[slot, at].astype(F32) * ok
                reward[k if before else 2 * rows + 3 + k] = (packed[at].astype(F32) * ok).astype(BF16)

        @pl.when(even)
        def _():
            take(got_odd, packed_odd, True, 0)
            take(got_even, packed_even, False, 1)

        @pl.when(jnp.logical_not(even))
        def _():
            take(got_even, packed_even, True, 0)
            take(got_odd, packed_odd, False, 1)

        reward[3 : 2 * rows + 3] = own[...]

        def row(ref, k):
            return ref[k * cols : (k + 1) * cols]

        state_rows = []
        for k in range(deep_rows):
            x = hidden[k].astype(F32) + row(conv, k)
            if 1 <= k <= rows + 2:
                x = x + row(acc, k - 1)
            if k < 3:
                x = x + row(edge, k)
            if k >= rows + 1:
                x = x + row(edge, k - rows + 2)
            if k < 2:
                x = x * top
            if k >= rows + 2:
                x = x * bottom
            x = x.astype(BF16)
            x32 = x.astype(F32)
            at = slice(k * cols, (k + 1) * cols)
            wide[at, 0:384] = from_left(x32).astype(BF16)
            wide[at, 384:768] = x
            wide[at, 768:1152] = from_right(x32).astype(BF16)

        for part in range(2):
            at = slice(part * size, (part + 1) * size)
            p0[at] = mm_t(wide[at, 0:768], fwd[0])
            p1[at] = mm_t(wide[at, 384:1152], fwd[1])

        lane = lax.broadcasted_iota(jnp.int32, (cols, 128), 1)
        low = lane < 64
        gains = [out_gain[:, 0:128], out_gain[:, 128:256]]

        def pull(v0, v1, vm, r, zero_low):
            mine = low if zero_low else jnp.logical_not(low)
            v0, v1, vm = (v.astype(BF16).astype(F32) for v in (v0, v1, vm))

            def both(a0, a1, am):
                s0 = jnp.sum(a0 + jnp.where(mine, am, 0.0), axis=1, keepdims=True)
                s1 = jnp.sum(a1 + jnp.where(mine, 0.0, am), axis=1, keepdims=True)
                return s0 * (1.0 / o), s1 * (1.0 / o)

            q0, q1 = both(v0 * v0, v1 * v1, vm * vm)
            i0, i1 = lax.rsqrt(q0 + EPS), lax.rsqrt(q1 + EPS)
            im = jnp.where(mine, i0, i1)
            out = []
            for v, i, g, k in ((v0, i0, gains[0], 0), (v1, i1, gains[0], 1), (vm, im, gains[1], 2)):
                s = v * i
                y = s * g
                d = r[:, k * 128 : k * 128 + 128].astype(F32) * pull_scale(y) * g
                out.append((s, d))
            m0, m1 = both(*(s * d for s, d in out))
            mm_ = jnp.where(mine, m0, m1)
            return [i * (d - s * m) for (s, d), i, m in zip(out, (i0, i1, im), (m0, m1, mm_))], mine

        def store(g, target, k):
            (a0, a1, am), mine = g
            at = slice(k * cols, (k + 1) * cols)
            target[at, 0:128] = a0.astype(BF16)
            target[at, 128:256] = a1.astype(BF16)
            target[at, 256:384] = am.astype(BF16)
            target[at, 384:512] = from_right(a0).astype(BF16)
            target[at, 512:640] = from_left(a1).astype(BF16)
            target[at, 640:768] = jnp.where(mine, from_right(am), from_left(am)).astype(BF16)

        fine = rows + 3
        for k in range(fine):
            a, b = slice(k * cols, (k + 1) * cols), slice((k + 1) * cols, (k + 2) * cols)
            v0 = p0[a, 256:384] + p0[b, 0:128]
            v1 = p1[a, 256:384] + p1[b, 0:128]
            vm = jnp.where(low, p0[a, 640:768] + p0[b, 512:640], p1[a, 640:768] + p1[b, 512:640])
            store(pull(v0, v1, vm, reward[2 * k], True), g_odd, k)
            v0 = p0[b, 128:256] + p0[a, 384:512]
            v1 = p1[b, 128:256] + p1[a, 384:512]
            vm = jnp.where(low, p1[b, 512:640] + p1[a, 640:768], p0[b, 512:640] + p0[a, 640:768])
            store(pull(v0, v1, vm, reward[2 * k + 1], False), g_even, k)

        span = fine * cols
        p0[0:span] = mm(g_odd[...], back_odd[...])
        p1[0:span] = mm(g_even[...], back_even[...])
        for k in range(rows + 2):
            a, b = slice(k * cols, (k + 1) * cols), slice((k + 1) * cols, (k + 2) * cols)
            x = p0[b, 0:384] + p0[a, 384:768] + p1[a, 0:384] + p1[b, 384:768]
            if k == 0:
                x = x * top
            if k == rows + 1:
                x = x * bottom
            x = x.astype(BF16)
            x32 = x.astype(F32)
            wide[a, 0:384] = from_right(x32).astype(BF16)
            wide[a, 384:768] = x
            wide[a, 768:1152] = from_left(x32).astype(BF16)

        total = None
        for i in range(3):
            kernel = jnp.concatenate([mid[2, i, j * 384 : (j + 1) * 384] for j in range(3)], axis=1)
            term = mm_t(wide[(2 - i) * cols : (2 - i) * cols + size], kernel)
            total = term if total is None else total + term
        p0[0:size, 0:384] = total
        g = gain[...]
        for k in range(rows):
            at = slice(k * cols, (k + 1) * cols)
            v = hidden[k + 2].astype(F32)
            inv = lax.rsqrt(jnp.mean(v * v, axis=1, keepdims=True) + EPS)
            s = v * inv
            d = p0[at, 0:384] * pull_scale(s * g) * g
            dv = inv * (d - s * jnp.mean(d * s, axis=1, keepdims=True))
            block = wide[(k + 1) * cols : (k + 2) * cols, 384:768].astype(F32)
            g_odd[at, 0:384] = (block + dv).astype(BF16)

        z = mm_t(w_in[...], g_odd[0:size, 0:384])
        place = lax.broadcasted_iota(jnp.int32, (chan, size), 1)
        col = lax.rem(place, cols)
        sums = []
        for i in range(3):
            z0, z1, z2 = (z[(i * 3 + j) * chan : (i * 3 + j + 1) * chan] for j in range(3))
            left = jnp.where(col == cols - 1, 0.0, pltpu.roll(z0, size - 1, 1))
            right = jnp.where(col == 0, 0.0, pltpu.roll(z2, 1, 1))
            sums.append(left + z1 + right)
        inner = sums[1]
        inner = inner + jnp.where(place < size - cols, pltpu.roll(sums[0], size - cols, 1), 0.0)
        inner = inner + jnp.where(place >= cols, pltpu.roll(sums[2], cols, 1), 0.0)
        lines[0:chan] = inner
        lines[chan : 2 * chan] = sums[0]
        lines[2 * chan : 3 * chan] = sums[2]
        per_row = count // 2
        for u in range(count):
            pair, piece = u // per_row, u % per_row
            for a in range(2):
                at = (2 * pair + a) * cols + piece * width
                payload[u, a * chan : (a + 1) * chan] = lines[0:chan, at : at + width].astype(BF16)
            if pair == 0:
                at = (rows - 1) * cols + piece * width
                payload[u, 2 * chan : 3 * chan] = lines[2 * chan : 3 * chan, at : at + width].astype(BF16)
            else:
                at = piece * width
                payload[u, 2 * chan : 3 * chan] = lines[chan : 2 * chan, at : at + width].astype(BF16)

    return body


def place_body(count, chan, width, tokens):
    piece = width // 2

    def body(info, order, got, out):
        pair = info[3]
        w = lax.broadcasted_iota(jnp.int32, (width, tokens), 0)
        pos = lax.broadcasted_iota(jnp.int32, (width, tokens), 1)
        inner, outer = [None, None], [None, None]
        for t in range(count):
            step = t + 1 - 2 * pair
            valid = jnp.logical_and(step >= 0, step < count)
            beside = order[jnp.clip(step, 0, count - 1)]
            for b in range(2):
                want = 2 * pos + b - w
                sel = (want == 2 * piece * order[t]).astype(F32).astype(BF16)
                sel_e = (want == jnp.where(valid, 2 * piece * beside, -99999)).astype(F32).astype(BF16)
                x = mm(got[t, 0 : 2 * chan], sel)
                e = mm(got[t, 2 * chan : 3 * chan], sel_e)
                inner[b] = x if inner[b] is None else inner[b] + x
                outer[b] = e if outer[b] is None else outer[b] + e
        for a in range(2):
            mine = (pair == a).astype(F32)
            for b in range(2):
                at = (2 * a + b) * chan
                out[at : at + chan] = inner[b][a * chan : (a + 1) * chan] + outer[b] * mine

    return body


def swaps(count):
    within = [(i, i ^ 1) for i in range(count)]
    across = [(0, 0), (count - 1, count - 1)]
    for i in range(1, count - 1, 2):
        across += [(i, i + 1), (i + 1, i)]
    return within, sorted(across)


def shards(
    latent, cached_latent, cached_features, reward_grad, conv_in_weight, conv_mid_weight, conv_up_weight, norm_gain, out_gain, shard_order
):
    count = lax.axis_size("tile")
    rows, cols, chan = latent.shape
    mid_chan = norm_gain.shape[0]
    o = out_gain.shape[0]
    tile = lax.axis_index("tile")
    info = jnp.stack(
        [tile % 2, (tile > 0).astype(jnp.int32), (tile < count - 1).astype(jnp.int32), (tile >= count // 2).astype(jnp.int32)]
    ).astype(jnp.int32)
    lat = jnp.transpose(latent, (0, 2, 1))
    lat_cached = jnp.transpose(cached_latent, (0, 1, 3, 2))
    reward_t = jnp.transpose(reward_grad, (0, 2, 1))
    up_t = jnp.transpose(conv_up_weight, (0, 1, 3, 2))
    mid = conv_mid_weight.reshape(3, 3, 3 * mid_chan, mid_chan)
    w_in = conv_in_weight.reshape(3, 3, 3 * chan, mid_chan)
    gain = norm_gain.reshape(1, mid_chan)
    gain_out = jnp.concatenate([out_gain, out_gain[128:]]).reshape(1, 256)
    within, across = swaps(count)
    size = rows * cols
    edge_rows = 3 * cols + 2 * chan * rows

    own, send_even, send_odd = call(
        pack_body(rows, cols, o, chan),
        [((2 * rows, cols, 384), BF16), ((edge_rows, 384), BF16), ((edge_rows, 384), BF16)],
        1, 3, [], 2e9, 16,
    )(info, reward_t, lat, lat_cached)
    packed_even = lax.ppermute(send_even, "tile", within)
    packed_odd = lax.ppermute(send_odd, "tile", across)

    fwd, back_odd, back_even = call(
        taps_body, [((2, 768, 768), BF16), ((768, 768), BF16), ((768, 768), BF16)], 0, 1, [], 1e9, 16
    )(up_t)

    acc, part_even, part_odd = call(
        cached_body(rows, cols),
        [((6 * cols, 384), F32), ((3 * cols, 384), BF16), ((3 * cols, 384), BF16)],
        1, 2, [pltpu.VMEM((size, 2304), BF16)], 4e9, 24,
    )(info, cached_features, mid)
    pairs = [[i, i + 1] for i in range(0, count, 2)]
    cross = [[i, i + 1] for i in range(1, count - 1, 2)] + [[count - 1, 0]]
    got_even = lax.all_gather(part_even, "tile", axis_index_groups=pairs)
    got_odd = lax.all_gather(part_odd, "tile", axis_index_groups=cross)

    hidden, conv = call(
        current_body(rows, cols, chan),
        [((rows + 4, cols, 384), BF16), ((2 * size, 384), F32)],
        1, 7,
        [
            pltpu.VMEM((9 * rows * chan, 256), F32),
            pltpu.VMEM((27 * rows * chan, 256), BF16),
            pltpu.VMEM(((rows + 6) * cols, 1152), BF16),
            pltpu.VMEM((27 * chan, 384), BF16),
        ],
        5e9, 24,
    )(info, lat, lat_cached, packed_even, packed_odd, w_in, mid, gain)

    width = 2 * cols // count
    (payload,) = call(
        back_body(rows, cols, chan, count, o),
        [((count, 3 * chan, width), BF16)],
        1, 15,
        [
            pltpu.VMEM((2 * rows + 6, cols, 384), BF16),
            pltpu.VMEM((6 * cols, 384), F32),
            pltpu.VMEM(((rows + 4) * cols, 768), F32),
            pltpu.VMEM(((rows + 4) * cols, 768), F32),
            pltpu.VMEM(((rows + 3) * cols, 768), BF16),
            pltpu.VMEM(((rows + 3) * cols, 768), BF16),
            pltpu.VMEM(((rows + 4) * cols, 1152), BF16),
            pltpu.VMEM((3 * chan, size), F32),
        ],
        8e9, 32,
    )(
        info, hidden, conv, acc, got_even, got_odd, packed_even, packed_odd, own, fwd, back_odd, back_even, mid,
        w_in[2].reshape(9 * chan, mid_chan), gain, gain_out,
    )
    gathered = lax.all_gather(payload, "tile")
    received = lax.dynamic_index_in_dim(gathered, tile, 1, keepdims=False)
    tokens = size // 4
    (placed,) = call(place_body(count, chan, width, tokens), [((4 * chan, tokens), F32)], 2, 1, [], 1e7, 16)(
        info, shard_order, received
    )
    return placed.T


def solution(mesh):
    return jax.shard_map(
        shards,
        mesh=mesh,
        in_specs=(
            P(("prompt", "tile"), None, None),
            P(None, ("prompt", "tile"), None, None),
            P(None, ("prompt", "tile"), None, None),
            P(("prompt", "tile"), None, None),
            P(),
            P(),
            P(),
            P(),
            P(),
            P("prompt"),
        ),
        out_specs=P(("prompt", "tile"), None),
        check_vma=False,
    )
```

```python
import jax
import jax.numpy as jnp
from jax import lax
from jax.experimental import pallas as pl
from jax.experimental.pallas import tpu as pltpu
from jax.sharding import PartitionSpec as P

EPS = 1e-06
F32 = jnp.float32
BF16 = jnp.bfloat16
VM = pl.BlockSpec(memory_space=pltpu.VMEM)
SM = pl.BlockSpec(memory_space=pltpu.SMEM)


def weave(*groups):
    total = max(len(g) for g in groups)
    done = [0] * len(groups)
    for k in range(total):
        for n, g in enumerate(groups):
            while done[n] * total < (k + 1) * len(g):
                g[done[n]]()
                done[n] += 1


def call(body, outs, n_smem, n_vmem, scratch, flops, limit, smem_outs=0):
    specs = [SM] * n_smem + [VM] * n_vmem
    return pl.pallas_call(
        body,
        out_shape=[jax.ShapeDtypeStruct(s, d) for s, d in outs],
        in_specs=specs,
        out_specs=[SM] * smem_outs + [VM] * (len(outs) - smem_outs),
        scratch_shapes=scratch,
        cost_estimate=pl.CostEstimate(flops=int(flops), bytes_accessed=2**20, transcendentals=0),
        compiler_params=pltpu.CompilerParams(vmem_limit_bytes=limit << 20),
    )


def mm(a, b):
    return jnp.dot(a, b, preferred_element_type=F32)


def mm_t(a, b):
    return lax.dot_general(a, b, (((1,), (1,)), ((), ())), preferred_element_type=F32)


def flag(info, k):
    return info[k].astype(F32)


def col_index(cols, lanes):
    return lax.broadcasted_iota(jnp.int32, (cols, lanes), 0)


def from_left(x):
    col = col_index(*x.shape)
    return jnp.where(col == 0, 0.0, pltpu.roll(x, 1, 0))


def from_right(x):
    cols = x.shape[0]
    col = col_index(*x.shape)
    return jnp.where(col == cols - 1, 0.0, pltpu.roll(x, cols - 1, 0))


def pack_body(rows, cols, o, chan):
    half = o - 128

    def body(info, reward, latent, cached, own, send_even, send_odd):
        x_index = lax.broadcasted_iota(jnp.int32, (cols, 2 * cols), 1)
        w_index = lax.broadcasted_iota(jnp.int32, (cols, 2 * cols), 0)
        pick = [(x_index == 2 * w_index + b).astype(F32).astype(BF16) for b in (0, 1)]
        zeros = jnp.zeros((128 - half, 2 * cols), BF16)
        for f in range(2 * rows):
            r = reward[f]
            first, rest = r[:128], r[128:]
            low = jnp.concatenate([first, rest, zeros], axis=0)
            high = jnp.concatenate([first, zeros, rest], axis=0)
            sides = (low, high) if f % 2 else (high, low)
            d0, d1 = mm_t(pick[0], sides[0]), mm_t(pick[1], sides[1])
            own[f, :, 0:128] = d0[:, :128].astype(BF16)
            own[f, :, 128:256] = d1[:, :128].astype(BF16)
            own[f, :, 256:384] = (d0[:, 128:] + d1[:, 128:]).astype(BF16)
        base = 3 * cols
        per = chan * rows
        for send, last in ((send_even, 1 - info[0]), (send_odd, info[0])):
            begin = last * (2 * rows - 3)
            for k in range(3):
                send[k * cols : (k + 1) * cols] = own[begin + k]
            for t in range(3):
                src = cached[t] if t < 2 else latent[...]
                lat = src.reshape(per, cols)
                send[base : base + per, t * 128 : t * 128 + 128] = lat[:, :128]
                send[base + per : base + 2 * per, t * 128 : t * 128 + cols - 128] = lat[:, 128:]

    return body


def taps_body(info, up, info_out, fwd, back_odd, back_even):
    for k in range(4):
        info_out[k] = info[k]

    def rows_of(q, j):
        parts = ((2,), (1, 2), (0, 1), (0,))[q]
        total = up[parts[0], j].astype(F32)
        for i in parts[1:]:
            total = total + up[i, j].astype(F32)
        return total

    for q in range(4):
        c0, c1, c2 = (rows_of(q, j) for j in range(3))
        tap = [t.astype(BF16) for t in (c2, c1 + c2, c0 + c1, c0)]
        for b, order in ((0, (3, 1)), (1, (2, 0))):
            place = q if b == 0 else (1, 0, 3, 2)[q]
            for side, p in enumerate(order):
                lanes = slice(side * 384, side * 384 + 384)
                fwd[b, q * 128 : q * 128 + 128, lanes] = tap[p][:128]
                fwd[b, 512 + place * 64 : 576 + place * 64, lanes] = tap[p][128:]
        target, side = ((back_odd, 1), (back_even, 0), (back_odd, 0), (back_even, 1))[q]
        lanes = slice(side * 384, side * 384 + 384)
        for block, (p0, p1) in enumerate(((1, 2), (3, 0))):
            base = block * 384
            target[base : base + 128, lanes] = tap[p0][:128]
            target[base + 128 : base + 256, lanes] = tap[p1][:128]
            low, high = (p0, p1) if q % 2 == 0 else (p1, p0)
            target[base + 256 : base + 320, lanes] = tap[low][128:]
            target[base + 320 : base + 384, lanes] = tap[high][128:]


def cached_body(rows, cols):
    size = rows * cols

    def body(info, features, mid, acc, send_even, send_odd, wide):
        for t in range(2):
            for r in range(rows):
                at = slice(r * cols, (r + 1) * cols)
                x = features[t, r]
                x32 = x.astype(F32)
                base = t * 1152
                wide[at, base : base + 384] = from_left(x32).astype(BF16)
                wide[at, base + 384 : base + 768] = x
                wide[at, base + 768 : base + 1152] = from_right(x32).astype(BF16)
        lhs = wide[...]
        kernels = [jnp.concatenate([mid[0, i], mid[1, i]], axis=0) for i in range(3)]
        pair = mm(lhs, jnp.concatenate([kernels[0], kernels[1]], axis=1))
        zero = jnp.zeros((cols, 384), F32)
        acc[0:cols] = zero
        acc[cols : 2 * cols] = zero
        acc[2 * cols :] = pair[:, :384]
        acc[cols : cols + size] += pair[:, 384:]
        acc[0:size] += mm(lhs, kernels[2])
        for send, last in ((send_even, 1 - info[0]), (send_odd, info[0])):
            send[...] = acc[pl.ds(pl.multiple_of(last * 3 * cols, 3 * cols), 3 * cols)].astype(BF16)

    return body


def current_body(rows, cols, chan):
    per = chan * rows
    base = 3 * cols

    def body(info, latent, cached, got_even, got_odd, w_in, mid, gain, hidden, conv, lat, tall, wide, w_order):
        even = info[0] == 0
        lat[...] = jnp.zeros_like(lat)

        def fill(first_row, got, ok):
            scale = ok.astype(F32)
            for t in range(3):
                x = got[base : base + per, t * 128 : t * 128 + 128].astype(F32) * scale
                y = got[base + per : base + 2 * per, t * 128 : t * 128 + cols - 128].astype(F32) * scale
                for r in range(rows):
                    at = pl.ds((first_row + r) * 3 * chan + t * chan, chan)
                    lat[at, 0:128] = x[r * chan : (r + 1) * chan]
                    lat[at, 128:cols] = y[r * chan : (r + 1) * chan]

        @pl.when(even)
        def _():
            fill(0, got_odd, info[1])
            fill(2 * rows, got_even, info[2])

        @pl.when(jnp.logical_not(even))
        def _():
            fill(0, got_even, info[1])
            fill(2 * rows, got_odd, info[2])

        for t in range(3):
            for r in range(rows):
                at = pl.ds((rows + r) * 3 * chan + t * chan, chan)
                lat[at, 0:cols] = (cached[t, r] if t < 2 else latent[r]).astype(F32)

        for r in range(3 * rows):
            for t in range(3):
                x = lat[pl.ds((r * 3 + t) * chan, chan), :]
                at = (r * 3 + t) * 3 * chan
                tall[at : at + chan] = pltpu.roll(x, 1, 1).astype(BF16)
                tall[at + chan : at + 2 * chan] = x.astype(BF16)
                tall[at + 2 * chan : at + 3 * chan] = pltpu.roll(x, 255, 1).astype(BF16)
        for i in range(3):
            for t in range(3):
                at = (i * 3 + t) * 3 * chan
                w_order[at : at + 3 * chan] = w_in[t, i]

        deep = 27 * chan

        def hidden_row(k):
            lhs = tall[k * 9 * chan : k * 9 * chan + deep, 0:cols]
            h = lax.dot_general(lhs, w_order[...], (((0,), (0,)), ((), ())), preferred_element_type=F32)
            h = h.astype(BF16)
            if 1 <= k <= rows + 4:
                hidden[k - 1] = h
            v = h.astype(F32)
            inv = lax.rsqrt(jnp.mean(v * v, axis=1, keepdims=True) + EPS)
            y = v * inv * gain[...]
            act = y * (0.5 * jnp.tanh(0.5 * y) + 0.5)
            if k < 3:
                act = act * flag(info, 1)
            if k >= rows + 3:
                act = act * flag(info, 2)
            at = slice(k * cols, (k + 1) * cols)
            wide[at, 0:384] = from_left(act).astype(BF16)
            wide[at, 384:768] = act.astype(BF16)
            wide[at, 768:1152] = from_right(act).astype(BF16)

        def conv_rows(p, lanes):
            start = 2 * p * cols
            lhs = [wide[start + i * cols : start + (i + 2) * cols] for i in range(3)]
            rhs = [mid[2, i, :, lanes] for i in range(3)]
            conv[start : start + 2 * cols, lanes] = mm(jnp.concatenate(lhs, axis=1), jnp.concatenate(rhs, axis=0))

        def rows_step(k):
            return lambda: hidden_row(k)

        def conv_step(p):
            return [lambda: conv_rows(p, slice(0, 256)), lambda: conv_rows(p, slice(256, 384))]

        for k in range(4):
            hidden_row(k)
        for p in range(rows // 2 + 2):
            after = [rows_step(k) for k in (2 * p + 4, 2 * p + 5) if k < rows + 6]
            weave(conv_step(p), after) if after else weave(conv_step(p))

    return body


def pull_scale(y):
    sig = 0.5 * jnp.tanh(0.5 * y) + 0.5
    return sig * (1.0 + y * (1.0 - sig))


def back_body(rows, cols, chan, count, o):
    deep_rows = rows + 4
    size = rows * cols
    width = 2 * cols // count

    def body(
        info, hidden, conv, acc, got_even, got_odd, packed_even, packed_odd, own, fwd, back_odd, back_even, mid, w_in, gain,
        out_gain, payload, reward, edge, p0, p1, g_odd, g_even, wide, t_odd, t_even, back, act_grad, hid, lines,
    ):
        even = info[0] == 0
        top, bottom = flag(info, 1), flag(info, 2)

        def take(got, packed, before):
            ok = top if before else bottom
            place = 0 if before else 3
            for k in range(3):
                at = slice(k * cols, (k + 1) * cols)
                edge[(place + k) * cols : (place + k + 1) * cols] = got[at].astype(F32) * ok
                reward[k if before else 2 * rows + 3 + k] = (packed[at].astype(F32) * ok).astype(BF16)

        @pl.when(even)
        def _():
            take(got_odd, packed_odd, True)
            take(got_even, packed_even, False)

        @pl.when(jnp.logical_not(even))
        def _():
            take(got_even, packed_even, True)
            take(got_odd, packed_odd, False)

        reward[3 : 2 * rows + 3] = own[...]

        def row(ref, k):
            return ref[k * cols : (k + 1) * cols]

        def state_row(k):
            x = hidden[k].astype(F32) + row(conv, k)
            if 1 <= k <= rows + 2:
                x = x + row(acc, k - 1)
            if k < 3:
                x = x + row(edge, k)
            if k >= rows + 1:
                x = x + row(edge, k - rows + 2)
            if k < 2:
                x = x * top
            if k >= rows + 2:
                x = x * bottom
            x = x.astype(BF16)
            x32 = x.astype(F32)
            at = slice(k * cols, (k + 1) * cols)
            wide[at, 0:384] = from_left(x32).astype(BF16)
            wide[at, 384:768] = x
            wide[at, 768:1152] = from_right(x32).astype(BF16)

        def up_dot(p, b, n):
            at = slice(2 * p * cols, (2 * p + 2) * cols)
            lanes = slice(n * 256, n * 256 + 256)
            (p0, p1)[b][at, lanes] = mm_t(wide[at, b * 384 : b * 384 + 768], fwd[b, lanes])

        lane = lax.broadcasted_iota(jnp.int32, (cols, 128), 1)
        low = lane < 64
        gains = [out_gain[:, 0:128], out_gain[:, 128:256]]

        def pull(v0, v1, vm, r, zero_low):
            mine = low if zero_low else jnp.logical_not(low)
            v0, v1, vm = (v.astype(BF16).astype(F32) for v in (v0, v1, vm))

            def both(a0, a1, am):
                s0 = jnp.sum(a0 + jnp.where(mine, am, 0.0), axis=1, keepdims=True)
                s1 = jnp.sum(a1 + jnp.where(mine, 0.0, am), axis=1, keepdims=True)
                return s0 * (1.0 / o), s1 * (1.0 / o)

            q0, q1 = both(v0 * v0, v1 * v1, vm * vm)
            i0, i1 = lax.rsqrt(q0 + EPS), lax.rsqrt(q1 + EPS)
            im = jnp.where(mine, i0, i1)
            out = []
            for v, i, g, k in ((v0, i0, gains[0], 0), (v1, i1, gains[0], 1), (vm, im, gains[1], 2)):
                s = v * i
                y = s * g
                d = r[:, k * 128 : k * 128 + 128].astype(F32) * pull_scale(y) * g
                out.append((s, d))
            m0, m1 = both(*(s * d for s, d in out))
            mx = jnp.where(mine, m0, m1)
            return [i * (d - s * m) for (s, d), i, m in zip(out, (i0, i1, im), (m0, m1, mx))], mine

        def store(g, target, k):
            (a0, a1, am), mine = g
            at = slice(k * cols, (k + 1) * cols)
            target[at, 0:128] = a0.astype(BF16)
            target[at, 128:256] = a1.astype(BF16)
            target[at, 256:384] = am.astype(BF16)
            target[at, 384:512] = from_right(a0).astype(BF16)
            target[at, 512:640] = from_left(a1).astype(BF16)
            target[at, 640:768] = jnp.where(mine, from_right(am), from_left(am)).astype(BF16)

        def pull_odd(k):
            a, b = slice(k * cols, (k + 1) * cols), slice((k + 1) * cols, (k + 2) * cols)
            v0 = p0[a, 256:384] + p0[b, 0:128]
            v1 = p1[a, 256:384] + p1[b, 0:128]
            vm = jnp.where(low, p0[a, 640:768] + p0[b, 512:640], p1[a, 640:768] + p1[b, 512:640])
            store(pull(v0, v1, vm, reward[2 * k], True), g_odd, k)

        def pull_even(k):
            a, b = slice(k * cols, (k + 1) * cols), slice((k + 1) * cols, (k + 2) * cols)
            v0 = p0[b, 128:256] + p0[a, 384:512]
            v1 = p1[b, 128:256] + p1[a, 384:512]
            vm = jnp.where(low, p1[b, 512:640] + p1[a, 640:768], p0[b, 512:640] + p0[a, 640:768])
            store(pull(v0, v1, vm, reward[2 * k + 1], False), g_even, k)

        fine = rows + 3

        def down_dot(first, number, odd, n):
            at = slice(first * cols, (first + number) * cols)
            lanes = slice(n * 256, n * 256 + 256)
            if odd:
                t_odd[at, lanes] = mm(g_odd[at], back_odd[:, lanes])
            else:
                t_even[at, lanes] = mm(g_even[at], back_even[:, lanes])

        def block_row(k):
            a, b = slice(k * cols, (k + 1) * cols), slice((k + 1) * cols, (k + 2) * cols)
            x = t_odd[b, 0:384] + t_odd[a, 384:768] + t_even[a, 0:384] + t_even[b, 384:768]
            if k == 0:
                x = x * top
            if k == rows + 1:
                x = x * bottom
            x = x.astype(BF16)
            x32 = x.astype(F32)
            back[a, 0:384] = from_right(x32).astype(BF16)
            back[a, 384:768] = x
            back[a, 768:1152] = from_left(x32).astype(BF16)

        def mid_dot(p, n):
            lanes = slice(n * 256, min(384, n * 256 + 256))
            lhs = [back[(2 * p + 2 - i) * cols : (2 * p + 4 - i) * cols] for i in range(3)]
            rhs = [mid[2, i, j * 384 + lanes.start : j * 384 + lanes.stop] for i in range(3) for j in range(3)]
            at = slice(2 * p * cols, (2 * p + 2) * cols)
            act_grad[at, lanes] = mm_t(jnp.concatenate(lhs, axis=1), jnp.concatenate(rhs, axis=1))

        def hidden_pull(k):
            g = gain[...]
            at = slice(k * cols, (k + 1) * cols)
            v = hidden[k + 2].astype(F32)
            inv = lax.rsqrt(jnp.mean(v * v, axis=1, keepdims=True) + EPS)
            s = v * inv
            d = act_grad[at] * pull_scale(s * g) * g
            dv = inv * (d - s * jnp.mean(d * s, axis=1, keepdims=True))
            block = back[(k + 1) * cols : (k + 2) * cols, 384:768].astype(F32)
            hid[at] = (block + dv).astype(BF16)

        def steps(f, *keys):
            return [lambda key=key: f(*key) for key in keys]

        def ups(p):
            return steps(up_dot, *[(p, b, n) for n in range(3) for b in range(2)])

        def downs(first, number):
            return steps(down_dot, *[(first, number, odd, n) for odd in (True, False) for n in range(3)])

        def pulls(*ks):
            return [step for k in ks for step in steps(pull_odd, (k,)) + steps(pull_even, (k,))]

        state_row(0)
        state_row(1)
        weave(ups(0), steps(state_row, (2,), (3,)))
        weave(ups(1), steps(state_row, (4,), (5,)) + pulls(0))
        weave(ups(2), steps(state_row, (6,), (7,)) + pulls(1, 2))
        weave(ups(3) + downs(0, 2), pulls(3, 4))
        weave(downs(2, 2), pulls(5, 6) + steps(block_row, (0,)))
        weave(downs(4, 3), steps(block_row, (1,), (2,)))
        block_row(3)
        weave(steps(mid_dot, (0, 0), (0, 1)), steps(block_row, (4,), (5,)))
        weave(steps(mid_dot, (1, 0), (1, 1)), steps(hidden_pull, (0,), (1,)))
        hidden_pull(2)
        hidden_pull(3)

        z = mm_t(w_in[...], hid[...])
        place = lax.broadcasted_iota(jnp.int32, (chan, size), 1)
        col = lax.rem(place, cols)
        sums = []
        for i in range(3):
            z0, z1, z2 = (z[(i * 3 + j) * chan : (i * 3 + j + 1) * chan] for j in range(3))
            left = jnp.where(col == cols - 1, 0.0, pltpu.roll(z0, size - 1, 1))
            right = jnp.where(col == 0, 0.0, pltpu.roll(z2, 1, 1))
            sums.append(left + z1 + right)
        inner = sums[1]
        inner = inner + jnp.where(place < size - cols, pltpu.roll(sums[0], size - cols, 1), 0.0)
        inner = inner + jnp.where(place >= cols, pltpu.roll(sums[2], cols, 1), 0.0)
        lines[0:chan] = inner
        lines[chan : 2 * chan] = sums[0]
        lines[2 * chan : 3 * chan] = sums[2]
        per_row = count // 2
        for u in range(count):
            pair, piece = u // per_row, u % per_row
            parts = []
            for a in range(2):
                at = (2 * pair + a) * cols + piece * width
                parts.append(lines[0:chan, at : at + width])
            at = piece * width + (0 if pair else (rows - 1) * cols)
            first = chan if pair else 2 * chan
            parts.append(lines[first : first + chan, at : at + width])
            parts.append(jnp.zeros((chan, 128 - 3 * width), F32))
            payload[u] = jnp.concatenate(parts, axis=1).astype(BF16)

    return body


def place_body(count, chan, width, tokens):
    piece = width // 2

    def body(info, order, got, out):
        pair = info[3]
        lane = lax.broadcasted_iota(jnp.int32, (128, 4 * tokens), 0)
        column = lax.broadcasted_iota(jnp.int32, (128, 4 * tokens), 1)
        group = (lane >= width).astype(jnp.int32) + (lane >= 2 * width).astype(jnp.int32)
        w = lane - group * width
        part = jnp.where(group == 2, pair, group)
        fixed = (2 * part + (w & 1)) * tokens + (w >> 1) - column
        fixed = jnp.where(lane < 3 * width, fixed, -99999)
        total = None
        for t in range(count):
            step = t + 1 - 2 * pair
            valid = jnp.logical_and(step >= 0, step < count)
            beside = jnp.where(valid, piece * order[jnp.clip(step, 0, count - 1)], -9999)
            begin = jnp.where(group == 2, beside, piece * order[t])
            sel = (fixed + begin == 0).astype(F32).astype(BF16)
            x = mm(got[t], sel)
            total = x if total is None else total + x
        for k in range(4):
            out[k * chan : (k + 1) * chan] = total[:, k * tokens : (k + 1) * tokens]

    return body


def swaps(count):
    within = [(i, i ^ 1) for i in range(count)]
    across = [(0, 0), (count - 1, count - 1)]
    for i in range(1, count - 1, 2):
        across += [(i, i + 1), (i + 1, i)]
    return within, sorted(across)


def shards(
    latent, cached_latent, cached_features, reward_grad, conv_in_weight, conv_mid_weight, conv_up_weight, norm_gain, out_gain, shard_order
):
    count = lax.axis_size("tile")
    rows, cols, chan = latent.shape
    mid_chan = norm_gain.shape[0]
    o = out_gain.shape[0]
    tile = lax.axis_index("tile")
    info = jnp.stack(
        [tile % 2, (tile > 0).astype(jnp.int32), (tile < count - 1).astype(jnp.int32), (tile >= count // 2).astype(jnp.int32)]
    ).astype(jnp.int32)
    lat = jnp.transpose(latent, (0, 2, 1))
    lat_cached = jnp.transpose(cached_latent, (0, 1, 3, 2))
    reward_t = jnp.transpose(reward_grad, (0, 2, 1))
    up_t = jnp.transpose(conv_up_weight, (0, 1, 3, 2))
    mid = conv_mid_weight.reshape(3, 3, 3 * mid_chan, mid_chan)
    w_in = conv_in_weight.reshape(3, 3, 3 * chan, mid_chan)
    gain = norm_gain.reshape(1, mid_chan)
    gain_out = jnp.concatenate([out_gain, out_gain[128:]]).reshape(1, 256)
    within, across = swaps(count)
    size = rows * cols
    edge_rows = 3 * cols + 2 * chan * rows

    info, fwd, back_odd, back_even = call(
        taps_body,
        [((4,), jnp.int32), ((2, 768, 768), BF16), ((768, 768), BF16), ((768, 768), BF16)],
        1, 1, [], 1e10, 16, 1,
    )(info, up_t)

    own, send_even, send_odd = call(
        pack_body(rows, cols, o, chan),
        [((2 * rows, cols, 384), BF16), ((edge_rows, 384), BF16), ((edge_rows, 384), BF16)],
        1, 3, [], 1e10, 16,
    )(info, reward_t, lat, lat_cached)
    packed_even = lax.ppermute(send_even, "tile", within)
    packed_odd = lax.ppermute(send_odd, "tile", across)

    acc, part_even, part_odd = call(
        cached_body(rows, cols),
        [((6 * cols, 384), F32), ((3 * cols, 384), BF16), ((3 * cols, 384), BF16)],
        1, 2, [pltpu.VMEM((size, 2304), BF16)], 4e9, 24,
    )(info, cached_features, mid)
    got_even = lax.ppermute(part_even, "tile", within)
    got_odd = lax.ppermute(part_odd, "tile", across)

    hidden, conv = call(
        current_body(rows, cols, chan),
        [((rows + 4, cols, 384), BF16), ((2 * size, 384), F32)],
        1, 7,
        [
            pltpu.VMEM((9 * rows * chan, 256), F32),
            pltpu.VMEM((27 * rows * chan, 256), BF16),
            pltpu.VMEM(((rows + 6) * cols, 1152), BF16),
            pltpu.VMEM((27 * chan, 384), BF16),
        ],
        5e9, 24,
    )(info, lat, lat_cached, packed_even, packed_odd, w_in, mid, gain)

    width = 2 * cols // count
    (payload,) = call(
        back_body(rows, cols, chan, count, o),
        [((count, chan, 128), BF16)],
        1, 15,
        [
            pltpu.VMEM((2 * rows + 6, cols, 384), BF16),
            pltpu.VMEM((6 * cols, 384), F32),
            pltpu.VMEM(((rows + 4) * cols, 768), F32),
            pltpu.VMEM(((rows + 4) * cols, 768), F32),
            pltpu.VMEM(((rows + 3) * cols, 768), BF16),
            pltpu.VMEM(((rows + 3) * cols, 768), BF16),
            pltpu.VMEM(((rows + 4) * cols, 1152), BF16),
            pltpu.VMEM(((rows + 3) * cols, 768), F32),
            pltpu.VMEM(((rows + 3) * cols, 768), F32),
            pltpu.VMEM(((rows + 2) * cols, 1152), BF16),
            pltpu.VMEM((size, 384), F32),
            pltpu.VMEM((size, 384), BF16),
            pltpu.VMEM((3 * chan, size), F32),
        ],
        8e9, 36,
    )(
        info, hidden, conv, acc, got_even, got_odd, packed_even, packed_odd, own, fwd, back_odd, back_even, mid,
        w_in[2].reshape(9 * chan, mid_chan), gain, gain_out,
    )
    received = lax.all_to_all(payload, "tile", split_axis=0, concat_axis=0, tiled=True)
    tokens = size // 4
    (placed,) = call(place_body(count, chan, width, tokens), [((4 * chan, tokens), F32)], 2, 1, [], 1e7, 16)(
        info, shard_order, received
    )
    return placed.T


def solution(mesh):
    return jax.shard_map(
        shards,
        mesh=mesh,
        in_specs=(
            P(("prompt", "tile"), None, None),
            P(None, ("prompt", "tile"), None, None),
            P(None, ("prompt", "tile"), None, None),
            P(("prompt", "tile"), None, None),
            P(),
            P(),
            P(),
            P(),
            P(),
            P("prompt"),
        ),
        out_specs=P(("prompt", "tile"), None),
        check_vma=False,
    )
```

```python
import jax
import jax.numpy as jnp
from jax import lax
from jax.experimental import pallas as pl
from jax.experimental.pallas import tpu as pltpu
from jax.sharding import PartitionSpec as P

EPS = 1e-06
F32 = jnp.float32
BF16 = jnp.bfloat16
VM = pl.BlockSpec(memory_space=pltpu.VMEM)
SM = pl.BlockSpec(memory_space=pltpu.SMEM)


def weave(*groups):
    total = max(len(g) for g in groups)
    done = [0] * len(groups)
    for k in range(total):
        for n, g in enumerate(groups):
            while done[n] * total < (k + 1) * len(g):
                g[done[n]]()
                done[n] += 1


def call(body, outs, n_smem, n_vmem, scratch, flops, limit, smem_outs=0):
    specs = [SM] * n_smem + [VM] * n_vmem
    return pl.pallas_call(
        body,
        out_shape=[jax.ShapeDtypeStruct(s, d) for s, d in outs],
        in_specs=specs,
        out_specs=[SM] * smem_outs + [VM] * (len(outs) - smem_outs),
        scratch_shapes=scratch,
        cost_estimate=pl.CostEstimate(flops=int(flops), bytes_accessed=2**20, transcendentals=0),
        compiler_params=pltpu.CompilerParams(vmem_limit_bytes=limit << 20),
    )


def mm(a, b):
    return jnp.dot(a, b, preferred_element_type=F32)


def mm_t(a, b):
    return lax.dot_general(a, b, (((1,), (1,)), ((), ())), preferred_element_type=F32)


def flag(info, k):
    return info[k].astype(F32)


def col_index(cols, lanes):
    return lax.broadcasted_iota(jnp.int32, (cols, lanes), 0)


def from_left(x):
    col = col_index(*x.shape)
    return jnp.where(col == 0, 0.0, pltpu.roll(x, 1, 0))


def from_right(x):
    cols = x.shape[0]
    col = col_index(*x.shape)
    return jnp.where(col == cols - 1, 0.0, pltpu.roll(x, cols - 1, 0))


def pack_body(rows, cols, o, chan):
    half = o - 128

    def body(info, reward, latent, cached, own, send_even, send_odd):
        x_index = lax.broadcasted_iota(jnp.int32, (cols, 2 * cols), 1)
        w_index = lax.broadcasted_iota(jnp.int32, (cols, 2 * cols), 0)
        pick = [(x_index == 2 * w_index + b).astype(F32).astype(BF16) for b in (0, 1)]
        zeros = jnp.zeros((128 - half, 2 * cols), BF16)
        for f in range(2 * rows):
            r = reward[f]
            first, rest = r[:128], r[128:]
            low = jnp.concatenate([first, rest, zeros], axis=0)
            high = jnp.concatenate([first, zeros, rest], axis=0)
            sides = (low, high) if f % 2 else (high, low)
            d0, d1 = mm_t(pick[0], sides[0]), mm_t(pick[1], sides[1])
            own[f, :, 0:128] = d0[:, :128].astype(BF16)
            own[f, :, 128:256] = d1[:, :128].astype(BF16)
            own[f, :, 256:384] = (d0[:, 128:] + d1[:, 128:]).astype(BF16)
        base = 3 * cols
        per = chan * rows
        for send, last in ((send_even, 1 - info[0]), (send_odd, info[0])):
            begin = last * (2 * rows - 3)
            for k in range(3):
                send[k * cols : (k + 1) * cols] = own[begin + k]
            for t in range(3):
                src = cached[t] if t < 2 else latent[...]
                lat = src.reshape(per, cols)
                send[base : base + per, t * 128 : t * 128 + 128] = lat[:, :128]
                send[base + per : base + 2 * per, t * 128 : t * 128 + cols - 128] = lat[:, 128:]

    return body


def taps_body(info, up, info_out, fwd, back_odd, back_even):
    for k in range(4):
        info_out[k] = info[k]

    def rows_of(q, j):
        parts = ((2,), (1, 2), (0, 1), (0,))[q]
        total = up[parts[0], j].astype(F32)
        for i in parts[1:]:
            total = total + up[i, j].astype(F32)
        return total

    rest = []
    for q in range(4):
        c0, c1, c2 = (rows_of(q, j) for j in range(3))
        tap = [t.astype(BF16) for t in (c2, c1 + c2, c0 + c1, c0)]
        rest.append([t[128:] for t in tap])
        for b, order in ((0, (3, 1)), (1, (2, 0))):
            for side, p in enumerate(order):
                fwd[b, side * 384 : side * 384 + 384, q * 128 : q * 128 + 128] = tap[p][:128].T
                if q % 2 == 1:
                    pair = (q - 1, q) if b == 0 else (q, q - 1)
                    both = jnp.concatenate([rest[k][p] for k in pair], axis=0)
                    at = 512 + (q // 2) * 128
                    fwd[b, side * 384 : side * 384 + 384, at : at + 128] = both.T
        target, side = ((back_odd, 1), (back_even, 0), (back_odd, 0), (back_even, 1))[q]
        lanes = slice(side * 384, side * 384 + 384)
        for block, (p0, p1) in enumerate(((1, 2), (3, 0))):
            base = block * 384
            target[base : base + 128, lanes] = tap[p0][:128]
            target[base + 128 : base + 256, lanes] = tap[p1][:128]
            low, high = (p0, p1) if q % 2 == 0 else (p1, p0)
            target[base + 256 : base + 320, lanes] = tap[low][128:]
            target[base + 320 : base + 384, lanes] = tap[high][128:]


def cached_body(rows, cols, count, width, tokens):
    size = rows * cols

    def body(info, order, features, mid, acc, send_even, send_odd, mid_t, sel, wide):
        for t in range(2):
            for r in range(rows):
                at = slice(r * cols, (r + 1) * cols)
                x = features[t, r]
                x32 = x.astype(F32)
                base = t * 1152
                wide[at, base : base + 384] = from_left(x32).astype(BF16)
                wide[at, base + 384 : base + 768] = x
                wide[at, base + 768 : base + 1152] = from_right(x32).astype(BF16)
        lhs = wide[...]
        kernels = [jnp.concatenate([mid[0, i], mid[1, i]], axis=0) for i in range(3)]
        pair = mm(lhs, jnp.concatenate([kernels[0], kernels[1]], axis=1))
        for i in range(3):
            for j in range(3):
                at = (i * 3 + j) * 384
                mid_t[at : at + 384] = mid[2, i, j * 384 : (j + 1) * 384].T
        placing(info, order, sel, count, width, tokens)
        zero = jnp.zeros((cols, 384), F32)
        acc[0:cols] = zero
        acc[cols : 2 * cols] = zero
        acc[2 * cols :] = pair[:, :384]
        acc[cols : cols + size] += pair[:, 384:]
        acc[0:size] += mm(lhs, kernels[2])
        for send, last in ((send_even, 1 - info[0]), (send_odd, info[0])):
            send[...] = acc[pl.ds(pl.multiple_of(last * 3 * cols, 3 * cols), 3 * cols)].astype(BF16)

    return body


def current_body(rows, cols, chan):
    per = chan * rows
    base = 3 * cols

    def body(info, latent, cached, got_even, got_odd, w_in, mid, gain, hidden, conv, lat, tall, wide, w_order, flat):
        even = info[0] == 0
        lat[...] = jnp.zeros_like(lat)

        def fill(first_row, got, ok):
            scale = ok.astype(F32)
            for t in range(3):
                x = got[base : base + per, t * 128 : t * 128 + 128].astype(F32) * scale
                y = got[base + per : base + 2 * per, t * 128 : t * 128 + cols - 128].astype(F32) * scale
                for r in range(rows):
                    at = pl.ds((first_row + r) * 3 * chan + t * chan, chan)
                    lat[at, 0:128] = x[r * chan : (r + 1) * chan]
                    lat[at, 128:cols] = y[r * chan : (r + 1) * chan]

        @pl.when(even)
        def _():
            fill(0, got_odd, info[1])
            fill(2 * rows, got_even, info[2])

        @pl.when(jnp.logical_not(even))
        def _():
            fill(0, got_even, info[1])
            fill(2 * rows, got_odd, info[2])

        for t in range(3):
            for r in range(rows):
                at = pl.ds((rows + r) * 3 * chan + t * chan, chan)
                lat[at, 0:cols] = (cached[t, r] if t < 2 else latent[r]).astype(F32)

        for r in range(3 * rows):
            for t in range(3):
                x = lat[pl.ds((r * 3 + t) * chan, chan), :]
                at = (r * 3 + t) * 3 * chan
                tall[at : at + chan] = pltpu.roll(x, 1, 1).astype(BF16)
                tall[at + chan : at + 2 * chan] = x.astype(BF16)
                tall[at + 2 * chan : at + 3 * chan] = pltpu.roll(x, 255, 1).astype(BF16)
            flat[r, :, 0 : 9 * chan] = tall[r * 9 * chan : (r + 1) * 9 * chan, 0:cols].T
        for i in range(3):
            for t in range(3):
                at = (i * 3 + t) * 3 * chan
                w_order[at : at + 3 * chan] = w_in[t, i]

        deep = 9 * chan

        def hidden_row(k):
            h = sum(mm(flat[k + i, :, 0:deep], w_order[i * deep : (i + 1) * deep]) for i in range(3))
            h = h.astype(BF16)
            if 1 <= k <= rows + 4:
                hidden[k - 1] = h
            v = h.astype(F32)
            inv = lax.rsqrt(jnp.mean(v * v, axis=1, keepdims=True) + EPS)
            y = v * inv * gain[...]
            act = y * (0.5 * jnp.tanh(0.5 * y) + 0.5)
            if k < 3:
                act = act * flag(info, 1)
            if k >= rows + 3:
                act = act * flag(info, 2)
            at = slice(k * cols, (k + 1) * cols)
            wide[at, 0:384] = from_left(act).astype(BF16)
            wide[at, 384:768] = act.astype(BF16)
            wide[at, 768:1152] = from_right(act).astype(BF16)

        def conv_rows(p, lanes):
            start = 2 * p * cols
            lhs = [wide[start + i * cols : start + (i + 2) * cols] for i in range(3)]
            rhs = [mid[2, i, :, lanes] for i in range(3)]
            conv[start : start + 2 * cols, lanes] = mm(jnp.concatenate(lhs, axis=1), jnp.concatenate(rhs, axis=0))

        def rows_step(k):
            return lambda: hidden_row(k)

        def conv_step(p):
            return [lambda: conv_rows(p, slice(0, 256)), lambda: conv_rows(p, slice(256, 384))]

        for k in range(4):
            hidden_row(k)
        for p in range(rows // 2 + 2):
            after = [rows_step(k) for k in (2 * p + 4, 2 * p + 5) if k < rows + 6]
            weave(conv_step(p), after) if after else weave(conv_step(p))

    return body


def pull_scale(y):
    sig = 0.5 * jnp.tanh(0.5 * y) + 0.5
    return sig * (1.0 + y * (1.0 - sig))


def back_body(rows, cols, chan, count, o):
    deep_rows = rows + 4
    size = rows * cols
    width = 2 * cols // count

    def body(
        info, hidden, conv, acc, got_even, got_odd, packed_even, packed_odd, own, fwd, back_odd, back_even, mid_t, w_in, gain,
        out_gain, payload, reward, edge, p0, p1, g_odd, g_even, wide, t_odd, t_even, back, act_grad, hid, lines,
    ):
        even = info[0] == 0
        top, bottom = flag(info, 1), flag(info, 2)

        def take(got, packed, before):
            ok = top if before else bottom
            place = 0 if before else 3
            for k in range(3):
                at = slice(k * cols, (k + 1) * cols)
                edge[(place + k) * cols : (place + k + 1) * cols] = got[at].astype(F32) * ok
                reward[k if before else 2 * rows + 3 + k] = (packed[at].astype(F32) * ok).astype(BF16)

        @pl.when(even)
        def _():
            take(got_odd, packed_odd, True)
            take(got_even, packed_even, False)

        @pl.when(jnp.logical_not(even))
        def _():
            take(got_even, packed_even, True)
            take(got_odd, packed_odd, False)

        reward[3 : 2 * rows + 3] = own[...]

        def row(ref, k):
            return ref[k * cols : (k + 1) * cols]

        def state_row(k):
            x = hidden[k].astype(F32) + row(conv, k)
            if 1 <= k <= rows + 2:
                x = x + row(acc, k - 1)
            if k < 3:
                x = x + row(edge, k)
            if k >= rows + 1:
                x = x + row(edge, k - rows + 2)
            if k < 2:
                x = x * top
            if k >= rows + 2:
                x = x * bottom
            x = x.astype(BF16)
            x32 = x.astype(F32)
            at = slice(k * cols, (k + 1) * cols)
            wide[at, 0:384] = from_left(x32).astype(BF16)
            wide[at, 384:768] = x
            wide[at, 768:1152] = from_right(x32).astype(BF16)

        def up_dot(p, b, n):
            at = slice(2 * p * cols, (2 * p + 2) * cols)
            lanes = slice(n * 256, n * 256 + 256)
            (p0, p1)[b][at, lanes] = mm(wide[at, b * 384 : b * 384 + 768], fwd[b, :, lanes])

        lane = lax.broadcasted_iota(jnp.int32, (cols, 128), 1)
        low = lane < 64
        gains = [out_gain[:, 0:128], out_gain[:, 128:256]]

        def pull(v0, v1, vm, r, zero_low):
            mine = low if zero_low else jnp.logical_not(low)
            v0, v1, vm = (v.astype(BF16).astype(F32) for v in (v0, v1, vm))

            def both(a0, a1, am):
                s0 = jnp.sum(a0 + jnp.where(mine, am, 0.0), axis=1, keepdims=True)
                s1 = jnp.sum(a1 + jnp.where(mine, 0.0, am), axis=1, keepdims=True)
                return s0 * (1.0 / o), s1 * (1.0 / o)

            q0, q1 = both(v0 * v0, v1 * v1, vm * vm)
            i0, i1 = lax.rsqrt(q0 + EPS), lax.rsqrt(q1 + EPS)
            im = jnp.where(mine, i0, i1)
            out = []
            for v, i, g, k in ((v0, i0, gains[0], 0), (v1, i1, gains[0], 1), (vm, im, gains[1], 2)):
                s = v * i
                y = s * g
                d = r[:, k * 128 : k * 128 + 128].astype(F32) * pull_scale(y) * g
                out.append((s, d))
            m0, m1 = both(*(s * d for s, d in out))
            mx = jnp.where(mine, m0, m1)
            return [i * (d - s * m) for (s, d), i, m in zip(out, (i0, i1, im), (m0, m1, mx))], mine

        def store(g, target, k):
            (a0, a1, am), mine = g
            at = slice(k * cols, (k + 1) * cols)
            target[at, 0:128] = a0.astype(BF16)
            target[at, 128:256] = a1.astype(BF16)
            target[at, 256:384] = am.astype(BF16)
            target[at, 384:512] = from_right(a0).astype(BF16)
            target[at, 512:640] = from_left(a1).astype(BF16)
            target[at, 640:768] = jnp.where(mine, from_right(am), from_left(am)).astype(BF16)

        def pull_odd(k):
            a, b = slice(k * cols, (k + 1) * cols), slice((k + 1) * cols, (k + 2) * cols)
            v0 = p0[a, 256:384] + p0[b, 0:128]
            v1 = p1[a, 256:384] + p1[b, 0:128]
            vm = jnp.where(low, p0[a, 640:768] + p0[b, 512:640], p1[a, 640:768] + p1[b, 512:640])
            store(pull(v0, v1, vm, reward[2 * k], True), g_odd, k)

        def pull_even(k):
            a, b = slice(k * cols, (k + 1) * cols), slice((k + 1) * cols, (k + 2) * cols)
            v0 = p0[b, 128:256] + p0[a, 384:512]
            v1 = p1[b, 128:256] + p1[a, 384:512]
            vm = jnp.where(low, p1[b, 512:640] + p1[a, 640:768], p0[b, 512:640] + p0[a, 640:768])
            store(pull(v0, v1, vm, reward[2 * k + 1], False), g_even, k)

        fine = rows + 3

        def down_dot(first, number, odd, n):
            at = slice(first * cols, (first + number) * cols)
            lanes = slice(n * 256, n * 256 + 256)
            if odd:
                t_odd[at, lanes] = mm(g_odd[at], back_odd[:, lanes])
            else:
                t_even[at, lanes] = mm(g_even[at], back_even[:, lanes])

        def block_row(k):
            a, b = slice(k * cols, (k + 1) * cols), slice((k + 1) * cols, (k + 2) * cols)
            x = t_odd[b, 0:384] + t_odd[a, 384:768] + t_even[a, 0:384] + t_even[b, 384:768]
            if k == 0:
                x = x * top
            if k == rows + 1:
                x = x * bottom
            x = x.astype(BF16)
            x32 = x.astype(F32)
            back[a, 0:384] = from_right(x32).astype(BF16)
            back[a, 384:768] = x
            back[a, 768:1152] = from_left(x32).astype(BF16)

        def mid_dot(p, n):
            lanes = slice(n * 256, min(384, n * 256 + 256))
            lhs = [back[(2 * p + 2 - i) * cols : (2 * p + 4 - i) * cols] for i in range(3)]
            at = slice(2 * p * cols, (2 * p + 2) * cols)
            act_grad[at, lanes] = mm(jnp.concatenate(lhs, axis=1), mid_t[:, lanes])

        def hidden_pull(k):
            g = gain[...]
            at = slice(k * cols, (k + 1) * cols)
            v = hidden[k + 2].astype(F32)
            inv = lax.rsqrt(jnp.mean(v * v, axis=1, keepdims=True) + EPS)
            s = v * inv
            d = act_grad[at] * pull_scale(s * g) * g
            dv = inv * (d - s * jnp.mean(d * s, axis=1, keepdims=True))
            block = back[(k + 1) * cols : (k + 2) * cols, 384:768].astype(F32)
            hid[at] = (block + dv).astype(BF16)

        def steps(f, *keys):
            return [lambda key=key: f(*key) for key in keys]

        def ups(p):
            return steps(up_dot, *[(p, b, n) for n in range(3) for b in range(2)])

        def downs(first, number):
            return steps(down_dot, *[(first, number, odd, n) for odd in (True, False) for n in range(3)])

        def pulls(*ks):
            return [step for k in ks for step in steps(pull_odd, (k,)) + steps(pull_even, (k,))]

        state_row(0)
        state_row(1)
        weave(ups(0), steps(state_row, (2,), (3,)))
        weave(ups(1), steps(state_row, (4,), (5,)) + pulls(0))
        weave(ups(2), steps(state_row, (6,), (7,)) + pulls(1, 2))
        weave(ups(3) + downs(0, 2), pulls(3, 4))
        weave(downs(2, 2), pulls(5, 6) + steps(block_row, (0,)))
        weave(downs(4, 3), steps(block_row, (1,), (2,)))
        block_row(3)
        weave(steps(mid_dot, (0, 0), (0, 1)), steps(block_row, (4,), (5,)))
        weave(steps(mid_dot, (1, 0), (1, 1)), steps(hidden_pull, (0,), (1,)))
        hidden_pull(2)
        hidden_pull(3)

        z = mm_t(w_in[...], hid[...])
        place = lax.broadcasted_iota(jnp.int32, (chan, size), 1)
        col = lax.rem(place, cols)
        sums = []
        for i in range(3):
            z0, z1, z2 = (z[(i * 3 + j) * chan : (i * 3 + j + 1) * chan] for j in range(3))
            left = jnp.where(col == cols - 1, 0.0, pltpu.roll(z0, size - 1, 1))
            right = jnp.where(col == 0, 0.0, pltpu.roll(z2, 1, 1))
            sums.append(left + z1 + right)
        inner = sums[1]
        inner = inner + jnp.where(place < size - cols, pltpu.roll(sums[0], size - cols, 1), 0.0)
        inner = inner + jnp.where(place >= cols, pltpu.roll(sums[2], cols, 1), 0.0)
        lines[0:chan] = inner
        lines[chan : 2 * chan] = sums[0]
        lines[2 * chan : 3 * chan] = sums[2]
        per_row = count // 2
        for u in range(count):
            pair, piece = u // per_row, u % per_row
            parts = []
            for a in range(2):
                at = (2 * pair + a) * cols + piece * width
                parts.append(lines[0:chan, at : at + width])
            at = piece * width + (0 if pair else (rows - 1) * cols)
            first = chan if pair else 2 * chan
            parts.append(lines[first : first + chan, at : at + width])
            parts.append(jnp.zeros((chan, 128 - 3 * width), F32))
            payload[u] = jnp.concatenate(parts, axis=1).astype(BF16)

    return body


def placing(info, order, sel, count, width, tokens):
    piece = width // 2
    pair = info[3]
    lane = lax.broadcasted_iota(jnp.int32, (128, 4 * tokens), 0)
    column = lax.broadcasted_iota(jnp.int32, (128, 4 * tokens), 1)
    group = (lane >= width).astype(jnp.int32) + (lane >= 2 * width).astype(jnp.int32)
    w = lane - group * width
    part = jnp.where(group == 2, pair, group)
    fixed = (2 * part + (w & 1)) * tokens + (w >> 1) - column
    fixed = jnp.where(lane < 3 * width, fixed, -99999)
    for t in range(count):
        step = t + 1 - 2 * pair
        valid = jnp.logical_and(step >= 0, step < count)
        beside = jnp.where(valid, piece * order[jnp.clip(step, 0, count - 1)], -9999)
        begin = jnp.where(group == 2, beside, piece * order[t])
        sel[t] = (fixed + begin == 0).astype(F32).astype(BF16)


def place_body(count, chan, tokens):
    def body(sel, got, out):
        total = mm(got[0], sel[0])
        for t in range(1, count):
            total += mm(got[t], sel[t])
        for k in range(4):
            out[k * chan : (k + 1) * chan] = total[:, k * tokens : (k + 1) * tokens]

    return body


def swaps(count):
    within = [(i, i ^ 1) for i in range(count)]
    across = [(0, 0), (count - 1, count - 1)]
    for i in range(1, count - 1, 2):
        across += [(i, i + 1), (i + 1, i)]
    return within, sorted(across)


def shards(
    latent, cached_latent, cached_features, reward_grad, conv_in_weight, conv_mid_weight, conv_up_weight, norm_gain, out_gain, shard_order
):
    count = lax.axis_size("tile")
    rows, cols, chan = latent.shape
    mid_chan = norm_gain.shape[0]
    o = out_gain.shape[0]
    tile = lax.axis_index("tile")
    info = jnp.stack(
        [tile % 2, (tile > 0).astype(jnp.int32), (tile < count - 1).astype(jnp.int32), (tile >= count // 2).astype(jnp.int32)]
    ).astype(jnp.int32)
    lat = jnp.transpose(latent, (0, 2, 1))
    lat_cached = jnp.transpose(cached_latent, (0, 1, 3, 2))
    reward_t = jnp.transpose(reward_grad, (0, 2, 1))
    up_t = jnp.transpose(conv_up_weight, (0, 1, 3, 2))
    mid = conv_mid_weight.reshape(3, 3, 3 * mid_chan, mid_chan)
    w_in = conv_in_weight.reshape(3, 3, 3 * chan, mid_chan)
    gain = norm_gain.reshape(1, mid_chan)
    gain_out = jnp.concatenate([out_gain, out_gain[128:]]).reshape(1, 256)
    within, across = swaps(count)
    size = rows * cols
    edge_rows = 3 * cols + 2 * chan * rows

    info, fwd, back_odd, back_even = call(
        taps_body,
        [((4,), jnp.int32), ((2, 768, 768), BF16), ((768, 768), BF16), ((768, 768), BF16)],
        1, 1, [], 1e10, 16, 1,
    )(info, up_t)

    own, send_even, send_odd = call(
        pack_body(rows, cols, o, chan),
        [((2 * rows, cols, 384), BF16), ((edge_rows, 384), BF16), ((edge_rows, 384), BF16)],
        1, 3, [], 1e10, 16,
    )(info, reward_t, lat, lat_cached)
    packed_even = lax.ppermute(send_even, "tile", within)
    packed_odd = lax.ppermute(send_odd, "tile", across)

    width = 2 * cols // count
    tokens = size // 4
    acc, part_even, part_odd, mid_t, sel = call(
        cached_body(rows, cols, count, width, tokens),
        [
            ((6 * cols, 384), F32), ((3 * cols, 384), BF16), ((3 * cols, 384), BF16), ((3456, 384), BF16),
            ((count, 128, 4 * tokens), BF16),
        ],
        2, 2, [pltpu.VMEM((size, 2304), BF16)], 4e9, 24,
    )(info, shard_order, cached_features, mid)
    got_even = lax.ppermute(part_even, "tile", within)
    got_odd = lax.ppermute(part_odd, "tile", across)

    hidden, conv = call(
        current_body(rows, cols, chan),
        [((rows + 4, cols, 384), BF16), ((2 * size, 384), F32)],
        1, 7,
        [
            pltpu.VMEM((9 * rows * chan, 256), F32),
            pltpu.VMEM((27 * rows * chan, 256), BF16),
            pltpu.VMEM(((rows + 6) * cols, 1152), BF16),
            pltpu.VMEM((27 * chan, 384), BF16),
            pltpu.VMEM((3 * rows, cols, 256), BF16),
        ],
        5e9, 24,
    )(info, lat, lat_cached, packed_even, packed_odd, w_in, mid, gain)

    (payload,) = call(
        back_body(rows, cols, chan, count, o),
        [((count, chan, 128), BF16)],
        1, 15,
        [
            pltpu.VMEM((2 * rows + 6, cols, 384), BF16),
            pltpu.VMEM((6 * cols, 384), F32),
            pltpu.VMEM(((rows + 4) * cols, 768), F32),
            pltpu.VMEM(((rows + 4) * cols, 768), F32),
            pltpu.VMEM(((rows + 3) * cols, 768), BF16),
            pltpu.VMEM(((rows + 3) * cols, 768), BF16),
            pltpu.VMEM(((rows + 4) * cols, 1152), BF16),
            pltpu.VMEM(((rows + 3) * cols, 768), F32),
            pltpu.VMEM(((rows + 3) * cols, 768), F32),
            pltpu.VMEM(((rows + 2) * cols, 1152), BF16),
            pltpu.VMEM((size, 384), F32),
            pltpu.VMEM((size, 384), BF16),
            pltpu.VMEM((3 * chan, size), F32),
        ],
        8e9, 36,
    )(
        info, hidden, conv, acc, got_even, got_odd, packed_even, packed_odd, own, fwd, back_odd, back_even, mid_t,
        w_in[2].reshape(9 * chan, mid_chan), gain, gain_out,
    )
    received = lax.all_to_all(payload, "tile", split_axis=0, concat_axis=0, tiled=True)
    (placed,) = call(place_body(count, chan, tokens), [((4 * chan, tokens), F32)], 0, 2, [], 1e7, 16)(sel, received)
    return placed.T


def solution(mesh):
    return jax.shard_map(
        shards,
        mesh=mesh,
        in_specs=(
            P(("prompt", "tile"), None, None),
            P(None, ("prompt", "tile"), None, None),
            P(None, ("prompt", "tile"), None, None),
            P(("prompt", "tile"), None, None),
            P(),
            P(),
            P(),
            P(),
            P(),
            P("prompt"),
        ),
        out_specs=P(("prompt", "tile"), None),
        check_vma=False,
    )
```

```python
import jax
import jax.numpy as jnp
from jax import lax
from jax.experimental import pallas as pl
from jax.experimental.pallas import tpu as pltpu
from jax.sharding import PartitionSpec as P

EPS = 1e-06
F32 = jnp.float32
BF16 = jnp.bfloat16
VM = pl.BlockSpec(memory_space=pltpu.VMEM)
SM = pl.BlockSpec(memory_space=pltpu.SMEM)


def call(body, outs, n_smem, n_vmem, scratch, flops, limit, smem_outs=0):
    specs = [SM] * n_smem + [VM] * n_vmem
    return pl.pallas_call(
        body,
        out_shape=[jax.ShapeDtypeStruct(s, d) for s, d in outs],
        in_specs=specs,
        out_specs=[SM] * smem_outs + [VM] * (len(outs) - smem_outs),
        scratch_shapes=scratch,
        cost_estimate=pl.CostEstimate(flops=int(flops), bytes_accessed=2**20, transcendentals=0),
        compiler_params=pltpu.CompilerParams(vmem_limit_bytes=limit << 20),
    )


def mm(a, b):
    return jnp.dot(a, b, preferred_element_type=F32)


def mm_t(a, b):
    return lax.dot_general(a, b, (((1,), (1,)), ((), ())), preferred_element_type=F32)


def flag(info, k):
    return info[k].astype(F32)


def col_index(cols, lanes):
    return lax.broadcasted_iota(jnp.int32, (cols, lanes), 0)


def from_left(x):
    col = col_index(*x.shape)
    return jnp.where(col == 0, 0.0, pltpu.roll(x, 1, 0))


def from_right(x):
    cols = x.shape[0]
    col = col_index(*x.shape)
    return jnp.where(col == cols - 1, 0.0, pltpu.roll(x, cols - 1, 0))


def pack_body(rows, cols, o, chan):
    half = o - 128

    def body(info, reward, latent, cached, own, send_even, send_odd):
        x_index = lax.broadcasted_iota(jnp.int32, (cols, 2 * cols), 1)
        w_index = lax.broadcasted_iota(jnp.int32, (cols, 2 * cols), 0)
        pick = [(x_index == 2 * w_index + b).astype(F32).astype(BF16) for b in (0, 1)]
        zeros = jnp.zeros((128 - half, 2 * cols), BF16)
        for f in range(2 * rows):
            r = reward[f]
            first, rest = r[:128], r[128:]
            low = jnp.concatenate([first, rest, zeros], axis=0)
            high = jnp.concatenate([first, zeros, rest], axis=0)
            sides = (low, high) if f % 2 else (high, low)
            d0, d1 = mm_t(pick[0], sides[0]), mm_t(pick[1], sides[1])
            own[f, :, 0:128] = d0[:, :128].astype(BF16)
            own[f, :, 128:256] = d1[:, :128].astype(BF16)
            own[f, :, 256:384] = (d0[:, 128:] + d1[:, 128:]).astype(BF16)
        base = 3 * cols
        per = chan * rows
        for send, last in ((send_even, 1 - info[0]), (send_odd, info[0])):
            begin = last * (2 * rows - 3)
            for k in range(3):
                send[k * cols : (k + 1) * cols] = own[begin + k]
            for t in range(3):
                src = cached[t] if t < 2 else latent[...]
                lat = src.reshape(per, cols)
                send[base : base + per, t * 128 : t * 128 + 128] = lat[:, :128]
                send[base + per : base + 2 * per, t * 128 : t * 128 + cols - 128] = lat[:, 128:]

    return body


def taps_body(info, up, info_out, fwd, back_odd, back_even):
    for k in range(4):
        info_out[k] = info[k]

    def rows_of(q, j):
        parts = ((2,), (1, 2), (0, 1), (0,))[q]
        total = up[parts[0], j].astype(F32)
        for i in parts[1:]:
            total = total + up[i, j].astype(F32)
        return total

    rest = []
    for q in range(4):
        c0, c1, c2 = (rows_of(q, j) for j in range(3))
        tap = [t.astype(BF16) for t in (c2, c1 + c2, c0 + c1, c0)]
        rest.append([t[128:] for t in tap])
        for b, order in ((0, (3, 1)), (1, (2, 0))):
            for side, p in enumerate(order):
                fwd[b, side * 384 : side * 384 + 384, q * 128 : q * 128 + 128] = tap[p][:128].T
                if q % 2 == 1:
                    pair = (q - 1, q) if b == 0 else (q, q - 1)
                    both = jnp.concatenate([rest[k][p] for k in pair], axis=0)
                    at = 512 + (q // 2) * 128
                    fwd[b, side * 384 : side * 384 + 384, at : at + 128] = both.T
        target, side = ((back_odd, 1), (back_even, 0), (back_odd, 0), (back_even, 1))[q]
        lanes = slice(side * 384, side * 384 + 384)
        for block, (p0, p1) in enumerate(((1, 2), (3, 0))):
            base = block * 384
            target[base : base + 128, lanes] = tap[p0][:128]
            target[base + 128 : base + 256, lanes] = tap[p1][:128]
            low, high = (p0, p1) if q % 2 == 0 else (p1, p0)
            target[base + 256 : base + 320, lanes] = tap[low][128:]
            target[base + 320 : base + 384, lanes] = tap[high][128:]


def cached_body(rows, cols, count, width, tokens):
    size = rows * cols

    def body(info, order, features, mid, acc, send_even, send_odd, mid_t, sel, wide):
        for t in range(2):
            for r in range(rows):
                at = slice(r * cols, (r + 1) * cols)
                x = features[t, r]
                x32 = x.astype(F32)
                base = t * 1152
                wide[at, base : base + 384] = from_left(x32).astype(BF16)
                wide[at, base + 384 : base + 768] = x
                wide[at, base + 768 : base + 1152] = from_right(x32).astype(BF16)
        lhs = wide[...]
        kernels = [jnp.concatenate([mid[0, i], mid[1, i]], axis=0) for i in range(3)]
        pair = mm(lhs, jnp.concatenate([kernels[0], kernels[1]], axis=1))
        for i in range(3):
            for j in range(3):
                at = (i * 3 + j) * 384
                mid_t[at : at + 384] = mid[2, i, j * 384 : (j + 1) * 384].T
        placing(info, order, sel, count, width, tokens)
        last_kernel = mm(lhs, kernels[2])
        for k in range(rows + 4):
            total = jnp.zeros((cols, 384), F32)
            for i, part in enumerate((pair[:, :384], pair[:, 384:], last_kernel)):
                r = k - 3 + i
                if 0 <= r < rows:
                    total = total + part[r * cols : (r + 1) * cols]
            acc[k] = total
        for send, last in ((send_even, 1 - info[0]), (send_odd, info[0])):
            for k in range(3):
                send[k * cols : (k + 1) * cols] = acc[1 + last * 3 + k].astype(BF16)

    return body


def current_body(rows, cols, chan):
    per = chan * rows
    base = 3 * cols

    def body(info, latent, cached, got_even, got_odd, w_in, mid, half_gain, hidden, conv, lat, tall, wide, w_order):
        even = info[0] == 0
        lat[...] = jnp.zeros_like(lat)

        def fill(first_row, got, ok):
            scale = ok.astype(F32)
            for t in range(3):
                x = got[base : base + per, t * 128 : t * 128 + 128].astype(F32) * scale
                y = got[base + per : base + 2 * per, t * 128 : t * 128 + cols - 128].astype(F32) * scale
                for r in range(rows):
                    at = pl.ds((first_row + r) * 3 * chan + t * chan, chan)
                    lat[at, 0:128] = x[r * chan : (r + 1) * chan]
                    lat[at, 128:cols] = y[r * chan : (r + 1) * chan]

        @pl.when(even)
        def _():
            fill(0, got_odd, info[1])
            fill(2 * rows, got_even, info[2])

        @pl.when(jnp.logical_not(even))
        def _():
            fill(0, got_even, info[1])
            fill(2 * rows, got_odd, info[2])

        for t in range(3):
            for r in range(rows):
                at = pl.ds((rows + r) * 3 * chan + t * chan, chan)
                lat[at, 0:cols] = (cached[t, r] if t < 2 else latent[r]).astype(F32)

        for r in range(3 * rows):
            for t in range(3):
                x = lat[pl.ds((r * 3 + t) * chan, chan), :]
                at = t * 3 * chan
                tall[r, at : at + chan] = pltpu.roll(x, 1, 1).astype(BF16)
                tall[r, at + chan : at + 2 * chan] = x.astype(BF16)
                tall[r, at + 2 * chan : at + 3 * chan] = pltpu.roll(x, 255, 1).astype(BF16)
        for i in range(3):
            for t in range(3):
                at = (i * 3 + t) * 3 * chan
                w_order[at : at + 3 * chan] = w_in[t, i]

        def hidden_row(k):
            lhs = tall[pl.ds(k, 3)].reshape(27 * chan, 256)[:, 0:cols]
            h = lax.dot_general(lhs, w_order[...], (((0,), (0,)), ((), ())), preferred_element_type=F32)
            h = h.astype(BF16)
            hidden[k] = h
            v = h.astype(F32)
            inv = lax.rsqrt(jnp.mean(v * v, axis=1, keepdims=True) + EPS)
            half = v * inv * half_gain[...]
            inside = jnp.where(k < 3, info[1], jnp.where(k >= rows + 3, info[2], 1)).astype(F32)
            act = half * (jnp.tanh(half) + 1.0) * inside
            wide[k, :, 0:384] = from_left(act).astype(BF16)
            wide[k, :, 384:768] = act.astype(BF16)
            wide[k, :, 768:1152] = from_right(act).astype(BF16)

        def conv_row(p):
            lhs = jnp.concatenate([wide[p], wide[p + 1], wide[p + 2]], axis=1)
            conv[p] = mm(lhs, mid[2].reshape(3456, 384))

        @pl.loop(0, 3)
        def _(k):
            hidden_row(k)

        @pl.loop(3, rows + 6)
        def _(k):
            conv_row(k - 3)
            hidden_row(k)

        conv_row(rows + 3)

    return body


def pulled(s, half_gain, grad):
    h = s * half_gain
    t = jnp.tanh(h)
    return (grad * half_gain) * ((1.0 + t) * (1.0 + h * (1.0 - t)))


def back_body(rows, cols, chan, count, o):
    size = rows * cols
    width = 2 * cols // count

    def body(
        info, hidden, conv, acc, got_even, got_odd, packed_even, packed_odd, own, fwd, back_odd, back_even, mid_t, w_in, half_gain,
        half_out, payload, reward, edge, p0, p1, g_odd, g_even, wide, t_odd, t_even, back, act_grad, hid, lines,
    ):
        even = info[0] == 0
        top, bottom = flag(info, 1), flag(info, 2)

        def take(got, packed, before):
            ok = top if before else bottom
            place = 0 if before else rows + 1
            for k in range(3):
                at = slice(k * cols, (k + 1) * cols)
                edge[place + k] = got[at].astype(F32) * ok
                reward[k if before else 2 * rows + 3 + k] = (packed[at].astype(F32) * ok).astype(BF16)

        for k in range(3, rows + 1):
            edge[k] = jnp.zeros((cols, 384), F32)

        @pl.when(even)
        def _():
            take(got_odd, packed_odd, True)
            take(got_even, packed_even, False)

        @pl.when(jnp.logical_not(even))
        def _():
            take(got_even, packed_even, True)
            take(got_odd, packed_odd, False)

        reward[3 : 2 * rows + 3] = own[...]

        def inside(k, first, last):
            return jnp.where(k < first, info[1], jnp.where(k >= last, info[2], 1)).astype(F32)

        def spread(ref, k, x, ahead):
            x = x.astype(BF16)
            x32 = x.astype(F32)
            sides = (from_right(x32), from_left(x32)) if ahead else (from_left(x32), from_right(x32))
            ref[k, :, 0:384] = sides[0].astype(BF16)
            ref[k, :, 384:768] = x
            ref[k, :, 768:1152] = sides[1].astype(BF16)

        def state_row(k):
            x = hidden[k + 1].astype(F32) + conv[k] + acc[k] + edge[k]
            spread(wide, k, x * inside(k, 2, rows + 2), False)

        def up_row(k):
            p0[k] = mm(wide[k, :, 0:768], fwd[0])
            p1[k] = mm(wide[k, :, 384:1152], fwd[1])

        lane = lax.broadcasted_iota(jnp.int32, (cols, 128), 1)
        low = lane < 64
        gains = [half_out[:, 0:128], half_out[:, 128:256]]

        def pull(v0, v1, vm, r, zero_low):
            mine = low if zero_low else jnp.logical_not(low)
            def both(a0, a1, am):
                s0 = jnp.sum(a0 + jnp.where(mine, am, 0.0), axis=1, keepdims=True)
                s1 = jnp.sum(a1 + jnp.where(mine, 0.0, am), axis=1, keepdims=True)
                return s0 * (1.0 / o), s1 * (1.0 / o)

            q0, q1 = both(v0 * v0, v1 * v1, vm * vm)
            i0, i1 = lax.rsqrt(q0 + EPS), lax.rsqrt(q1 + EPS)
            im = jnp.where(mine, i0, i1)
            out = []
            for v, i, g, k in ((v0, i0, gains[0], 0), (v1, i1, gains[0], 1), (vm, im, gains[1], 2)):
                s = v * i
                out.append((s, pulled(s, g, r[:, k * 128 : k * 128 + 128].astype(F32))))
            m0, m1 = both(*(s * d for s, d in out))
            mx = jnp.where(mine, m0, m1)
            return [i * (d - s * m) for (s, d), i, m in zip(out, (i0, i1, im), (m0, m1, mx))], mine

        def store(g, target, k):
            (a0, a1, am), mine = g
            target[k, :, 0:128] = a0.astype(BF16)
            target[k, :, 128:256] = a1.astype(BF16)
            target[k, :, 256:384] = am.astype(BF16)
            target[k, :, 384:512] = from_right(a0).astype(BF16)
            target[k, :, 512:640] = from_left(a1).astype(BF16)
            target[k, :, 640:768] = jnp.where(mine, from_right(am), from_left(am)).astype(BF16)

        def pull_rows(k):
            v0 = p0[k, :, 256:384] + p0[k + 1, :, 0:128]
            v1 = p1[k, :, 256:384] + p1[k + 1, :, 0:128]
            vm = jnp.where(low, p0[k, :, 640:768] + p0[k + 1, :, 512:640], p1[k, :, 640:768] + p1[k + 1, :, 512:640])
            store(pull(v0, v1, vm, reward[2 * k], True), g_odd, k)
            v0 = p0[k + 1, :, 128:256] + p0[k, :, 384:512]
            v1 = p1[k + 1, :, 128:256] + p1[k, :, 384:512]
            vm = jnp.where(low, p1[k + 1, :, 512:640] + p1[k, :, 640:768], p0[k + 1, :, 512:640] + p0[k, :, 640:768])
            store(pull(v0, v1, vm, reward[2 * k + 1], False), g_even, k)

        def down_row(k):
            t_odd[k] = mm(g_odd[k], back_odd[...])
            t_even[k] = mm(g_even[k], back_even[...])

        def block_row(k):
            x = t_odd[k + 1, :, 0:384] + t_odd[k, :, 384:768] + t_even[k, :, 0:384] + t_even[k + 1, :, 384:768]
            spread(back, k, x * inside(k, 1, rows + 1), True)

        def mid_row(p):
            act_grad[p] = mm(jnp.concatenate([back[p + 2], back[p + 1], back[p]], axis=1), mid_t[...])

        def hidden_pull(k):
            v = hidden[k + 3].astype(F32)
            inv = lax.rsqrt(jnp.mean(v * v, axis=1, keepdims=True) + EPS)
            s = v * inv
            d = pulled(s, half_gain[...], act_grad[k])
            dv = inv * (d - s * jnp.mean(d * s, axis=1, keepdims=True))
            hid[k] = (back[k + 1, :, 384:768].astype(F32) + dv).astype(BF16)

        fine = rows + 3

        @pl.loop(0, 4)
        def _(k):
            state_row(k)

        @pl.loop(0, 2)
        def _(k):
            up_row(k)

        up_row(2)
        pull_rows(0)

        @pl.loop(1, fine - 1)
        def _(k):
            up_row(k + 2)
            pull_rows(k)
            down_row(k - 1)
            state_row(jnp.minimum(k + 3, rows + 3))

        pull_rows(fine - 1)
        down_row(fine - 2)
        down_row(fine - 1)

        @pl.loop(0, 3)
        def _(k):
            block_row(k)

        @pl.loop(0, rows - 1)
        def _(p):
            mid_row(p)
            block_row(p + 3)

        mid_row(rows - 1)
        for k in range(rows):
            hidden_pull(k)

        z = mm_t(w_in[...], hid[...].reshape(size, 384))
        place = lax.broadcasted_iota(jnp.int32, (chan, size), 1)
        col = lax.rem(place, cols)
        sums = []
        for i in range(3):
            z0, z1, z2 = (z[(i * 3 + j) * chan : (i * 3 + j + 1) * chan] for j in range(3))
            left = jnp.where(col == cols - 1, 0.0, pltpu.roll(z0, size - 1, 1))
            right = jnp.where(col == 0, 0.0, pltpu.roll(z2, 1, 1))
            sums.append(left + z1 + right)
        inner = sums[1]
        inner = inner + jnp.where(place < size - cols, pltpu.roll(sums[0], size - cols, 1), 0.0)
        inner = inner + jnp.where(place >= cols, pltpu.roll(sums[2], cols, 1), 0.0)
        lines[0:chan] = inner
        lines[chan : 2 * chan] = sums[0]
        lines[2 * chan : 3 * chan] = sums[2]
        per_row = count // 2
        for u in range(count):
            pair, piece = u // per_row, u % per_row
            parts = []
            for a in range(2):
                at = (2 * pair + a) * cols + piece * width
                parts.append(lines[0:chan, at : at + width])
            at = piece * width + (0 if pair else (rows - 1) * cols)
            first = chan if pair else 2 * chan
            parts.append(lines[first : first + chan, at : at + width])
            parts.append(jnp.zeros((chan, 128 - 3 * width), F32))
            payload[u] = jnp.concatenate(parts, axis=1).astype(BF16)

    return body


def placing(info, order, sel, count, width, tokens):
    piece = width // 2
    pair = info[3]
    lane = lax.broadcasted_iota(jnp.int32, (128, 4 * tokens), 0)
    column = lax.broadcasted_iota(jnp.int32, (128, 4 * tokens), 1)
    group = (lane >= width).astype(jnp.int32) + (lane >= 2 * width).astype(jnp.int32)
    w = lane - group * width
    part = jnp.where(group == 2, pair, group)
    fixed = (2 * part + (w & 1)) * tokens + (w >> 1) - column
    fixed = jnp.where(lane < 3 * width, fixed, -99999)
    for t in range(count):
        step = t + 1 - 2 * pair
        valid = jnp.logical_and(step >= 0, step < count)
        beside = jnp.where(valid, piece * order[jnp.clip(step, 0, count - 1)], -9999)
        begin = jnp.where(group == 2, beside, piece * order[t])
        sel[t] = (fixed + begin == 0).astype(F32).astype(BF16)


def place_body(count, chan, tokens):
    def body(sel, got, out):
        total = mm(got[0], sel[0])
        for t in range(1, count):
            total += mm(got[t], sel[t])
        for k in range(4):
            out[k * chan : (k + 1) * chan] = total[:, k * tokens : (k + 1) * tokens]

    return body


def swaps(count):
    within = [(i, i ^ 1) for i in range(count)]
    across = [(0, 0), (count - 1, count - 1)]
    for i in range(1, count - 1, 2):
        across += [(i, i + 1), (i + 1, i)]
    return within, sorted(across)


def shards(
    latent, cached_latent, cached_features, reward_grad, conv_in_weight, conv_mid_weight, conv_up_weight, norm_gain, out_gain, shard_order
):
    count = lax.axis_size("tile")
    rows, cols, chan = latent.shape
    mid_chan = norm_gain.shape[0]
    o = out_gain.shape[0]
    tile = lax.axis_index("tile")
    info = jnp.stack(
        [tile % 2, (tile > 0).astype(jnp.int32), (tile < count - 1).astype(jnp.int32), (tile >= count // 2).astype(jnp.int32)]
    ).astype(jnp.int32)
    lat = jnp.transpose(latent, (0, 2, 1))
    lat_cached = jnp.transpose(cached_latent, (0, 1, 3, 2))
    reward_t = jnp.transpose(reward_grad, (0, 2, 1))
    up_t = jnp.transpose(conv_up_weight, (0, 1, 3, 2))
    mid = conv_mid_weight.reshape(3, 3, 3 * mid_chan, mid_chan)
    w_in = conv_in_weight.reshape(3, 3, 3 * chan, mid_chan)
    gain = 0.5 * norm_gain.reshape(1, mid_chan)
    gain_out = 0.5 * jnp.concatenate([out_gain, out_gain[128:]]).reshape(1, 256)
    within, across = swaps(count)
    size = rows * cols
    edge_rows = 3 * cols + 2 * chan * rows

    info, fwd, back_odd, back_even = call(
        taps_body,
        [((4,), jnp.int32), ((2, 768, 768), BF16), ((768, 768), BF16), ((768, 768), BF16)],
        1, 1, [], 1e10, 16, 1,
    )(info, up_t)

    own, send_even, send_odd = call(
        pack_body(rows, cols, o, chan),
        [((2 * rows, cols, 384), BF16), ((edge_rows, 384), BF16), ((edge_rows, 384), BF16)],
        1, 3, [], 1e10, 16,
    )(info, reward_t, lat, lat_cached)
    packed_even = lax.ppermute(send_even, "tile", within)
    packed_odd = lax.ppermute(send_odd, "tile", across)

    width = 2 * cols // count
    tokens = size // 4
    acc, part_even, part_odd, mid_t, sel = call(
        cached_body(rows, cols, count, width, tokens),
        [
            ((rows + 4, cols, 384), F32), ((3 * cols, 384), BF16), ((3 * cols, 384), BF16), ((3456, 384), BF16),
            ((count, 128, 4 * tokens), BF16),
        ],
        2, 2, [pltpu.VMEM((size, 2304), BF16)], 4e9, 24,
    )(info, shard_order, cached_features, mid)
    got_even = lax.ppermute(part_even, "tile", within)
    got_odd = lax.ppermute(part_odd, "tile", across)

    hidden, conv = call(
        current_body(rows, cols, chan),
        [((rows + 6, cols, 384), BF16), ((rows + 4, cols, 384), F32)],
        1, 7,
        [
            pltpu.VMEM((9 * rows * chan, 256), F32),
            pltpu.VMEM((3 * rows, 9 * chan, 256), BF16),
            pltpu.VMEM((rows + 6, cols, 1152), BF16),
            pltpu.VMEM((27 * chan, 384), BF16),
        ],
        5e9, 24,
    )(info, lat, lat_cached, packed_even, packed_odd, w_in, mid, gain)

    (payload,) = call(
        back_body(rows, cols, chan, count, o),
        [((count, chan, 128), BF16)],
        1, 15,
        [
            pltpu.VMEM((2 * rows + 6, cols, 384), BF16),
            pltpu.VMEM((rows + 4, cols, 384), F32),
            pltpu.VMEM((rows + 4, cols, 768), F32),
            pltpu.VMEM((rows + 4, cols, 768), F32),
            pltpu.VMEM((rows + 3, cols, 768), BF16),
            pltpu.VMEM((rows + 3, cols, 768), BF16),
            pltpu.VMEM((rows + 4, cols, 1152), BF16),
            pltpu.VMEM((rows + 3, cols, 768), F32),
            pltpu.VMEM((rows + 3, cols, 768), F32),
            pltpu.VMEM((rows + 2, cols, 1152), BF16),
            pltpu.VMEM((rows, cols, 384), F32),
            pltpu.VMEM((rows, cols, 384), BF16),
            pltpu.VMEM((3 * chan, size), F32),
        ],
        8e9, 36,
    )(
        info, hidden, conv, acc, got_even, got_odd, packed_even, packed_odd, own, fwd, back_odd, back_even, mid_t,
        w_in[2].reshape(9 * chan, mid_chan), gain, gain_out,
    )
    received = lax.all_to_all(payload, "tile", split_axis=0, concat_axis=0, tiled=True)
    (placed,) = call(place_body(count, chan, tokens), [((4 * chan, tokens), F32)], 0, 2, [], 1e7, 16)(sel, received)
    return placed.T


def solution(mesh):
    return jax.shard_map(
        shards,
        mesh=mesh,
        in_specs=(
            P(("prompt", "tile"), None, None),
            P(None, ("prompt", "tile"), None, None),
            P(None, ("prompt", "tile"), None, None),
            P(("prompt", "tile"), None, None),
            P(),
            P(),
            P(),
            P(),
            P(),
            P("prompt"),
        ),
        out_specs=P(("prompt", "tile"), None),
        check_vma=False,
    )
```

```python
import jax
import jax.numpy as jnp
from jax import lax
from jax.experimental import pallas as pl
from jax.experimental.pallas import tpu as pltpu
from jax.sharding import PartitionSpec as P

EPS = 1e-06
F32 = jnp.float32
BF16 = jnp.bfloat16
VM = pl.BlockSpec(memory_space=pltpu.VMEM)
SM = pl.BlockSpec(memory_space=pltpu.SMEM)


def call(body, outs, n_smem, n_vmem, scratch, flops, limit, smem_outs=0):
    specs = [SM] * n_smem + [VM] * n_vmem
    return pl.pallas_call(
        body,
        out_shape=[jax.ShapeDtypeStruct(s, d) for s, d in outs],
        in_specs=specs,
        out_specs=[SM] * smem_outs + [VM] * (len(outs) - smem_outs),
        scratch_shapes=scratch,
        cost_estimate=pl.CostEstimate(flops=int(flops), bytes_accessed=2**20, transcendentals=0),
        compiler_params=pltpu.CompilerParams(vmem_limit_bytes=limit << 20),
    )


def mm(a, b):
    return jnp.dot(a, b, preferred_element_type=F32)


def mm_t(a, b):
    return lax.dot_general(a, b, (((1,), (1,)), ((), ())), preferred_element_type=F32)


def flag(info, k):
    return info[k].astype(F32)


def col_index(cols, lanes):
    return lax.broadcasted_iota(jnp.int32, (cols, lanes), 0)


def from_left(x):
    col = col_index(*x.shape)
    return jnp.where(col == 0, 0.0, pltpu.roll(x, 1, 0))


def from_right(x):
    cols = x.shape[0]
    col = col_index(*x.shape)
    return jnp.where(col == cols - 1, 0.0, pltpu.roll(x, cols - 1, 0))


def pack_body(rows, cols, o, chan):
    half = o - 128

    def body(info, reward, latent, cached, own, send_even, send_odd):
        x_index = lax.broadcasted_iota(jnp.int32, (cols, 2 * cols), 1)
        w_index = lax.broadcasted_iota(jnp.int32, (cols, 2 * cols), 0)
        pick = [(x_index == 2 * w_index + b).astype(F32).astype(BF16) for b in (0, 1)]
        zeros = jnp.zeros((128 - half, 2 * cols), BF16)
        for f in range(2 * rows):
            r = reward[f]
            first, rest = r[:128], r[128:]
            low = jnp.concatenate([first, rest, zeros], axis=0)
            high = jnp.concatenate([first, zeros, rest], axis=0)
            sides = (low, high) if f % 2 else (high, low)
            d0, d1 = mm_t(pick[0], sides[0]), mm_t(pick[1], sides[1])
            own[f, :, 0:128] = d0[:, :128].astype(BF16)
            own[f, :, 128:256] = d1[:, :128].astype(BF16)
            own[f, :, 256:384] = (d0[:, 128:] + d1[:, 128:]).astype(BF16)
        base = 3 * cols
        per = chan * rows
        for send, last in ((send_even, 1 - info[0]), (send_odd, info[0])):
            begin = last * (2 * rows - 3)
            for k in range(3):
                send[k * cols : (k + 1) * cols] = own[begin + k]
            for t in range(3):
                src = cached[t] if t < 2 else latent[...]
                lat = src.reshape(per, cols)
                send[base : base + per, t * 128 : t * 128 + 128] = lat[:, :128]
                send[base + per : base + 2 * per, t * 128 : t * 128 + cols - 128] = lat[:, 128:]

    return body


def taps_body(info, up, info_out, fwd, back_odd, back_even):
    for k in range(4):
        info_out[k] = info[k]

    def rows_of(q, j):
        parts = ((2,), (1, 2), (0, 1), (0,))[q]
        total = up[parts[0], j].astype(F32)
        for i in parts[1:]:
            total = total + up[i, j].astype(F32)
        return total

    rest = []
    for q in range(4):
        c0, c1, c2 = (rows_of(q, j) for j in range(3))
        tap = [t.astype(BF16) for t in (c2, c1 + c2, c0 + c1, c0)]
        rest.append([t[128:] for t in tap])
        for b, order in ((0, (3, 1)), (1, (2, 0))):
            for side, p in enumerate(order):
                fwd[b, side * 384 : side * 384 + 384, q * 128 : q * 128 + 128] = tap[p][:128].T
                if q % 2 == 1:
                    pair = (q - 1, q) if b == 0 else (q, q - 1)
                    both = jnp.concatenate([rest[k][p] for k in pair], axis=0)
                    at = 512 + (q // 2) * 128
                    fwd[b, side * 384 : side * 384 + 384, at : at + 128] = both.T
        target, side = ((back_odd, 1), (back_even, 0), (back_odd, 0), (back_even, 1))[q]
        lanes = slice(side * 384, side * 384 + 384)
        for block, (p0, p1) in enumerate(((1, 2), (3, 0))):
            base = block * 384
            target[base : base + 128, lanes] = tap[p0][:128]
            target[base + 128 : base + 256, lanes] = tap[p1][:128]
            low, high = (p0, p1) if q % 2 == 0 else (p1, p0)
            target[base + 256 : base + 320, lanes] = tap[low][128:]
            target[base + 320 : base + 384, lanes] = tap[high][128:]


def cached_body(rows, cols, count, width, tokens):
    size = rows * cols

    def body(info, order, features, mid, acc, send_even, send_odd, mid_t, sel, wide):
        for t in range(2):
            for r in range(rows):
                at = slice(r * cols, (r + 1) * cols)
                x = features[t, r]
                x32 = x.astype(F32)
                base = t * 1152
                wide[at, base : base + 384] = from_left(x32).astype(BF16)
                wide[at, base + 384 : base + 768] = x
                wide[at, base + 768 : base + 1152] = from_right(x32).astype(BF16)
        lhs = wide[...]
        kernels = [jnp.concatenate([mid[0, i], mid[1, i]], axis=0) for i in range(3)]
        pair = mm(lhs, jnp.concatenate([kernels[0], kernels[1]], axis=1))
        for i in range(3):
            for j in range(3):
                at = (i * 3 + j) * 384
                mid_t[at : at + 384] = mid[2, i, j * 384 : (j + 1) * 384].T
        placing(info, order, sel, count, width, tokens)
        last_kernel = mm(lhs, kernels[2])
        for k in range(rows + 4):
            total = jnp.zeros((cols, 384), F32)
            for i, part in enumerate((pair[:, :384], pair[:, 384:], last_kernel)):
                r = k - 3 + i
                if 0 <= r < rows:
                    total = total + part[r * cols : (r + 1) * cols]
            acc[k] = total
        for send, last in ((send_even, 1 - info[0]), (send_odd, info[0])):
            for k in range(3):
                send[k * cols : (k + 1) * cols] = acc[1 + last * 3 + k].astype(BF16)

    return body


def current_body(rows, cols, chan):
    per = chan * rows
    base = 3 * cols

    def body(info, latent, cached, got_even, got_odd, w_in, mid, half_gain, hidden, conv, lat, tall, wide, w_order):
        even = info[0] == 0
        lat[...] = jnp.zeros_like(lat)

        def fill(first_row, got, ok):
            scale = ok.astype(F32)
            for t in range(3):
                x = got[base : base + per, t * 128 : t * 128 + 128].astype(F32) * scale
                y = got[base + per : base + 2 * per, t * 128 : t * 128 + cols - 128].astype(F32) * scale
                for r in range(rows):
                    at = pl.ds((first_row + r) * 3 * chan + t * chan, chan)
                    lat[at, 0:128] = x[r * chan : (r + 1) * chan]
                    lat[at, 128:cols] = y[r * chan : (r + 1) * chan]

        @pl.when(even)
        def _():
            fill(0, got_odd, info[1])
            fill(2 * rows, got_even, info[2])

        @pl.when(jnp.logical_not(even))
        def _():
            fill(0, got_even, info[1])
            fill(2 * rows, got_odd, info[2])

        for t in range(3):
            for r in range(rows):
                at = pl.ds((rows + r) * 3 * chan + t * chan, chan)
                lat[at, 0:cols] = (cached[t, r] if t < 2 else latent[r]).astype(F32)

        for r in range(3 * rows):
            for t in range(3):
                x = lat[pl.ds((r * 3 + t) * chan, chan), :]
                at = t * 3 * chan
                tall[r, at : at + chan] = pltpu.roll(x, 1, 1).astype(BF16)
                tall[r, at + chan : at + 2 * chan] = x.astype(BF16)
                tall[r, at + 2 * chan : at + 3 * chan] = pltpu.roll(x, 255, 1).astype(BF16)
        for i in range(3):
            for t in range(3):
                at = (i * 3 + t) * 3 * chan
                w_order[at : at + 3 * chan] = w_in[t, i]

        def hidden_row(k):
            lhs = tall[k : k + 3].reshape(27 * chan, 256)[:, 0:cols]
            h = lax.dot_general(lhs, w_order[...], (((0,), (0,)), ((), ())), preferred_element_type=F32)
            h = h.astype(BF16)
            hidden[k] = h
            v = h.astype(F32)
            inv = lax.rsqrt(jnp.mean(v * v, axis=1, keepdims=True) + EPS)
            half = v * inv * half_gain[...]
            act = half * (jnp.tanh(half) + 1.0)
            if k < 3:
                act = act * flag(info, 1)
            if k >= rows + 3:
                act = act * flag(info, 2)
            wide[k, :, 0:384] = from_left(act).astype(BF16)
            wide[k, :, 384:768] = act.astype(BF16)
            wide[k, :, 768:1152] = from_right(act).astype(BF16)

        def conv_rows(p, count):
            lhs = [wide[p + i : p + i + count].reshape(count * cols, 1152) for i in range(3)]
            total = mm(jnp.concatenate(lhs, axis=1), mid[2].reshape(3456, 384))
            conv[p : p + count] = total.reshape(count, cols, 384)

        for k in range(rows + 2):
            hidden_row(k)
        conv_rows(0, rows)
        for k in range(rows + 2, rows + 6):
            hidden_row(k)
        conv_rows(rows, 4)

    return body


def pulled(s, half_gain, grad):
    h = s * half_gain
    t = jnp.tanh(h)
    return (grad * half_gain) * ((1.0 + t) * (1.0 + h * (1.0 - t)))


def back_body(rows, cols, chan, count, o):
    size = rows * cols
    width = 2 * cols // count

    def body(
        info, hidden, conv, acc, got_even, got_odd, packed_even, packed_odd, own, fwd, back_odd, back_even, mid_t, w_in, half_gain,
        half_out, payload, reward, edge, p0, p1, g_odd, g_even, wide, t_odd, t_even, back, act_grad, hid, lines,
    ):
        even = info[0] == 0
        top, bottom = flag(info, 1), flag(info, 2)

        def take(got, packed, before):
            ok = top if before else bottom
            place = 0 if before else rows + 1
            for k in range(3):
                at = slice(k * cols, (k + 1) * cols)
                edge[place + k] = got[at].astype(F32) * ok
                reward[k if before else 2 * rows + 3 + k] = (packed[at].astype(F32) * ok).astype(BF16)

        @pl.when(even)
        def _():
            take(got_odd, packed_odd, True)
            take(got_even, packed_even, False)

        @pl.when(jnp.logical_not(even))
        def _():
            take(got_even, packed_even, True)
            take(got_odd, packed_odd, False)

        reward[3 : 2 * rows + 3] = own[...]

        def inside(x, k, first, last):
            return x * top if k < first else x * bottom if k >= last else x

        def spread(ref, k, x, ahead):
            x = x.astype(BF16)
            x32 = x.astype(F32)
            sides = (from_right(x32), from_left(x32)) if ahead else (from_left(x32), from_right(x32))
            ref[k, :, 0:384] = sides[0].astype(BF16)
            ref[k, :, 384:768] = x
            ref[k, :, 768:1152] = sides[1].astype(BF16)

        def state_row(k):
            x = hidden[k + 1].astype(F32) + conv[k]
            if 1 <= k <= rows + 2:
                x = x + acc[k]
            if k < 3 or k > rows:
                x = x + edge[k]
            spread(wide, k, inside(x, k, 2, rows + 2), False)

        def up_rows(k, count):
            x = wide[k : k + count].reshape(count * cols, 1152)
            p0[k : k + count] = mm(x[:, 0:768], fwd[0]).reshape(count, cols, 768)
            p1[k : k + count] = mm(x[:, 384:1152], fwd[1]).reshape(count, cols, 768)

        lane = lax.broadcasted_iota(jnp.int32, (cols, 128), 1)
        low = lane < 64
        gains = [half_out[:, 0:128], half_out[:, 128:256]]

        def pull(v0, v1, vm, r, zero_low):
            mine = low if zero_low else jnp.logical_not(low)
            def both(a0, a1, am):
                s0 = jnp.sum(a0 + jnp.where(mine, am, 0.0), axis=1, keepdims=True)
                s1 = jnp.sum(a1 + jnp.where(mine, 0.0, am), axis=1, keepdims=True)
                return s0 * (1.0 / o), s1 * (1.0 / o)

            q0, q1 = both(v0 * v0, v1 * v1, vm * vm)
            i0, i1 = lax.rsqrt(q0 + EPS), lax.rsqrt(q1 + EPS)
            im = jnp.where(mine, i0, i1)
            out = []
            for v, i, g, k in ((v0, i0, gains[0], 0), (v1, i1, gains[0], 1), (vm, im, gains[1], 2)):
                s = v * i
                out.append((s, pulled(s, g, r[:, k * 128 : k * 128 + 128].astype(F32))))
            m0, m1 = both(*(s * d for s, d in out))
            mx = jnp.where(mine, m0, m1)
            return [i * (d - s * m) for (s, d), i, m in zip(out, (i0, i1, im), (m0, m1, mx))], mine

        def store(g, target, k):
            (a0, a1, am), mine = g
            target[k, :, 0:128] = a0.astype(BF16)
            target[k, :, 128:256] = a1.astype(BF16)
            target[k, :, 256:384] = am.astype(BF16)
            target[k, :, 384:512] = from_right(a0).astype(BF16)
            target[k, :, 512:640] = from_left(a1).astype(BF16)
            target[k, :, 640:768] = jnp.where(mine, from_right(am), from_left(am)).astype(BF16)

        def pull_rows(k):
            v0 = p0[k, :, 256:384] + p0[k + 1, :, 0:128]
            v1 = p1[k, :, 256:384] + p1[k + 1, :, 0:128]
            vm = jnp.where(low, p0[k, :, 640:768] + p0[k + 1, :, 512:640], p1[k, :, 640:768] + p1[k + 1, :, 512:640])
            store(pull(v0, v1, vm, reward[2 * k], True), g_odd, k)
            v0 = p0[k + 1, :, 128:256] + p0[k, :, 384:512]
            v1 = p1[k + 1, :, 128:256] + p1[k, :, 384:512]
            vm = jnp.where(low, p1[k + 1, :, 512:640] + p1[k, :, 640:768], p0[k + 1, :, 512:640] + p0[k, :, 640:768])
            store(pull(v0, v1, vm, reward[2 * k + 1], False), g_even, k)

        def block_row(k):
            x = t_odd[k + 1, :, 0:384] + t_odd[k, :, 384:768] + t_even[k, :, 0:384] + t_even[k + 1, :, 384:768]
            spread(back, k, inside(x, k, 1, rows + 1), True)

        def hidden_pull(k):
            v = hidden[k + 3].astype(F32)
            inv = lax.rsqrt(jnp.mean(v * v, axis=1, keepdims=True) + EPS)
            s = v * inv
            d = pulled(s, half_gain[...], act_grad[k])
            dv = inv * (d - s * jnp.mean(d * s, axis=1, keepdims=True))
            hid[k] = (back[k + 1, :, 384:768].astype(F32) + dv).astype(BF16)

        fine = rows + 3
        for k in range(rows):
            state_row(k)
        up_rows(0, rows)
        for k in range(rows, rows + 4):
            state_row(k)
        up_rows(rows, 4)
        for k in range(fine):
            pull_rows(k)
        t_odd[...] = mm(g_odd[...].reshape(fine * cols, 768), back_odd[...]).reshape(fine, cols, 768)
        t_even[...] = mm(g_even[...].reshape(fine * cols, 768), back_even[...]).reshape(fine, cols, 768)
        for k in range(rows + 2):
            block_row(k)
        lhs = [back[2 - i : 2 - i + rows].reshape(size, 1152) for i in range(3)]
        act_grad[...] = mm(jnp.concatenate(lhs, axis=1), mid_t[...]).reshape(rows, cols, 384)
        for k in range(rows):
            hidden_pull(k)

        z = mm_t(w_in[...], hid[...].reshape(size, 384))
        place = lax.broadcasted_iota(jnp.int32, (chan, size), 1)
        col = lax.rem(place, cols)
        sums = []
        for i in range(3):
            z0, z1, z2 = (z[(i * 3 + j) * chan : (i * 3 + j + 1) * chan] for j in range(3))
            left = jnp.where(col == cols - 1, 0.0, pltpu.roll(z0, size - 1, 1))
            right = jnp.where(col == 0, 0.0, pltpu.roll(z2, 1, 1))
            sums.append(left + z1 + right)
        inner = sums[1]
        inner = inner + jnp.where(place < size - cols, pltpu.roll(sums[0], size - cols, 1), 0.0)
        inner = inner + jnp.where(place >= cols, pltpu.roll(sums[2], cols, 1), 0.0)
        lines[0:chan] = inner
        lines[chan : 2 * chan] = sums[0]
        lines[2 * chan : 3 * chan] = sums[2]
        per_row = count // 2
        for u in range(count):
            pair, piece = u // per_row, u % per_row
            parts = []
            for a in range(2):
                at = (2 * pair + a) * cols + piece * width
                parts.append(lines[0:chan, at : at + width])
            at = piece * width + (0 if pair else (rows - 1) * cols)
            first = chan if pair else 2 * chan
            parts.append(lines[first : first + chan, at : at + width])
            parts.append(jnp.zeros((chan, 128 - 3 * width), F32))
            payload[u] = jnp.concatenate(parts, axis=1).astype(BF16)

    return body


def placing(info, order, sel, count, width, tokens):
    piece = width // 2
    pair = info[3]
    lane = lax.broadcasted_iota(jnp.int32, (128, 4 * tokens), 0)
    column = lax.broadcasted_iota(jnp.int32, (128, 4 * tokens), 1)
    group = (lane >= width).astype(jnp.int32) + (lane >= 2 * width).astype(jnp.int32)
    w = lane - group * width
    part = jnp.where(group == 2, pair, group)
    fixed = (2 * part + (w & 1)) * tokens + (w >> 1) - column
    fixed = jnp.where(lane < 3 * width, fixed, -99999)
    for t in range(count):
        step = t + 1 - 2 * pair
        valid = jnp.logical_and(step >= 0, step < count)
        beside = jnp.where(valid, piece * order[jnp.clip(step, 0, count - 1)], -9999)
        begin = jnp.where(group == 2, beside, piece * order[t])
        sel[t] = (fixed + begin == 0).astype(F32).astype(BF16)


def place_body(count, chan, tokens):
    def body(sel, got, out):
        total = mm(got[0], sel[0])
        for t in range(1, count):
            total += mm(got[t], sel[t])
        for k in range(4):
            out[k * chan : (k + 1) * chan] = total[:, k * tokens : (k + 1) * tokens]

    return body


def swaps(count):
    within = [(i, i ^ 1) for i in range(count)]
    across = [(0, 0), (count - 1, count - 1)]
    for i in range(1, count - 1, 2):
        across += [(i, i + 1), (i + 1, i)]
    return within, sorted(across)


def shards(
    latent, cached_latent, cached_features, reward_grad, conv_in_weight, conv_mid_weight, conv_up_weight, norm_gain, out_gain, shard_order
):
    count = lax.axis_size("tile")
    rows, cols, chan = latent.shape
    mid_chan = norm_gain.shape[0]
    o = out_gain.shape[0]
    tile = lax.axis_index("tile")
    info = jnp.stack(
        [tile % 2, (tile > 0).astype(jnp.int32), (tile < count - 1).astype(jnp.int32), (tile >= count // 2).astype(jnp.int32)]
    ).astype(jnp.int32)
    lat = jnp.transpose(latent, (0, 2, 1))
    lat_cached = jnp.transpose(cached_latent, (0, 1, 3, 2))
    reward_t = jnp.transpose(reward_grad, (0, 2, 1))
    up_t = jnp.transpose(conv_up_weight, (0, 1, 3, 2))
    mid = conv_mid_weight.reshape(3, 3, 3 * mid_chan, mid_chan)
    w_in = conv_in_weight.reshape(3, 3, 3 * chan, mid_chan)
    gain = 0.5 * norm_gain.reshape(1, mid_chan)
    gain_out = 0.5 * jnp.concatenate([out_gain, out_gain[128:]]).reshape(1, 256)
    within, across = swaps(count)
    size = rows * cols
    edge_rows = 3 * cols + 2 * chan * rows

    info, fwd, back_odd, back_even = call(
        taps_body,
        [((4,), jnp.int32), ((2, 768, 768), BF16), ((768, 768), BF16), ((768, 768), BF16)],
        1, 1, [], 1e10, 16, 1,
    )(info, up_t)

    own, send_even, send_odd = call(
        pack_body(rows, cols, o, chan),
        [((2 * rows, cols, 384), BF16), ((edge_rows, 384), BF16), ((edge_rows, 384), BF16)],
        1, 3, [], 1e10, 16,
    )(info, reward_t, lat, lat_cached)
    packed_even = lax.ppermute(send_even, "tile", within)
    packed_odd = lax.ppermute(send_odd, "tile", across)

    width = 2 * cols // count
    tokens = size // 4
    acc, part_even, part_odd, mid_t, sel = call(
        cached_body(rows, cols, count, width, tokens),
        [
            ((rows + 4, cols, 384), F32), ((3 * cols, 384), BF16), ((3 * cols, 384), BF16), ((3456, 384), BF16),
            ((count, 128, 4 * tokens), BF16),
        ],
        2, 2, [pltpu.VMEM((size, 2304), BF16)], 4e9, 24,
    )(info, shard_order, cached_features, mid)
    got_even = lax.ppermute(part_even, "tile", within)
    got_odd = lax.ppermute(part_odd, "tile", across)

    hidden, conv = call(
        current_body(rows, cols, chan),
        [((rows + 6, cols, 384), BF16), ((rows + 4, cols, 384), F32)],
        1, 7,
        [
            pltpu.VMEM((9 * rows * chan, 256), F32),
            pltpu.VMEM((3 * rows, 9 * chan, 256), BF16),
            pltpu.VMEM((rows + 6, cols, 1152), BF16),
            pltpu.VMEM((27 * chan, 384), BF16),
        ],
        5e9, 24,
    )(info, lat, lat_cached, packed_even, packed_odd, w_in, mid, gain)

    (payload,) = call(
        back_body(rows, cols, chan, count, o),
        [((count, chan, 128), BF16)],
        1, 15,
        [
            pltpu.VMEM((2 * rows + 6, cols, 384), BF16),
            pltpu.VMEM((rows + 4, cols, 384), F32),
            pltpu.VMEM((rows + 4, cols, 768), F32),
            pltpu.VMEM((rows + 4, cols, 768), F32),
            pltpu.VMEM((rows + 3, cols, 768), BF16),
            pltpu.VMEM((rows + 3, cols, 768), BF16),
            pltpu.VMEM((rows + 4, cols, 1152), BF16),
            pltpu.VMEM((rows + 3, cols, 768), F32),
            pltpu.VMEM((rows + 3, cols, 768), F32),
            pltpu.VMEM((rows + 2, cols, 1152), BF16),
            pltpu.VMEM((rows, cols, 384), F32),
            pltpu.VMEM((rows, cols, 384), BF16),
            pltpu.VMEM((3 * chan, size), F32),
        ],
        8e9, 36,
    )(
        info, hidden, conv, acc, got_even, got_odd, packed_even, packed_odd, own, fwd, back_odd, back_even, mid_t,
        w_in[2].reshape(9 * chan, mid_chan), gain, gain_out,
    )
    received = lax.all_to_all(payload, "tile", split_axis=0, concat_axis=0, tiled=True)
    (placed,) = call(place_body(count, chan, tokens), [((4 * chan, tokens), F32)], 0, 2, [], 1e7, 16)(sel, received)
    return placed.T


def solution(mesh):
    return jax.shard_map(
        shards,
        mesh=mesh,
        in_specs=(
            P(("prompt", "tile"), None, None),
            P(None, ("prompt", "tile"), None, None),
            P(None, ("prompt", "tile"), None, None),
            P(("prompt", "tile"), None, None),
            P(),
            P(),
            P(),
            P(),
            P(),
            P("prompt"),
        ),
        out_specs=P(("prompt", "tile"), None),
        check_vma=False,
    )
```

```python
import jax
import jax.numpy as jnp
from jax import lax
from jax.experimental import pallas as pl
from jax.experimental.pallas import tpu as pltpu
from jax.sharding import PartitionSpec as P

EPS = 1e-06
F32 = jnp.float32
BF16 = jnp.bfloat16
VM = pl.BlockSpec(memory_space=pltpu.VMEM)
SM = pl.BlockSpec(memory_space=pltpu.SMEM)


def phase(info, *groups):
    @pl.when(info[1] >= 0)
    def _():
        total = max(len(g) for g in groups)
        done = [0] * len(groups)
        for k in range(total):
            for n, g in enumerate(groups):
                while done[n] * total < (k + 1) * len(g):
                    g[done[n]]()
                    done[n] += 1


def steps(f, *keys):
    return [lambda key=key: f(*key) for key in keys]


def call(body, outs, n_smem, n_vmem, scratch, flops, limit, smem_outs=0):
    specs = [SM] * n_smem + [VM] * n_vmem
    return pl.pallas_call(
        body,
        out_shape=[jax.ShapeDtypeStruct(s, d) for s, d in outs],
        in_specs=specs,
        out_specs=[SM] * smem_outs + [VM] * (len(outs) - smem_outs),
        scratch_shapes=scratch,
        cost_estimate=pl.CostEstimate(flops=int(flops), bytes_accessed=2**20, transcendentals=0),
        compiler_params=pltpu.CompilerParams(vmem_limit_bytes=limit << 20),
    )


def mm(a, b):
    return jnp.dot(a, b, preferred_element_type=F32)


def mm_t(a, b):
    return lax.dot_general(a, b, (((1,), (1,)), ((), ())), preferred_element_type=F32)


def flag(info, k):
    return info[k].astype(F32)


def col_index(cols, lanes):
    return lax.broadcasted_iota(jnp.int32, (cols, lanes), 0)


def from_left(x):
    col = col_index(*x.shape)
    return jnp.where(col == 0, 0.0, pltpu.roll(x, 1, 0))


def from_right(x):
    cols = x.shape[0]
    col = col_index(*x.shape)
    return jnp.where(col == cols - 1, 0.0, pltpu.roll(x, cols - 1, 0))


def pack_body(rows, cols, o, chan):
    half = o - 128

    def body(info, reward, latent, cached, own, send_even, send_odd):
        x_index = lax.broadcasted_iota(jnp.int32, (cols, 2 * cols), 1)
        w_index = lax.broadcasted_iota(jnp.int32, (cols, 2 * cols), 0)
        pick = [(x_index == 2 * w_index + b).astype(F32).astype(BF16) for b in (0, 1)]
        zeros = jnp.zeros((128 - half, 2 * cols), BF16)
        for f in range(2 * rows):
            r = reward[f]
            first, rest = r[:128], r[128:]
            low = jnp.concatenate([first, rest, zeros], axis=0)
            high = jnp.concatenate([first, zeros, rest], axis=0)
            sides = (low, high) if f % 2 else (high, low)
            d0, d1 = mm_t(pick[0], sides[0]), mm_t(pick[1], sides[1])
            own[f, :, 0:128] = d0[:, :128].astype(BF16)
            own[f, :, 128:256] = d1[:, :128].astype(BF16)
            own[f, :, 256:384] = (d0[:, 128:] + d1[:, 128:]).astype(BF16)
        base = 3 * cols
        per = chan * rows
        for send, last in ((send_even, 1 - info[0]), (send_odd, info[0])):
            begin = last * (2 * rows - 3)
            for k in range(3):
                send[k * cols : (k + 1) * cols] = own[begin + k]
            for t in range(3):
                src = cached[t] if t < 2 else latent[...]
                lat = src.reshape(per, cols)
                send[base : base + per, t * 128 : t * 128 + 128] = lat[:, :128]
                send[base + per : base + 2 * per, t * 128 : t * 128 + cols - 128] = lat[:, 128:]

    return body


def taps_body(info, up, info_out, fwd, back_odd, back_even):
    for k in range(4):
        info_out[k] = info[k]

    def rows_of(q, j):
        parts = ((2,), (1, 2), (0, 1), (0,))[q]
        total = up[parts[0], j].astype(F32)
        for i in parts[1:]:
            total = total + up[i, j].astype(F32)
        return total

    rest = []
    for q in range(4):
        c0, c1, c2 = (rows_of(q, j) for j in range(3))
        tap = [t.astype(BF16) for t in (c2, c1 + c2, c0 + c1, c0)]
        rest.append([t[128:] for t in tap])
        for b, order in ((0, (3, 1)), (1, (2, 0))):
            for side, p in enumerate(order):
                fwd[b, side * 384 : side * 384 + 384, q * 128 : q * 128 + 128] = tap[p][:128].T
                if q % 2 == 1:
                    pair = (q - 1, q) if b == 0 else (q, q - 1)
                    both = jnp.concatenate([rest[k][p] for k in pair], axis=0)
                    at = 512 + (q // 2) * 128
                    fwd[b, side * 384 : side * 384 + 384, at : at + 128] = both.T
        target, side = ((back_odd, 1), (back_even, 0), (back_odd, 0), (back_even, 1))[q]
        lanes = slice(side * 384, side * 384 + 384)
        for block, (p0, p1) in enumerate(((1, 2), (3, 0))):
            base = block * 384
            target[base : base + 128, lanes] = tap[p0][:128]
            target[base + 128 : base + 256, lanes] = tap[p1][:128]
            low, high = (p0, p1) if q % 2 == 0 else (p1, p0)
            target[base + 256 : base + 320, lanes] = tap[low][128:]
            target[base + 320 : base + 384, lanes] = tap[high][128:]


def cached_body(rows, cols, count, width, tokens):
    size = rows * cols

    def body(info, order, features, mid, acc, send_even, send_odd, mid_t, sel, wide, parts):
        def spread(t, r):
            at = slice(r * cols, (r + 1) * cols)
            x = features[t, r]
            x32 = x.astype(F32)
            base = t * 1152
            wide[at, base : base + 384] = from_left(x32).astype(BF16)
            wide[at, base + 384 : base + 768] = x
            wide[at, base + 768 : base + 1152] = from_right(x32).astype(BF16)

        def product(i, lanes):
            parts[i, :, lanes] = mm(wide[...], jnp.concatenate([mid[0, i, :, lanes], mid[1, i, :, lanes]], axis=0))

        def double():
            left = jnp.concatenate([mid[0, 0, :, 256:384], mid[1, 0, :, 256:384]], axis=0)
            right = jnp.concatenate([mid[0, 1, :, 256:384], mid[1, 1, :, 256:384]], axis=0)
            both = mm(wide[...], jnp.concatenate([left, right], axis=1))
            parts[0, :, 256:384] = both[:, :128]
            parts[1, :, 256:384] = both[:, 128:]

        def turn(i, j):
            at = (i * 3 + j) * 384
            mid_t[at : at + 384] = mid[2, i, j * 384 : (j + 1) * 384].T

        def total_row(k):
            total = jnp.zeros((cols, 384), F32)
            for i in range(3):
                r = k - 3 + i
                if 0 <= r < rows:
                    total = total + parts[i, r * cols : (r + 1) * cols]
            acc[k] = total

        most, rest = slice(0, 256), slice(256, 384)
        phase(info, steps(spread, *[(t, r) for t in range(2) for r in range(rows)]))
        phase(info, steps(product, (0, most), (1, most)) + steps(double, ()), steps(turn, *[(i, j) for i in range(3) for j in range(3)]))
        phase(info, steps(product, (2, most), (2, rest)), steps(placing(info, order, sel, count, width, tokens), *[(t,) for t in range(count)]))
        phase(info, steps(total_row, *[(k,) for k in range(rows + 4)]))
        for send, last in ((send_even, 1 - info[0]), (send_odd, info[0])):
            for k in range(3):
                send[k * cols : (k + 1) * cols] = acc[1 + last * 3 + k].astype(BF16)

    return body


def current_body(rows, cols, chan):
    per = chan * rows
    base = 3 * cols

    def body(info, latent, cached, got_even, got_odd, w_in, mid, half_gain, hidden, conv, lat, tall, wide, w_order):
        even = info[0] == 0
        lat[...] = jnp.zeros_like(lat)

        def fill(first_row, got, ok):
            scale = ok.astype(F32)
            for t in range(3):
                x = got[base : base + per, t * 128 : t * 128 + 128].astype(F32) * scale
                y = got[base + per : base + 2 * per, t * 128 : t * 128 + cols - 128].astype(F32) * scale
                for r in range(rows):
                    at = pl.ds((first_row + r) * 3 * chan + t * chan, chan)
                    lat[at, 0:128] = x[r * chan : (r + 1) * chan]
                    lat[at, 128:cols] = y[r * chan : (r + 1) * chan]

        @pl.when(even)
        def _():
            fill(0, got_odd, info[1])
            fill(2 * rows, got_even, info[2])

        @pl.when(jnp.logical_not(even))
        def _():
            fill(0, got_even, info[1])
            fill(2 * rows, got_odd, info[2])

        for t in range(3):
            for r in range(rows):
                at = pl.ds((rows + r) * 3 * chan + t * chan, chan)
                lat[at, 0:cols] = (cached[t, r] if t < 2 else latent[r]).astype(F32)

        for r in range(3 * rows):
            for t in range(3):
                x = lat[pl.ds((r * 3 + t) * chan, chan), :]
                at = t * 3 * chan
                tall[r, at : at + chan] = pltpu.roll(x, 1, 1).astype(BF16)
                tall[r, at + chan : at + 2 * chan] = x.astype(BF16)
                tall[r, at + 2 * chan : at + 3 * chan] = pltpu.roll(x, 255, 1).astype(BF16)
        for i in range(3):
            for t in range(3):
                at = (i * 3 + t) * 3 * chan
                w_order[at : at + 3 * chan] = w_in[t, i]

        def hidden_row(k):
            lhs = tall[k : k + 3].reshape(27 * chan, 256)[:, 0:cols]
            h = lax.dot_general(lhs, w_order[...], (((0,), (0,)), ((), ())), preferred_element_type=F32)
            h = h.astype(BF16)
            hidden[k] = h
            v = h.astype(F32)
            inv = lax.rsqrt(jnp.mean(v * v, axis=1, keepdims=True) + EPS)
            half = v * inv * half_gain[...]
            act = half * (jnp.tanh(half) + 1.0)
            if k < 3:
                act = act * flag(info, 1)
            if k >= rows + 3:
                act = act * flag(info, 2)
            wide[k, :, 0:384] = from_left(act).astype(BF16)
            wide[k, :, 384:768] = act.astype(BF16)
            wide[k, :, 768:1152] = from_right(act).astype(BF16)

        def conv_rows(p, number, lanes):
            lhs = [wide[p + i : p + i + number].reshape(number * cols, 1152) for i in range(3)]
            total = mm(jnp.concatenate(lhs, axis=1), mid[2, :, :, lanes].reshape(3456, lanes.stop - lanes.start))
            conv[p : p + number, :, lanes] = total.reshape(number, cols, lanes.stop - lanes.start)

        def hiddens(first, last):
            return steps(hidden_row, *[(k,) for k in range(first, last)])

        def convs(p, number):
            return steps(conv_rows, (p, number, slice(0, 256)), (p, number, slice(256, 384)))

        phase(info, hiddens(0, 4))
        phase(info, convs(0, 2), hiddens(4, rows + 3))
        phase(info, convs(2, rows - 1), hiddens(rows + 3, rows + 6))
        phase(info, convs(rows + 1, 3))

    return body


def pulled(s, half_gain, grad):
    h = s * half_gain
    t = jnp.tanh(h)
    return (grad * half_gain) * ((1.0 + t) * (1.0 + h * (1.0 - t)))


def back_body(rows, cols, chan, count, o):
    size = rows * cols
    width = 2 * cols // count

    def body(
        info, hidden, conv, acc, got_even, got_odd, packed_even, packed_odd, own, fwd, back_odd, back_even, mid_t, w_in, half_gain,
        half_out, payload, reward, edge, p0, p1, g_odd, g_even, wide, t_odd, t_even, back, act_grad, hid, lines,
    ):
        even = info[0] == 0
        top, bottom = flag(info, 1), flag(info, 2)

        def take(got, packed, before):
            ok = top if before else bottom
            place = 0 if before else rows + 1
            for k in range(3):
                at = slice(k * cols, (k + 1) * cols)
                edge[place + k] = got[at].astype(F32) * ok
                reward[k if before else 2 * rows + 3 + k] = (packed[at].astype(F32) * ok).astype(BF16)

        @pl.when(even)
        def _():
            take(got_odd, packed_odd, True)
            take(got_even, packed_even, False)

        @pl.when(jnp.logical_not(even))
        def _():
            take(got_even, packed_even, True)
            take(got_odd, packed_odd, False)

        reward[3 : 2 * rows + 3] = own[...]

        def inside(x, k, first, last):
            return x * top if k < first else x * bottom if k >= last else x

        def spread(ref, k, x, ahead):
            x = x.astype(BF16)
            x32 = x.astype(F32)
            sides = (from_right(x32), from_left(x32)) if ahead else (from_left(x32), from_right(x32))
            ref[k, :, 0:384] = sides[0].astype(BF16)
            ref[k, :, 384:768] = x
            ref[k, :, 768:1152] = sides[1].astype(BF16)

        def state_row(k):
            x = hidden[k + 1].astype(F32) + conv[k]
            if 1 <= k <= rows + 2:
                x = x + acc[k]
            if k < 3 or k > rows:
                x = x + edge[k]
            spread(wide, k, inside(x, k, 2, rows + 2), False)

        def up_rows(k, number, b, n):
            x = wide[k : k + number, :, b * 384 : b * 384 + 768].reshape(number * cols, 768)
            lanes = slice(n * 256, n * 256 + 256)
            (p0, p1)[b][k : k + number, :, lanes] = mm(x, fwd[b, :, lanes]).reshape(number, cols, 256)

        def down_rows(k, number, odd, n):
            g, kernel, t = (g_odd, back_odd, t_odd) if odd else (g_even, back_even, t_even)
            lanes = slice(n * 256, n * 256 + 256)
            x = g[k : k + number].reshape(number * cols, 768)
            t[k : k + number, :, lanes] = mm(x, kernel[:, lanes]).reshape(number, cols, 256)

        def mid_rows(k, number, lanes):
            lhs = [back[k + 2 - i : k + 2 - i + number].reshape(number * cols, 1152) for i in range(3)]
            total = mm(jnp.concatenate(lhs, axis=1), mid_t[:, lanes])
            act_grad[k : k + number, :, lanes] = total.reshape(number, cols, lanes.stop - lanes.start)

        lane = lax.broadcasted_iota(jnp.int32, (cols, 128), 1)
        low = lane < 64
        gains = [half_out[:, 0:128], half_out[:, 128:256]]

        def pull(v0, v1, vm, r, zero_low):
            mine = low if zero_low else jnp.logical_not(low)
            def both(a0, a1, am):
                s0 = jnp.sum(a0 + jnp.where(mine, am, 0.0), axis=1, keepdims=True)
                s1 = jnp.sum(a1 + jnp.where(mine, 0.0, am), axis=1, keepdims=True)
                return s0 * (1.0 / o), s1 * (1.0 / o)

            q0, q1 = both(v0 * v0, v1 * v1, vm * vm)
            i0, i1 = lax.rsqrt(q0 + EPS), lax.rsqrt(q1 + EPS)
            im = jnp.where(mine, i0, i1)
            out = []
            for v, i, g, k in ((v0, i0, gains[0], 0), (v1, i1, gains[0], 1), (vm, im, gains[1], 2)):
                s = v * i
                out.append((s, pulled(s, g, r[:, k * 128 : k * 128 + 128].astype(F32))))
            m0, m1 = both(*(s * d for s, d in out))
            mx = jnp.where(mine, m0, m1)
            return [i * (d - s * m) for (s, d), i, m in zip(out, (i0, i1, im), (m0, m1, mx))], mine

        def store(g, target, k):
            (a0, a1, am), mine = g
            target[k, :, 0:128] = a0.astype(BF16)
            target[k, :, 128:256] = a1.astype(BF16)
            target[k, :, 256:384] = am.astype(BF16)
            target[k, :, 384:512] = from_right(a0).astype(BF16)
            target[k, :, 512:640] = from_left(a1).astype(BF16)
            target[k, :, 640:768] = jnp.where(mine, from_right(am), from_left(am)).astype(BF16)

        def pull_odd(k):
            v0 = p0[k, :, 256:384] + p0[k + 1, :, 0:128]
            v1 = p1[k, :, 256:384] + p1[k + 1, :, 0:128]
            vm = jnp.where(low, p0[k, :, 640:768] + p0[k + 1, :, 512:640], p1[k, :, 640:768] + p1[k + 1, :, 512:640])
            store(pull(v0, v1, vm, reward[2 * k], True), g_odd, k)

        def pull_even(k):
            v0 = p0[k + 1, :, 128:256] + p0[k, :, 384:512]
            v1 = p1[k + 1, :, 128:256] + p1[k, :, 384:512]
            vm = jnp.where(low, p1[k + 1, :, 512:640] + p1[k, :, 640:768], p0[k + 1, :, 512:640] + p0[k, :, 640:768])
            store(pull(v0, v1, vm, reward[2 * k + 1], False), g_even, k)

        def block_row(k):
            x = t_odd[k + 1, :, 0:384] + t_odd[k, :, 384:768] + t_even[k, :, 0:384] + t_even[k + 1, :, 384:768]
            spread(back, k, inside(x, k, 1, rows + 1), True)

        def hidden_pull(k):
            v = hidden[k + 3].astype(F32)
            inv = lax.rsqrt(jnp.mean(v * v, axis=1, keepdims=True) + EPS)
            s = v * inv
            d = pulled(s, half_gain[...], act_grad[k])
            dv = inv * (d - s * jnp.mean(d * s, axis=1, keepdims=True))
            hid[k] = (back[k + 1, :, 384:768].astype(F32) + dv).astype(BF16)

        def each(f, first, last):
            return steps(f, *[(k,) for k in range(first, last)])

        def ups(k, number):
            return steps(up_rows, *[(k, number, b, n) for n in range(3) for b in range(2)])

        def downs(k, number):
            return steps(down_rows, *[(k, number, odd, n) for n in range(3) for odd in (True, False)])

        def mids(k, number):
            return steps(mid_rows, (k, number, slice(0, 256)), (k, number, slice(256, 384)))

        def pulls(first, last):
            return [step for k in range(first, last) for step in steps(pull_odd, (k,)) + steps(pull_even, (k,))]

        phase(info, each(state_row, 0, rows))
        phase(info, ups(0, rows), each(state_row, rows, rows + 4))
        phase(info, ups(rows, 4), pulls(0, rows - 1))
        phase(info, downs(0, rows - 1), pulls(rows - 1, rows + 1))
        phase(info, downs(rows - 1, 2), pulls(rows + 1, rows + 3), each(block_row, 0, 2))
        phase(info, downs(rows + 1, 2), each(block_row, 2, rows))
        phase(info, each(block_row, rows, rows + 2), mids(0, 2))
        phase(info, mids(2, rows - 2), each(hidden_pull, 0, 2))
        for k in range(2, rows):
            hidden_pull(k)

        z = mm_t(w_in[...], hid[...].reshape(size, 384))
        place = lax.broadcasted_iota(jnp.int32, (chan, size), 1)
        col = lax.rem(place, cols)
        sums = []
        for i in range(3):
            z0, z1, z2 = (z[(i * 3 + j) * chan : (i * 3 + j + 1) * chan] for j in range(3))
            left = jnp.where(col == cols - 1, 0.0, pltpu.roll(z0, size - 1, 1))
            right = jnp.where(col == 0, 0.0, pltpu.roll(z2, 1, 1))
            sums.append(left + z1 + right)
        inner = sums[1]
        inner = inner + jnp.where(place < size - cols, pltpu.roll(sums[0], size - cols, 1), 0.0)
        inner = inner + jnp.where(place >= cols, pltpu.roll(sums[2], cols, 1), 0.0)
        lines[0:chan] = inner
        lines[chan : 2 * chan] = sums[0]
        lines[2 * chan : 3 * chan] = sums[2]
        per_row = count // 2
        for u in range(count):
            pair, piece = u // per_row, u % per_row
            parts = []
            for a in range(2):
                at = (2 * pair + a) * cols + piece * width
                parts.append(lines[0:chan, at : at + width])
            at = piece * width + (0 if pair else (rows - 1) * cols)
            first = chan if pair else 2 * chan
            parts.append(lines[first : first + chan, at : at + width])
            parts.append(jnp.zeros((chan, 128 - 3 * width), F32))
            payload[u] = jnp.concatenate(parts, axis=1).astype(BF16)

    return body


def placing(info, order, sel, count, width, tokens):
    piece = width // 2
    pair = info[3]
    lane = lax.broadcasted_iota(jnp.int32, (128, 4 * tokens), 0)
    column = lax.broadcasted_iota(jnp.int32, (128, 4 * tokens), 1)
    group = (lane >= width).astype(jnp.int32) + (lane >= 2 * width).astype(jnp.int32)
    w = lane - group * width
    part = jnp.where(group == 2, pair, group)
    fixed = (2 * part + (w & 1)) * tokens + (w >> 1) - column
    fixed = jnp.where(lane < 3 * width, fixed, -99999)

    def one(t):
        step = t + 1 - 2 * pair
        valid = jnp.logical_and(step >= 0, step < count)
        beside = jnp.where(valid, piece * order[jnp.clip(step, 0, count - 1)], -9999)
        begin = jnp.where(group == 2, beside, piece * order[t])
        sel[t] = (fixed + begin == 0).astype(F32).astype(BF16)

    return one


def place_body(count, chan, tokens):
    def body(sel, got, out):
        total = mm(got[0], sel[0])
        for t in range(1, count):
            total += mm(got[t], sel[t])
        for k in range(4):
            out[k * chan : (k + 1) * chan] = total[:, k * tokens : (k + 1) * tokens]

    return body


def swaps(count):
    within = [(i, i ^ 1) for i in range(count)]
    across = [(0, 0), (count - 1, count - 1)]
    for i in range(1, count - 1, 2):
        across += [(i, i + 1), (i + 1, i)]
    return within, sorted(across)


def shards(
    latent, cached_latent, cached_features, reward_grad, conv_in_weight, conv_mid_weight, conv_up_weight, norm_gain, out_gain, shard_order
):
    count = lax.axis_size("tile")
    rows, cols, chan = latent.shape
    mid_chan = norm_gain.shape[0]
    o = out_gain.shape[0]
    tile = lax.axis_index("tile")
    info = jnp.stack(
        [tile % 2, (tile > 0).astype(jnp.int32), (tile < count - 1).astype(jnp.int32), (tile >= count // 2).astype(jnp.int32)]
    ).astype(jnp.int32)
    lat = jnp.transpose(latent, (0, 2, 1))
    lat_cached = jnp.transpose(cached_latent, (0, 1, 3, 2))
    reward_t = jnp.transpose(reward_grad, (0, 2, 1))
    up_t = jnp.transpose(conv_up_weight, (0, 1, 3, 2))
    mid = conv_mid_weight.reshape(3, 3, 3 * mid_chan, mid_chan)
    w_in = conv_in_weight.reshape(3, 3, 3 * chan, mid_chan)
    gain = 0.5 * norm_gain.reshape(1, mid_chan)
    gain_out = 0.5 * jnp.concatenate([out_gain, out_gain[128:]]).reshape(1, 256)
    within, across = swaps(count)
    size = rows * cols
    edge_rows = 3 * cols + 2 * chan * rows

    info, fwd, back_odd, back_even = call(
        taps_body,
        [((4,), jnp.int32), ((2, 768, 768), BF16), ((768, 768), BF16), ((768, 768), BF16)],
        1, 1, [], 1e10, 16, 1,
    )(info, up_t)

    own, send_even, send_odd = call(
        pack_body(rows, cols, o, chan),
        [((2 * rows, cols, 384), BF16), ((edge_rows, 384), BF16), ((edge_rows, 384), BF16)],
        1, 3, [], 1e10, 16,
    )(info, reward_t, lat, lat_cached)
    packed_even = lax.ppermute(send_even, "tile", within)
    packed_odd = lax.ppermute(send_odd, "tile", across)

    width = 2 * cols // count
    tokens = size // 4
    acc, part_even, part_odd, mid_t, sel = call(
        cached_body(rows, cols, count, width, tokens),
        [
            ((rows + 4, cols, 384), F32), ((3 * cols, 384), BF16), ((3 * cols, 384), BF16), ((3456, 384), BF16),
            ((count, 128, 4 * tokens), BF16),
        ],
        2, 2, [pltpu.VMEM((size, 2304), BF16), pltpu.VMEM((3, size, 384), F32)], 4e9, 24,
    )(info, shard_order, cached_features, mid)
    got_even = lax.ppermute(part_even, "tile", within)
    got_odd = lax.ppermute(part_odd, "tile", across)

    hidden, conv = call(
        current_body(rows, cols, chan),
        [((rows + 6, cols, 384), BF16), ((rows + 4, cols, 384), F32)],
        1, 7,
        [
            pltpu.VMEM((9 * rows * chan, 256), F32),
            pltpu.VMEM((3 * rows, 9 * chan, 256), BF16),
            pltpu.VMEM((rows + 6, cols, 1152), BF16),
            pltpu.VMEM((27 * chan, 384), BF16),
        ],
        5e9, 24,
    )(info, lat, lat_cached, packed_even, packed_odd, w_in, mid, gain)

    (payload,) = call(
        back_body(rows, cols, chan, count, o),
        [((count, chan, 128), BF16)],
        1, 15,
        [
            pltpu.VMEM((2 * rows + 6, cols, 384), BF16),
            pltpu.VMEM((rows + 4, cols, 384), F32),
            pltpu.VMEM((rows + 4, cols, 768), F32),
            pltpu.VMEM((rows + 4, cols, 768), F32),
            pltpu.VMEM((rows + 3, cols, 768), BF16),
            pltpu.VMEM((rows + 3, cols, 768), BF16),
            pltpu.VMEM((rows + 4, cols, 1152), BF16),
            pltpu.VMEM((rows + 3, cols, 768), F32),
            pltpu.VMEM((rows + 3, cols, 768), F32),
            pltpu.VMEM((rows + 2, cols, 1152), BF16),
            pltpu.VMEM((rows, cols, 384), F32),
            pltpu.VMEM((rows, cols, 384), BF16),
            pltpu.VMEM((3 * chan, size), F32),
        ],
        8e9, 36,
    )(
        info, hidden, conv, acc, got_even, got_odd, packed_even, packed_odd, own, fwd, back_odd, back_even, mid_t,
        w_in[2].reshape(9 * chan, mid_chan), gain, gain_out,
    )
    received = lax.all_to_all(payload, "tile", split_axis=0, concat_axis=0, tiled=True)
    (placed,) = call(place_body(count, chan, tokens), [((4 * chan, tokens), F32)], 0, 2, [], 1e7, 16)(sel, received)
    return placed.T


def solution(mesh):
    return jax.shard_map(
        shards,
        mesh=mesh,
        in_specs=(
            P(("prompt", "tile"), None, None),
            P(None, ("prompt", "tile"), None, None),
            P(None, ("prompt", "tile"), None, None),
            P(("prompt", "tile"), None, None),
            P(),
            P(),
            P(),
            P(),
            P(),
            P("prompt"),
        ),
        out_specs=P(("prompt", "tile"), None),
        check_vma=False,
    )
```

```python
import jax
import jax.numpy as jnp
from jax import lax
from jax.experimental import pallas as pl
from jax.experimental.pallas import tpu as pltpu
from jax.sharding import PartitionSpec as P

EPS = 1e-06
F32 = jnp.float32
BF16 = jnp.bfloat16
VM = pl.BlockSpec(memory_space=pltpu.VMEM)
SM = pl.BlockSpec(memory_space=pltpu.SMEM)


def call(body, outs, n_smem, n_vmem, scratch, flops, limit, smem_outs=0):
    specs = [SM] * n_smem + [VM] * n_vmem
    return pl.pallas_call(
        body,
        out_shape=[jax.ShapeDtypeStruct(s, d) for s, d in outs],
        in_specs=specs,
        out_specs=[SM] * smem_outs + [VM] * (len(outs) - smem_outs),
        scratch_shapes=scratch,
        cost_estimate=pl.CostEstimate(flops=int(flops), bytes_accessed=2**20, transcendentals=0),
        compiler_params=pltpu.CompilerParams(vmem_limit_bytes=limit << 20),
    )


def mm(a, b):
    return jnp.dot(a, b, preferred_element_type=F32)


def mm_t(a, b):
    return lax.dot_general(a, b, (((1,), (1,)), ((), ())), preferred_element_type=F32)


def flag(info, k):
    return info[k].astype(F32)


def from_left(x):
    moved = pltpu.roll(x, 1, 0)
    first = lax.broadcasted_iota(jnp.int32, (8, x.shape[1]), 0) == 0
    return jnp.concatenate([jnp.where(first, 0.0, moved[:8]), moved[8:]], axis=0)


def from_right(x):
    size = x.shape[0]
    moved = pltpu.roll(x, size - 1, 0)
    last = lax.broadcasted_iota(jnp.int32, (8, x.shape[1]), 0) == 7
    return jnp.concatenate([moved[: size - 8], jnp.where(last, 0.0, moved[size - 8 :])], axis=0)


def beside(target, base, lanes, x, ahead):
    sides = (from_right, from_left) if ahead else (from_left, from_right)
    for group, value in enumerate((sides[0](x), x, sides[1](x))):
        at = base + group * 384 + lanes
        target[:, at : at + 128] = value.astype(BF16)


CHUNK = 32


def pack_body(rows, cols, o, chan):
    half = o - 128

    def body(info, reward, latent, cached, own, send_even, send_odd):
        x_index = lax.broadcasted_iota(jnp.int32, (cols, 2 * cols), 1)
        w_index = lax.broadcasted_iota(jnp.int32, (cols, 2 * cols), 0)
        pick = [(x_index == 2 * w_index + b).astype(F32).astype(BF16) for b in (0, 1)]
        zeros = jnp.zeros((128 - half, 2 * cols), BF16)
        for f in range(2 * rows):
            r = reward[f]
            first, rest = r[:128], r[128:]
            low = jnp.concatenate([first, rest, zeros], axis=0)
            high = jnp.concatenate([first, zeros, rest], axis=0)
            sides = (low, high) if f % 2 else (high, low)
            d0, d1 = mm_t(pick[0], sides[0]), mm_t(pick[1], sides[1])
            own[f, :, 0:128] = d0[:, :128].astype(BF16)
            own[f, :, 128:256] = d1[:, :128].astype(BF16)
            own[f, :, 256:384] = (d0[:, 128:] + d1[:, 128:]).astype(BF16)
        base = 3 * cols
        per = chan * rows
        for send, last in ((send_even, 1 - info[0]), (send_odd, info[0])):
            begin = last * (2 * rows - 3)
            for k in range(3):
                send[k * cols : (k + 1) * cols] = own[begin + k]
            for t in range(3):
                src = cached[t] if t < 2 else latent[...]
                lat = src.reshape(per, cols)
                send[base : base + per, t * 128 : t * 128 + 128] = lat[:, :128]
                send[base + per : base + 2 * per, t * 128 : t * 128 + cols - 128] = lat[:, 128:]

    return body


def taps_body(info, up, info_out, fwd, back_odd, back_even):
    for k in range(4):
        info_out[k] = info[k]

    parts = ((2,), (1, 2), (0, 1), (0,))
    targets = ((back_odd, 1), (back_even, 0), (back_odd, 0), (back_even, 1))

    def home(q, p, tile):
        block, second = ((1, 1), (0, 0), (0, 1), (1, 0))[p]
        target, side = targets[q]
        if tile < 2:
            row = block * 384 + second * 128 + tile * 64
        else:
            row = block * 384 + 256 + 64 * (second if q % 2 == 0 else 1 - second)
        return target, row, side * 384

    for tile in range(3):
        for lanes in range(0, 384, 128):
            w = [[up[i, j, tile * 64 : tile * 64 + 64, lanes : lanes + 128].astype(F32) for j in range(3)] for i in range(3)]
            for q in range(4):
                c = [w[parts[q][0]][j] + w[parts[q][1]][j] if len(parts[q]) > 1 else w[parts[q][0]][j] for j in range(3)]
                for p, tap in enumerate((c[2], c[1] + c[2], c[0] + c[1], c[0])):
                    target, row, side = home(q, p, tile)
                    target[row : row + 64, side + lanes : side + lanes + 128] = tap.astype(BF16)

    def tap_tile(q, p, tile, lanes):
        target, row, side = home(q, p, tile)
        return target[row : row + 64, side + lanes : side + lanes + 128]

    for b, order in ((0, (3, 1)), (1, (2, 0))):
        for side, p in enumerate(order):
            for lanes in range(0, 384, 128):
                at = slice(side * 384 + lanes, side * 384 + lanes + 128)
                for q in range(4):
                    both = jnp.concatenate([tap_tile(q, p, 0, lanes), tap_tile(q, p, 1, lanes)], axis=0)
                    fwd[b, at, q * 128 : q * 128 + 128] = both.T
                for half in range(2):
                    pair = (2 * half, 2 * half + 1) if b == 0 else (2 * half + 1, 2 * half)
                    both = jnp.concatenate([tap_tile(q, p, 2, lanes) for q in pair], axis=0)
                    fwd[b, at, 512 + half * 128 : 640 + half * 128] = both.T


def cached_body(rows, cols, count, width, tokens):
    size = rows * cols

    def body(info, order, features, mid, acc, send_even, send_odd, mid_t, sel, wide):
        for t in range(2):
            for r in range(rows):
                for lanes in range(0, 384, 128):
                    x = features[t, r, :, lanes : lanes + 128].astype(F32)
                    beside(wide.at[r * cols : (r + 1) * cols], t * 1152, lanes, x, False)
        lhs = wide[...]
        kernels = [jnp.concatenate([mid[0, i], mid[1, i]], axis=0) for i in range(3)]
        pair = mm(lhs, jnp.concatenate([kernels[0], kernels[1]], axis=1))
        for i in range(3):
            for j in range(3):
                at = (i * 3 + j) * 384
                mid_t[at : at + 384] = mid[2, i, j * 384 : (j + 1) * 384].T
        placing(info, order, sel, count, width, tokens)
        last_kernel = mm(lhs, kernels[2])
        for k in range(rows + 4):
            total = jnp.zeros((cols, 384), F32)
            for i, part in enumerate((pair[:, :384], pair[:, 384:], last_kernel)):
                r = k - 3 + i
                if 0 <= r < rows:
                    total = total + part[r * cols : (r + 1) * cols]
            acc[k] = total
        for send, last in ((send_even, 1 - info[0]), (send_odd, info[0])):
            for k in range(3):
                send[k * cols : (k + 1) * cols] = acc[1 + last * 3 + k].astype(BF16)

    return body


def current_body(rows, cols, chan):
    per = chan * rows
    base = 3 * cols

    def body(info, latent, cached, got_even, got_odd, w_in, mid, half_gain, hidden, conv, lat, tall, wide, w_order, plain):
        even = info[0] == 0
        lat[...] = jnp.zeros_like(lat)

        def fill(first_row, got, ok):
            scale = ok.astype(F32)
            for t in range(3):
                x = got[base : base + per, t * 128 : t * 128 + 128].astype(F32) * scale
                y = got[base + per : base + 2 * per, t * 128 : t * 128 + cols - 128].astype(F32) * scale
                for r in range(rows):
                    at = pl.ds((first_row + r) * 3 * chan + t * chan, chan)
                    lat[at, 0:128] = x[r * chan : (r + 1) * chan]
                    lat[at, 128:cols] = y[r * chan : (r + 1) * chan]

        @pl.when(even)
        def _():
            fill(0, got_odd, info[1])
            fill(2 * rows, got_even, info[2])

        @pl.when(jnp.logical_not(even))
        def _():
            fill(0, got_even, info[1])
            fill(2 * rows, got_odd, info[2])

        for t in range(3):
            for r in range(rows):
                at = pl.ds((rows + r) * 3 * chan + t * chan, chan)
                lat[at, 0:cols] = (cached[t, r] if t < 2 else latent[r]).astype(F32)

        for r in range(3 * rows):
            for t in range(3):
                x = lat[pl.ds((r * 3 + t) * chan, chan), :]
                at = t * 3 * chan
                tall[r, at : at + chan] = pltpu.roll(x, 1, 1).astype(BF16)
                tall[r, at + chan : at + 2 * chan] = x.astype(BF16)
                tall[r, at + 2 * chan : at + 3 * chan] = pltpu.roll(x, 255, 1).astype(BF16)
        for i in range(3):
            for t in range(3):
                at = (i * 3 + t) * 3 * chan
                w_order[at : at + 3 * chan] = w_in[t, i]

        def hidden_row(k):
            lhs = tall[k : k + 3].reshape(27 * chan, 256)[:, 0:cols]
            h = lax.dot_general(lhs, w_order[...], (((0,), (0,)), ((), ())), preferred_element_type=F32)
            plain[k % 2] = h
            for c in range(0, cols, CHUNK):
                at = slice(c, c + CHUNK)
                v = plain[k % 2, at].astype(BF16)
                hidden[k, at] = v
                v = v.astype(F32)
                inv = lax.rsqrt(jnp.mean(v * v, axis=1, keepdims=True) + EPS)
                half = v * inv * half_gain[...]
                act = half * (jnp.tanh(half) + 1.0)
                if k < 3:
                    act = act * flag(info, 1)
                if k >= rows + 3:
                    act = act * flag(info, 2)
                plain[k % 2, at] = act
            for lanes in range(0, 384, 128):
                beside(wide.at[k], 0, lanes, plain[k % 2, :, lanes : lanes + 128], False)

        def conv_rows(p, count):
            lhs = [wide[p + i : p + i + count].reshape(count * cols, 1152) for i in range(3)]
            total = mm(jnp.concatenate(lhs, axis=1), mid[2].reshape(3456, 384))
            conv[p : p + count] = total.reshape(count, cols, 384)

        for k in range(rows + 2):
            hidden_row(k)
        conv_rows(0, rows)
        for k in range(rows + 2, rows + 6):
            hidden_row(k)
        conv_rows(rows, 4)

    return body


def pulled(s, half_gain, grad):
    h = s * half_gain
    t = jnp.tanh(h)
    return (grad * half_gain) * ((1.0 + t) * (1.0 + h * (1.0 - t)))


def back_body(rows, cols, chan, count, o):
    size = rows * cols
    width = 2 * cols // count

    def body(
        info, hidden, conv, acc, got_even, got_odd, packed_even, packed_odd, own, fwd, back_odd, back_even, mid_t, w_in, half_gain,
        half_out, payload, reward, edge, p0, p1, g_odd, g_even, wide, t_odd, t_even, back, act_grad, hid, tmp_odd, tmp_even, lines,
    ):
        even = info[0] == 0
        top, bottom = flag(info, 1), flag(info, 2)

        def take(got, packed, before):
            ok = top if before else bottom
            place = 0 if before else rows + 1
            for k in range(3):
                at = slice(k * cols, (k + 1) * cols)
                edge[place + k] = got[at].astype(F32) * ok
                reward[k if before else 2 * rows + 3 + k] = (packed[at].astype(F32) * ok).astype(BF16)

        @pl.when(even)
        def _():
            take(got_odd, packed_odd, True)
            take(got_even, packed_even, False)

        @pl.when(jnp.logical_not(even))
        def _():
            take(got_even, packed_even, True)
            take(got_odd, packed_odd, False)

        reward[3 : 2 * rows + 3] = own[...]

        def inside(x, k, first, last):
            return x * top if k < first else x * bottom if k >= last else x

        def state_row(k):
            for lanes in range(0, 384, 128):
                at = slice(lanes, lanes + 128)
                x = hidden[k + 1, :, at].astype(F32) + conv[k, :, at]
                if 1 <= k <= rows + 2:
                    x = x + acc[k, :, at]
                if k < 3 or k > rows:
                    x = x + edge[k, :, at]
                beside(wide.at[k], 0, lanes, inside(x, k, 2, rows + 2), False)

        def up_rows(k, count):
            x = wide[k : k + count].reshape(count * cols, 1152)
            p0[k : k + count] = mm(x[:, 0:768], fwd[0]).reshape(count, cols, 768)
            p1[k : k + count] = mm(x[:, 384:1152], fwd[1]).reshape(count, cols, 768)

        low = lax.broadcasted_iota(jnp.int32, (CHUNK, 128), 1) < 64
        tall_low = lax.broadcasted_iota(jnp.int32, (cols, 128), 1) < 64
        gains = [half_out[:, 0:128], half_out[:, 128:256]]

        def pull(v0, v1, vm, r, zero_low):
            mine = low if zero_low else jnp.logical_not(low)
            def both(a0, a1, am):
                s0 = jnp.sum(a0 + jnp.where(mine, am, 0.0), axis=1, keepdims=True)
                s1 = jnp.sum(a1 + jnp.where(mine, 0.0, am), axis=1, keepdims=True)
                return s0 * (1.0 / o), s1 * (1.0 / o)

            q0, q1 = both(v0 * v0, v1 * v1, vm * vm)
            i0, i1 = lax.rsqrt(q0 + EPS), lax.rsqrt(q1 + EPS)
            im = jnp.where(mine, i0, i1)
            out = []
            for v, i, g, k in ((v0, i0, gains[0], 0), (v1, i1, gains[0], 1), (vm, im, gains[1], 2)):
                s = v * i
                out.append((s, pulled(s, g, r[:, k * 128 : k * 128 + 128].astype(F32))))
            m0, m1 = both(*(s * d for s, d in out))
            mx = jnp.where(mine, m0, m1)
            return [i * (d - s * m) for (s, d), i, m in zip(out, (i0, i1, im), (m0, m1, mx))]

        def pull_row(k, odd):
            target, tmp = (g_odd, tmp_odd) if odd else (g_even, tmp_even)
            for c in range(0, cols, CHUNK):
                at = slice(c, c + CHUNK)
                if odd:
                    v0 = p0[k, at, 256:384] + p0[k + 1, at, 0:128]
                    v1 = p1[k, at, 256:384] + p1[k + 1, at, 0:128]
                    m0 = p0[k, at, 640:768] + p0[k + 1, at, 512:640]
                    m1 = p1[k, at, 640:768] + p1[k + 1, at, 512:640]
                else:
                    v0 = p0[k + 1, at, 128:256] + p0[k, at, 384:512]
                    v1 = p1[k + 1, at, 128:256] + p1[k, at, 384:512]
                    m0 = p1[k + 1, at, 512:640] + p1[k, at, 640:768]
                    m1 = p0[k + 1, at, 512:640] + p0[k, at, 640:768]
                out = pull(v0, v1, jnp.where(low, m0, m1), reward[2 * k + (0 if odd else 1), at], odd)
                for n, value in enumerate(out):
                    lanes = slice(n * 128, n * 128 + 128)
                    target[k, at, lanes] = value.astype(BF16)
                    tmp[k % 2, at, lanes] = value
            target[k, :, 384:512] = from_right(tmp[k % 2, :, 0:128]).astype(BF16)
            target[k, :, 512:640] = from_left(tmp[k % 2, :, 128:256]).astype(BF16)
            x = tmp[k % 2, :, 256:384]
            sides = (from_right(x), from_left(x)) if odd else (from_left(x), from_right(x))
            target[k, :, 640:768] = jnp.where(tall_low, *sides).astype(BF16)

        def block_row(k):
            for lanes in range(0, 384, 128):
                at, far = slice(lanes, lanes + 128), slice(lanes + 384, lanes + 512)
                x = t_odd[k + 1, :, at] + t_odd[k, :, far] + t_even[k, :, at] + t_even[k + 1, :, far]
                beside(back.at[k], 0, lanes, inside(x, k, 1, rows + 1), True)

        def hidden_pull(k):
            for c in range(0, cols, CHUNK):
                at = slice(c, c + CHUNK)
                v = hidden[k + 3, at].astype(F32)
                inv = lax.rsqrt(jnp.mean(v * v, axis=1, keepdims=True) + EPS)
                s = v * inv
                d = pulled(s, half_gain[...], act_grad[k, at])
                dv = inv * (d - s * jnp.mean(d * s, axis=1, keepdims=True))
                hid[k, at] = (back[k + 1, at, 384:768].astype(F32) + dv).astype(BF16)

        fine = rows + 3
        for k in range(rows):
            state_row(k)
        up_rows(0, rows)
        for k in range(rows, rows + 4):
            state_row(k)
        up_rows(rows, 4)
        for k in range(fine):
            pull_row(k, True)
            pull_row(k, False)
        t_odd[...] = mm(g_odd[...].reshape(fine * cols, 768), back_odd[...]).reshape(fine, cols, 768)
        t_even[...] = mm(g_even[...].reshape(fine * cols, 768), back_even[...]).reshape(fine, cols, 768)
        for k in range(rows + 2):
            block_row(k)
        lhs = [back[2 - i : 2 - i + rows].reshape(size, 1152) for i in range(3)]
        act_grad[...] = mm(jnp.concatenate(lhs, axis=1), mid_t[...]).reshape(rows, cols, 384)
        for k in range(rows):
            hidden_pull(k)

        z = mm_t(w_in[...], hid[...].reshape(size, 384))
        place = lax.broadcasted_iota(jnp.int32, (chan, size), 1)
        col = lax.rem(place, cols)
        sums = []
        for i in range(3):
            z0, z1, z2 = (z[(i * 3 + j) * chan : (i * 3 + j + 1) * chan] for j in range(3))
            left = jnp.where(col == cols - 1, 0.0, pltpu.roll(z0, size - 1, 1))
            right = jnp.where(col == 0, 0.0, pltpu.roll(z2, 1, 1))
            sums.append(left + z1 + right)
        inner = sums[1]
        inner = inner + jnp.where(place < size - cols, pltpu.roll(sums[0], size - cols, 1), 0.0)
        inner = inner + jnp.where(place >= cols, pltpu.roll(sums[2], cols, 1), 0.0)
        lines[0:chan] = inner
        lines[chan : 2 * chan] = sums[0]
        lines[2 * chan : 3 * chan] = sums[2]
        per_row = count // 2
        for u in range(count):
            pair, piece = u // per_row, u % per_row
            parts = []
            for a in range(2):
                at = (2 * pair + a) * cols + piece * width
                parts.append(lines[0:chan, at : at + width])
            at = piece * width + (0 if pair else (rows - 1) * cols)
            first = chan if pair else 2 * chan
            parts.append(lines[first : first + chan, at : at + width])
            parts.append(jnp.zeros((chan, 128 - 3 * width), F32))
            payload[u] = jnp.concatenate(parts, axis=1).astype(BF16)

    return body


def placing(info, order, sel, count, width, tokens):
    piece = width // 2
    pair = info[3]
    lane = lax.broadcasted_iota(jnp.int32, (128, 4 * tokens), 0)
    column = lax.broadcasted_iota(jnp.int32, (128, 4 * tokens), 1)
    group = (lane >= width).astype(jnp.int32) + (lane >= 2 * width).astype(jnp.int32)
    w = lane - group * width
    part = jnp.where(group == 2, pair, group)
    fixed = (2 * part + (w & 1)) * tokens + (w >> 1) - column
    fixed = jnp.where(lane < 3 * width, fixed, -99999)
    for t in range(count):
        step = t + 1 - 2 * pair
        valid = jnp.logical_and(step >= 0, step < count)
        beside = jnp.where(valid, piece * order[jnp.clip(step, 0, count - 1)], -9999)
        begin = jnp.where(group == 2, beside, piece * order[t])
        sel[t] = (fixed + begin == 0).astype(F32).astype(BF16)


def place_body(count, chan, tokens):
    def body(sel, got, out):
        total = mm(got[0], sel[0])
        for t in range(1, count):
            total += mm(got[t], sel[t])
        for k in range(4):
            out[k * chan : (k + 1) * chan] = total[:, k * tokens : (k + 1) * tokens]

    return body


def swaps(count):
    within = [(i, i ^ 1) for i in range(count)]
    across = [(0, 0), (count - 1, count - 1)]
    for i in range(1, count - 1, 2):
        across += [(i, i + 1), (i + 1, i)]
    return within, sorted(across)


def shards(
    latent, cached_latent, cached_features, reward_grad, conv_in_weight, conv_mid_weight, conv_up_weight, norm_gain, out_gain, shard_order
):
    count = lax.axis_size("tile")
    rows, cols, chan = latent.shape
    mid_chan = norm_gain.shape[0]
    o = out_gain.shape[0]
    tile = lax.axis_index("tile")
    info = jnp.stack(
        [tile % 2, (tile > 0).astype(jnp.int32), (tile < count - 1).astype(jnp.int32), (tile >= count // 2).astype(jnp.int32)]
    ).astype(jnp.int32)
    lat = jnp.transpose(latent, (0, 2, 1))
    lat_cached = jnp.transpose(cached_latent, (0, 1, 3, 2))
    reward_t = jnp.transpose(reward_grad, (0, 2, 1))
    up_t = jnp.transpose(conv_up_weight, (0, 1, 3, 2))
    mid = conv_mid_weight.reshape(3, 3, 3 * mid_chan, mid_chan)
    w_in = conv_in_weight.reshape(3, 3, 3 * chan, mid_chan)
    gain = 0.5 * norm_gain.reshape(1, mid_chan)
    gain_out = 0.5 * jnp.concatenate([out_gain, out_gain[128:]]).reshape(1, 256)
    within, across = swaps(count)
    size = rows * cols
    edge_rows = 3 * cols + 2 * chan * rows

    info, fwd, back_odd, back_even = call(
        taps_body,
        [((4,), jnp.int32), ((2, 768, 768), BF16), ((768, 768), BF16), ((768, 768), BF16)],
        1, 1, [], 1e10, 16, 1,
    )(info, up_t)

    own, send_even, send_odd = call(
        pack_body(rows, cols, o, chan),
        [((2 * rows, cols, 384), BF16), ((edge_rows, 384), BF16), ((edge_rows, 384), BF16)],
        1, 3, [], 1e10, 16,
    )(info, reward_t, lat, lat_cached)
    packed_even = lax.ppermute(send_even, "tile", within)
    packed_odd = lax.ppermute(send_odd, "tile", across)

    width = 2 * cols // count
    tokens = size // 4
    acc, part_even, part_odd, mid_t, sel = call(
        cached_body(rows, cols, count, width, tokens),
        [
            ((rows + 4, cols, 384), F32), ((3 * cols, 384), BF16), ((3 * cols, 384), BF16), ((3456, 384), BF16),
            ((count, 128, 4 * tokens), BF16),
        ],
        2, 2, [pltpu.VMEM((size, 2304), BF16)], 4e9, 24,
    )(info, shard_order, cached_features, mid)
    got_even = lax.ppermute(part_even, "tile", within)
    got_odd = lax.ppermute(part_odd, "tile", across)

    hidden, conv = call(
        current_body(rows, cols, chan),
        [((rows + 6, cols, 384), BF16), ((rows + 4, cols, 384), F32)],
        1, 7,
        [
            pltpu.VMEM((9 * rows * chan, 256), F32),
            pltpu.VMEM((3 * rows, 9 * chan, 256), BF16),
            pltpu.VMEM((rows + 6, cols, 1152), BF16),
            pltpu.VMEM((27 * chan, 384), BF16),
            pltpu.VMEM((2, cols, 384), F32),
        ],
        5e9, 24,
    )(info, lat, lat_cached, packed_even, packed_odd, w_in, mid, gain)

    (payload,) = call(
        back_body(rows, cols, chan, count, o),
        [((count, chan, 128), BF16)],
        1, 15,
        [
            pltpu.VMEM((2 * rows + 6, cols, 384), BF16),
            pltpu.VMEM((rows + 4, cols, 384), F32),
            pltpu.VMEM((rows + 4, cols, 768), F32),
            pltpu.VMEM((rows + 4, cols, 768), F32),
            pltpu.VMEM((rows + 3, cols, 768), BF16),
            pltpu.VMEM((rows + 3, cols, 768), BF16),
            pltpu.VMEM((rows + 4, cols, 1152), BF16),
            pltpu.VMEM((rows + 3, cols, 768), F32),
            pltpu.VMEM((rows + 3, cols, 768), F32),
            pltpu.VMEM((rows + 2, cols, 1152), BF16),
            pltpu.VMEM((rows, cols, 384), F32),
            pltpu.VMEM((rows, cols, 384), BF16),
            pltpu.VMEM((2, cols, 384), F32),
            pltpu.VMEM((2, cols, 384), F32),
            pltpu.VMEM((3 * chan, size), F32),
        ],
        8e9, 36,
    )(
        info, hidden, conv, acc, got_even, got_odd, packed_even, packed_odd, own, fwd, back_odd, back_even, mid_t,
        w_in[2].reshape(9 * chan, mid_chan), gain, gain_out,
    )
    received = lax.all_to_all(payload, "tile", split_axis=0, concat_axis=0, tiled=True)
    (placed,) = call(place_body(count, chan, tokens), [((4 * chan, tokens), F32)], 0, 2, [], 1e7, 16)(sel, received)
    return placed.T


def solution(mesh):
    return jax.shard_map(
        shards,
        mesh=mesh,
        in_specs=(
            P(("prompt", "tile"), None, None),
            P(None, ("prompt", "tile"), None, None),
            P(None, ("prompt", "tile"), None, None),
            P(("prompt", "tile"), None, None),
            P(),
            P(),
            P(),
            P(),
            P(),
            P("prompt"),
        ),
        out_specs=P(("prompt", "tile"), None),
        check_vma=False,
    )
```

```python
import jax
import jax.numpy as jnp
from jax import lax
from jax.experimental import pallas as pl
from jax.experimental.pallas import tpu as pltpu
from jax.sharding import PartitionSpec as P

EPS = 1e-06
F32 = jnp.float32
BF16 = jnp.bfloat16
VM = pl.BlockSpec(memory_space=pltpu.VMEM)
SM = pl.BlockSpec(memory_space=pltpu.SMEM)


def weave(*groups):
    total = max(len(g) for g in groups)
    done = [0] * len(groups)
    for k in range(total):
        for n, g in enumerate(groups):
            while done[n] * total < (k + 1) * len(g):
                g[done[n]]()
                done[n] += 1


def steps(f, *keys):
    return [lambda key=key: f(*key) for key in keys]


def call(body, outs, n_smem, n_vmem, scratch, flops, limit, smem_outs=0):
    specs = [SM] * n_smem + [VM] * n_vmem
    return pl.pallas_call(
        body,
        out_shape=[jax.ShapeDtypeStruct(s, d) for s, d in outs],
        in_specs=specs,
        out_specs=[SM] * smem_outs + [VM] * (len(outs) - smem_outs),
        scratch_shapes=scratch,
        cost_estimate=pl.CostEstimate(flops=int(flops), bytes_accessed=2**20, transcendentals=0),
        compiler_params=pltpu.CompilerParams(vmem_limit_bytes=limit << 20),
    )


def mm(a, b):
    return jnp.dot(a, b, preferred_element_type=F32)


def mm_t(a, b):
    return lax.dot_general(a, b, (((1,), (1,)), ((), ())), preferred_element_type=F32)


def flag(info, k):
    return info[k].astype(F32)


def from_left(x):
    moved = pltpu.roll(x, 1, 0)
    first = lax.broadcasted_iota(jnp.int32, (8, x.shape[1]), 0) == 0
    return jnp.concatenate([jnp.where(first, 0.0, moved[:8]), moved[8:]], axis=0)


def from_right(x):
    size = x.shape[0]
    moved = pltpu.roll(x, size - 1, 0)
    last = lax.broadcasted_iota(jnp.int32, (8, x.shape[1]), 0) == 7
    return jnp.concatenate([moved[: size - 8], jnp.where(last, 0.0, moved[size - 8 :])], axis=0)


def beside(target, base, lanes, x, ahead):
    sides = (from_right, from_left) if ahead else (from_left, from_right)
    for group, value in enumerate((sides[0](x), x, sides[1](x))):
        at = base + group * 384 + lanes
        target[:, at : at + 128] = value.astype(BF16)


CHUNK = 32


def picker(cols, o):
    half = o - 128
    x_index = lax.broadcasted_iota(jnp.int32, (cols, 2 * cols), 1)
    w_index = lax.broadcasted_iota(jnp.int32, (cols, 2 * cols), 0)
    pick = [(x_index == 2 * w_index + b).astype(F32).astype(BF16) for b in (0, 1)]
    zeros = jnp.zeros((128 - half, 2 * cols), BF16)

    def one(reward, f, own, k):
        r = reward[f]
        first, rest = r[:128], r[128:]
        low = jnp.concatenate([first, rest, zeros], axis=0)
        high = jnp.concatenate([first, zeros, rest], axis=0)
        sides = (low, high) if f % 2 else (high, low)
        d0, d1 = mm_t(pick[0], sides[0]), mm_t(pick[1], sides[1])
        own[k, :, 0:128] = d0[:, :128].astype(BF16)
        own[k, :, 128:256] = d1[:, :128].astype(BF16)
        own[k, :, 256:384] = (d0[:, 128:] + d1[:, 128:]).astype(BF16)

    return one


def pack_body(rows, cols, o, chan):
    def body(info, reward, latent, cached, own, send_even, send_odd):
        one = picker(cols, o)
        for k in range(6):
            one(reward, k if k < 3 else 2 * rows - 6 + k, own, k)
        base = 3 * cols
        per = chan * rows
        for send, last in ((send_even, 1 - info[0]), (send_odd, info[0])):
            begin = last * 3
            for k in range(3):
                send[k * cols : (k + 1) * cols] = own[begin + k]
            for t in range(3):
                src = cached[t] if t < 2 else latent[...]
                lat = src.reshape(per, cols)
                send[base : base + per, t * 128 : t * 128 + 128] = lat[:, :128]
                send[base + per : base + 2 * per, t * 128 : t * 128 + cols - 128] = lat[:, 128:]

    return body


def home(targets, q, p, tile):
    block, second = ((1, 1), (0, 0), (0, 1), (1, 0))[p]
    target, side = targets[q]
    if tile < 2:
        row = block * 384 + second * 128 + tile * 64
    else:
        row = block * 384 + 256 + 64 * (second if q % 2 == 0 else 1 - second)
    return target, row, side * 384


def turning(back_odd, back_even, fwd):
    targets = ((back_odd, 1), (back_even, 0), (back_odd, 0), (back_even, 1))

    def tap_tile(q, p, tile, lanes):
        target, row, side = home(targets, q, p, tile)
        return target[row : row + 64, side + lanes : side + lanes + 128]

    def one(b, side, lanes):
        p = ((3, 1), (2, 0))[b][side]
        at = slice(side * 384 + lanes, side * 384 + lanes + 128)
        for q in range(4):
            both = jnp.concatenate([tap_tile(q, p, 0, lanes), tap_tile(q, p, 1, lanes)], axis=0)
            fwd[b, at, q * 128 : q * 128 + 128] = both.T
        for half in range(2):
            pair = (2 * half, 2 * half + 1) if b == 0 else (2 * half + 1, 2 * half)
            both = jnp.concatenate([tap_tile(q, p, 2, lanes) for q in pair], axis=0)
            fwd[b, at, 512 + half * 128 : 640 + half * 128] = both.T

    return steps(one, *[(b, side, lanes) for b in range(2) for side in range(2) for lanes in range(0, 384, 128)])


def taps_body(info, up, info_out, back_odd, back_even):
    for k in range(4):
        info_out[k] = info[k]

    parts = ((2,), (1, 2), (0, 1), (0,))
    targets = ((back_odd, 1), (back_even, 0), (back_odd, 0), (back_even, 1))

    for tile in range(3):
        for lanes in range(0, 384, 128):
            w = [[up[i, j, tile * 64 : tile * 64 + 64, lanes : lanes + 128].astype(F32) for j in range(3)] for i in range(3)]
            for q in range(4):
                c = [w[parts[q][0]][j] + w[parts[q][1]][j] if len(parts[q]) > 1 else w[parts[q][0]][j] for j in range(3)]
                for p, tap in enumerate((c[2], c[1] + c[2], c[0] + c[1], c[0])):
                    target, row, side = home(targets, q, p, tile)
                    target[row : row + 64, side + lanes : side + lanes + 128] = tap.astype(BF16)


def cached_body(rows, cols, count, width, tokens, o):
    size = rows * cols

    def body(
        info, order, features, mid, back_odd, back_even, reward, acc, send_even, send_odd, mid_t, sel, fwd, own, wide, parts
    ):
        for t in range(2):
            for r in range(rows):
                for lanes in range(0, 384, 128):
                    x = features[t, r, :, lanes : lanes + 128].astype(F32)
                    beside(wide.at[r * cols : (r + 1) * cols], t * 1152, lanes, x, False)
        def product(i, lanes):
            parts[i, :, lanes] = mm(wide[...], jnp.concatenate([mid[0, i, :, lanes], mid[1, i, :, lanes]], axis=0))

        def double():
            left = jnp.concatenate([mid[0, 0, :, 256:384], mid[1, 0, :, 256:384]], axis=0)
            right = jnp.concatenate([mid[0, 1, :, 256:384], mid[1, 1, :, 256:384]], axis=0)
            both = mm(wide[...], jnp.concatenate([left, right], axis=1))
            parts[0, :, 256:384] = both[:, :128]
            parts[1, :, 256:384] = both[:, 128:]

        def turn(i, j):
            at = (i * 3 + j) * 384
            mid_t[at : at + 384] = mid[2, i, j * 384 : (j + 1) * 384].T

        most, rest = slice(0, 256), slice(256, 384)
        products = steps(product, (0, most), (1, most)) + steps(double, ()) + steps(product, (2, most), (2, rest))
        one = picker(cols, o)
        others = steps(turn, *[(i, j) for i in range(3) for j in range(3)])
        others += turning(back_odd, back_even, fwd)
        others += steps(placing(info, order, sel, count, width, tokens), *[(t,) for t in range(count)])
        others += steps(one, (reward, rows - 1, own, 0), (reward, rows, own, 1))
        weave(others, products)
        for k in range(rows + 4):
            total = jnp.zeros((cols, 384), F32)
            for i in range(3):
                r = k - 3 + i
                if 0 <= r < rows:
                    total = total + parts[i, r * cols : (r + 1) * cols]
            acc[k] = total
        for send, last in ((send_even, 1 - info[0]), (send_odd, info[0])):
            for k in range(3):
                send[k * cols : (k + 1) * cols] = acc[1 + last * 3 + k].astype(BF16)

    return body


def current_body(rows, cols, chan):
    per = chan * rows
    base = 3 * cols

    def body(info, latent, cached, got_even, got_odd, w_in, mid, half_gain, hidden, conv, lat, tall, wide, w_order, plain):
        even = info[0] == 0
        lat[...] = jnp.zeros_like(lat)

        def fill(first_row, got, ok):
            scale = ok.astype(F32)
            for t in range(3):
                x = got[base : base + per, t * 128 : t * 128 + 128].astype(F32) * scale
                y = got[base + per : base + 2 * per, t * 128 : t * 128 + cols - 128].astype(F32) * scale
                for r in range(rows):
                    at = pl.ds((first_row + r) * 3 * chan + t * chan, chan)
                    lat[at, 0:128] = x[r * chan : (r + 1) * chan]
                    lat[at, 128:cols] = y[r * chan : (r + 1) * chan]

        @pl.when(even)
        def _():
            fill(0, got_odd, info[1])
            fill(2 * rows, got_even, info[2])

        @pl.when(jnp.logical_not(even))
        def _():
            fill(0, got_even, info[1])
            fill(2 * rows, got_odd, info[2])

        for t in range(3):
            for r in range(rows):
                at = pl.ds((rows + r) * 3 * chan + t * chan, chan)
                lat[at, 0:cols] = (cached[t, r] if t < 2 else latent[r]).astype(F32)

        for r in range(3 * rows):
            for t in range(3):
                x = lat[pl.ds((r * 3 + t) * chan, chan), :]
                at = t * 3 * chan
                tall[r, at : at + chan] = pltpu.roll(x, 1, 1).astype(BF16)
                tall[r, at + chan : at + 2 * chan] = x.astype(BF16)
                tall[r, at + 2 * chan : at + 3 * chan] = pltpu.roll(x, 255, 1).astype(BF16)
        for i in range(3):
            for t in range(3):
                at = (i * 3 + t) * 3 * chan
                w_order[at : at + 3 * chan] = w_in[t, i]

        def hidden_row(k):
            lhs = tall[k : k + 3].reshape(27 * chan, 256)[:, 0:cols]
            h = lax.dot_general(lhs, w_order[...], (((0,), (0,)), ((), ())), preferred_element_type=F32)
            plain[k % 2] = h
            for c in range(0, cols, CHUNK):
                at = slice(c, c + CHUNK)
                v = plain[k % 2, at].astype(BF16)
                hidden[k, at] = v
                v = v.astype(F32)
                inv = lax.rsqrt(jnp.mean(v * v, axis=1, keepdims=True) + EPS)
                half = v * inv * half_gain[...]
                act = half * (jnp.tanh(half) + 1.0)
                if k < 3:
                    act = act * flag(info, 1)
                if k >= rows + 3:
                    act = act * flag(info, 2)
                plain[k % 2, at] = act
            for lanes in range(0, 384, 128):
                beside(wide.at[k], 0, lanes, plain[k % 2, :, lanes : lanes + 128], False)

        def conv_rows(p, number, lanes):
            lhs = [wide[p + i : p + i + number].reshape(number * cols, 1152) for i in range(3)]
            total = mm(jnp.concatenate(lhs, axis=1), mid[2, :, :, lanes].reshape(3456, lanes.stop - lanes.start))
            conv[p : p + number, :, lanes] = total.reshape(number, cols, lanes.stop - lanes.start)

        def convs(p, number):
            return steps(conv_rows, (p, number, slice(0, 256)), (p, number, slice(256, 384)))

        for k in range(rows + 2):
            hidden_row(k)
        weave(steps(hidden_row, *[(k,) for k in range(rows + 2, rows + 6)]), convs(0, rows))
        weave(convs(rows, 4))

    return body


def pulled(s, half_gain, grad):
    h = s * half_gain
    t = jnp.tanh(h)
    return (grad * half_gain) * ((1.0 + t) * (1.0 + h * (1.0 - t)))


def back_body(rows, cols, chan, count, o):
    size = rows * cols
    width = 2 * cols // count

    def body(
        info, hidden, conv, acc, got_even, got_odd, packed_even, packed_odd, own, own_mid, fwd, back_odd, back_even, mid_t, w_in, half_gain,
        half_out, payload, reward, edge, p0, p1, g_odd, g_even, wide, t_odd, t_even, back, act_grad, hid, tmp_odd, tmp_even, lines,
    ):
        even = info[0] == 0
        top, bottom = flag(info, 1), flag(info, 2)

        def take(got, packed, before):
            ok = top if before else bottom
            place = 0 if before else rows + 1
            for k in range(3):
                at = slice(k * cols, (k + 1) * cols)
                edge[place + k] = got[at].astype(F32) * ok
                reward[k if before else 2 * rows + 3 + k] = (packed[at].astype(F32) * ok).astype(BF16)

        @pl.when(even)
        def _():
            take(got_odd, packed_odd, True)
            take(got_even, packed_even, False)

        @pl.when(jnp.logical_not(even))
        def _():
            take(got_even, packed_even, True)
            take(got_odd, packed_odd, False)

        reward[3:6] = own[0:3]
        reward[6 : 2 * rows] = own_mid[...]
        reward[2 * rows : 2 * rows + 3] = own[3:6]

        def inside(x, k, first, last):
            return x * top if k < first else x * bottom if k >= last else x

        def state_row(k):
            for lanes in range(0, 384, 128):
                at = slice(lanes, lanes + 128)
                x = hidden[k + 1, :, at].astype(F32) + conv[k, :, at]
                if 1 <= k <= rows + 2:
                    x = x + acc[k, :, at]
                if k < 3 or k > rows:
                    x = x + edge[k, :, at]
                beside(wide.at[k], 0, lanes, inside(x, k, 2, rows + 2), False)

        def up_rows(k, number, b, n):
            x = wide[k : k + number, :, b * 384 : b * 384 + 768].reshape(number * cols, 768)
            lanes = slice(n * 256, n * 256 + 256)
            (p0, p1)[b][k : k + number, :, lanes] = mm(x, fwd[b, :, lanes]).reshape(number, cols, 256)

        def down_rows(k, number, odd, n):
            g, kernel, t = (g_odd, back_odd, t_odd) if odd else (g_even, back_even, t_even)
            lanes = slice(n * 256, n * 256 + 256)
            x = g[k : k + number].reshape(number * cols, 768)
            t[k : k + number, :, lanes] = mm(x, kernel[:, lanes]).reshape(number, cols, 256)

        low = lax.broadcasted_iota(jnp.int32, (CHUNK, 128), 1) < 64
        tall_low = lax.broadcasted_iota(jnp.int32, (cols, 128), 1) < 64
        gains = [half_out[:, 0:128], half_out[:, 128:256]]

        def pull(v0, v1, vm, r, zero_low):
            mine = low if zero_low else jnp.logical_not(low)
            def both(a0, a1, am):
                s0 = jnp.sum(a0 + jnp.where(mine, am, 0.0), axis=1, keepdims=True)
                s1 = jnp.sum(a1 + jnp.where(mine, 0.0, am), axis=1, keepdims=True)
                return s0 * (1.0 / o), s1 * (1.0 / o)

            q0, q1 = both(v0 * v0, v1 * v1, vm * vm)
            i0, i1 = lax.rsqrt(q0 + EPS), lax.rsqrt(q1 + EPS)
            im = jnp.where(mine, i0, i1)
            out = []
            for v, i, g, k in ((v0, i0, gains[0], 0), (v1, i1, gains[0], 1), (vm, im, gains[1], 2)):
                s = v * i
                out.append((s, pulled(s, g, r[:, k * 128 : k * 128 + 128].astype(F32))))
            m0, m1 = both(*(s * d for s, d in out))
            mx = jnp.where(mine, m0, m1)
            return [i * (d - s * m) for (s, d), i, m in zip(out, (i0, i1, im), (m0, m1, mx))]

        def pull_row(k, odd):
            target, tmp = (g_odd, tmp_odd) if odd else (g_even, tmp_even)
            for c in range(0, cols, CHUNK):
                at = slice(c, c + CHUNK)
                if odd:
                    v0 = p0[k, at, 256:384] + p0[k + 1, at, 0:128]
                    v1 = p1[k, at, 256:384] + p1[k + 1, at, 0:128]
                    m0 = p0[k, at, 640:768] + p0[k + 1, at, 512:640]
                    m1 = p1[k, at, 640:768] + p1[k + 1, at, 512:640]
                else:
                    v0 = p0[k + 1, at, 128:256] + p0[k, at, 384:512]
                    v1 = p1[k + 1, at, 128:256] + p1[k, at, 384:512]
                    m0 = p1[k + 1, at, 512:640] + p1[k, at, 640:768]
                    m1 = p0[k + 1, at, 512:640] + p0[k, at, 640:768]
                out = pull(v0, v1, jnp.where(low, m0, m1), reward[2 * k + (0 if odd else 1), at], odd)
                for n, value in enumerate(out):
                    lanes = slice(n * 128, n * 128 + 128)
                    target[k, at, lanes] = value.astype(BF16)
                    tmp[k % 2, at, lanes] = value
            target[k, :, 384:512] = from_right(tmp[k % 2, :, 0:128]).astype(BF16)
            target[k, :, 512:640] = from_left(tmp[k % 2, :, 128:256]).astype(BF16)
            x = tmp[k % 2, :, 256:384]
            sides = (from_right(x), from_left(x)) if odd else (from_left(x), from_right(x))
            target[k, :, 640:768] = jnp.where(tall_low, *sides).astype(BF16)

        def block_row(k):
            for lanes in range(0, 384, 128):
                at, far = slice(lanes, lanes + 128), slice(lanes + 384, lanes + 512)
                x = t_odd[k + 1, :, at] + t_odd[k, :, far] + t_even[k, :, at] + t_even[k + 1, :, far]
                beside(back.at[k], 0, lanes, inside(x, k, 1, rows + 1), True)

        def hidden_pull(k):
            for c in range(0, cols, CHUNK):
                at = slice(c, c + CHUNK)
                v = hidden[k + 3, at].astype(F32)
                inv = lax.rsqrt(jnp.mean(v * v, axis=1, keepdims=True) + EPS)
                s = v * inv
                d = pulled(s, half_gain[...], act_grad[k, at])
                dv = inv * (d - s * jnp.mean(d * s, axis=1, keepdims=True))
                hid[k, at] = (back[k + 1, at, 384:768].astype(F32) + dv).astype(BF16)

        def each(f, first, last):
            return steps(f, *[(k,) for k in range(first, last)])

        def ups(k, number):
            return steps(up_rows, *[(k, number, b, n) for n in range(3) for b in range(2)])

        def downs(k, number):
            return steps(down_rows, *[(k, number, odd, n) for n in range(3) for odd in (True, False)])

        def pulls(first, last):
            return steps(pull_row, *[(k, odd) for k in range(first, last) for odd in (True, False)])

        weave(each(state_row, 0, rows))
        weave(each(state_row, rows, rows + 4), ups(0, rows))
        weave(pulls(0, rows - 1), ups(rows, 4))
        weave(pulls(rows - 1, rows + 3), downs(0, rows - 1))
        weave(each(block_row, 0, rows - 2), downs(rows - 1, 4))
        weave(each(block_row, rows - 2, rows + 2))
        lhs = [back[2 - i : 2 - i + rows].reshape(size, 1152) for i in range(3)]
        act_grad[...] = mm(jnp.concatenate(lhs, axis=1), mid_t[...]).reshape(rows, cols, 384)
        for k in range(rows):
            hidden_pull(k)

        z = mm_t(w_in[...], hid[...].reshape(size, 384))
        place = lax.broadcasted_iota(jnp.int32, (chan, size), 1)
        col = lax.rem(place, cols)
        sums = []
        for i in range(3):
            z0, z1, z2 = (z[(i * 3 + j) * chan : (i * 3 + j + 1) * chan] for j in range(3))
            left = jnp.where(col == cols - 1, 0.0, pltpu.roll(z0, size - 1, 1))
            right = jnp.where(col == 0, 0.0, pltpu.roll(z2, 1, 1))
            sums.append(left + z1 + right)
        inner = sums[1]
        inner = inner + jnp.where(place < size - cols, pltpu.roll(sums[0], size - cols, 1), 0.0)
        inner = inner + jnp.where(place >= cols, pltpu.roll(sums[2], cols, 1), 0.0)
        lines[0:chan] = inner
        lines[chan : 2 * chan] = sums[0]
        lines[2 * chan : 3 * chan] = sums[2]
        per_row = count // 2
        for u in range(count):
            pair, piece = u // per_row, u % per_row
            parts = []
            for a in range(2):
                at = (2 * pair + a) * cols + piece * width
                parts.append(lines[0:chan, at : at + width])
            at = piece * width + (0 if pair else (rows - 1) * cols)
            first = chan if pair else 2 * chan
            parts.append(lines[first : first + chan, at : at + width])
            parts.append(jnp.zeros((chan, 128 - 3 * width), F32))
            payload[u] = jnp.concatenate(parts, axis=1).astype(BF16)

    return body


def placing(info, order, sel, count, width, tokens):
    piece = width // 2
    pair = info[3]
    lane = lax.broadcasted_iota(jnp.int32, (128, 4 * tokens), 0)
    column = lax.broadcasted_iota(jnp.int32, (128, 4 * tokens), 1)
    group = (lane >= width).astype(jnp.int32) + (lane >= 2 * width).astype(jnp.int32)
    w = lane - group * width
    part = jnp.where(group == 2, pair, group)
    fixed = (2 * part + (w & 1)) * tokens + (w >> 1) - column
    fixed = jnp.where(lane < 3 * width, fixed, -99999)

    def one(t):
        step = t + 1 - 2 * pair
        valid = jnp.logical_and(step >= 0, step < count)
        beside = jnp.where(valid, piece * order[jnp.clip(step, 0, count - 1)], -9999)
        begin = jnp.where(group == 2, beside, piece * order[t])
        sel[t] = (fixed + begin == 0).astype(F32).astype(BF16)

    return one


def place_body(count, chan, tokens):
    def body(sel, got, out):
        total = mm(got[0], sel[0])
        for t in range(1, count):
            total += mm(got[t], sel[t])
        for k in range(4):
            out[k * chan : (k + 1) * chan] = total[:, k * tokens : (k + 1) * tokens]

    return body


def swaps(count):
    within = [(i, i ^ 1) for i in range(count)]
    across = [(0, 0), (count - 1, count - 1)]
    for i in range(1, count - 1, 2):
        across += [(i, i + 1), (i + 1, i)]
    return within, sorted(across)


def shards(
    latent, cached_latent, cached_features, reward_grad, conv_in_weight, conv_mid_weight, conv_up_weight, norm_gain, out_gain, shard_order
):
    count = lax.axis_size("tile")
    rows, cols, chan = latent.shape
    mid_chan = norm_gain.shape[0]
    o = out_gain.shape[0]
    tile = lax.axis_index("tile")
    info = jnp.stack(
        [tile % 2, (tile > 0).astype(jnp.int32), (tile < count - 1).astype(jnp.int32), (tile >= count // 2).astype(jnp.int32)]
    ).astype(jnp.int32)
    lat = jnp.transpose(latent, (0, 2, 1))
    lat_cached = jnp.transpose(cached_latent, (0, 1, 3, 2))
    reward_t = jnp.transpose(reward_grad, (0, 2, 1))
    up_t = jnp.transpose(conv_up_weight, (0, 1, 3, 2))
    mid = conv_mid_weight.reshape(3, 3, 3 * mid_chan, mid_chan)
    w_in = conv_in_weight.reshape(3, 3, 3 * chan, mid_chan)
    gain = 0.5 * norm_gain.reshape(1, mid_chan)
    gain_out = 0.5 * jnp.concatenate([out_gain, out_gain[128:]]).reshape(1, 256)
    within, across = swaps(count)
    size = rows * cols
    edge_rows = 3 * cols + 2 * chan * rows

    info, back_odd, back_even = call(
        taps_body,
        [((4,), jnp.int32), ((768, 768), BF16), ((768, 768), BF16)],
        1, 1, [], 1e10, 8, 1,
    )(info, up_t)

    own, send_even, send_odd = call(
        pack_body(rows, cols, o, chan),
        [((6, cols, 384), BF16), ((edge_rows, 384), BF16), ((edge_rows, 384), BF16)],
        1, 3, [], 1e10, 8,
    )(info, reward_t, lat, lat_cached)
    packed_even = lax.ppermute(send_even, "tile", within)
    packed_odd = lax.ppermute(send_odd, "tile", across)

    width = 2 * cols // count
    tokens = size // 4
    acc, part_even, part_odd, mid_t, sel, fwd, own_mid = call(
        cached_body(rows, cols, count, width, tokens, o),
        [
            ((rows + 4, cols, 384), F32), ((3 * cols, 384), BF16), ((3 * cols, 384), BF16), ((3456, 384), BF16),
            ((count, 128, 4 * tokens), BF16), ((2, 768, 768), BF16), ((2, cols, 384), BF16),
        ],
        2, 5, [pltpu.VMEM((size, 2304), BF16), pltpu.VMEM((3, size, 384), F32)], 4e9, 14,
    )(info, shard_order, cached_features, mid, back_odd, back_even, reward_t)
    got_even = lax.ppermute(part_even, "tile", within)
    got_odd = lax.ppermute(part_odd, "tile", across)

    hidden, conv = call(
        current_body(rows, cols, chan),
        [((rows + 6, cols, 384), BF16), ((rows + 4, cols, 384), F32)],
        1, 7,
        [
            pltpu.VMEM((9 * rows * chan, 256), F32),
            pltpu.VMEM((3 * rows, 9 * chan, 256), BF16),
            pltpu.VMEM((rows + 6, cols, 1152), BF16),
            pltpu.VMEM((27 * chan, 384), BF16),
            pltpu.VMEM((2, cols, 384), F32),
        ],
        5e9, 14,
    )(info, lat, lat_cached, packed_even, packed_odd, w_in, mid, gain)

    (payload,) = call(
        back_body(rows, cols, chan, count, o),
        [((count, chan, 128), BF16)],
        1, 16,
        [
            pltpu.VMEM((2 * rows + 6, cols, 384), BF16),
            pltpu.VMEM((rows + 4, cols, 384), F32),
            pltpu.VMEM((rows + 4, cols, 768), F32),
            pltpu.VMEM((rows + 4, cols, 768), F32),
            pltpu.VMEM((rows + 3, cols, 768), BF16),
            pltpu.VMEM((rows + 3, cols, 768), BF16),
            pltpu.VMEM((rows + 4, cols, 1152), BF16),
            pltpu.VMEM((rows + 3, cols, 768), F32),
            pltpu.VMEM((rows + 3, cols, 768), F32),
            pltpu.VMEM((rows + 2, cols, 1152), BF16),
            pltpu.VMEM((rows, cols, 384), F32),
            pltpu.VMEM((rows, cols, 384), BF16),
            pltpu.VMEM((2, cols, 384), F32),
            pltpu.VMEM((2, cols, 384), F32),
            pltpu.VMEM((3 * chan, size), F32),
        ],
        8e9, 34,
    )(
        info, hidden, conv, acc, got_even, got_odd, packed_even, packed_odd, own, own_mid, fwd, back_odd, back_even, mid_t,
        w_in[2].reshape(9 * chan, mid_chan), gain, gain_out,
    )
    received = lax.all_to_all(payload, "tile", split_axis=0, concat_axis=0, tiled=True)
    (placed,) = call(place_body(count, chan, tokens), [((4 * chan, tokens), F32)], 0, 2, [], 1e7, 8)(sel, received)
    return placed.T


def solution(mesh):
    return jax.shard_map(
        shards,
        mesh=mesh,
        in_specs=(
            P(("prompt", "tile"), None, None),
            P(None, ("prompt", "tile"), None, None),
            P(None, ("prompt", "tile"), None, None),
            P(("prompt", "tile"), None, None),
            P(),
            P(),
            P(),
            P(),
            P(),
            P("prompt"),
        ),
        out_specs=P(("prompt", "tile"), None),
        check_vma=False,
    )
```

```python
import jax
import jax.numpy as jnp
from jax import lax
from jax.experimental import pallas as pl
from jax.experimental.pallas import tpu as pltpu
from jax.sharding import PartitionSpec as P

EPS = 1e-06
F32 = jnp.float32
BF16 = jnp.bfloat16
VM = pl.BlockSpec(memory_space=pltpu.VMEM)
SM = pl.BlockSpec(memory_space=pltpu.SMEM)


def weave(*groups):
    total = max(len(g) for g in groups)
    done = [0] * len(groups)
    for k in range(total):
        for n, g in enumerate(groups):
            while done[n] * total < (k + 1) * len(g):
                g[done[n]]()
                done[n] += 1


def steps(f, *keys):
    return [lambda key=key: f(*key) for key in keys]


def call(body, outs, n_smem, n_vmem, scratch, flops, limit, smem_outs=0):
    specs = [SM] * n_smem + [VM] * n_vmem
    return pl.pallas_call(
        body,
        out_shape=[jax.ShapeDtypeStruct(s, d) for s, d in outs],
        in_specs=specs,
        out_specs=[SM] * smem_outs + [VM] * (len(outs) - smem_outs),
        scratch_shapes=scratch,
        cost_estimate=pl.CostEstimate(flops=int(flops), bytes_accessed=2**20, transcendentals=0),
        compiler_params=pltpu.CompilerParams(vmem_limit_bytes=limit << 20),
    )


def mm(a, b):
    return jnp.dot(a, b, preferred_element_type=F32)


def mm_t(a, b):
    return lax.dot_general(a, b, (((1,), (1,)), ((), ())), preferred_element_type=F32)


def flag(info, k):
    return info[k].astype(F32)


def from_left(x):
    moved = pltpu.roll(x, 1, 0)
    first = lax.broadcasted_iota(jnp.int32, (8, x.shape[1]), 0) == 0
    return jnp.concatenate([jnp.where(first, 0.0, moved[:8]), moved[8:]], axis=0)


def from_right(x):
    size = x.shape[0]
    moved = pltpu.roll(x, size - 1, 0)
    last = lax.broadcasted_iota(jnp.int32, (8, x.shape[1]), 0) == 7
    return jnp.concatenate([moved[: size - 8], jnp.where(last, 0.0, moved[size - 8 :])], axis=0)


def beside(target, base, lanes, x, ahead):
    sides = (from_right, from_left) if ahead else (from_left, from_right)
    for group, value in enumerate((sides[0](x), x, sides[1](x))):
        at = base + group * 384 + lanes
        target[:, at : at + 128] = value.astype(BF16)


CHUNK = 32


def picker(cols, o):
    half = o - 128
    x_index = lax.broadcasted_iota(jnp.int32, (cols, 2 * cols), 1)
    w_index = lax.broadcasted_iota(jnp.int32, (cols, 2 * cols), 0)
    pick = [(x_index == 2 * w_index + b).astype(F32).astype(BF16) for b in (0, 1)]
    zeros = jnp.zeros((128 - half, 2 * cols), BF16)

    def one(reward, f, own, k):
        r = reward[f]
        first, rest = r[:128], r[128:]
        low = jnp.concatenate([first, rest, zeros], axis=0)
        high = jnp.concatenate([first, zeros, rest], axis=0)
        sides = (low, high) if f % 2 else (high, low)
        d0, d1 = mm_t(pick[0], sides[0]), mm_t(pick[1], sides[1])
        own[k, :, 0:128] = d0[:, :128].astype(BF16)
        own[k, :, 128:256] = d1[:, :128].astype(BF16)
        own[k, :, 256:384] = (d0[:, 128:] + d1[:, 128:]).astype(BF16)

    return one


def pack_body(rows, cols, o, chan):
    def body(info, reward, latent, cached, own, send_even, send_odd):
        one = picker(cols, o)
        for k in range(6):
            one(reward, k if k < 3 else 2 * rows - 6 + k, own, k)
        base = 3 * cols
        per = chan * rows
        for send, last in ((send_even, 1 - info[0]), (send_odd, info[0])):
            begin = last * 3
            for k in range(3):
                send[k * cols : (k + 1) * cols] = own[begin + k]
            for t in range(3):
                src = cached[t] if t < 2 else latent[...]
                lat = src.reshape(per, cols)
                send[base : base + per, t * 128 : t * 128 + 128] = lat[:, :128]
                send[base + per : base + 2 * per, t * 128 : t * 128 + cols - 128] = lat[:, 128:]

    return body


def home(targets, q, p, tile):
    block, second = ((1, 1), (0, 0), (0, 1), (1, 0))[p]
    target, side = targets[q]
    if tile < 2:
        row = block * 384 + second * 128 + tile * 64
    else:
        row = block * 384 + 256 + 64 * (second if q % 2 == 0 else 1 - second)
    return target, row, side * 384


def turning(back_odd, back_even, fwd):
    targets = ((back_odd, 1), (back_even, 0), (back_odd, 0), (back_even, 1))

    def tap_tile(q, p, tile, lanes):
        target, row, side = home(targets, q, p, tile)
        return target[row : row + 64, side + lanes : side + lanes + 128]

    def one(b, side, lanes):
        p = ((3, 1), (2, 0))[b][side]
        at = slice(side * 384 + lanes, side * 384 + lanes + 128)
        for q in range(4):
            both = jnp.concatenate([tap_tile(q, p, 0, lanes), tap_tile(q, p, 1, lanes)], axis=0)
            fwd[b, at, q * 128 : q * 128 + 128] = both.T
        for half in range(2):
            pair = (2 * half, 2 * half + 1) if b == 0 else (2 * half + 1, 2 * half)
            both = jnp.concatenate([tap_tile(q, p, 2, lanes) for q in pair], axis=0)
            fwd[b, at, 512 + half * 128 : 640 + half * 128] = both.T

    return steps(one, *[(b, side, lanes) for b in range(2) for side in range(2) for lanes in range(0, 384, 128)])


def taps_body(info, up, info_out, back_odd, back_even):
    for k in range(4):
        info_out[k] = info[k]

    parts = ((2,), (1, 2), (0, 1), (0,))
    targets = ((back_odd, 1), (back_even, 0), (back_odd, 0), (back_even, 1))

    for tile in range(3):
        for lanes in range(0, 384, 128):
            w = [[up[i, j, tile * 64 : tile * 64 + 64, lanes : lanes + 128].astype(F32) for j in range(3)] for i in range(3)]
            for q in range(4):
                c = [w[parts[q][0]][j] + w[parts[q][1]][j] if len(parts[q]) > 1 else w[parts[q][0]][j] for j in range(3)]
                for p, tap in enumerate((c[2], c[1] + c[2], c[0] + c[1], c[0])):
                    target, row, side = home(targets, q, p, tile)
                    target[row : row + 64, side + lanes : side + lanes + 128] = tap.astype(BF16)


def cached_body(rows, cols, count, width, tokens, o):
    size = rows * cols

    def body(
        info, order, features, mid, back_odd, back_even, reward, acc, send_even, send_odd, mid_t, sel, fwd, own, wide, parts
    ):
        for t in range(2):
            for r in range(rows):
                for lanes in range(0, 384, 128):
                    x = features[t, r, :, lanes : lanes + 128].astype(F32)
                    beside(wide.at[r * cols : (r + 1) * cols], t * 1152, lanes, x, False)
        def product(i, lanes):
            parts[i, :, lanes] = mm(wide[...], jnp.concatenate([mid[0, i, :, lanes], mid[1, i, :, lanes]], axis=0))

        def double():
            left = jnp.concatenate([mid[0, 0, :, 256:384], mid[1, 0, :, 256:384]], axis=0)
            right = jnp.concatenate([mid[0, 1, :, 256:384], mid[1, 1, :, 256:384]], axis=0)
            both = mm(wide[...], jnp.concatenate([left, right], axis=1))
            parts[0, :, 256:384] = both[:, :128]
            parts[1, :, 256:384] = both[:, 128:]

        def turn(i, j):
            at = (i * 3 + j) * 384
            mid_t[at : at + 384] = mid[2, i, j * 384 : (j + 1) * 384].T

        most, rest = slice(0, 256), slice(256, 384)
        products = steps(product, (0, most), (1, most)) + steps(double, ()) + steps(product, (2, most), (2, rest))
        one = picker(cols, o)
        others = steps(turn, *[(i, j) for i in range(3) for j in range(3)])
        others += turning(back_odd, back_even, fwd)
        others += steps(placing(info, order, sel, count, width, tokens), *[(t,) for t in range(count)])
        others += steps(one, (reward, rows - 1, own, 0), (reward, rows, own, 1))
        weave(others, products)
        for k in range(rows + 4):
            total = jnp.zeros((cols, 384), F32)
            for i in range(3):
                r = k - 3 + i
                if 0 <= r < rows:
                    total = total + parts[i, r * cols : (r + 1) * cols]
            acc[k] = total
        for send, last in ((send_even, 1 - info[0]), (send_odd, info[0])):
            for k in range(3):
                send[k * cols : (k + 1) * cols] = acc[1 + last * 3 + k].astype(BF16)

    return body


def current_body(rows, cols, chan):
    per = chan * rows
    base = 3 * cols

    def body(info, latent, cached, got_even, got_odd, w_in, mid, half_gain, hidden, conv, lat, tall, wide, w_order, plain):
        even = info[0] == 0
        lat[...] = jnp.zeros_like(lat)

        def fill(first_row, got, ok):
            scale = ok.astype(F32)
            for t in range(3):
                x = got[base : base + per, t * 128 : t * 128 + 128].astype(F32) * scale
                y = got[base + per : base + 2 * per, t * 128 : t * 128 + cols - 128].astype(F32) * scale
                for r in range(rows):
                    at = pl.ds((first_row + r) * 3 * chan + t * chan, chan)
                    lat[at, 0:128] = x[r * chan : (r + 1) * chan]
                    lat[at, 128:cols] = y[r * chan : (r + 1) * chan]

        @pl.when(even)
        def _():
            fill(0, got_odd, info[1])
            fill(2 * rows, got_even, info[2])

        @pl.when(jnp.logical_not(even))
        def _():
            fill(0, got_even, info[1])
            fill(2 * rows, got_odd, info[2])

        for t in range(3):
            for r in range(rows):
                at = pl.ds((rows + r) * 3 * chan + t * chan, chan)
                lat[at, 0:cols] = (cached[t, r] if t < 2 else latent[r]).astype(F32)

        for r in range(3 * rows):
            for t in range(3):
                x = lat[pl.ds((r * 3 + t) * chan, chan), :]
                at = t * 3 * chan
                tall[r, at : at + chan] = pltpu.roll(x, 1, 1).astype(BF16)
                tall[r, at + chan : at + 2 * chan] = x.astype(BF16)
                tall[r, at + 2 * chan : at + 3 * chan] = pltpu.roll(x, 255, 1).astype(BF16)
        for i in range(3):
            for t in range(3):
                at = (i * 3 + t) * 3 * chan
                w_order[at : at + 3 * chan] = w_in[t, i]

        def hidden_row(k):
            lhs = tall[k : k + 3].reshape(27 * chan, 256)[:, 0:cols]
            h = lax.dot_general(lhs, w_order[...], (((0,), (0,)), ((), ())), preferred_element_type=F32)
            plain[k % 2] = h
            for c in range(0, cols, CHUNK):
                at = slice(c, c + CHUNK)
                v = plain[k % 2, at].astype(BF16)
                hidden[k, at] = v
                v = v.astype(F32)
                inv = lax.rsqrt(jnp.mean(v * v, axis=1, keepdims=True) + EPS)
                half = v * inv * half_gain[...]
                act = half * (jnp.tanh(half) + 1.0)
                if k < 3:
                    act = act * flag(info, 1)
                if k >= rows + 3:
                    act = act * flag(info, 2)
                plain[k % 2, at] = act
            for lanes in range(0, 384, 128):
                beside(wide.at[k], 0, lanes, plain[k % 2, :, lanes : lanes + 128], False)

        def conv_rows(p, number):
            lhs = [wide[p + i : p + i + number].reshape(number * cols, 1152) for i in range(3)]
            total = mm(jnp.concatenate(lhs, axis=1), mid[2, :, :, 0:256].reshape(3456, 256))
            conv[p : p + number, :, 0:256] = total.reshape(number, cols, 256)

        for k in range(rows + 2):
            hidden_row(k)
        conv_rows(0, rows)
        for k in range(rows + 2, rows + 6):
            hidden_row(k)
        conv_rows(rows, 4)
        both = mm(
            wide[0 : rows + 5].reshape((rows + 5) * cols, 1152),
            jnp.concatenate([mid[2, 0, :, 256:384], mid[2, 1, :, 256:384]], axis=1),
        )
        rest = mm(wide[2 : rows + 6].reshape((rows + 4) * cols, 1152), mid[2, 2, :, 256:384])
        for p in range(rows + 4):
            at, after = slice(p * cols, (p + 1) * cols), slice((p + 1) * cols, (p + 2) * cols)
            conv[p, :, 256:384] = both[at, :128] + both[after, 128:] + rest[at]

    return body


def pulled(s, half_gain, grad):
    h = s * half_gain
    t = jnp.tanh(h)
    return (grad * half_gain) * ((1.0 + t) * (1.0 + h * (1.0 - t)))


def back_body(rows, cols, chan, count, o):
    size = rows * cols
    width = 2 * cols // count

    def body(
        info, hidden, conv, acc, got_even, got_odd, packed_even, packed_odd, own, own_mid, fwd, back_odd, back_even, mid_t, w_in, half_gain,
        half_out, payload, reward, edge, p0, p1, g_odd, g_even, wide, t_odd, t_even, back, act_grad, hid, tmp_odd, tmp_even, lines,
    ):
        even = info[0] == 0
        top, bottom = flag(info, 1), flag(info, 2)

        def take(got, packed, before):
            ok = top if before else bottom
            place = 0 if before else rows + 1
            for k in range(3):
                at = slice(k * cols, (k + 1) * cols)
                edge[place + k] = got[at].astype(F32) * ok
                reward[k if before else 2 * rows + 3 + k] = (packed[at].astype(F32) * ok).astype(BF16)

        @pl.when(even)
        def _():
            take(got_odd, packed_odd, True)
            take(got_even, packed_even, False)

        @pl.when(jnp.logical_not(even))
        def _():
            take(got_even, packed_even, True)
            take(got_odd, packed_odd, False)

        reward[3:6] = own[0:3]
        reward[6 : 2 * rows] = own_mid[...]
        reward[2 * rows : 2 * rows + 3] = own[3:6]

        def inside(x, k, first, last):
            return x * top if k < first else x * bottom if k >= last else x

        def state_row(k):
            for lanes in range(0, 384, 128):
                at = slice(lanes, lanes + 128)
                x = hidden[k + 1, :, at].astype(F32) + conv[k, :, at]
                if 1 <= k <= rows + 2:
                    x = x + acc[k, :, at]
                if k < 3 or k > rows:
                    x = x + edge[k, :, at]
                beside(wide.at[k], 0, lanes, inside(x, k, 2, rows + 2), False)

        def up_rows(first, last, b, n):
            count = last - first
            x = wide[first:last, :, b * 384 : b * 384 + 768].reshape(count * cols, 768)
            lanes = slice(n * 256, n * 256 + 256)
            (p0, p1)[b][first:last, :, lanes] = mm(x, fwd[b, :, lanes]).reshape(count, cols, 256)

        def down_rows(first, last, odd, n):
            count = last - first
            g, kernel, t = (g_odd, back_odd, t_odd) if odd else (g_even, back_even, t_even)
            lanes = slice(n * 256, n * 256 + 256)
            x = g[first:last].reshape(count * cols, 768)
            t[first:last, :, lanes] = mm(x, kernel[:, lanes]).reshape(count, cols, 256)

        low = lax.broadcasted_iota(jnp.int32, (CHUNK, 128), 1) < 64
        tall_low = lax.broadcasted_iota(jnp.int32, (cols, 128), 1) < 64
        gains = [half_out[:, 0:128], half_out[:, 128:256]]

        def pull(v0, v1, vm, r, zero_low):
            mine = low if zero_low else jnp.logical_not(low)
            def both(a0, a1, am):
                s0 = jnp.sum(a0 + jnp.where(mine, am, 0.0), axis=1, keepdims=True)
                s1 = jnp.sum(a1 + jnp.where(mine, 0.0, am), axis=1, keepdims=True)
                return s0 * (1.0 / o), s1 * (1.0 / o)

            q0, q1 = both(v0 * v0, v1 * v1, vm * vm)
            i0, i1 = lax.rsqrt(q0 + EPS), lax.rsqrt(q1 + EPS)
            im = jnp.where(mine, i0, i1)
            out = []
            for v, i, g, k in ((v0, i0, gains[0], 0), (v1, i1, gains[0], 1), (vm, im, gains[1], 2)):
                s = v * i
                out.append((s, pulled(s, g, r[:, k * 128 : k * 128 + 128].astype(F32))))
            m0, m1 = both(*(s * d for s, d in out))
            mx = jnp.where(mine, m0, m1)
            return [i * (d - s * m) for (s, d), i, m in zip(out, (i0, i1, im), (m0, m1, mx))]

        def pull_row(k, odd):
            target, tmp = (g_odd, tmp_odd) if odd else (g_even, tmp_even)
            for c in range(0, cols, CHUNK):
                at = slice(c, c + CHUNK)
                if odd:
                    v0 = p0[k, at, 256:384] + p0[k + 1, at, 0:128]
                    v1 = p1[k, at, 256:384] + p1[k + 1, at, 0:128]
                    m0 = p0[k, at, 640:768] + p0[k + 1, at, 512:640]
                    m1 = p1[k, at, 640:768] + p1[k + 1, at, 512:640]
                else:
                    v0 = p0[k + 1, at, 128:256] + p0[k, at, 384:512]
                    v1 = p1[k + 1, at, 128:256] + p1[k, at, 384:512]
                    m0 = p1[k + 1, at, 512:640] + p1[k, at, 640:768]
                    m1 = p0[k + 1, at, 512:640] + p0[k, at, 640:768]
                out = pull(v0, v1, jnp.where(low, m0, m1), reward[2 * k + (0 if odd else 1), at], odd)
                for n, value in enumerate(out):
                    lanes = slice(n * 128, n * 128 + 128)
                    target[k, at, lanes] = value.astype(BF16)
                    tmp[k % 2, at, lanes] = value
            target[k, :, 384:512] = from_right(tmp[k % 2, :, 0:128]).astype(BF16)
            target[k, :, 512:640] = from_left(tmp[k % 2, :, 128:256]).astype(BF16)
            x = tmp[k % 2, :, 256:384]
            sides = (from_right(x), from_left(x)) if odd else (from_left(x), from_right(x))
            target[k, :, 640:768] = jnp.where(tall_low, *sides).astype(BF16)

        def block_row(k):
            for lanes in range(0, 384, 128):
                at, far = slice(lanes, lanes + 128), slice(lanes + 384, lanes + 512)
                x = t_odd[k + 1, :, at] + t_odd[k, :, far] + t_even[k, :, at] + t_even[k + 1, :, far]
                beside(back.at[k], 0, lanes, inside(x, k, 1, rows + 1), True)

        def hidden_pull(k):
            for c in range(0, cols, CHUNK):
                at = slice(c, c + CHUNK)
                v = hidden[k + 3, at].astype(F32)
                inv = lax.rsqrt(jnp.mean(v * v, axis=1, keepdims=True) + EPS)
                s = v * inv
                d = pulled(s, half_gain[...], act_grad[k, at])
                dv = inv * (d - s * jnp.mean(d * s, axis=1, keepdims=True))
                hid[k, at] = (back[k + 1, at, 384:768].astype(F32) + dv).astype(BF16)

        fine = rows + 3
        for k in range(rows + 4):
            state_row(k)
        for b in range(2):
            up_rows(1, rows + 4, b, 0)
            up_rows(0, rows + 3, b, 1)
            up_rows(0, rows + 4, b, 2)
        for k in range(fine):
            pull_row(k, True)
            pull_row(k, False)
        for odd in (True, False):
            down_rows(1 if odd else 0, fine if odd else fine - 1, odd, 0)
            down_rows(0, fine, odd, 1)
            down_rows(0 if odd else 1, fine - 1 if odd else fine, odd, 2)
        for k in range(rows + 2):
            block_row(k)
        lhs = [back[2 - i : 2 - i + rows].reshape(size, 1152) for i in range(3)]
        act_grad[:, :, 0:256] = mm(jnp.concatenate(lhs, axis=1), mid_t[:, 0:256]).reshape(rows, cols, 256)
        both = mm(
            back[1 : rows + 2].reshape((rows + 1) * cols, 1152),
            jnp.concatenate([mid_t[1152:2304, 256:384], mid_t[0:1152, 256:384]], axis=1),
        )
        rest = mm(back[0:rows].reshape(size, 1152), mid_t[2304:3456, 256:384])
        for p in range(rows):
            at, after = slice(p * cols, (p + 1) * cols), slice((p + 1) * cols, (p + 2) * cols)
            act_grad[p, :, 256:384] = both[at, :128] + both[after, 128:] + rest[at]
        for k in range(rows):
            hidden_pull(k)

        z = mm_t(w_in[...], hid[...].reshape(size, 384))
        place = lax.broadcasted_iota(jnp.int32, (chan, size), 1)
        col = lax.rem(place, cols)
        sums = []
        for i in range(3):
            z0, z1, z2 = (z[(i * 3 + j) * chan : (i * 3 + j + 1) * chan] for j in range(3))
            left = jnp.where(col == cols - 1, 0.0, pltpu.roll(z0, size - 1, 1))
            right = jnp.where(col == 0, 0.0, pltpu.roll(z2, 1, 1))
            sums.append(left + z1 + right)
        inner = sums[1]
        inner = inner + jnp.where(place < size - cols, pltpu.roll(sums[0], size - cols, 1), 0.0)
        inner = inner + jnp.where(place >= cols, pltpu.roll(sums[2], cols, 1), 0.0)
        lines[0:chan] = inner
        lines[chan : 2 * chan] = sums[0]
        lines[2 * chan : 3 * chan] = sums[2]
        per_row = count // 2
        for u in range(count):
            pair, piece = u // per_row, u % per_row
            parts = []
            for a in range(2):
                at = (2 * pair + a) * cols + piece * width
                parts.append(lines[0:chan, at : at + width])
            at = piece * width + (0 if pair else (rows - 1) * cols)
            first = chan if pair else 2 * chan
            parts.append(lines[first : first + chan, at : at + width])
            parts.append(jnp.zeros((chan, 128 - 3 * width), F32))
            payload[u] = jnp.concatenate(parts, axis=1).astype(BF16)

    return body


def placing(info, order, sel, count, width, tokens):
    piece = width // 2
    pair = info[3]
    lane = lax.broadcasted_iota(jnp.int32, (128, 4 * tokens), 0)
    column = lax.broadcasted_iota(jnp.int32, (128, 4 * tokens), 1)
    group = (lane >= width).astype(jnp.int32) + (lane >= 2 * width).astype(jnp.int32)
    w = lane - group * width
    part = jnp.where(group == 2, pair, group)
    fixed = (2 * part + (w & 1)) * tokens + (w >> 1) - column
    fixed = jnp.where(lane < 3 * width, fixed, -99999)

    def one(t):
        step = t + 1 - 2 * pair
        valid = jnp.logical_and(step >= 0, step < count)
        beside = jnp.where(valid, piece * order[jnp.clip(step, 0, count - 1)], -9999)
        begin = jnp.where(group == 2, beside, piece * order[t])
        sel[t] = (fixed + begin == 0).astype(F32).astype(BF16)

    return one


def place_body(count, chan, tokens):
    def body(sel, got, out):
        total = mm(got[0], sel[0])
        for t in range(1, count):
            total += mm(got[t], sel[t])
        for k in range(4):
            out[k * chan : (k + 1) * chan] = total[:, k * tokens : (k + 1) * tokens]

    return body


def swaps(count):
    within = [(i, i ^ 1) for i in range(count)]
    across = [(0, 0), (count - 1, count - 1)]
    for i in range(1, count - 1, 2):
        across += [(i, i + 1), (i + 1, i)]
    return within, sorted(across)


def shards(
    latent, cached_latent, cached_features, reward_grad, conv_in_weight, conv_mid_weight, conv_up_weight, norm_gain, out_gain, shard_order
):
    count = lax.axis_size("tile")
    rows, cols, chan = latent.shape
    mid_chan = norm_gain.shape[0]
    o = out_gain.shape[0]
    tile = lax.axis_index("tile")
    info = jnp.stack(
        [tile % 2, (tile > 0).astype(jnp.int32), (tile < count - 1).astype(jnp.int32), (tile >= count // 2).astype(jnp.int32)]
    ).astype(jnp.int32)
    lat = jnp.transpose(latent, (0, 2, 1))
    lat_cached = jnp.transpose(cached_latent, (0, 1, 3, 2))
    reward_t = jnp.transpose(reward_grad, (0, 2, 1))
    up_t = jnp.transpose(conv_up_weight, (0, 1, 3, 2))
    mid = conv_mid_weight.reshape(3, 3, 3 * mid_chan, mid_chan)
    w_in = conv_in_weight.reshape(3, 3, 3 * chan, mid_chan)
    gain = 0.5 * norm_gain.reshape(1, mid_chan)
    gain_out = 0.5 * jnp.concatenate([out_gain, out_gain[128:]]).reshape(1, 256)
    within, across = swaps(count)
    size = rows * cols
    edge_rows = 3 * cols + 2 * chan * rows

    info, back_odd, back_even = call(
        taps_body,
        [((4,), jnp.int32), ((768, 768), BF16), ((768, 768), BF16)],
        1, 1, [], 1e10, 8, 1,
    )(info, up_t)

    own, send_even, send_odd = call(
        pack_body(rows, cols, o, chan),
        [((6, cols, 384), BF16), ((edge_rows, 384), BF16), ((edge_rows, 384), BF16)],
        1, 3, [], 1e10, 8,
    )(info, reward_t, lat, lat_cached)
    packed_even = lax.ppermute(send_even, "tile", within)
    packed_odd = lax.ppermute(send_odd, "tile", across)

    width = 2 * cols // count
    tokens = size // 4
    acc, part_even, part_odd, mid_t, sel, fwd, own_mid = call(
        cached_body(rows, cols, count, width, tokens, o),
        [
            ((rows + 4, cols, 384), F32), ((3 * cols, 384), BF16), ((3 * cols, 384), BF16), ((3456, 384), BF16),
            ((count, 128, 4 * tokens), BF16), ((2, 768, 768), BF16), ((2, cols, 384), BF16),
        ],
        2, 5, [pltpu.VMEM((size, 2304), BF16), pltpu.VMEM((3, size, 384), F32)], 4e9, 14,
    )(info, shard_order, cached_features, mid, back_odd, back_even, reward_t)
    got_even = lax.ppermute(part_even, "tile", within)
    got_odd = lax.ppermute(part_odd, "tile", across)

    hidden, conv = call(
        current_body(rows, cols, chan),
        [((rows + 6, cols, 384), BF16), ((rows + 4, cols, 384), F32)],
        1, 7,
        [
            pltpu.VMEM((9 * rows * chan, 256), F32),
            pltpu.VMEM((3 * rows, 9 * chan, 256), BF16),
            pltpu.VMEM((rows + 6, cols, 1152), BF16),
            pltpu.VMEM((27 * chan, 384), BF16),
            pltpu.VMEM((2, cols, 384), F32),
        ],
        5e9, 14,
    )(info, lat, lat_cached, packed_even, packed_odd, w_in, mid, gain)

    (payload,) = call(
        back_body(rows, cols, chan, count, o),
        [((count, chan, 128), BF16)],
        1, 16,
        [
            pltpu.VMEM((2 * rows + 6, cols, 384), BF16),
            pltpu.VMEM((rows + 4, cols, 384), F32),
            pltpu.VMEM((rows + 4, cols, 768), F32),
            pltpu.VMEM((rows + 4, cols, 768), F32),
            pltpu.VMEM((rows + 3, cols, 768), BF16),
            pltpu.VMEM((rows + 3, cols, 768), BF16),
            pltpu.VMEM((rows + 4, cols, 1152), BF16),
            pltpu.VMEM((rows + 3, cols, 768), F32),
            pltpu.VMEM((rows + 3, cols, 768), F32),
            pltpu.VMEM((rows + 2, cols, 1152), BF16),
            pltpu.VMEM((rows, cols, 384), F32),
            pltpu.VMEM((rows, cols, 384), BF16),
            pltpu.VMEM((2, cols, 384), F32),
            pltpu.VMEM((2, cols, 384), F32),
            pltpu.VMEM((3 * chan, size), F32),
        ],
        8e9, 34,
    )(
        info, hidden, conv, acc, got_even, got_odd, packed_even, packed_odd, own, own_mid, fwd, back_odd, back_even, mid_t,
        w_in[2].reshape(9 * chan, mid_chan), gain, gain_out,
    )
    received = lax.all_to_all(payload, "tile", split_axis=0, concat_axis=0, tiled=True)
    (placed,) = call(place_body(count, chan, tokens), [((4 * chan, tokens), F32)], 0, 2, [], 1e7, 8)(sel, received)
    return placed.T


def solution(mesh):
    return jax.shard_map(
        shards,
        mesh=mesh,
        in_specs=(
            P(("prompt", "tile"), None, None),
            P(None, ("prompt", "tile"), None, None),
            P(None, ("prompt", "tile"), None, None),
            P(("prompt", "tile"), None, None),
            P(),
            P(),
            P(),
            P(),
            P(),
            P("prompt"),
        ),
        out_specs=P(("prompt", "tile"), None),
        check_vma=False,
    )
```

```python
import jax
import jax.numpy as jnp
from jax import lax
from jax.experimental import pallas as pl
from jax.experimental.pallas import tpu as pltpu
from jax.sharding import PartitionSpec as P

EPS = 1e-06
F32 = jnp.float32
BF16 = jnp.bfloat16
VM = pl.BlockSpec(memory_space=pltpu.VMEM)
SM = pl.BlockSpec(memory_space=pltpu.SMEM)


def weave(*groups):
    total = max(len(g) for g in groups)
    done = [0] * len(groups)
    for k in range(total):
        for n, g in enumerate(groups):
            while done[n] * total < (k + 1) * len(g):
                g[done[n]]()
                done[n] += 1


def joined(refs, lanes=slice(None)):
    return jnp.concatenate([ref[:, lanes] for ref in refs], axis=0)


def shared(refs, lanes, value):
    size = refs[0].shape[0]
    for k, ref in enumerate(refs):
        ref[:, lanes] = value[k * size : (k + 1) * size]


def steps(f, *keys):
    return [lambda key=key: f(*key) for key in keys]


def call(body, outs, n_smem, n_vmem, scratch, flops, limit, smem_outs=0):
    specs = [SM] * n_smem + [VM] * n_vmem
    return pl.pallas_call(
        body,
        out_shape=[jax.ShapeDtypeStruct(s, d) for s, d in outs],
        in_specs=specs,
        out_specs=[SM] * smem_outs + [VM] * (len(outs) - smem_outs),
        scratch_shapes=scratch,
        cost_estimate=pl.CostEstimate(flops=int(flops), bytes_accessed=2**20, transcendentals=0),
        compiler_params=pltpu.CompilerParams(vmem_limit_bytes=limit << 20),
    )


def mm(a, b):
    return jnp.dot(a, b, preferred_element_type=F32)


def mm_t(a, b):
    return lax.dot_general(a, b, (((1,), (1,)), ((), ())), preferred_element_type=F32)


def flag(info, k):
    return info[k].astype(F32)


def from_left(x):
    moved = pltpu.roll(x, 1, 0)
    first = lax.broadcasted_iota(jnp.int32, (8, x.shape[1]), 0) == 0
    return jnp.concatenate([jnp.where(first, 0.0, moved[:8]), moved[8:]], axis=0)


def from_right(x):
    size = x.shape[0]
    moved = pltpu.roll(x, size - 1, 0)
    last = lax.broadcasted_iota(jnp.int32, (8, x.shape[1]), 0) == 7
    return jnp.concatenate([moved[: size - 8], jnp.where(last, 0.0, moved[size - 8 :])], axis=0)


def beside(target, base, lanes, x, ahead):
    sides = (from_right, from_left) if ahead else (from_left, from_right)
    for group, value in enumerate((sides[0](x), x, sides[1](x))):
        at = base + group * 384 + lanes
        target[:, at : at + 128] = value.astype(BF16)


CHUNK = 32


def picker(cols, o):
    half = o - 128
    x_index = lax.broadcasted_iota(jnp.int32, (cols, 2 * cols), 1)
    w_index = lax.broadcasted_iota(jnp.int32, (cols, 2 * cols), 0)
    pick = [(x_index == 2 * w_index + b).astype(F32).astype(BF16) for b in (0, 1)]
    zeros = jnp.zeros((128 - half, 2 * cols), BF16)

    def one(reward, f, own, k):
        r = reward[f]
        first, rest = r[:128], r[128:]
        low = jnp.concatenate([first, rest, zeros], axis=0)
        high = jnp.concatenate([first, zeros, rest], axis=0)
        sides = (low, high) if f % 2 else (high, low)
        d0, d1 = mm_t(pick[0], sides[0]), mm_t(pick[1], sides[1])
        own[k, :, 0:128] = d0[:, :128].astype(BF16)
        own[k, :, 128:256] = d1[:, :128].astype(BF16)
        own[k, :, 256:384] = (d0[:, 128:] + d1[:, 128:]).astype(BF16)

    return one


def pack_body(rows, cols, o, chan):
    def body(info, reward, latent, cached, own, send_even, send_odd):
        one = picker(cols, o)
        for k in range(6):
            one(reward, k if k < 3 else 2 * rows - 6 + k, own, k)
        base = 3 * cols
        per = chan * rows
        for send, last in ((send_even, 1 - info[0]), (send_odd, info[0])):
            begin = last * 3
            for k in range(3):
                send[k * cols : (k + 1) * cols] = own[begin + k]
            for t in range(3):
                src = cached[t] if t < 2 else latent[...]
                lat = src.reshape(per, cols)
                send[base : base + per, t * 128 : t * 128 + 128] = lat[:, :128]
                send[base + per : base + 2 * per, t * 128 : t * 128 + cols - 128] = lat[:, 128:]

    return body


def home(targets, q, p, tile):
    block, second = ((1, 1), (0, 0), (0, 1), (1, 0))[p]
    target, side = targets[q]
    if tile < 2:
        row = block * 384 + second * 128 + tile * 64
    else:
        row = block * 384 + 256 + 64 * (second if q % 2 == 0 else 1 - second)
    return target, row, side * 384


def turning(back_odd, back_even, fwd):
    targets = ((back_odd, 1), (back_even, 0), (back_odd, 0), (back_even, 1))

    def tap_tile(q, p, tile, lanes):
        target, row, side = home(targets, q, p, tile)
        return target[row : row + 64, side + lanes : side + lanes + 128]

    def one(b, side, lanes):
        p = ((3, 1), (2, 0))[b][side]
        at = slice(side * 384 + lanes, side * 384 + lanes + 128)
        for q in range(4):
            both = jnp.concatenate([tap_tile(q, p, 0, lanes), tap_tile(q, p, 1, lanes)], axis=0)
            fwd[b, at, q * 128 : q * 128 + 128] = both.T
        for half in range(2):
            pair = (2 * half, 2 * half + 1) if b == 0 else (2 * half + 1, 2 * half)
            both = jnp.concatenate([tap_tile(q, p, 2, lanes) for q in pair], axis=0)
            fwd[b, at, 512 + half * 128 : 640 + half * 128] = both.T

    return steps(one, *[(b, side, lanes) for b in range(2) for side in range(2) for lanes in range(0, 384, 128)])


def taps_body(info, up, info_out, back_odd, back_even):
    for k in range(4):
        info_out[k] = info[k]

    parts = ((2,), (1, 2), (0, 1), (0,))
    targets = ((back_odd, 1), (back_even, 0), (back_odd, 0), (back_even, 1))

    for tile in range(3):
        for lanes in range(0, 384, 128):
            w = [[up[i, j, tile * 64 : tile * 64 + 64, lanes : lanes + 128].astype(F32) for j in range(3)] for i in range(3)]
            for q in range(4):
                c = [w[parts[q][0]][j] + w[parts[q][1]][j] if len(parts[q]) > 1 else w[parts[q][0]][j] for j in range(3)]
                for p, tap in enumerate((c[2], c[1] + c[2], c[0] + c[1], c[0])):
                    target, row, side = home(targets, q, p, tile)
                    target[row : row + 64, side + lanes : side + lanes + 128] = tap.astype(BF16)


def cached_body(rows, cols, count, width, tokens, o):
    size = rows * cols

    def body(
        info, order, features, mid, back_odd, back_even, reward, acc, send_even, send_odd, mid_t, sel, fwd, own, wide, parts
    ):
        for t in range(2):
            for r in range(rows):
                for lanes in range(0, 384, 128):
                    x = features[t, r, :, lanes : lanes + 128].astype(F32)
                    beside(wide.at[r * cols : (r + 1) * cols], t * 1152, lanes, x, False)
        def product(i, lanes):
            parts[i, :, lanes] = mm(wide[...], jnp.concatenate([mid[0, i, :, lanes], mid[1, i, :, lanes]], axis=0))

        def double():
            left = jnp.concatenate([mid[0, 0, :, 256:384], mid[1, 0, :, 256:384]], axis=0)
            right = jnp.concatenate([mid[0, 1, :, 256:384], mid[1, 1, :, 256:384]], axis=0)
            both = mm(wide[...], jnp.concatenate([left, right], axis=1))
            parts[0, :, 256:384] = both[:, :128]
            parts[1, :, 256:384] = both[:, 128:]

        def turn(i, j):
            at = (i * 3 + j) * 384
            mid_t[at : at + 384] = mid[2, i, j * 384 : (j + 1) * 384].T

        most, rest = slice(0, 256), slice(256, 384)
        products = steps(product, (0, most), (1, most)) + steps(double, ()) + steps(product, (2, most), (2, rest))
        one = picker(cols, o)
        others = steps(turn, *[(i, j) for i in range(3) for j in range(3)])
        others += turning(back_odd, back_even, fwd)
        others += steps(placing(info, order, sel, count, width, tokens), *[(t,) for t in range(count)])
        others += steps(one, (reward, rows - 1, own, 0), (reward, rows, own, 1))
        weave(others, products)
        for k in range(rows + 4):
            total = jnp.zeros((cols, 384), F32)
            for i in range(3):
                r = k - 3 + i
                if 0 <= r < rows:
                    total = total + parts[i, r * cols : (r + 1) * cols]
            acc[k] = total
        for send, last in ((send_even, 1 - info[0]), (send_odd, info[0])):
            for k in range(3):
                send[k * cols : (k + 1) * cols] = acc[1 + last * 3 + k].astype(BF16)

    return body


def current_body(rows, cols, chan):
    per = chan * rows
    base = 3 * cols

    def body(info, latent, cached, got_even, got_odd, w_in, mid, half_gain, hidden, conv, lat, tall, w_order, *buffers):
        even = info[0] == 0
        wide, plain = buffers[: rows + 6], buffers[rows + 6 :]
        lat[...] = jnp.zeros_like(lat)

        def fill(first_row, got, ok):
            scale = ok.astype(F32)
            for t in range(3):
                x = got[base : base + per, t * 128 : t * 128 + 128].astype(F32) * scale
                y = got[base + per : base + 2 * per, t * 128 : t * 128 + cols - 128].astype(F32) * scale
                for r in range(rows):
                    at = pl.ds((first_row + r) * 3 * chan + t * chan, chan)
                    lat[at, 0:128] = x[r * chan : (r + 1) * chan]
                    lat[at, 128:cols] = y[r * chan : (r + 1) * chan]

        @pl.when(even)
        def _():
            fill(0, got_odd, info[1])
            fill(2 * rows, got_even, info[2])

        @pl.when(jnp.logical_not(even))
        def _():
            fill(0, got_even, info[1])
            fill(2 * rows, got_odd, info[2])

        for t in range(3):
            for r in range(rows):
                at = pl.ds((rows + r) * 3 * chan + t * chan, chan)
                lat[at, 0:cols] = (cached[t, r] if t < 2 else latent[r]).astype(F32)

        for r in range(3 * rows):
            for t in range(3):
                x = lat[pl.ds((r * 3 + t) * chan, chan), :]
                at = t * 3 * chan
                tall[r, at : at + chan] = pltpu.roll(x, 1, 1).astype(BF16)
                tall[r, at + chan : at + 2 * chan] = x.astype(BF16)
                tall[r, at + 2 * chan : at + 3 * chan] = pltpu.roll(x, 255, 1).astype(BF16)
        for i in range(3):
            for t in range(3):
                at = (i * 3 + t) * 3 * chan
                w_order[at : at + 3 * chan] = w_in[t, i]

        def hidden_row(k):
            lhs = tall[k : k + 3].reshape(27 * chan, 256)[:, 0:cols]
            h = lax.dot_general(lhs, w_order[...], (((0,), (0,)), ((), ())), preferred_element_type=F32)
            plain[k][...] = h
            for c in range(0, cols, CHUNK):
                at = slice(c, c + CHUNK)
                v = plain[k][at].astype(BF16)
                hidden[k, at] = v
                v = v.astype(F32)
                inv = lax.rsqrt(jnp.mean(v * v, axis=1, keepdims=True) + EPS)
                half = v * inv * half_gain[...]
                act = half * (jnp.tanh(half) + 1.0)
                if k < 3:
                    act = act * flag(info, 1)
                if k >= rows + 3:
                    act = act * flag(info, 2)
                plain[k][at] = act
            for lanes in range(0, 384, 128):
                beside(wide[k], 0, lanes, plain[k][:, lanes : lanes + 128], False)

        def conv_rows(p, number):
            lhs = [joined(wide[p + i : p + i + number]) for i in range(3)]
            total = mm(jnp.concatenate(lhs, axis=1), mid[2, :, :, 0:256].reshape(3456, 256))
            conv[p : p + number, :, 0:256] = total.reshape(number, cols, 256)

        for k in range(rows + 1):
            hidden_row(k)
        weave(steps(hidden_row, *[(k,) for k in range(rows + 1, rows + 6)]), steps(conv_rows, (0, rows - 1)))
        conv_rows(rows - 1, 5)
        both = mm(joined(wide[0 : rows + 5]), jnp.concatenate([mid[2, 0, :, 256:384], mid[2, 1, :, 256:384]], axis=1))
        rest = mm(joined(wide[2 : rows + 6]), mid[2, 2, :, 256:384])
        for p in range(rows + 4):
            at, after = slice(p * cols, (p + 1) * cols), slice((p + 1) * cols, (p + 2) * cols)
            conv[p, :, 256:384] = both[at, :128] + both[after, 128:] + rest[at]

    return body


def pulled(s, half_gain, grad):
    h = s * half_gain
    t = jnp.tanh(h)
    return (grad * half_gain) * ((1.0 + t) * (1.0 + h * (1.0 - t)))


def back_body(rows, cols, chan, count, o):
    size = rows * cols
    width = 2 * cols // count

    def body(
        info, hidden, conv, acc, got_even, got_odd, packed_even, packed_odd, own, own_mid, fwd, back_odd, back_even, mid_t, w_in, half_gain,
        half_out, payload, reward, edge, lines, *buffers
    ):
        fine = rows + 3
        buffers = list(buffers)

        def part(count):
            taken = buffers[:count]
            del buffers[:count]
            return taken

        p0, p1, wide = part(rows + 4), part(rows + 4), part(rows + 4)
        g_odd, g_even, t_odd, t_even = part(fine), part(fine), part(fine), part(fine)
        tmp_odd, tmp_even, back = part(fine), part(fine), part(rows + 2)
        act_grad, hid = part(rows), part(rows)
        even = info[0] == 0
        top, bottom = flag(info, 1), flag(info, 2)

        def take(got, packed, before):
            ok = top if before else bottom
            place = 0 if before else rows + 1
            for k in range(3):
                at = slice(k * cols, (k + 1) * cols)
                edge[place + k] = got[at].astype(F32) * ok
                reward[k if before else 2 * rows + 3 + k] = (packed[at].astype(F32) * ok).astype(BF16)

        @pl.when(even)
        def _():
            take(got_odd, packed_odd, True)
            take(got_even, packed_even, False)

        @pl.when(jnp.logical_not(even))
        def _():
            take(got_even, packed_even, True)
            take(got_odd, packed_odd, False)

        reward[3:6] = own[0:3]
        reward[6 : 2 * rows] = own_mid[...]
        reward[2 * rows : 2 * rows + 3] = own[3:6]

        def inside(x, k, first, last):
            return x * top if k < first else x * bottom if k >= last else x

        def state_row(k):
            for lanes in range(0, 384, 128):
                at = slice(lanes, lanes + 128)
                x = hidden[k + 1, :, at].astype(F32) + conv[k, :, at]
                if 1 <= k <= rows + 2:
                    x = x + acc[k, :, at]
                if k < 3 or k > rows:
                    x = x + edge[k, :, at]
                beside(wide[k], 0, lanes, inside(x, k, 2, rows + 2), False)

        def up_rows(first, last, b, n):
            lanes = slice(n * 256, n * 256 + 256)
            x = joined(wide[first:last], slice(b * 384, b * 384 + 768))
            shared((p0, p1)[b][first:last], lanes, mm(x, fwd[b, :, lanes]))

        def down_rows(first, last, odd, n):
            g, kernel, t = (g_odd, back_odd, t_odd) if odd else (g_even, back_even, t_even)
            lanes = slice(n * 256, n * 256 + 256)
            shared(t[first:last], lanes, mm(joined(g[first:last]), kernel[:, lanes]))

        low = lax.broadcasted_iota(jnp.int32, (CHUNK, 128), 1) < 64
        tall_low = lax.broadcasted_iota(jnp.int32, (cols, 128), 1) < 64
        gains = [half_out[:, 0:128], half_out[:, 128:256]]

        def pull(v0, v1, vm, r, zero_low):
            mine = low if zero_low else jnp.logical_not(low)
            def both(a0, a1, am):
                s0 = jnp.sum(a0 + jnp.where(mine, am, 0.0), axis=1, keepdims=True)
                s1 = jnp.sum(a1 + jnp.where(mine, 0.0, am), axis=1, keepdims=True)
                return s0 * (1.0 / o), s1 * (1.0 / o)

            q0, q1 = both(v0 * v0, v1 * v1, vm * vm)
            i0, i1 = lax.rsqrt(q0 + EPS), lax.rsqrt(q1 + EPS)
            im = jnp.where(mine, i0, i1)
            out = []
            for v, i, g, k in ((v0, i0, gains[0], 0), (v1, i1, gains[0], 1), (vm, im, gains[1], 2)):
                s = v * i
                out.append((s, pulled(s, g, r[:, k * 128 : k * 128 + 128].astype(F32))))
            m0, m1 = both(*(s * d for s, d in out))
            mx = jnp.where(mine, m0, m1)
            return [i * (d - s * m) for (s, d), i, m in zip(out, (i0, i1, im), (m0, m1, mx))]

        def pull_row(k, odd):
            target, tmp = (g_odd, tmp_odd) if odd else (g_even, tmp_even)
            for c in range(0, cols, CHUNK):
                at = slice(c, c + CHUNK)
                if odd:
                    v0 = p0[k][at, 256:384] + p0[k + 1][at, 0:128]
                    v1 = p1[k][at, 256:384] + p1[k + 1][at, 0:128]
                    m0 = p0[k][at, 640:768] + p0[k + 1][at, 512:640]
                    m1 = p1[k][at, 640:768] + p1[k + 1][at, 512:640]
                else:
                    v0 = p0[k + 1][at, 128:256] + p0[k][at, 384:512]
                    v1 = p1[k + 1][at, 128:256] + p1[k][at, 384:512]
                    m0 = p1[k + 1][at, 512:640] + p1[k][at, 640:768]
                    m1 = p0[k + 1][at, 512:640] + p0[k][at, 640:768]
                out = pull(v0, v1, jnp.where(low, m0, m1), reward[2 * k + (0 if odd else 1), at], odd)
                for n, value in enumerate(out):
                    lanes = slice(n * 128, n * 128 + 128)
                    target[k][at, lanes] = value.astype(BF16)
                    tmp[k][at, lanes] = value
            target[k][:, 384:512] = from_right(tmp[k][:, 0:128]).astype(BF16)
            target[k][:, 512:640] = from_left(tmp[k][:, 128:256]).astype(BF16)
            x = tmp[k][:, 256:384]
            sides = (from_right(x), from_left(x)) if odd else (from_left(x), from_right(x))
            target[k][:, 640:768] = jnp.where(tall_low, *sides).astype(BF16)

        def block_row(k):
            for lanes in range(0, 384, 128):
                at, far = slice(lanes, lanes + 128), slice(lanes + 384, lanes + 512)
                x = t_odd[k + 1][:, at] + t_odd[k][:, far] + t_even[k][:, at] + t_even[k + 1][:, far]
                beside(back[k], 0, lanes, inside(x, k, 1, rows + 1), True)

        def hidden_pull(k):
            for c in range(0, cols, CHUNK):
                at = slice(c, c + CHUNK)
                v = hidden[k + 3, at].astype(F32)
                inv = lax.rsqrt(jnp.mean(v * v, axis=1, keepdims=True) + EPS)
                s = v * inv
                d = pulled(s, half_gain[...], act_grad[k][at])
                dv = inv * (d - s * jnp.mean(d * s, axis=1, keepdims=True))
                hid[k][at] = (back[k + 1][at, 384:768].astype(F32) + dv).astype(BF16)

        def mid_rows(p, number):
            lhs = [joined(back[p + 2 - i : p + 2 - i + number]) for i in range(3)]
            shared(act_grad[p : p + number], slice(0, 256), mm(jnp.concatenate(lhs, axis=1), mid_t[:, 0:256]))

        def mid_rest(p, number):
            pair = jnp.concatenate([mid_t[1152:2304, 256:384], mid_t[0:1152, 256:384]], axis=1)
            both = mm(joined(back[p + 1 : p + number + 2]), pair)
            rest = mm(joined(back[p : p + number]), mid_t[2304:3456, 256:384])
            for k in range(number):
                at, after = slice(k * cols, (k + 1) * cols), slice((k + 1) * cols, (k + 2) * cols)
                act_grad[p + k][:, 256:384] = both[at, :128] + both[after, 128:] + rest[at]

        def each(f, first, last):
            return steps(f, *[(k,) for k in range(first, last)])

        def ups(first, last):
            full = rows + 4
            return steps(
                up_rows,
                *[
                    key
                    for b in range(2)
                    for key in (
                        (max(first, 1), last, b, 0), (first, min(last, full - 1), b, 1), (first, last, b, 2),
                    )
                ],
            )

        def downs(first, last):
            keys = []
            for odd in (True, False):
                skip_first, skip_last = max(first, 1), min(last, fine - 1)
                keys.append((skip_first, last, odd, 0) if odd else (first, skip_last, odd, 0))
                keys.append((first, last, odd, 1))
                keys.append((first, skip_last, odd, 2) if odd else (skip_first, last, odd, 2))
            return steps(down_rows, *keys)

        def pulls(first, last):
            return steps(pull_row, *[(k, odd) for k in range(first, last) for odd in (True, False)])

        weave(each(state_row, 0, rows))
        weave(each(state_row, rows, rows + 4), ups(0, rows))
        weave(pulls(0, rows - 1), ups(rows, rows + 4))
        weave(pulls(rows - 1, fine), downs(0, rows - 1))
        weave(each(block_row, 0, rows - 2), downs(rows - 1, fine))
        weave(each(block_row, rows - 2, rows + 2))
        mid_rows(0, rows)
        mid_rest(0, rows)
        for k in range(rows):
            hidden_pull(k)

        z = mm_t(w_in[...], joined(hid))
        place = lax.broadcasted_iota(jnp.int32, (chan, size), 1)
        col = lax.rem(place, cols)
        sums = []
        for i in range(3):
            z0, z1, z2 = (z[(i * 3 + j) * chan : (i * 3 + j + 1) * chan] for j in range(3))
            left = jnp.where(col == cols - 1, 0.0, pltpu.roll(z0, size - 1, 1))
            right = jnp.where(col == 0, 0.0, pltpu.roll(z2, 1, 1))
            sums.append(left + z1 + right)
        inner = sums[1]
        inner = inner + jnp.where(place < size - cols, pltpu.roll(sums[0], size - cols, 1), 0.0)
        inner = inner + jnp.where(place >= cols, pltpu.roll(sums[2], cols, 1), 0.0)
        lines[0:chan] = inner
        lines[chan : 2 * chan] = sums[0]
        lines[2 * chan : 3 * chan] = sums[2]
        per_row = count // 2
        for u in range(count):
            pair, piece = u // per_row, u % per_row
            parts = []
            for a in range(2):
                at = (2 * pair + a) * cols + piece * width
                parts.append(lines[0:chan, at : at + width])
            at = piece * width + (0 if pair else (rows - 1) * cols)
            first = chan if pair else 2 * chan
            parts.append(lines[first : first + chan, at : at + width])
            parts.append(jnp.zeros((chan, 128 - 3 * width), F32))
            payload[u] = jnp.concatenate(parts, axis=1).astype(BF16)

    return body


def placing(info, order, sel, count, width, tokens):
    piece = width // 2
    pair = info[3]
    lane = lax.broadcasted_iota(jnp.int32, (128, 4 * tokens), 0)
    column = lax.broadcasted_iota(jnp.int32, (128, 4 * tokens), 1)
    group = (lane >= width).astype(jnp.int32) + (lane >= 2 * width).astype(jnp.int32)
    w = lane - group * width
    part = jnp.where(group == 2, pair, group)
    fixed = (2 * part + (w & 1)) * tokens + (w >> 1) - column
    fixed = jnp.where(lane < 3 * width, fixed, -99999)

    def one(t):
        step = t + 1 - 2 * pair
        valid = jnp.logical_and(step >= 0, step < count)
        beside = jnp.where(valid, piece * order[jnp.clip(step, 0, count - 1)], -9999)
        begin = jnp.where(group == 2, beside, piece * order[t])
        sel[t] = (fixed + begin == 0).astype(F32).astype(BF16)

    return one


def place_body(count, chan, tokens):
    def body(sel, got, out):
        total = mm(got[0], sel[0])
        for t in range(1, count):
            total += mm(got[t], sel[t])
        for k in range(4):
            out[k * chan : (k + 1) * chan] = total[:, k * tokens : (k + 1) * tokens]

    return body


def swaps(count):
    within = [(i, i ^ 1) for i in range(count)]
    across = [(0, 0), (count - 1, count - 1)]
    for i in range(1, count - 1, 2):
        across += [(i, i + 1), (i + 1, i)]
    return within, sorted(across)


def shards(
    latent, cached_latent, cached_features, reward_grad, conv_in_weight, conv_mid_weight, conv_up_weight, norm_gain, out_gain, shard_order
):
    count = lax.axis_size("tile")
    rows, cols, chan = latent.shape
    mid_chan = norm_gain.shape[0]
    o = out_gain.shape[0]
    tile = lax.axis_index("tile")
    info = jnp.stack(
        [tile % 2, (tile > 0).astype(jnp.int32), (tile < count - 1).astype(jnp.int32), (tile >= count // 2).astype(jnp.int32)]
    ).astype(jnp.int32)
    lat = jnp.transpose(latent, (0, 2, 1))
    lat_cached = jnp.transpose(cached_latent, (0, 1, 3, 2))
    reward_t = jnp.transpose(reward_grad, (0, 2, 1))
    up_t = jnp.transpose(conv_up_weight, (0, 1, 3, 2))
    mid = conv_mid_weight.reshape(3, 3, 3 * mid_chan, mid_chan)
    w_in = conv_in_weight.reshape(3, 3, 3 * chan, mid_chan)
    gain = 0.5 * norm_gain.reshape(1, mid_chan)
    gain_out = 0.5 * jnp.concatenate([out_gain, out_gain[128:]]).reshape(1, 256)
    within, across = swaps(count)
    size = rows * cols
    edge_rows = 3 * cols + 2 * chan * rows

    info, back_odd, back_even = call(
        taps_body,
        [((4,), jnp.int32), ((768, 768), BF16), ((768, 768), BF16)],
        1, 1, [], 1e10, 8, 1,
    )(info, up_t)

    own, send_even, send_odd = call(
        pack_body(rows, cols, o, chan),
        [((6, cols, 384), BF16), ((edge_rows, 384), BF16), ((edge_rows, 384), BF16)],
        1, 3, [], 1e10, 8,
    )(info, reward_t, lat, lat_cached)
    packed_even = lax.ppermute(send_even, "tile", within)
    packed_odd = lax.ppermute(send_odd, "tile", across)

    width = 2 * cols // count
    tokens = size // 4
    acc, part_even, part_odd, mid_t, sel, fwd, own_mid = call(
        cached_body(rows, cols, count, width, tokens, o),
        [
            ((rows + 4, cols, 384), F32), ((3 * cols, 384), BF16), ((3 * cols, 384), BF16), ((3456, 384), BF16),
            ((count, 128, 4 * tokens), BF16), ((2, 768, 768), BF16), ((2, cols, 384), BF16),
        ],
        2, 5, [pltpu.VMEM((size, 2304), BF16), pltpu.VMEM((3, size, 384), F32)], 4e9, 14,
    )(info, shard_order, cached_features, mid, back_odd, back_even, reward_t)
    got_even = lax.ppermute(part_even, "tile", within)
    got_odd = lax.ppermute(part_odd, "tile", across)

    hidden, conv = call(
        current_body(rows, cols, chan),
        [((rows + 6, cols, 384), BF16), ((rows + 4, cols, 384), F32)],
        1, 7,
        [
            pltpu.VMEM((9 * rows * chan, 256), F32),
            pltpu.VMEM((3 * rows, 9 * chan, 256), BF16),
            pltpu.VMEM((27 * chan, 384), BF16),
        ]
        + [pltpu.VMEM((cols, 1152), BF16)] * (rows + 6)
        + [pltpu.VMEM((cols, 384), F32)] * (rows + 6),
        5e9, 14,
    )(info, lat, lat_cached, packed_even, packed_odd, w_in, mid, gain)

    (payload,) = call(
        back_body(rows, cols, chan, count, o),
        [((count, chan, 128), BF16)],
        1, 16,
        [
            pltpu.VMEM((2 * rows + 6, cols, 384), BF16),
            pltpu.VMEM((rows + 4, cols, 384), F32),
            pltpu.VMEM((3 * chan, size), F32),
        ]
        + [pltpu.VMEM((cols, 768), F32)] * (2 * (rows + 4))
        + [pltpu.VMEM((cols, 1152), BF16)] * (rows + 4)
        + [pltpu.VMEM((cols, 768), BF16)] * (2 * (rows + 3))
        + [pltpu.VMEM((cols, 768), F32)] * (2 * (rows + 3))
        + [pltpu.VMEM((cols, 384), F32)] * (2 * (rows + 3))
        + [pltpu.VMEM((cols, 1152), BF16)] * (rows + 2)
        + [pltpu.VMEM((cols, 384), F32)] * rows
        + [pltpu.VMEM((cols, 384), BF16)] * rows,
        8e9, 36,
    )(
        info, hidden, conv, acc, got_even, got_odd, packed_even, packed_odd, own, own_mid, fwd, back_odd, back_even, mid_t,
        w_in[2].reshape(9 * chan, mid_chan), gain, gain_out,
    )
    received = lax.all_to_all(payload, "tile", split_axis=0, concat_axis=0, tiled=True)
    (placed,) = call(place_body(count, chan, tokens), [((4 * chan, tokens), F32)], 0, 2, [], 1e7, 8)(sel, received)
    return placed.T


def solution(mesh):
    return jax.shard_map(
        shards,
        mesh=mesh,
        in_specs=(
            P(("prompt", "tile"), None, None),
            P(None, ("prompt", "tile"), None, None),
            P(None, ("prompt", "tile"), None, None),
            P(("prompt", "tile"), None, None),
            P(),
            P(),
            P(),
            P(),
            P(),
            P("prompt"),
        ),
        out_specs=P(("prompt", "tile"), None),
        check_vma=False,
    )
```

```python
import jax
import jax.numpy as jnp
from jax import lax
from jax.experimental import pallas as pl
from jax.experimental.pallas import tpu as pltpu
from jax.sharding import PartitionSpec as P

EPS = 1e-06
F32 = jnp.float32
BF16 = jnp.bfloat16
VM = pl.BlockSpec(memory_space=pltpu.VMEM)
SM = pl.BlockSpec(memory_space=pltpu.SMEM)


def weave(*groups):
    total = max(len(g) for g in groups)
    done = [0] * len(groups)
    for k in range(total):
        for n, g in enumerate(groups):
            while done[n] * total < (k + 1) * len(g):
                g[done[n]]()
                done[n] += 1


def steps(f, *keys):
    return [lambda key=key: f(*key) for key in keys]


def call(body, outs, n_smem, n_vmem, scratch, flops, limit, smem_outs=0):
    specs = [SM] * n_smem + [VM] * n_vmem
    return pl.pallas_call(
        body,
        out_shape=[jax.ShapeDtypeStruct(s, d) for s, d in outs],
        in_specs=specs,
        out_specs=[SM] * smem_outs + [VM] * (len(outs) - smem_outs),
        scratch_shapes=scratch,
        cost_estimate=pl.CostEstimate(flops=int(flops), bytes_accessed=2**20, transcendentals=0),
        compiler_params=pltpu.CompilerParams(vmem_limit_bytes=limit << 20),
    )


def mm(a, b):
    return jnp.dot(a, b, preferred_element_type=F32)


def mm_t(a, b):
    return lax.dot_general(a, b, (((1,), (1,)), ((), ())), preferred_element_type=F32)


def flag(info, k):
    return info[k].astype(F32)


def from_left(x):
    moved = pltpu.roll(x, 1, 0)
    first = lax.broadcasted_iota(jnp.int32, (16, x.shape[1]), 0) == 0
    head = jnp.where(first, 0.0, moved[:16].astype(F32)).astype(BF16)
    return jnp.concatenate([head, moved[16:]], axis=0)


def from_right(x):
    size = x.shape[0]
    moved = pltpu.roll(x, size - 1, 0)
    last = lax.broadcasted_iota(jnp.int32, (16, x.shape[1]), 0) == 15
    tail = jnp.where(last, 0.0, moved[size - 16 :].astype(F32)).astype(BF16)
    return jnp.concatenate([moved[: size - 16], tail], axis=0)


def beside(target, base, lanes, x, ahead):
    sides = (from_right, from_left) if ahead else (from_left, from_right)
    for group, value in enumerate((sides[0](x), x, sides[1](x))):
        at = base + group * 384 + lanes
        target[:, at : at + 128] = value


CHUNK = 32


def picker(cols, o):
    half = o - 128
    x_index = lax.broadcasted_iota(jnp.int32, (cols, 2 * cols), 1)
    w_index = lax.broadcasted_iota(jnp.int32, (cols, 2 * cols), 0)
    pick = [(x_index == 2 * w_index + b).astype(F32).astype(BF16) for b in (0, 1)]
    zeros = jnp.zeros((128 - half, 2 * cols), BF16)

    def one(reward, f, own, k):
        r = reward[f]
        first, rest = r[:128], r[128:]
        low = jnp.concatenate([first, rest, zeros], axis=0)
        high = jnp.concatenate([first, zeros, rest], axis=0)
        sides = (low, high) if f % 2 else (high, low)
        d0, d1 = mm_t(pick[0], sides[0]), mm_t(pick[1], sides[1])
        own[k, :, 0:128] = d0[:, :128].astype(BF16)
        own[k, :, 128:256] = d1[:, :128].astype(BF16)
        own[k, :, 256:384] = (d0[:, 128:] + d1[:, 128:]).astype(BF16)

    return one


def pack_body(rows, cols, o, chan):
    def body(info, reward, latent, cached, own, send_even, send_odd):
        one = picker(cols, o)
        for k in range(6):
            one(reward, k if k < 3 else 2 * rows - 6 + k, own, k)
        base = 3 * cols
        per = chan * rows
        for send, last in ((send_even, 1 - info[0]), (send_odd, info[0])):
            begin = last * 3
            for k in range(3):
                send[k * cols : (k + 1) * cols] = own[begin + k]
            for t in range(3):
                src = cached[t] if t < 2 else latent[...]
                lat = src.reshape(per, cols)
                send[base : base + per, t * 128 : t * 128 + 128] = lat[:, :128]
                send[base + per : base + 2 * per, t * 128 : t * 128 + cols - 128] = lat[:, 128:]

    return body


def home(targets, q, p, tile):
    block, second = ((1, 1), (0, 0), (0, 1), (1, 0))[p]
    target, side = targets[q]
    if tile < 2:
        row = block * 384 + second * 128 + tile * 64
    else:
        row = block * 384 + 256 + 64 * (second if q % 2 == 0 else 1 - second)
    return target, row, side * 384


def turning(back_odd, back_even, fwd):
    targets = ((back_odd, 1), (back_even, 0), (back_odd, 0), (back_even, 1))

    def tap_tile(q, p, tile, lanes):
        target, row, side = home(targets, q, p, tile)
        return target[row : row + 64, side + lanes : side + lanes + 128]

    def one(b, side, lanes):
        p = ((3, 1), (2, 0))[b][side]
        at = slice(side * 384 + lanes, side * 384 + lanes + 128)
        for q in range(4):
            both = jnp.concatenate([tap_tile(q, p, 0, lanes), tap_tile(q, p, 1, lanes)], axis=0)
            fwd[b, at, q * 128 : q * 128 + 128] = both.T
        for half in range(2):
            pair = (2 * half, 2 * half + 1) if b == 0 else (2 * half + 1, 2 * half)
            both = jnp.concatenate([tap_tile(q, p, 2, lanes) for q in pair], axis=0)
            fwd[b, at, 512 + half * 128 : 640 + half * 128] = both.T

    return steps(one, *[(b, side, lanes) for b in range(2) for side in range(2) for lanes in range(0, 384, 128)])


def taps_body(info, up, info_out, back_odd, back_even):
    for k in range(4):
        info_out[k] = info[k]

    parts = ((2,), (1, 2), (0, 1), (0,))
    targets = ((back_odd, 1), (back_even, 0), (back_odd, 0), (back_even, 1))

    for tile in range(3):
        for lanes in range(0, 384, 128):
            w = [[up[i, j, tile * 64 : tile * 64 + 64, lanes : lanes + 128].astype(F32) for j in range(3)] for i in range(3)]
            for q in range(4):
                c = [w[parts[q][0]][j] + w[parts[q][1]][j] if len(parts[q]) > 1 else w[parts[q][0]][j] for j in range(3)]
                for p, tap in enumerate((c[2], c[1] + c[2], c[0] + c[1], c[0])):
                    target, row, side = home(targets, q, p, tile)
                    target[row : row + 64, side + lanes : side + lanes + 128] = tap.astype(BF16)


def cached_body(rows, cols, count, width, tokens, o):
    size = rows * cols

    def body(
        info, order, features, mid, back_odd, back_even, reward, acc, send_even, send_odd, mid_t, sel, fwd, own, wide, parts
    ):
        for t in range(2):
            for r in range(rows):
                for lanes in range(0, 384, 128):
                    x = features[t, r, :, lanes : lanes + 128]
                    beside(wide.at[r * cols : (r + 1) * cols], t * 1152, lanes, x, False)
        def product(i, lanes):
            parts[i, :, lanes] = mm(wide[...], jnp.concatenate([mid[0, i, :, lanes], mid[1, i, :, lanes]], axis=0))

        def double():
            left = jnp.concatenate([mid[0, 0, :, 256:384], mid[1, 0, :, 256:384]], axis=0)
            right = jnp.concatenate([mid[0, 1, :, 256:384], mid[1, 1, :, 256:384]], axis=0)
            both = mm(wide[...], jnp.concatenate([left, right], axis=1))
            parts[0, :, 256:384] = both[:, :128]
            parts[1, :, 256:384] = both[:, 128:]

        def turn(i, j):
            at = (i * 3 + j) * 384
            mid_t[at : at + 384] = mid[2, i, j * 384 : (j + 1) * 384].T

        most, rest = slice(0, 256), slice(256, 384)
        products = steps(product, (0, most), (1, most)) + steps(double, ()) + steps(product, (2, most), (2, rest))
        one = picker(cols, o)
        others = steps(turn, *[(i, j) for i in range(3) for j in range(3)])
        others += turning(back_odd, back_even, fwd)
        others += steps(placing(info, order, sel, count, width, tokens), *[(t,) for t in range(count)])
        others += steps(one, (reward, rows - 1, own, 0), (reward, rows, own, 1))
        weave(others, products)
        for k in range(rows + 4):
            total = jnp.zeros((cols, 384), F32)
            for i in range(3):
                r = k - 3 + i
                if 0 <= r < rows:
                    total = total + parts[i, r * cols : (r + 1) * cols]
            acc[k] = total
        for send, last in ((send_even, 1 - info[0]), (send_odd, info[0])):
            for k in range(3):
                send[k * cols : (k + 1) * cols] = acc[1 + last * 3 + k].astype(BF16)

    return body


def current_body(rows, cols, chan):
    per = chan * rows
    base = 3 * cols

    def body(info, latent, cached, got_even, got_odd, w_in, mid, half_gain, hidden, conv, lat, tall, wide, w_order, plain):
        even = info[0] == 0
        lat[...] = jnp.zeros_like(lat)

        def fill(first_row, got, ok):
            scale = ok.astype(F32)
            for t in range(3):
                x = got[base : base + per, t * 128 : t * 128 + 128].astype(F32) * scale
                y = got[base + per : base + 2 * per, t * 128 : t * 128 + cols - 128].astype(F32) * scale
                for r in range(rows):
                    at = pl.ds((first_row + r) * 3 * chan + t * chan, chan)
                    lat[at, 0:128] = x[r * chan : (r + 1) * chan]
                    lat[at, 128:cols] = y[r * chan : (r + 1) * chan]

        @pl.when(even)
        def _():
            fill(0, got_odd, info[1])
            fill(2 * rows, got_even, info[2])

        @pl.when(jnp.logical_not(even))
        def _():
            fill(0, got_even, info[1])
            fill(2 * rows, got_odd, info[2])

        for t in range(3):
            for r in range(rows):
                at = pl.ds((rows + r) * 3 * chan + t * chan, chan)
                lat[at, 0:cols] = (cached[t, r] if t < 2 else latent[r]).astype(F32)

        for r in range(3 * rows):
            for t in range(3):
                x = lat[pl.ds((r * 3 + t) * chan, chan), :]
                at = t * 3 * chan
                tall[r, at : at + chan] = pltpu.roll(x, 1, 1).astype(BF16)
                tall[r, at + chan : at + 2 * chan] = x.astype(BF16)
                tall[r, at + 2 * chan : at + 3 * chan] = pltpu.roll(x, 255, 1).astype(BF16)
        for i in range(3):
            for t in range(3):
                at = (i * 3 + t) * 3 * chan
                w_order[at : at + 3 * chan] = w_in[t, i]

        def hidden_row(k):
            lhs = tall[k : k + 3].reshape(27 * chan, 256)[:, 0:cols]
            h = lax.dot_general(lhs, w_order[...], (((0,), (0,)), ((), ())), preferred_element_type=F32)
            plain[k % 2] = h
            for c in range(0, cols, CHUNK):
                at = slice(c, c + CHUNK)
                v = plain[k % 2, at].astype(BF16)
                hidden[k, at] = v
                v = v.astype(F32)
                inv = lax.rsqrt(jnp.mean(v * v, axis=1, keepdims=True) + EPS)
                half = v * inv * half_gain[...]
                act = half * (jnp.tanh(half) + 1.0)
                if k < 3:
                    act = act * flag(info, 1)
                if k >= rows + 3:
                    act = act * flag(info, 2)
                wide[k, at, 384:768] = act.astype(BF16)
            for lanes in range(0, 384, 128):
                beside(wide.at[k], 0, lanes, wide[k, :, 384 + lanes : 512 + lanes], False)

        def conv_rows(p, number):
            lhs = [wide[p + i : p + i + number].reshape(number * cols, 1152) for i in range(3)]
            total = mm(jnp.concatenate(lhs, axis=1), mid[2, :, :, 0:256].reshape(3456, 256))
            conv[p : p + number, :, 0:256] = total.reshape(number, cols, 256)

        for k in range(rows + 2):
            hidden_row(k)
        conv_rows(0, rows)
        for k in range(rows + 2, rows + 6):
            hidden_row(k)
        conv_rows(rows, 4)
        both = mm(
            wide[0 : rows + 5].reshape((rows + 5) * cols, 1152),
            jnp.concatenate([mid[2, 0, :, 256:384], mid[2, 1, :, 256:384]], axis=1),
        )
        rest = mm(wide[2 : rows + 6].reshape((rows + 4) * cols, 1152), mid[2, 2, :, 256:384])
        for p in range(rows + 4):
            at, after = slice(p * cols, (p + 1) * cols), slice((p + 1) * cols, (p + 2) * cols)
            conv[p, :, 256:384] = both[at, :128] + both[after, 128:] + rest[at]

    return body


def pulled(s, half_gain, grad):
    h = s * half_gain
    t = jnp.tanh(h)
    return (grad * half_gain) * ((1.0 + t) * (1.0 + h * (1.0 - t)))


def back_body(rows, cols, chan, count, o):
    size = rows * cols
    width = 2 * cols // count

    def body(
        info, hidden, conv, acc, got_even, got_odd, packed_even, packed_odd, own, own_mid, fwd, back_odd, back_even, mid_t, w_in, half_gain,
        half_out, payload, reward, edge, p0, p1, g_odd, g_even, wide, t_odd, t_even, back, act_grad, hid, lines,
    ):
        even = info[0] == 0
        top, bottom = flag(info, 1), flag(info, 2)

        def take(got, packed, before):
            ok = top if before else bottom
            place = 0 if before else rows + 1
            for k in range(3):
                at = slice(k * cols, (k + 1) * cols)
                edge[place + k] = got[at].astype(F32) * ok
                reward[k if before else 2 * rows + 3 + k] = (packed[at].astype(F32) * ok).astype(BF16)

        @pl.when(even)
        def _():
            take(got_odd, packed_odd, True)
            take(got_even, packed_even, False)

        @pl.when(jnp.logical_not(even))
        def _():
            take(got_even, packed_even, True)
            take(got_odd, packed_odd, False)

        reward[3:6] = own[0:3]
        reward[6 : 2 * rows] = own_mid[...]
        reward[2 * rows : 2 * rows + 3] = own[3:6]

        def inside(x, k, first, last):
            return x * top if k < first else x * bottom if k >= last else x

        def state_row(k):
            for lanes in range(0, 384, 128):
                at = slice(lanes, lanes + 128)
                x = hidden[k + 1, :, at].astype(F32) + conv[k, :, at]
                if 1 <= k <= rows + 2:
                    x = x + acc[k, :, at]
                if k < 3 or k > rows:
                    x = x + edge[k, :, at]
                beside(wide.at[k], 0, lanes, inside(x, k, 2, rows + 2).astype(BF16), False)

        def up_rows(first, last, b, n):
            count = last - first
            x = wide[first:last, :, b * 384 : b * 384 + 768].reshape(count * cols, 768)
            lanes = slice(n * 256, n * 256 + 256)
            (p0, p1)[b][first:last, :, lanes] = mm(x, fwd[b, :, lanes]).reshape(count, cols, 256)

        def down_rows(first, last, odd, n):
            count = last - first
            g, kernel, t = (g_odd, back_odd, t_odd) if odd else (g_even, back_even, t_even)
            lanes = slice(n * 256, n * 256 + 256)
            x = g[first:last].reshape(count * cols, 768)
            t[first:last, :, lanes] = mm(x, kernel[:, lanes]).reshape(count, cols, 256)

        low = lax.broadcasted_iota(jnp.int32, (CHUNK, 128), 1) < 64
        gains = [half_out[:, 0:128], half_out[:, 128:256]]

        def pull(v0, v1, vm, r, zero_low):
            mine = low if zero_low else jnp.logical_not(low)
            def both(a0, a1, am):
                s0 = jnp.sum(a0 + jnp.where(mine, am, 0.0), axis=1, keepdims=True)
                s1 = jnp.sum(a1 + jnp.where(mine, 0.0, am), axis=1, keepdims=True)
                return s0 * (1.0 / o), s1 * (1.0 / o)

            q0, q1 = both(v0 * v0, v1 * v1, vm * vm)
            i0, i1 = lax.rsqrt(q0 + EPS), lax.rsqrt(q1 + EPS)
            im = jnp.where(mine, i0, i1)
            out = []
            for v, i, g, k in ((v0, i0, gains[0], 0), (v1, i1, gains[0], 1), (vm, im, gains[1], 2)):
                s = v * i
                out.append((s, pulled(s, g, r[:, k * 128 : k * 128 + 128].astype(F32))))
            m0, m1 = both(*(s * d for s, d in out))
            mx = jnp.where(mine, m0, m1)
            return [i * (d - s * m) for (s, d), i, m in zip(out, (i0, i1, im), (m0, m1, mx))]

        def pull_row(k, odd):
            target = g_odd if odd else g_even
            for c in range(0, cols, CHUNK):
                at = slice(c, c + CHUNK)
                if odd:
                    v0 = p0[k, at, 256:384] + p0[k + 1, at, 0:128]
                    v1 = p1[k, at, 256:384] + p1[k + 1, at, 0:128]
                    m0 = p0[k, at, 640:768] + p0[k + 1, at, 512:640]
                    m1 = p1[k, at, 640:768] + p1[k + 1, at, 512:640]
                else:
                    v0 = p0[k + 1, at, 128:256] + p0[k, at, 384:512]
                    v1 = p1[k + 1, at, 128:256] + p1[k, at, 384:512]
                    m0 = p1[k + 1, at, 512:640] + p1[k, at, 640:768]
                    m1 = p0[k + 1, at, 512:640] + p0[k, at, 640:768]
                out = pull(v0, v1, jnp.where(low, m0, m1), reward[2 * k + (0 if odd else 1), at], odd)
                for n, value in enumerate(out):
                    lanes = slice(n * 128, n * 128 + 128)
                    target[k, at, lanes] = value.astype(BF16)
            target[k, :, 384:512] = from_right(target[k, :, 0:128])
            target[k, :, 512:640] = from_left(target[k, :, 128:256])
            x = target[k, :, 256:384]
            sides = (from_right(x), from_left(x)) if odd else (from_left(x), from_right(x))
            target[k, :, 640:704] = sides[0][:, 0:64]
            target[k, :, 704:768] = sides[1][:, 64:128]

        def block_row(k):
            for lanes in range(0, 384, 128):
                at, far = slice(lanes, lanes + 128), slice(lanes + 384, lanes + 512)
                x = t_odd[k + 1, :, at] + t_odd[k, :, far] + t_even[k, :, at] + t_even[k + 1, :, far]
                beside(back.at[k], 0, lanes, inside(x, k, 1, rows + 1).astype(BF16), True)

        def hidden_pull(k):
            for c in range(0, cols, CHUNK):
                at = slice(c, c + CHUNK)
                v = hidden[k + 3, at].astype(F32)
                inv = lax.rsqrt(jnp.mean(v * v, axis=1, keepdims=True) + EPS)
                s = v * inv
                d = pulled(s, half_gain[...], act_grad[k, at])
                dv = inv * (d - s * jnp.mean(d * s, axis=1, keepdims=True))
                hid[k, at] = (back[k + 1, at, 384:768].astype(F32) + dv).astype(BF16)

        fine = rows + 3
        for k in range(rows + 4):
            state_row(k)
        for b in range(2):
            up_rows(1, rows + 4, b, 0)
            up_rows(0, rows + 3, b, 1)
            up_rows(0, rows + 4, b, 2)
        for k in range(fine):
            pull_row(k, True)
            pull_row(k, False)
        for odd in (True, False):
            down_rows(1 if odd else 0, fine if odd else fine - 1, odd, 0)
            down_rows(0, fine, odd, 1)
            down_rows(0 if odd else 1, fine - 1 if odd else fine, odd, 2)
        for k in range(rows + 2):
            block_row(k)
        lhs = [back[2 - i : 2 - i + rows].reshape(size, 1152) for i in range(3)]
        act_grad[:, :, 0:256] = mm(jnp.concatenate(lhs, axis=1), mid_t[:, 0:256]).reshape(rows, cols, 256)
        both = mm(
            back[1 : rows + 2].reshape((rows + 1) * cols, 1152),
            jnp.concatenate([mid_t[1152:2304, 256:384], mid_t[0:1152, 256:384]], axis=1),
        )
        rest = mm(back[0:rows].reshape(size, 1152), mid_t[2304:3456, 256:384])
        for p in range(rows):
            at, after = slice(p * cols, (p + 1) * cols), slice((p + 1) * cols, (p + 2) * cols)
            act_grad[p, :, 256:384] = both[at, :128] + both[after, 128:] + rest[at]
        for k in range(rows):
            hidden_pull(k)

        z = mm_t(w_in[...], hid[...].reshape(size, 384))
        place = lax.broadcasted_iota(jnp.int32, (chan, size), 1)
        col = lax.rem(place, cols)
        sums = []
        for i in range(3):
            z0, z1, z2 = (z[(i * 3 + j) * chan : (i * 3 + j + 1) * chan] for j in range(3))
            left = jnp.where(col == cols - 1, 0.0, pltpu.roll(z0, size - 1, 1))
            right = jnp.where(col == 0, 0.0, pltpu.roll(z2, 1, 1))
            sums.append(left + z1 + right)
        inner = sums[1]
        inner = inner + jnp.where(place < size - cols, pltpu.roll(sums[0], size - cols, 1), 0.0)
        inner = inner + jnp.where(place >= cols, pltpu.roll(sums[2], cols, 1), 0.0)
        lines[0:chan] = inner
        lines[chan : 2 * chan] = sums[0]
        lines[2 * chan : 3 * chan] = sums[2]
        per_row = count // 2
        for u in range(count):
            pair, piece = u // per_row, u % per_row
            parts = []
            for a in range(2):
                at = (2 * pair + a) * cols + piece * width
                parts.append(lines[0:chan, at : at + width])
            at = piece * width + (0 if pair else (rows - 1) * cols)
            first = chan if pair else 2 * chan
            parts.append(lines[first : first + chan, at : at + width])
            parts.append(jnp.zeros((chan, 128 - 3 * width), F32))
            payload[u] = jnp.concatenate(parts, axis=1).astype(BF16)

    return body


def placing(info, order, sel, count, width, tokens):
    piece = width // 2
    pair = info[3]
    lane = lax.broadcasted_iota(jnp.int32, (128, 4 * tokens), 0)
    column = lax.broadcasted_iota(jnp.int32, (128, 4 * tokens), 1)
    group = (lane >= width).astype(jnp.int32) + (lane >= 2 * width).astype(jnp.int32)
    w = lane - group * width
    part = jnp.where(group == 2, pair, group)
    fixed = (2 * part + (w & 1)) * tokens + (w >> 1) - column
    fixed = jnp.where(lane < 3 * width, fixed, -99999)

    def one(t):
        step = t + 1 - 2 * pair
        valid = jnp.logical_and(step >= 0, step < count)
        beside = jnp.where(valid, piece * order[jnp.clip(step, 0, count - 1)], -9999)
        begin = jnp.where(group == 2, beside, piece * order[t])
        sel[t] = (fixed + begin == 0).astype(F32).astype(BF16)

    return one


def place_body(count, chan, tokens):
    def body(sel, got, out):
        total = mm(got[0], sel[0])
        for t in range(1, count):
            total += mm(got[t], sel[t])
        for k in range(4):
            out[k * chan : (k + 1) * chan] = total[:, k * tokens : (k + 1) * tokens]

    return body


def swaps(count):
    within = [(i, i ^ 1) for i in range(count)]
    across = [(0, 0), (count - 1, count - 1)]
    for i in range(1, count - 1, 2):
        across += [(i, i + 1), (i + 1, i)]
    return within, sorted(across)


def shards(
    latent, cached_latent, cached_features, reward_grad, conv_in_weight, conv_mid_weight, conv_up_weight, norm_gain, out_gain, shard_order
):
    count = lax.axis_size("tile")
    rows, cols, chan = latent.shape
    mid_chan = norm_gain.shape[0]
    o = out_gain.shape[0]
    tile = lax.axis_index("tile")
    info = jnp.stack(
        [tile % 2, (tile > 0).astype(jnp.int32), (tile < count - 1).astype(jnp.int32), (tile >= count // 2).astype(jnp.int32)]
    ).astype(jnp.int32)
    lat = jnp.transpose(latent, (0, 2, 1))
    lat_cached = jnp.transpose(cached_latent, (0, 1, 3, 2))
    reward_t = jnp.transpose(reward_grad, (0, 2, 1))
    up_t = jnp.transpose(conv_up_weight, (0, 1, 3, 2))
    mid = conv_mid_weight.reshape(3, 3, 3 * mid_chan, mid_chan)
    w_in = conv_in_weight.reshape(3, 3, 3 * chan, mid_chan)
    gain = 0.5 * norm_gain.reshape(1, mid_chan)
    gain_out = 0.5 * jnp.concatenate([out_gain, out_gain[128:]]).reshape(1, 256)
    within, across = swaps(count)
    size = rows * cols
    edge_rows = 3 * cols + 2 * chan * rows

    info, back_odd, back_even = call(
        taps_body,
        [((4,), jnp.int32), ((768, 768), BF16), ((768, 768), BF16)],
        1, 1, [], 1e10, 8, 1,
    )(info, up_t)

    own, send_even, send_odd = call(
        pack_body(rows, cols, o, chan),
        [((6, cols, 384), BF16), ((edge_rows, 384), BF16), ((edge_rows, 384), BF16)],
        1, 3, [], 1e10, 8,
    )(info, reward_t, lat, lat_cached)
    packed_even = lax.ppermute(send_even, "tile", within)
    packed_odd = lax.ppermute(send_odd, "tile", across)

    width = 2 * cols // count
    tokens = size // 4
    acc, part_even, part_odd, mid_t, sel, fwd, own_mid = call(
        cached_body(rows, cols, count, width, tokens, o),
        [
            ((rows + 4, cols, 384), F32), ((3 * cols, 384), BF16), ((3 * cols, 384), BF16), ((3456, 384), BF16),
            ((count, 128, 4 * tokens), BF16), ((2, 768, 768), BF16), ((2, cols, 384), BF16),
        ],
        2, 5, [pltpu.VMEM((size, 2304), BF16), pltpu.VMEM((3, size, 384), F32)], 4e9, 14,
    )(info, shard_order, cached_features, mid, back_odd, back_even, reward_t)
    got_even = lax.ppermute(part_even, "tile", within)
    got_odd = lax.ppermute(part_odd, "tile", across)

    hidden, conv = call(
        current_body(rows, cols, chan),
        [((rows + 6, cols, 384), BF16), ((rows + 4, cols, 384), F32)],
        1, 7,
        [
            pltpu.VMEM((9 * rows * chan, 256), F32),
            pltpu.VMEM((3 * rows, 9 * chan, 256), BF16),
            pltpu.VMEM((rows + 6, cols, 1152), BF16),
            pltpu.VMEM((27 * chan, 384), BF16),
            pltpu.VMEM((2, cols, 384), F32),
        ],
        5e9, 14,
    )(info, lat, lat_cached, packed_even, packed_odd, w_in, mid, gain)

    (payload,) = call(
        back_body(rows, cols, chan, count, o),
        [((count, chan, 128), BF16)],
        1, 16,
        [
            pltpu.VMEM((2 * rows + 6, cols, 384), BF16),
            pltpu.VMEM((rows + 4, cols, 384), F32),
            pltpu.VMEM((rows + 4, cols, 768), F32),
            pltpu.VMEM((rows + 4, cols, 768), F32),
            pltpu.VMEM((rows + 3, cols, 768), BF16),
            pltpu.VMEM((rows + 3, cols, 768), BF16),
            pltpu.VMEM((rows + 4, cols, 1152), BF16),
            pltpu.VMEM((rows + 3, cols, 768), F32),
            pltpu.VMEM((rows + 3, cols, 768), F32),
            pltpu.VMEM((rows + 2, cols, 1152), BF16),
            pltpu.VMEM((rows, cols, 384), F32),
            pltpu.VMEM((rows, cols, 384), BF16),
            pltpu.VMEM((3 * chan, size), F32),
        ],
        8e9, 34,
    )(
        info, hidden, conv, acc, got_even, got_odd, packed_even, packed_odd, own, own_mid, fwd, back_odd, back_even, mid_t,
        w_in[2].reshape(9 * chan, mid_chan), gain, gain_out,
    )
    received = lax.all_to_all(payload, "tile", split_axis=0, concat_axis=0, tiled=True)
    (placed,) = call(place_body(count, chan, tokens), [((4 * chan, tokens), F32)], 0, 2, [], 1e7, 8)(sel, received)
    return placed.T


def solution(mesh):
    return jax.shard_map(
        shards,
        mesh=mesh,
        in_specs=(
            P(("prompt", "tile"), None, None),
            P(None, ("prompt", "tile"), None, None),
            P(None, ("prompt", "tile"), None, None),
            P(("prompt", "tile"), None, None),
            P(),
            P(),
            P(),
            P(),
            P(),
            P("prompt"),
        ),
        out_specs=P(("prompt", "tile"), None),
        check_vma=False,
    )
```

```python
import jax
import jax.numpy as jnp
from jax import lax
from jax.experimental import pallas as pl
from jax.experimental.pallas import tpu as pltpu
from jax.sharding import PartitionSpec as P

EPS = 1e-06
F32 = jnp.float32
BF16 = jnp.bfloat16
VM = pl.BlockSpec(memory_space=pltpu.VMEM)
SM = pl.BlockSpec(memory_space=pltpu.SMEM)


def weave(*groups):
    total = max(len(g) for g in groups)
    done = [0] * len(groups)
    for k in range(total):
        for n, g in enumerate(groups):
            while done[n] * total < (k + 1) * len(g):
                g[done[n]]()
                done[n] += 1


def steps(f, *keys):
    return [lambda key=key: f(*key) for key in keys]


def call(body, outs, n_smem, n_vmem, scratch, flops, limit, smem_outs=0):
    specs = [SM] * n_smem + [VM] * n_vmem
    return pl.pallas_call(
        body,
        out_shape=[jax.ShapeDtypeStruct(s, d) for s, d in outs],
        in_specs=specs,
        out_specs=[SM] * smem_outs + [VM] * (len(outs) - smem_outs),
        scratch_shapes=scratch,
        cost_estimate=pl.CostEstimate(flops=int(flops), bytes_accessed=2**20, transcendentals=0),
        compiler_params=pltpu.CompilerParams(vmem_limit_bytes=limit << 20),
    )


def mm(a, b):
    return jnp.dot(a, b, preferred_element_type=F32)


def mm_t(a, b):
    return lax.dot_general(a, b, (((1,), (1,)), ((), ())), preferred_element_type=F32)


def flag(info, k):
    return info[k].astype(F32)


def from_left(x):
    moved = pltpu.roll(x, 1, 0)
    first = lax.broadcasted_iota(jnp.int32, (8, x.shape[1]), 0) == 0
    return jnp.concatenate([jnp.where(first, 0.0, moved[:8]), moved[8:]], axis=0)


def from_right(x):
    size = x.shape[0]
    moved = pltpu.roll(x, size - 1, 0)
    last = lax.broadcasted_iota(jnp.int32, (8, x.shape[1]), 0) == 7
    return jnp.concatenate([moved[: size - 8], jnp.where(last, 0.0, moved[size - 8 :])], axis=0)


def beside(target, base, lanes, x, ahead):
    sides = (from_right, from_left) if ahead else (from_left, from_right)
    for group, value in enumerate((sides[0](x), x, sides[1](x))):
        at = base + group * 384 + lanes
        target[:, at : at + 128] = value.astype(BF16)


CHUNK = 32


def picker(cols, o):
    half = o - 128
    x_index = lax.broadcasted_iota(jnp.int32, (cols, 2 * cols), 1)
    w_index = lax.broadcasted_iota(jnp.int32, (cols, 2 * cols), 0)
    pick = [(x_index == 2 * w_index + b).astype(F32).astype(BF16) for b in (0, 1)]
    zeros = jnp.zeros((128 - half, 2 * cols), BF16)

    def one(reward, f, own, k):
        r = reward[f]
        first, rest = r[:128], r[128:]
        low = jnp.concatenate([first, rest, zeros], axis=0)
        high = jnp.concatenate([first, zeros, rest], axis=0)
        sides = (low, high) if f % 2 else (high, low)
        d0, d1 = mm_t(pick[0], sides[0]), mm_t(pick[1], sides[1])
        own[k, :, 0:128] = d0[:, :128].astype(BF16)
        own[k, :, 128:256] = d1[:, :128].astype(BF16)
        own[k, :, 256:384] = (d0[:, 128:] + d1[:, 128:]).astype(BF16)

    return one


def pack_body(rows, cols, o, chan):
    def body(info, reward, latents, info_out, own, send_even, send_odd):
        for k in range(4):
            info_out[k] = info[k]
        one = picker(cols, o)
        for k in range(6):
            one(reward, k if k < 3 else 2 * rows - 6 + k, own, k)
        base = 3 * cols
        per = chan * rows
        for send, last in ((send_even, 1 - info[0]), (send_odd, info[0])):
            begin = last * 3
            for k in range(3):
                send[k * cols : (k + 1) * cols] = own[begin + k]
            for t in range(3):
                lat = latents[t].reshape(per, cols)
                send[base : base + per, t * 128 : t * 128 + 128] = lat[:, :128]
                send[base + per : base + 2 * per, t * 128 : t * 128 + cols - 128] = lat[:, 128:]

    return body


def home(targets, q, p, tile):
    block, second = ((1, 1), (0, 0), (0, 1), (1, 0))[p]
    target, side = targets[q]
    if tile < 2:
        row = block * 384 + second * 128 + tile * 64
    else:
        row = block * 384 + 256 + 64 * (second if q % 2 == 0 else 1 - second)
    return target, row, side * 384


def turning(back_odd, back_even, fwd):
    targets = ((back_odd, 1), (back_even, 0), (back_odd, 0), (back_even, 1))

    def tap_tile(q, p, tile, lanes):
        target, row, side = home(targets, q, p, tile)
        return target[row : row + 64, side + lanes : side + lanes + 128]

    def one(b, side, lanes):
        p = ((3, 1), (2, 0))[b][side]
        at = slice(side * 384 + lanes, side * 384 + lanes + 128)
        for q in range(4):
            both = jnp.concatenate([tap_tile(q, p, 0, lanes), tap_tile(q, p, 1, lanes)], axis=0)
            fwd[b, at, q * 128 : q * 128 + 128] = both.T
        for half in range(2):
            pair = (2 * half, 2 * half + 1) if b == 0 else (2 * half + 1, 2 * half)
            both = jnp.concatenate([tap_tile(q, p, 2, lanes) for q in pair], axis=0)
            fwd[b, at, 512 + half * 128 : 640 + half * 128] = both.T

    return steps(one, *[(b, side, lanes) for b in range(2) for side in range(2) for lanes in range(0, 384, 128)])


def summing(up, back_odd, back_even):
    parts = ((2,), (1, 2), (0, 1), (0,))
    targets = ((back_odd, 1), (back_even, 0), (back_odd, 0), (back_even, 1))

    def one(tile, lanes):
        w = [[up[i, j, tile * 64 : tile * 64 + 64, lanes : lanes + 128].astype(F32) for j in range(3)] for i in range(3)]
        for q in range(4):
            c = [w[parts[q][0]][j] + w[parts[q][1]][j] if len(parts[q]) > 1 else w[parts[q][0]][j] for j in range(3)]
            for p, tap in enumerate((c[2], c[1] + c[2], c[0] + c[1], c[0])):
                target, row, side = home(targets, q, p, tile)
                target[row : row + 64, side + lanes : side + lanes + 128] = tap.astype(BF16)

    return steps(one, *[(tile, lanes) for tile in range(3) for lanes in range(0, 384, 128)])


def cached_body(rows, cols, count, width, tokens, o):
    size = rows * cols

    def body(
        info, order, features, mid, up, reward, acc, send_even, send_odd, mid_t, sel, fwd, own, back_odd, back_even, wide,
        parts,
    ):
        for t in range(2):
            for r in range(rows):
                for lanes in range(0, 384, 128):
                    x = features[t, r, :, lanes : lanes + 128].astype(F32)
                    beside(wide.at[r * cols : (r + 1) * cols], t * 1152, lanes, x, False)
        def product(i, lanes):
            parts[i, :, lanes] = mm(wide[...], jnp.concatenate([mid[0, i, :, lanes], mid[1, i, :, lanes]], axis=0))

        def double():
            left = jnp.concatenate([mid[0, 0, :, 256:384], mid[1, 0, :, 256:384]], axis=0)
            right = jnp.concatenate([mid[0, 1, :, 256:384], mid[1, 1, :, 256:384]], axis=0)
            both = mm(wide[...], jnp.concatenate([left, right], axis=1))
            parts[0, :, 256:384] = both[:, :128]
            parts[1, :, 256:384] = both[:, 128:]

        def turn(i, j):
            at = (i * 3 + j) * 384
            mid_t[at : at + 384] = mid[2, i, j * 384 : (j + 1) * 384].T

        most, rest = slice(0, 256), slice(256, 384)
        products = steps(product, (0, most), (1, most)) + steps(double, ()) + steps(product, (2, most), (2, rest))
        one = picker(cols, o)
        others = steps(turn, *[(i, j) for i in range(3) for j in range(3)])
        others += summing(up, back_odd, back_even) + turning(back_odd, back_even, fwd)
        others += steps(placing(info, order, sel, count, width, tokens), *[(t,) for t in range(count)])
        others += steps(one, (reward, rows - 1, own, 0), (reward, rows, own, 1))
        weave(others, products)
        for k in range(rows + 4):
            total = jnp.zeros((cols, 384), F32)
            for i in range(3):
                r = k - 3 + i
                if 0 <= r < rows:
                    total = total + parts[i, r * cols : (r + 1) * cols]
            acc[k] = total
        for send, last in ((send_even, 1 - info[0]), (send_odd, info[0])):
            for k in range(3):
                send[k * cols : (k + 1) * cols] = acc[1 + last * 3 + k].astype(BF16)

    return body


def current_body(rows, cols, chan):
    per = chan * rows
    base = 3 * cols

    def body(info, latents, got_even, got_odd, w_in, mid, half_gain, hidden, conv, lat, tall, wide, w_order, plain):
        even = info[0] == 0
        lat[...] = jnp.zeros_like(lat)

        def fill(first_row, got, ok):
            scale = ok.astype(F32)
            for t in range(3):
                x = got[base : base + per, t * 128 : t * 128 + 128].astype(F32) * scale
                y = got[base + per : base + 2 * per, t * 128 : t * 128 + cols - 128].astype(F32) * scale
                for r in range(rows):
                    at = pl.ds((first_row + r) * 3 * chan + t * chan, chan)
                    lat[at, 0:128] = x[r * chan : (r + 1) * chan]
                    lat[at, 128:cols] = y[r * chan : (r + 1) * chan]

        @pl.when(even)
        def _():
            fill(0, got_odd, info[1])
            fill(2 * rows, got_even, info[2])

        @pl.when(jnp.logical_not(even))
        def _():
            fill(0, got_even, info[1])
            fill(2 * rows, got_odd, info[2])

        for t in range(3):
            for r in range(rows):
                at = pl.ds((rows + r) * 3 * chan + t * chan, chan)
                lat[at, 0:cols] = latents[t, r].astype(F32)

        for r in range(3 * rows):
            for t in range(3):
                x = lat[pl.ds((r * 3 + t) * chan, chan), :]
                at = t * 3 * chan
                tall[r, at : at + chan] = pltpu.roll(x, 1, 1).astype(BF16)
                tall[r, at + chan : at + 2 * chan] = x.astype(BF16)
                tall[r, at + 2 * chan : at + 3 * chan] = pltpu.roll(x, 255, 1).astype(BF16)
        for i in range(3):
            for t in range(3):
                at = (i * 3 + t) * 3 * chan
                w_order[at : at + 3 * chan] = w_in[t, i]

        def hidden_row(k):
            lhs = tall[k : k + 3].reshape(27 * chan, 256)[:, 0:cols]
            h = lax.dot_general(lhs, w_order[...], (((0,), (0,)), ((), ())), preferred_element_type=F32)
            plain[k % 2] = h
            for c in range(0, cols, CHUNK):
                at = slice(c, c + CHUNK)
                v = plain[k % 2, at].astype(BF16)
                hidden[k, at] = v
                v = v.astype(F32)
                inv = lax.rsqrt(jnp.mean(v * v, axis=1, keepdims=True) + EPS)
                half = v * inv * half_gain[...]
                act = half * (jnp.tanh(half) + 1.0)
                if k < 3:
                    act = act * flag(info, 1)
                if k >= rows + 3:
                    act = act * flag(info, 2)
                plain[k % 2, at] = act
            for lanes in range(0, 384, 128):
                beside(wide.at[k], 0, lanes, plain[k % 2, :, lanes : lanes + 128], False)

        def conv_rows(p, number):
            lhs = [wide[p + i : p + i + number].reshape(number * cols, 1152) for i in range(3)]
            total = mm(jnp.concatenate(lhs, axis=1), mid[2, :, :, 0:256].reshape(3456, 256))
            conv[p : p + number, :, 0:256] = total.reshape(number, cols, 256)

        for k in range(rows + 2):
            hidden_row(k)
        conv_rows(0, rows)
        for k in range(rows + 2, rows + 6):
            hidden_row(k)
        conv_rows(rows, 4)
        both = mm(
            wide[0 : rows + 5].reshape((rows + 5) * cols, 1152),
            jnp.concatenate([mid[2, 0, :, 256:384], mid[2, 1, :, 256:384]], axis=1),
        )
        rest = mm(wide[2 : rows + 6].reshape((rows + 4) * cols, 1152), mid[2, 2, :, 256:384])
        for p in range(rows + 4):
            at, after = slice(p * cols, (p + 1) * cols), slice((p + 1) * cols, (p + 2) * cols)
            conv[p, :, 256:384] = both[at, :128] + both[after, 128:] + rest[at]

    return body


def pulled(s, half_gain, grad):
    h = s * half_gain
    t = jnp.tanh(h)
    return (grad * half_gain) * ((1.0 + t) * (1.0 + h * (1.0 - t)))


def back_body(rows, cols, chan, count, o):
    size = rows * cols
    width = 2 * cols // count

    def body(
        info, hidden, conv, acc, got_even, got_odd, packed_even, packed_odd, own, own_mid, fwd, back_odd, back_even, mid_t, w_in, half_gain,
        half_out, payload, reward, p0, p1, g_odd, g_even, wide, t_odd, t_even, back, act_grad, hid, tmp_odd, tmp_even, lines,
    ):
        top, bottom = flag(info, 1), flag(info, 2)
        odd_tile = flag(info, 0)
        above = (top * odd_tile, top * (1.0 - odd_tile))
        below = (bottom * (1.0 - odd_tile), bottom * odd_tile)

        def halo(of_even, of_odd, k, lanes, before):
            scale = above if before else below
            at = slice(k * cols, (k + 1) * cols)
            return of_even[at, lanes].astype(F32) * scale[0] + of_odd[at, lanes].astype(F32) * scale[1]

        for k in range(3):
            for lanes in (slice(0, 128), slice(128, 256), slice(256, 384)):
                reward[k, :, lanes] = halo(packed_even, packed_odd, k, lanes, True).astype(BF16)
                reward[2 * rows + 3 + k, :, lanes] = halo(packed_even, packed_odd, k, lanes, False).astype(BF16)
        reward[3:6] = own[0:3]
        reward[6 : 2 * rows] = own_mid[...]
        reward[2 * rows : 2 * rows + 3] = own[3:6]

        def inside(x, k, first, last):
            return x * top if k < first else x * bottom if k >= last else x

        def state_row(k):
            for lanes in range(0, 384, 128):
                at = slice(lanes, lanes + 128)
                x = hidden[k + 1, :, at].astype(F32) + conv[k, :, at]
                if 1 <= k <= rows + 2:
                    x = x + acc[k, :, at]
                if k < 3:
                    x = x + halo(got_even, got_odd, k, at, True)
                if k > rows:
                    x = x + halo(got_even, got_odd, k - rows - 1, at, False)
                beside(wide.at[k], 0, lanes, inside(x, k, 2, rows + 2), False)

        def up_rows(first, last, b, n):
            count = last - first
            x = wide[first:last, :, b * 384 : b * 384 + 768].reshape(count * cols, 768)
            lanes = slice(n * 256, n * 256 + 256)
            (p0, p1)[b][first:last, :, lanes] = mm(x, fwd[b, :, lanes]).reshape(count, cols, 256)

        def down_rows(first, last, odd, n):
            count = last - first
            g, kernel, t = (g_odd, back_odd, t_odd) if odd else (g_even, back_even, t_even)
            lanes = slice(n * 256, n * 256 + 256)
            x = g[first:last].reshape(count * cols, 768)
            t[first:last, :, lanes] = mm(x, kernel[:, lanes]).reshape(count, cols, 256)

        low = lax.broadcasted_iota(jnp.int32, (CHUNK, 128), 1) < 64
        tall_low = lax.broadcasted_iota(jnp.int32, (cols, 128), 1) < 64
        gains = [half_out[:, 0:128], half_out[:, 128:256]]

        def pull(v0, v1, vm, r, zero_low):
            mine = low if zero_low else jnp.logical_not(low)
            def both(a0, a1, am):
                s0 = jnp.sum(a0 + jnp.where(mine, am, 0.0), axis=1, keepdims=True)
                s1 = jnp.sum(a1 + jnp.where(mine, 0.0, am), axis=1, keepdims=True)
                return s0 * (1.0 / o), s1 * (1.0 / o)

            q0, q1 = both(v0 * v0, v1 * v1, vm * vm)
            i0, i1 = lax.rsqrt(q0 + EPS), lax.rsqrt(q1 + EPS)
            im = jnp.where(mine, i0, i1)
            out = []
            for v, i, g, k in ((v0, i0, gains[0], 0), (v1, i1, gains[0], 1), (vm, im, gains[1], 2)):
                s = v * i
                out.append((s, pulled(s, g, r[:, k * 128 : k * 128 + 128].astype(F32))))
            m0, m1 = both(*(s * d for s, d in out))
            mx = jnp.where(mine, m0, m1)
            return [i * (d - s * m) for (s, d), i, m in zip(out, (i0, i1, im), (m0, m1, mx))]

        def pull_row(k, odd):
            target, tmp = (g_odd, tmp_odd) if odd else (g_even, tmp_even)
            for c in range(0, cols, CHUNK):
                at = slice(c, c + CHUNK)
                if odd:
                    v0 = p0[k, at, 256:384] + p0[k + 1, at, 0:128]
                    v1 = p1[k, at, 256:384] + p1[k + 1, at, 0:128]
                    m0 = p0[k, at, 640:768] + p0[k + 1, at, 512:640]
                    m1 = p1[k, at, 640:768] + p1[k + 1, at, 512:640]
                else:
                    v0 = p0[k + 1, at, 128:256] + p0[k, at, 384:512]
                    v1 = p1[k + 1, at, 128:256] + p1[k, at, 384:512]
                    m0 = p1[k + 1, at, 512:640] + p1[k, at, 640:768]
                    m1 = p0[k + 1, at, 512:640] + p0[k, at, 640:768]
                out = pull(v0, v1, jnp.where(low, m0, m1), reward[2 * k + (0 if odd else 1), at], odd)
                for n, value in enumerate(out):
                    lanes = slice(n * 128, n * 128 + 128)
                    target[k, at, lanes] = value.astype(BF16)
                    tmp[0, at, lanes] = value
            target[k, :, 384:512] = from_right(tmp[0, :, 0:128]).astype(BF16)
            target[k, :, 512:640] = from_left(tmp[0, :, 128:256]).astype(BF16)
            x = tmp[0, :, 256:384]
            sides = (from_right(x), from_left(x)) if odd else (from_left(x), from_right(x))
            target[k, :, 640:768] = jnp.where(tall_low, *sides).astype(BF16)

        def block_row(k):
            for lanes in range(0, 384, 128):
                at, far = slice(lanes, lanes + 128), slice(lanes + 384, lanes + 512)
                x = t_odd[k + 1, :, at] + t_odd[k, :, far] + t_even[k, :, at] + t_even[k + 1, :, far]
                beside(back.at[k], 0, lanes, inside(x, k, 1, rows + 1), True)

        def hidden_pull(k):
            for c in range(0, cols, CHUNK):
                at = slice(c, c + CHUNK)
                v = hidden[k + 3, at].astype(F32)
                inv = lax.rsqrt(jnp.mean(v * v, axis=1, keepdims=True) + EPS)
                s = v * inv
                d = pulled(s, half_gain[...], act_grad[k, at])
                dv = inv * (d - s * jnp.mean(d * s, axis=1, keepdims=True))
                hid[k, at] = (back[k + 1, at, 384:768].astype(F32) + dv).astype(BF16)

        fine = rows + 3
        for k in range(rows + 4):
            state_row(k)
        for b in range(2):
            up_rows(1, rows + 4, b, 0)
            up_rows(0, rows + 3, b, 1)
            up_rows(0, rows + 4, b, 2)

        @pl.loop(0, fine)
        def _(k):
            pull_row(k, True)
            pull_row(k, False)

        for odd in (True, False):
            down_rows(1 if odd else 0, fine if odd else fine - 1, odd, 0)
            down_rows(0, fine, odd, 1)
            down_rows(0 if odd else 1, fine - 1 if odd else fine, odd, 2)
        for k in range(rows + 2):
            block_row(k)
        lhs = [back[2 - i : 2 - i + rows].reshape(size, 1152) for i in range(3)]
        act_grad[:, :, 0:256] = mm(jnp.concatenate(lhs, axis=1), mid_t[:, 0:256]).reshape(rows, cols, 256)
        both = mm(
            back[1 : rows + 2].reshape((rows + 1) * cols, 1152),
            jnp.concatenate([mid_t[1152:2304, 256:384], mid_t[0:1152, 256:384]], axis=1),
        )
        rest = mm(back[0:rows].reshape(size, 1152), mid_t[2304:3456, 256:384])
        for p in range(rows):
            at, after = slice(p * cols, (p + 1) * cols), slice((p + 1) * cols, (p + 2) * cols)
            act_grad[p, :, 256:384] = both[at, :128] + both[after, 128:] + rest[at]
        for k in range(rows):
            hidden_pull(k)

        z = mm_t(w_in[...], hid[...].reshape(size, 384))
        place = lax.broadcasted_iota(jnp.int32, (chan, size), 1)
        col = lax.rem(place, cols)
        sums = []
        for i in range(3):
            z0, z1, z2 = (z[(i * 3 + j) * chan : (i * 3 + j + 1) * chan] for j in range(3))
            left = jnp.where(col == cols - 1, 0.0, pltpu.roll(z0, size - 1, 1))
            right = jnp.where(col == 0, 0.0, pltpu.roll(z2, 1, 1))
            sums.append(left + z1 + right)
        inner = sums[1]
        inner = inner + jnp.where(place < size - cols, pltpu.roll(sums[0], size - cols, 1), 0.0)
        inner = inner + jnp.where(place >= cols, pltpu.roll(sums[2], cols, 1), 0.0)
        lines[0:chan] = inner
        lines[chan : 2 * chan] = sums[0]
        lines[2 * chan : 3 * chan] = sums[2]
        per_row = count // 2
        for u in range(count):
            pair, piece = u // per_row, u % per_row
            parts = []
            for a in range(2):
                at = (2 * pair + a) * cols + piece * width
                parts.append(lines[0:chan, at : at + width])
            at = piece * width + (0 if pair else (rows - 1) * cols)
            first = chan if pair else 2 * chan
            parts.append(lines[first : first + chan, at : at + width])
            parts.append(jnp.zeros((chan, 128 - 3 * width), F32))
            payload[u] = jnp.concatenate(parts, axis=1).astype(BF16)

    return body


def placing(info, order, sel, count, width, tokens):
    piece = width // 2
    pair = info[3]
    lane = lax.broadcasted_iota(jnp.int32, (128, 4 * tokens), 0)
    column = lax.broadcasted_iota(jnp.int32, (128, 4 * tokens), 1)
    group = (lane >= width).astype(jnp.int32) + (lane >= 2 * width).astype(jnp.int32)
    w = lane - group * width
    part = jnp.where(group == 2, pair, group)
    fixed = (2 * part + (w & 1)) * tokens + (w >> 1) - column
    fixed = jnp.where(lane < 3 * width, fixed, -99999)

    def one(t):
        step = t + 1 - 2 * pair
        valid = jnp.logical_and(step >= 0, step < count)
        beside = jnp.where(valid, piece * order[jnp.clip(step, 0, count - 1)], -9999)
        begin = jnp.where(group == 2, beside, piece * order[t])
        sel[t // 2, t % 2 * 128 : t % 2 * 128 + 128] = (fixed + begin == 0).astype(F32).astype(BF16)

    return one


def place_body(count, chan, tokens):
    def body(sel, got, out):
        total = None
        for t in range(count // 2):
            x = mm(jnp.concatenate([got[2 * t], got[2 * t + 1]], axis=1), sel[t])
            total = x if total is None else total + x
        for k in range(4):
            out[k * chan : (k + 1) * chan] = total[:, k * tokens : (k + 1) * tokens]

    return body


def swaps(count):
    within = [(i, i ^ 1) for i in range(count)]
    across = [(0, 0), (count - 1, count - 1)]
    for i in range(1, count - 1, 2):
        across += [(i, i + 1), (i + 1, i)]
    return within, sorted(across)


def shards(
    latent, cached_latent, cached_features, reward_grad, conv_in_weight, conv_mid_weight, conv_up_weight, norm_gain, out_gain, shard_order
):
    count = lax.axis_size("tile")
    rows, cols, chan = latent.shape
    mid_chan = norm_gain.shape[0]
    o = out_gain.shape[0]
    tile = lax.axis_index("tile")
    info = jnp.stack(
        [tile % 2, (tile > 0).astype(jnp.int32), (tile < count - 1).astype(jnp.int32), (tile >= count // 2).astype(jnp.int32)]
    ).astype(jnp.int32)
    latents = jnp.concatenate([jnp.transpose(cached_latent, (0, 1, 3, 2)), jnp.transpose(latent, (0, 2, 1))[None]], axis=0)
    reward_t = jnp.transpose(reward_grad, (0, 2, 1))
    up_t = jnp.transpose(conv_up_weight, (0, 1, 3, 2))
    mid = conv_mid_weight.reshape(3, 3, 3 * mid_chan, mid_chan)
    w_in = conv_in_weight.reshape(3, 3, 3 * chan, mid_chan)
    gain = 0.5 * norm_gain.reshape(1, mid_chan)
    gain_out = 0.5 * jnp.concatenate([out_gain, out_gain[128:]]).reshape(1, 256)
    within, across = swaps(count)
    size = rows * cols
    edge_rows = 3 * cols + 2 * chan * rows

    info, own, send_even, send_odd = call(
        pack_body(rows, cols, o, chan),
        [((4,), jnp.int32), ((6, cols, 384), BF16), ((edge_rows, 384), BF16), ((edge_rows, 384), BF16)],
        1, 2, [], 2e10, 8, 1,
    )(info, reward_t, latents)
    packed_even = lax.ppermute(send_even, "tile", within)
    packed_odd = lax.ppermute(send_odd, "tile", across)

    width = 2 * cols // count
    tokens = size // 4
    acc, part_even, part_odd, mid_t, sel, fwd, own_mid, back_odd, back_even = call(
        cached_body(rows, cols, count, width, tokens, o),
        [
            ((rows + 4, cols, 384), F32), ((3 * cols, 384), BF16), ((3 * cols, 384), BF16), ((3456, 384), BF16),
            ((count // 2, 256, 4 * tokens), BF16), ((2, 768, 768), BF16), ((2, cols, 384), BF16),
            ((768, 768), BF16), ((768, 768), BF16),
        ],
        2, 4, [pltpu.VMEM((size, 2304), BF16), pltpu.VMEM((3, size, 384), F32)], 4e9, 14,
    )(info, shard_order, cached_features, mid, up_t, reward_t)
    got_even = lax.ppermute(part_even, "tile", within)
    got_odd = lax.ppermute(part_odd, "tile", across)

    hidden, conv = call(
        current_body(rows, cols, chan),
        [((rows + 6, cols, 384), BF16), ((rows + 4, cols, 384), F32)],
        1, 6,
        [
            pltpu.VMEM((9 * rows * chan, 256), F32),
            pltpu.VMEM((3 * rows, 9 * chan, 256), BF16),
            pltpu.VMEM((rows + 6, cols, 1152), BF16),
            pltpu.VMEM((27 * chan, 384), BF16),
            pltpu.VMEM((2, cols, 384), F32),
        ],
        5e9, 14,
    )(info, latents, packed_even, packed_odd, w_in, mid, gain)

    (payload,) = call(
        back_body(rows, cols, chan, count, o),
        [((count, chan, 128), BF16)],
        1, 16,
        [
            pltpu.VMEM((2 * rows + 6, cols, 384), BF16),
            pltpu.VMEM((rows + 4, cols, 768), F32),
            pltpu.VMEM((rows + 4, cols, 768), F32),
            pltpu.VMEM((rows + 3, cols, 768), BF16),
            pltpu.VMEM((rows + 3, cols, 768), BF16),
            pltpu.VMEM((rows + 4, cols, 1152), BF16),
            pltpu.VMEM((rows + 3, cols, 768), F32),
            pltpu.VMEM((rows + 3, cols, 768), F32),
            pltpu.VMEM((rows + 2, cols, 1152), BF16),
            pltpu.VMEM((rows, cols, 384), F32),
            pltpu.VMEM((rows, cols, 384), BF16),
            pltpu.VMEM((2, cols, 384), F32),
            pltpu.VMEM((2, cols, 384), F32),
            pltpu.VMEM((3 * chan, size), F32),
        ],
        8e9, 34,
    )(
        info, hidden, conv, acc, got_even, got_odd, packed_even, packed_odd, own, own_mid, fwd, back_odd, back_even, mid_t,
        w_in[2].reshape(9 * chan, mid_chan), gain, gain_out,
    )
    received = lax.all_to_all(payload, "tile", split_axis=0, concat_axis=0, tiled=True)
    (placed,) = call(place_body(count, chan, tokens), [((4 * chan, tokens), F32)], 0, 2, [], 1e7, 8)(sel, received)
    return placed.T


def solution(mesh):
    return jax.shard_map(
        shards,
        mesh=mesh,
        in_specs=(
            P(("prompt", "tile"), None, None),
            P(None, ("prompt", "tile"), None, None),
            P(None, ("prompt", "tile"), None, None),
            P(("prompt", "tile"), None, None),
            P(),
            P(),
            P(),
            P(),
            P(),
            P("prompt"),
        ),
        out_specs=P(("prompt", "tile"), None),
        check_vma=False,
    )
```

```python
import jax
import jax.numpy as jnp
from jax import lax
from jax.experimental import pallas as pl
from jax.experimental.pallas import tpu as pltpu
from jax.sharding import PartitionSpec as P

EPS = 1e-06
F32 = jnp.float32
BF16 = jnp.bfloat16
VM = pl.BlockSpec(memory_space=pltpu.VMEM)
SM = pl.BlockSpec(memory_space=pltpu.SMEM)


def weave(*groups):
    total = max(len(g) for g in groups)
    done = [0] * len(groups)
    for k in range(total):
        for n, g in enumerate(groups):
            while done[n] * total < (k + 1) * len(g):
                g[done[n]]()
                done[n] += 1


def joined(refs, lanes=slice(None)):
    return jnp.concatenate([ref[:, lanes] for ref in refs], axis=0)


def shared(refs, lanes, value):
    size = refs[0].shape[0]
    for k, ref in enumerate(refs):
        ref[:, lanes] = value[k * size : (k + 1) * size]


def steps(f, *keys):
    return [lambda key=key: f(*key) for key in keys]


def call(body, outs, n_smem, n_vmem, scratch, flops, limit, smem_outs=0):
    specs = [SM] * n_smem + [VM] * n_vmem
    return pl.pallas_call(
        body,
        out_shape=[jax.ShapeDtypeStruct(s, d) for s, d in outs],
        in_specs=specs,
        out_specs=[SM] * smem_outs + [VM] * (len(outs) - smem_outs),
        scratch_shapes=scratch,
        cost_estimate=pl.CostEstimate(flops=int(flops), bytes_accessed=2**20, transcendentals=0),
        compiler_params=pltpu.CompilerParams(vmem_limit_bytes=limit << 20),
    )


def mm(a, b):
    return jnp.dot(a, b, preferred_element_type=F32)


def mm_t(a, b):
    return lax.dot_general(a, b, (((1,), (1,)), ((), ())), preferred_element_type=F32)


def flag(info, k):
    return info[k].astype(F32)


def from_left(x):
    moved = pltpu.roll(x, 1, 0)
    first = lax.broadcasted_iota(jnp.int32, (8, x.shape[1]), 0) == 0
    return jnp.concatenate([jnp.where(first, 0.0, moved[:8]), moved[8:]], axis=0)


def from_right(x):
    size = x.shape[0]
    moved = pltpu.roll(x, size - 1, 0)
    last = lax.broadcasted_iota(jnp.int32, (8, x.shape[1]), 0) == 7
    return jnp.concatenate([moved[: size - 8], jnp.where(last, 0.0, moved[size - 8 :])], axis=0)


def beside(target, base, lanes, x, ahead):
    sides = (from_right, from_left) if ahead else (from_left, from_right)
    for group, value in enumerate((sides[0](x), x, sides[1](x))):
        at = base + group * 384 + lanes
        target[:, at : at + 128] = value.astype(BF16)


CHUNK = 32


def picker(cols, o):
    half = o - 128
    x_index = lax.broadcasted_iota(jnp.int32, (cols, 2 * cols), 1)
    w_index = lax.broadcasted_iota(jnp.int32, (cols, 2 * cols), 0)
    pick = [(x_index == 2 * w_index + b).astype(F32).astype(BF16) for b in (0, 1)]
    zeros = jnp.zeros((128 - half, 2 * cols), BF16)

    def one(reward, f, own, k):
        r = reward[f]
        first, rest = r[:128], r[128:]
        low = jnp.concatenate([first, rest, zeros], axis=0)
        high = jnp.concatenate([first, zeros, rest], axis=0)
        sides = (low, high) if f % 2 else (high, low)
        d0, d1 = mm_t(pick[0], sides[0]), mm_t(pick[1], sides[1])
        own[k, :, 0:128] = d0[:, :128].astype(BF16)
        own[k, :, 128:256] = d1[:, :128].astype(BF16)
        own[k, :, 256:384] = (d0[:, 128:] + d1[:, 128:]).astype(BF16)

    return one


def pack_body(rows, cols, o, chan):
    def body(info, reward, latent, cached, own, send_even, send_odd):
        one = picker(cols, o)
        for k in range(6):
            one(reward, k if k < 3 else 2 * rows - 6 + k, own, k)
        base = 3 * cols
        per = chan * rows
        for send, last in ((send_even, 1 - info[0]), (send_odd, info[0])):
            begin = last * 3
            for k in range(3):
                send[k * cols : (k + 1) * cols] = own[begin + k]
            for t in range(3):
                src = cached[t] if t < 2 else latent[...]
                lat = src.reshape(per, cols)
                send[base : base + per, t * 128 : t * 128 + 128] = lat[:, :128]
                send[base + per : base + 2 * per, t * 128 : t * 128 + cols - 128] = lat[:, 128:]

    return body


def home(targets, q, p, tile):
    block, second = ((1, 1), (0, 0), (0, 1), (1, 0))[p]
    target, side = targets[q]
    if tile < 2:
        row = block * 384 + second * 128 + tile * 64
    else:
        row = block * 384 + 256 + 64 * (second if q % 2 == 0 else 1 - second)
    return target, row, side * 384


def turning(back_odd, back_even, fwd):
    targets = ((back_odd, 1), (back_even, 0), (back_odd, 0), (back_even, 1))

    def tap_tile(q, p, tile, lanes):
        target, row, side = home(targets, q, p, tile)
        return target[row : row + 64, side + lanes : side + lanes + 128]

    def one(b, side, lanes):
        p = ((3, 1), (2, 0))[b][side]
        at = slice(side * 384 + lanes, side * 384 + lanes + 128)
        for q in range(4):
            both = jnp.concatenate([tap_tile(q, p, 0, lanes), tap_tile(q, p, 1, lanes)], axis=0)
            fwd[b, at, q * 128 : q * 128 + 128] = both.T
        for half in range(2):
            pair = (2 * half, 2 * half + 1) if b == 0 else (2 * half + 1, 2 * half)
            both = jnp.concatenate([tap_tile(q, p, 2, lanes) for q in pair], axis=0)
            fwd[b, at, 512 + half * 128 : 640 + half * 128] = both.T

    return steps(one, *[(b, side, lanes) for b in range(2) for side in range(2) for lanes in range(0, 384, 128)])


def taps_body(info, up, info_out, back_odd, back_even):
    for k in range(4):
        info_out[k] = info[k]

    parts = ((2,), (1, 2), (0, 1), (0,))
    targets = ((back_odd, 1), (back_even, 0), (back_odd, 0), (back_even, 1))

    for tile in range(3):
        for lanes in range(0, 384, 128):
            w = [[up[i, j, tile * 64 : tile * 64 + 64, lanes : lanes + 128].astype(F32) for j in range(3)] for i in range(3)]
            for q in range(4):
                c = [w[parts[q][0]][j] + w[parts[q][1]][j] if len(parts[q]) > 1 else w[parts[q][0]][j] for j in range(3)]
                for p, tap in enumerate((c[2], c[1] + c[2], c[0] + c[1], c[0])):
                    target, row, side = home(targets, q, p, tile)
                    target[row : row + 64, side + lanes : side + lanes + 128] = tap.astype(BF16)


def cached_body(rows, cols, count, width, tokens, o):
    size = rows * cols

    def body(
        info, order, features, mid, back_odd, back_even, reward, acc, send_even, send_odd, mid_t, sel, fwd, own, wide, parts
    ):
        for t in range(2):
            for r in range(rows):
                for lanes in range(0, 384, 128):
                    x = features[t, r, :, lanes : lanes + 128].astype(F32)
                    beside(wide.at[r * cols : (r + 1) * cols], t * 1152, lanes, x, False)
        def product(i, lanes):
            parts[i, :, lanes] = mm(wide[...], jnp.concatenate([mid[0, i, :, lanes], mid[1, i, :, lanes]], axis=0))

        def double():
            left = jnp.concatenate([mid[0, 0, :, 256:384], mid[1, 0, :, 256:384]], axis=0)
            right = jnp.concatenate([mid[0, 1, :, 256:384], mid[1, 1, :, 256:384]], axis=0)
            both = mm(wide[...], jnp.concatenate([left, right], axis=1))
            parts[0, :, 256:384] = both[:, :128]
            parts[1, :, 256:384] = both[:, 128:]

        def turn(i, j):
            at = (i * 3 + j) * 384
            mid_t[at : at + 384] = mid[2, i, j * 384 : (j + 1) * 384].T

        most, rest = slice(0, 256), slice(256, 384)
        products = steps(product, (0, most), (1, most)) + steps(double, ()) + steps(product, (2, most), (2, rest))
        one = picker(cols, o)
        others = steps(turn, *[(i, j) for i in range(3) for j in range(3)])
        others += turning(back_odd, back_even, fwd)
        others += steps(placing(info, order, sel, count, width, tokens), *[(t,) for t in range(count)])
        others += steps(one, (reward, rows - 1, own, 0), (reward, rows, own, 1))
        weave(others, products)
        for k in range(rows + 4):
            total = jnp.zeros((cols, 384), F32)
            for i in range(3):
                r = k - 3 + i
                if 0 <= r < rows:
                    total = total + parts[i, r * cols : (r + 1) * cols]
            acc[k] = total
        for send, last in ((send_even, 1 - info[0]), (send_odd, info[0])):
            for k in range(3):
                send[k * cols : (k + 1) * cols] = acc[1 + last * 3 + k].astype(BF16)

    return body


def current_body(rows, cols, chan):
    per = chan * rows
    base = 3 * cols

    def body(info, latent, cached, got_even, got_odd, w_in, mid, half_gain, hidden, conv, lat, tall, w_order, *buffers):
        even = info[0] == 0
        wide, plain = buffers[: rows + 6], buffers[rows + 6 :]
        lat[...] = jnp.zeros_like(lat)

        def fill(first_row, got, ok):
            scale = ok.astype(F32)
            for t in range(3):
                x = got[base : base + per, t * 128 : t * 128 + 128].astype(F32) * scale
                y = got[base + per : base + 2 * per, t * 128 : t * 128 + cols - 128].astype(F32) * scale
                for r in range(rows):
                    at = pl.ds((first_row + r) * 3 * chan + t * chan, chan)
                    lat[at, 0:128] = x[r * chan : (r + 1) * chan]
                    lat[at, 128:cols] = y[r * chan : (r + 1) * chan]

        @pl.when(even)
        def _():
            fill(0, got_odd, info[1])
            fill(2 * rows, got_even, info[2])

        @pl.when(jnp.logical_not(even))
        def _():
            fill(0, got_even, info[1])
            fill(2 * rows, got_odd, info[2])

        for t in range(3):
            for r in range(rows):
                at = pl.ds((rows + r) * 3 * chan + t * chan, chan)
                lat[at, 0:cols] = (cached[t, r] if t < 2 else latent[r]).astype(F32)

        for r in range(3 * rows):
            for t in range(3):
                x = lat[pl.ds((r * 3 + t) * chan, chan), :]
                at = t * 3 * chan
                tall[r, at : at + chan] = pltpu.roll(x, 1, 1).astype(BF16)
                tall[r, at + chan : at + 2 * chan] = x.astype(BF16)
                tall[r, at + 2 * chan : at + 3 * chan] = pltpu.roll(x, 255, 1).astype(BF16)
        for i in range(3):
            for t in range(3):
                at = (i * 3 + t) * 3 * chan
                w_order[at : at + 3 * chan] = w_in[t, i]

        def hidden_product(k):
            lhs = tall[k : k + 3].reshape(27 * chan, 256)[:, 0:cols]
            h = lax.dot_general(lhs, w_order[...], (((0,), (0,)), ((), ())), preferred_element_type=F32)
            plain[k][...] = h

        def hidden_norm(k):
            for c in range(0, cols, CHUNK):
                at = slice(c, c + CHUNK)
                v = plain[k][at].astype(BF16)
                hidden[k, at] = v
                v = v.astype(F32)
                inv = lax.rsqrt(jnp.mean(v * v, axis=1, keepdims=True) + EPS)
                half = v * inv * half_gain[...]
                act = half * (jnp.tanh(half) + 1.0)
                if k < 3:
                    act = act * flag(info, 1)
                if k >= rows + 3:
                    act = act * flag(info, 2)
                plain[k][at] = act
            for lanes in range(0, 384, 128):
                beside(wide[k], 0, lanes, plain[k][:, lanes : lanes + 128], False)

        def conv_rows(p, number):
            lhs = [joined(wide[p + i : p + i + number]) for i in range(3)]
            total = mm(jnp.concatenate(lhs, axis=1), mid[2, :, :, 0:256].reshape(3456, 256))
            conv[p : p + number, :, 0:256] = total.reshape(number, cols, 256)

        full = rows + 6
        early = rows + 1
        for k in range(full):
            hidden_product(k)
            if 2 <= k < early + 2:
                hidden_norm(k - 2)
        weave(steps(conv_rows, (0, rows - 1)), steps(hidden_norm, *[(k,) for k in range(early, full)]))
        conv_rows(rows - 1, 5)
        both = mm(joined(wide[0 : rows + 5]), jnp.concatenate([mid[2, 0, :, 256:384], mid[2, 1, :, 256:384]], axis=1))
        rest = mm(joined(wide[2 : rows + 6]), mid[2, 2, :, 256:384])
        for p in range(rows + 4):
            at, after = slice(p * cols, (p + 1) * cols), slice((p + 1) * cols, (p + 2) * cols)
            conv[p, :, 256:384] = both[at, :128] + both[after, 128:] + rest[at]

    return body


def pulled(s, half_gain, grad):
    h = s * half_gain
    t = jnp.tanh(h)
    return (grad * half_gain) * ((1.0 + t) * (1.0 + h * (1.0 - t)))


def back_body(rows, cols, chan, count, o):
    size = rows * cols
    width = 2 * cols // count

    def body(
        info, hidden, conv, acc, got_even, got_odd, packed_even, packed_odd, own, own_mid, fwd, back_odd, back_even, mid_t, w_in, half_gain,
        half_out, payload, reward, lines, *buffers
    ):
        fine = rows + 3
        buffers = list(buffers)

        def part(count):
            taken = buffers[:count]
            del buffers[:count]
            return taken

        p0, p1, wide = part(rows + 4), part(rows + 4), part(rows + 4)
        g_odd, g_even, t_odd, t_even = part(fine), part(fine), part(fine), part(fine)
        tmp_odd, tmp_even, back = part(fine), part(fine), part(rows + 2)
        act_grad, hid = part(rows), part(rows)
        top, bottom = flag(info, 1), flag(info, 2)
        odd_tile = flag(info, 0)
        above = (top * odd_tile, top * (1.0 - odd_tile))
        below = (bottom * (1.0 - odd_tile), bottom * odd_tile)

        def halo(of_even, of_odd, k, lanes, before):
            scale = above if before else below
            at = slice(k * cols, (k + 1) * cols)
            return of_even[at, lanes].astype(F32) * scale[0] + of_odd[at, lanes].astype(F32) * scale[1]

        for k in range(3):
            for lanes in (slice(0, 128), slice(128, 256), slice(256, 384)):
                reward[k, :, lanes] = halo(packed_even, packed_odd, k, lanes, True).astype(BF16)
                reward[2 * rows + 3 + k, :, lanes] = halo(packed_even, packed_odd, k, lanes, False).astype(BF16)
        reward[3:6] = own[0:3]
        reward[6 : 2 * rows] = own_mid[...]
        reward[2 * rows : 2 * rows + 3] = own[3:6]

        def inside(x, k, first, last):
            return x * top if k < first else x * bottom if k >= last else x

        def state_row(k):
            for lanes in range(0, 384, 128):
                at = slice(lanes, lanes + 128)
                x = hidden[k + 1, :, at].astype(F32) + conv[k, :, at]
                if 1 <= k <= rows + 2:
                    x = x + acc[k, :, at]
                if k < 3:
                    x = x + halo(got_even, got_odd, k, at, True)
                if k > rows:
                    x = x + halo(got_even, got_odd, k - rows - 1, at, False)
                beside(wide[k], 0, lanes, inside(x, k, 2, rows + 2), False)

        def up_rows(first, last, b, n):
            lanes = slice(n * 256, n * 256 + 256)
            x = joined(wide[first:last], slice(b * 384, b * 384 + 768))
            shared((p0, p1)[b][first:last], lanes, mm(x, fwd[b, :, lanes]))

        def down_rows(first, last, odd, n):
            g, kernel, t = (g_odd, back_odd, t_odd) if odd else (g_even, back_even, t_even)
            lanes = slice(n * 256, n * 256 + 256)
            shared(t[first:last], lanes, mm(joined(g[first:last]), kernel[:, lanes]))

        low = lax.broadcasted_iota(jnp.int32, (CHUNK, 128), 1) < 64
        tall_low = lax.broadcasted_iota(jnp.int32, (cols, 128), 1) < 64
        gains = [half_out[:, 0:128], half_out[:, 128:256]]

        def pull(v0, v1, vm, r, zero_low):
            mine = low if zero_low else jnp.logical_not(low)
            def both(a0, a1, am):
                s0 = jnp.sum(a0 + jnp.where(mine, am, 0.0), axis=1, keepdims=True)
                s1 = jnp.sum(a1 + jnp.where(mine, 0.0, am), axis=1, keepdims=True)
                return s0 * (1.0 / o), s1 * (1.0 / o)

            q0, q1 = both(v0 * v0, v1 * v1, vm * vm)
            i0, i1 = lax.rsqrt(q0 + EPS), lax.rsqrt(q1 + EPS)
            im = jnp.where(mine, i0, i1)
            out = []
            for v, i, g, k in ((v0, i0, gains[0], 0), (v1, i1, gains[0], 1), (vm, im, gains[1], 2)):
                s = v * i
                out.append((s, pulled(s, g, r[:, k * 128 : k * 128 + 128].astype(F32))))
            m0, m1 = both(*(s * d for s, d in out))
            mx = jnp.where(mine, m0, m1)
            return [i * (d - s * m) for (s, d), i, m in zip(out, (i0, i1, im), (m0, m1, mx))]

        def pull_row(k, odd):
            target, tmp = (g_odd, tmp_odd) if odd else (g_even, tmp_even)
            for c in range(0, cols, CHUNK):
                at = slice(c, c + CHUNK)
                if odd:
                    v0 = p0[k][at, 256:384] + p0[k + 1][at, 0:128]
                    v1 = p1[k][at, 256:384] + p1[k + 1][at, 0:128]
                    m0 = p0[k][at, 640:768] + p0[k + 1][at, 512:640]
                    m1 = p1[k][at, 640:768] + p1[k + 1][at, 512:640]
                else:
                    v0 = p0[k + 1][at, 128:256] + p0[k][at, 384:512]
                    v1 = p1[k + 1][at, 128:256] + p1[k][at, 384:512]
                    m0 = p1[k + 1][at, 512:640] + p1[k][at, 640:768]
                    m1 = p0[k + 1][at, 512:640] + p0[k][at, 640:768]
                out = pull(v0, v1, jnp.where(low, m0, m1), reward[2 * k + (0 if odd else 1), at], odd)
                for n, value in enumerate(out):
                    lanes = slice(n * 128, n * 128 + 128)
                    target[k][at, lanes] = value.astype(BF16)
                    tmp[k][at, lanes] = value
            target[k][:, 384:512] = from_right(tmp[k][:, 0:128]).astype(BF16)
            target[k][:, 512:640] = from_left(tmp[k][:, 128:256]).astype(BF16)
            x = tmp[k][:, 256:384]
            sides = (from_right(x), from_left(x)) if odd else (from_left(x), from_right(x))
            target[k][:, 640:768] = jnp.where(tall_low, *sides).astype(BF16)

        def block_row(k):
            for lanes in range(0, 384, 128):
                at, far = slice(lanes, lanes + 128), slice(lanes + 384, lanes + 512)
                x = t_odd[k + 1][:, at] + t_odd[k][:, far] + t_even[k][:, at] + t_even[k + 1][:, far]
                beside(back[k], 0, lanes, inside(x, k, 1, rows + 1), True)

        def hidden_pull(k):
            for c in range(0, cols, CHUNK):
                at = slice(c, c + CHUNK)
                v = hidden[k + 3, at].astype(F32)
                inv = lax.rsqrt(jnp.mean(v * v, axis=1, keepdims=True) + EPS)
                s = v * inv
                d = pulled(s, half_gain[...], act_grad[k][at])
                dv = inv * (d - s * jnp.mean(d * s, axis=1, keepdims=True))
                hid[k][at] = (back[k + 1][at, 384:768].astype(F32) + dv).astype(BF16)

        def mid_rows(p, number):
            lhs = [joined(back[p + 2 - i : p + 2 - i + number]) for i in range(3)]
            shared(act_grad[p : p + number], slice(0, 256), mm(jnp.concatenate(lhs, axis=1), mid_t[:, 0:256]))

        def mid_rest(p, number):
            pair = jnp.concatenate([mid_t[1152:2304, 256:384], mid_t[0:1152, 256:384]], axis=1)
            both = mm(joined(back[p + 1 : p + number + 2]), pair)
            rest = mm(joined(back[p : p + number]), mid_t[2304:3456, 256:384])
            for k in range(number):
                at, after = slice(k * cols, (k + 1) * cols), slice((k + 1) * cols, (k + 2) * cols)
                act_grad[p + k][:, 256:384] = both[at, :128] + both[after, 128:] + rest[at]

        def each(f, first, last):
            return steps(f, *[(k,) for k in range(first, last)])

        def ups(first, last):
            full = rows + 4
            return steps(
                up_rows,
                *[
                    key
                    for b in range(2)
                    for key in (
                        (max(first, 1), last, b, 0), (first, min(last, full - 1), b, 1), (first, last, b, 2),
                    )
                ],
            )

        def downs(first, last):
            keys = []
            for odd in (True, False):
                skip_first, skip_last = max(first, 1), min(last, fine - 1)
                keys.append((skip_first, last, odd, 0) if odd else (first, skip_last, odd, 0))
                keys.append((first, last, odd, 1))
                keys.append((first, skip_last, odd, 2) if odd else (skip_first, last, odd, 2))
            return steps(down_rows, *keys)

        def pulls(first, last):
            return steps(pull_row, *[(k, odd) for k in range(first, last) for odd in (True, False)])

        weave(each(state_row, 0, rows))
        weave(each(state_row, rows, rows + 4), ups(0, rows))
        weave(pulls(0, rows - 1), ups(rows, rows + 4))
        weave(pulls(rows - 1, fine), downs(0, rows - 1))
        weave(each(block_row, 0, rows - 2), downs(rows - 1, fine))
        weave(each(block_row, rows - 2, rows + 2))
        mid_rest(0, rows)
        mid_rows(0, 2)
        weave(steps(mid_rows, (2, rows - 2)), each(hidden_pull, 0, 2))
        for k in range(2, rows):
            hidden_pull(k)

        z = mm_t(w_in[...], joined(hid))
        place = lax.broadcasted_iota(jnp.int32, (chan, size), 1)
        col = lax.rem(place, cols)
        sums = []
        for i in range(3):
            z0, z1, z2 = (z[(i * 3 + j) * chan : (i * 3 + j + 1) * chan] for j in range(3))
            left = jnp.where(col == cols - 1, 0.0, pltpu.roll(z0, size - 1, 1))
            right = jnp.where(col == 0, 0.0, pltpu.roll(z2, 1, 1))
            sums.append(left + z1 + right)
        inner = sums[1]
        inner = inner + jnp.where(place < size - cols, pltpu.roll(sums[0], size - cols, 1), 0.0)
        inner = inner + jnp.where(place >= cols, pltpu.roll(sums[2], cols, 1), 0.0)
        lines[0:chan] = inner
        lines[chan : 2 * chan] = sums[0]
        lines[2 * chan : 3 * chan] = sums[2]
        per_row = count // 2
        for u in range(count):
            pair, piece = u // per_row, u % per_row
            parts = []
            for a in range(2):
                at = (2 * pair + a) * cols + piece * width
                parts.append(lines[0:chan, at : at + width])
            at = piece * width + (0 if pair else (rows - 1) * cols)
            first = chan if pair else 2 * chan
            parts.append(lines[first : first + chan, at : at + width])
            parts.append(jnp.zeros((chan, 128 - 3 * width), F32))
            payload[u] = jnp.concatenate(parts, axis=1).astype(BF16)

    return body


def placing(info, order, sel, count, width, tokens):
    piece = width // 2
    pair = info[3]
    lane = lax.broadcasted_iota(jnp.int32, (128, 4 * tokens), 0)
    column = lax.broadcasted_iota(jnp.int32, (128, 4 * tokens), 1)
    group = (lane >= width).astype(jnp.int32) + (lane >= 2 * width).astype(jnp.int32)
    w = lane - group * width
    part = jnp.where(group == 2, pair, group)
    fixed = (2 * part + (w & 1)) * tokens + (w >> 1) - column
    fixed = jnp.where(lane < 3 * width, fixed, -99999)

    def one(t):
        step = t + 1 - 2 * pair
        valid = jnp.logical_and(step >= 0, step < count)
        beside = jnp.where(valid, piece * order[jnp.clip(step, 0, count - 1)], -9999)
        begin = jnp.where(group == 2, beside, piece * order[t])
        sel[t] = (fixed + begin == 0).astype(F32).astype(BF16)

    return one


def place_body(count, chan, tokens):
    def body(sel, got, out):
        total = mm(got[0], sel[0])
        for t in range(1, count):
            total += mm(got[t], sel[t])
        for k in range(4):
            out[k * chan : (k + 1) * chan] = total[:, k * tokens : (k + 1) * tokens]

    return body


def swaps(count):
    within = [(i, i ^ 1) for i in range(count)]
    across = [(0, 0), (count - 1, count - 1)]
    for i in range(1, count - 1, 2):
        across += [(i, i + 1), (i + 1, i)]
    return within, sorted(across)


def shards(
    latent, cached_latent, cached_features, reward_grad, conv_in_weight, conv_mid_weight, conv_up_weight, norm_gain, out_gain, shard_order
):
    count = lax.axis_size("tile")
    rows, cols, chan = latent.shape
    mid_chan = norm_gain.shape[0]
    o = out_gain.shape[0]
    tile = lax.axis_index("tile")
    info = jnp.stack(
        [tile % 2, (tile > 0).astype(jnp.int32), (tile < count - 1).astype(jnp.int32), (tile >= count // 2).astype(jnp.int32)]
    ).astype(jnp.int32)
    lat = jnp.transpose(latent, (0, 2, 1))
    lat_cached = jnp.transpose(cached_latent, (0, 1, 3, 2))
    reward_t = jnp.transpose(reward_grad, (0, 2, 1))
    up_t = jnp.transpose(conv_up_weight, (0, 1, 3, 2))
    mid = conv_mid_weight.reshape(3, 3, 3 * mid_chan, mid_chan)
    w_in = conv_in_weight.reshape(3, 3, 3 * chan, mid_chan)
    gain = 0.5 * norm_gain.reshape(1, mid_chan)
    gain_out = 0.5 * jnp.concatenate([out_gain, out_gain[128:]]).reshape(1, 256)
    within, across = swaps(count)
    size = rows * cols
    edge_rows = 3 * cols + 2 * chan * rows

    info, back_odd, back_even = call(
        taps_body,
        [((4,), jnp.int32), ((768, 768), BF16), ((768, 768), BF16)],
        1, 1, [], 1e10, 8, 1,
    )(info, up_t)

    own, send_even, send_odd = call(
        pack_body(rows, cols, o, chan),
        [((6, cols, 384), BF16), ((edge_rows, 384), BF16), ((edge_rows, 384), BF16)],
        1, 3, [], 1e10, 8,
    )(info, reward_t, lat, lat_cached)
    packed_even = lax.ppermute(send_even, "tile", within)
    packed_odd = lax.ppermute(send_odd, "tile", across)

    width = 2 * cols // count
    tokens = size // 4
    acc, part_even, part_odd, mid_t, sel, fwd, own_mid = call(
        cached_body(rows, cols, count, width, tokens, o),
        [
            ((rows + 4, cols, 384), F32), ((3 * cols, 384), BF16), ((3 * cols, 384), BF16), ((3456, 384), BF16),
            ((count, 128, 4 * tokens), BF16), ((2, 768, 768), BF16), ((2, cols, 384), BF16),
        ],
        2, 5, [pltpu.VMEM((size, 2304), BF16), pltpu.VMEM((3, size, 384), F32)], 4e9, 14,
    )(info, shard_order, cached_features, mid, back_odd, back_even, reward_t)
    got_even = lax.ppermute(part_even, "tile", within)
    got_odd = lax.ppermute(part_odd, "tile", across)

    hidden, conv = call(
        current_body(rows, cols, chan),
        [((rows + 6, cols, 384), BF16), ((rows + 4, cols, 384), F32)],
        1, 7,
        [
            pltpu.VMEM((9 * rows * chan, 256), F32),
            pltpu.VMEM((3 * rows, 9 * chan, 256), BF16),
            pltpu.VMEM((27 * chan, 384), BF16),
        ]
        + [pltpu.VMEM((cols, 1152), BF16)] * (rows + 6)
        + [pltpu.VMEM((cols, 384), F32)] * (rows + 6),
        5e9, 14,
    )(info, lat, lat_cached, packed_even, packed_odd, w_in, mid, gain)

    (payload,) = call(
        back_body(rows, cols, chan, count, o),
        [((count, chan, 128), BF16)],
        1, 16,
        [
            pltpu.VMEM((2 * rows + 6, cols, 384), BF16),
            pltpu.VMEM((3 * chan, size), F32),
        ]
        + [pltpu.VMEM((cols, 768), F32)] * (2 * (rows + 4))
        + [pltpu.VMEM((cols, 1152), BF16)] * (rows + 4)
        + [pltpu.VMEM((cols, 768), BF16)] * (2 * (rows + 3))
        + [pltpu.VMEM((cols, 768), F32)] * (2 * (rows + 3))
        + [pltpu.VMEM((cols, 384), F32)] * (2 * (rows + 3))
        + [pltpu.VMEM((cols, 1152), BF16)] * (rows + 2)
        + [pltpu.VMEM((cols, 384), F32)] * rows
        + [pltpu.VMEM((cols, 384), BF16)] * rows,
        8e9, 36,
    )(
        info, hidden, conv, acc, got_even, got_odd, packed_even, packed_odd, own, own_mid, fwd, back_odd, back_even, mid_t,
        w_in[2].reshape(9 * chan, mid_chan), gain, gain_out,
    )
    received = lax.all_to_all(payload, "tile", split_axis=0, concat_axis=0, tiled=True)
    (placed,) = call(place_body(count, chan, tokens), [((4 * chan, tokens), F32)], 0, 2, [], 1e7, 8)(sel, received)
    return placed.T


def solution(mesh):
    return jax.shard_map(
        shards,
        mesh=mesh,
        in_specs=(
            P(("prompt", "tile"), None, None),
            P(None, ("prompt", "tile"), None, None),
            P(None, ("prompt", "tile"), None, None),
            P(("prompt", "tile"), None, None),
            P(),
            P(),
            P(),
            P(),
            P(),
            P("prompt"),
        ),
        out_specs=P(("prompt", "tile"), None),
        check_vma=False,
    )
```

```python
import jax
import jax.numpy as jnp
from jax import lax
from jax.experimental import pallas as pl
from jax.experimental.pallas import tpu as pltpu
from jax.sharding import PartitionSpec as P

EPS = 1e-06
F32 = jnp.float32
BF16 = jnp.bfloat16
VM = pl.BlockSpec(memory_space=pltpu.VMEM)
SM = pl.BlockSpec(memory_space=pltpu.SMEM)


def weave(*groups):
    total = max(len(g) for g in groups)
    done = [0] * len(groups)
    for k in range(total):
        for n, g in enumerate(groups):
            while done[n] * total < (k + 1) * len(g):
                g[done[n]]()
                done[n] += 1


def steps(f, *keys):
    return [lambda key=key: f(*key) for key in keys]


def call(body, outs, n_smem, n_vmem, scratch, flops, limit, smem_outs=0):
    specs = [SM] * n_smem + [VM] * n_vmem
    return pl.pallas_call(
        body,
        out_shape=[jax.ShapeDtypeStruct(s, d) for s, d in outs],
        in_specs=specs,
        out_specs=[SM] * smem_outs + [VM] * (len(outs) - smem_outs),
        scratch_shapes=scratch,
        cost_estimate=pl.CostEstimate(flops=int(flops), bytes_accessed=2**20, transcendentals=0),
        compiler_params=pltpu.CompilerParams(vmem_limit_bytes=limit << 20),
    )


def mm(a, b):
    return jnp.dot(a, b, preferred_element_type=F32)


def mm_t(a, b):
    return lax.dot_general(a, b, (((1,), (1,)), ((), ())), preferred_element_type=F32)


def flag(info, k):
    return info[k].astype(F32)


def from_left(x):
    moved = pltpu.roll(x, 1, 0)
    first = lax.broadcasted_iota(jnp.int32, (8, x.shape[1]), 0) == 0
    return jnp.concatenate([jnp.where(first, 0.0, moved[:8]), moved[8:]], axis=0)


def from_right(x):
    size = x.shape[0]
    moved = pltpu.roll(x, size - 1, 0)
    last = lax.broadcasted_iota(jnp.int32, (8, x.shape[1]), 0) == 7
    return jnp.concatenate([moved[: size - 8], jnp.where(last, 0.0, moved[size - 8 :])], axis=0)


def beside(target, base, lanes, x, ahead):
    sides = (from_right, from_left) if ahead else (from_left, from_right)
    for group, value in enumerate((sides[0](x), x, sides[1](x))):
        at = base + group * 384 + lanes
        target[:, at : at + 128] = value.astype(BF16)


CHUNK = 32


def picker(cols, o):
    half = o - 128
    x_index = lax.broadcasted_iota(jnp.int32, (cols, 2 * cols), 1)
    w_index = lax.broadcasted_iota(jnp.int32, (cols, 2 * cols), 0)
    pick = [(x_index == 2 * w_index + b).astype(F32).astype(BF16) for b in (0, 1)]
    zeros = jnp.zeros((128 - half, 2 * cols), BF16)

    def one(reward, f, own, k):
        r = reward[f]
        first, rest = r[:128], r[128:]
        low = jnp.concatenate([first, rest, zeros], axis=0)
        high = jnp.concatenate([first, zeros, rest], axis=0)
        sides = (low, high) if f % 2 else (high, low)
        d0, d1 = mm_t(pick[0], sides[0]), mm_t(pick[1], sides[1])
        own[k, :, 0:128] = d0[:, :128].astype(BF16)
        own[k, :, 128:256] = d1[:, :128].astype(BF16)
        own[k, :, 256:384] = (d0[:, 128:] + d1[:, 128:]).astype(BF16)

    return one


def pack_body(rows, cols, o, chan):
    def body(info, reward, latent, cached, own, send_even, send_odd):
        one = picker(cols, o)
        for k in range(6):
            one(reward, k if k < 3 else 2 * rows - 6 + k, own, k)
        base = 3 * cols
        per = chan * rows
        for send, last in ((send_even, 1 - info[0]), (send_odd, info[0])):
            begin = last * 3
            for k in range(3):
                send[k * cols : (k + 1) * cols] = own[begin + k]
            for t in range(3):
                src = cached[t] if t < 2 else latent[...]
                lat = src.reshape(per, cols)
                send[base : base + per, t * 128 : t * 128 + 128] = lat[:, :128]
                send[base + per : base + 2 * per, t * 128 : t * 128 + cols - 128] = lat[:, 128:]

    return body


def home(targets, q, p, tile):
    block, second = ((1, 1), (0, 0), (0, 1), (1, 0))[p]
    target, side = targets[q]
    if tile < 2:
        row = block * 384 + second * 128 + tile * 64
    else:
        row = block * 384 + 256 + 64 * (second if q % 2 == 0 else 1 - second)
    return target, row, side * 384


def turning(back_odd, back_even, fwd):
    targets = ((back_odd, 1), (back_even, 0), (back_odd, 0), (back_even, 1))

    def tap_tile(q, p, tile, lanes):
        target, row, side = home(targets, q, p, tile)
        return target[row : row + 64, side + lanes : side + lanes + 128]

    def one(b, side, lanes):
        p = ((3, 1), (2, 0))[b][side]
        at = slice(side * 384 + lanes, side * 384 + lanes + 128)
        for q in range(4):
            both = jnp.concatenate([tap_tile(q, p, 0, lanes), tap_tile(q, p, 1, lanes)], axis=0)
            fwd[b, at, q * 128 : q * 128 + 128] = both.T
        for half in range(2):
            pair = (2 * half, 2 * half + 1) if b == 0 else (2 * half + 1, 2 * half)
            both = jnp.concatenate([tap_tile(q, p, 2, lanes) for q in pair], axis=0)
            fwd[b, at, 512 + half * 128 : 640 + half * 128] = both.T

    return steps(one, *[(b, side, lanes) for b in range(2) for side in range(2) for lanes in range(0, 384, 128)])


def taps_body(info, up, info_out, back_odd, back_even):
    for k in range(4):
        info_out[k] = info[k]

    parts = ((2,), (1, 2), (0, 1), (0,))
    targets = ((back_odd, 1), (back_even, 0), (back_odd, 0), (back_even, 1))

    for tile in range(3):
        for lanes in range(0, 384, 128):
            w = [[up[i, j, tile * 64 : tile * 64 + 64, lanes : lanes + 128].astype(F32) for j in range(3)] for i in range(3)]
            for q in range(4):
                c = [w[parts[q][0]][j] + w[parts[q][1]][j] if len(parts[q]) > 1 else w[parts[q][0]][j] for j in range(3)]
                for p, tap in enumerate((c[2], c[1] + c[2], c[0] + c[1], c[0])):
                    target, row, side = home(targets, q, p, tile)
                    target[row : row + 64, side + lanes : side + lanes + 128] = tap.astype(BF16)


def cached_body(rows, cols, count, width, tokens, o):
    size = rows * cols

    def body(
        info, order, features, mid, back_odd, back_even, reward, acc, send_even, send_odd, mid_t, sel, fwd, own, wide, parts
    ):
        for t in range(2):
            for r in range(rows):
                for lanes in range(0, 384, 128):
                    x = features[t, r, :, lanes : lanes + 128].astype(F32)
                    beside(wide.at[r * cols : (r + 1) * cols], t * 1152, lanes, x, False)
        def product(i, lanes):
            parts[i, :, lanes] = mm(wide[...], jnp.concatenate([mid[0, i, :, lanes], mid[1, i, :, lanes]], axis=0))

        def double():
            left = jnp.concatenate([mid[0, 0, :, 256:384], mid[1, 0, :, 256:384]], axis=0)
            right = jnp.concatenate([mid[0, 1, :, 256:384], mid[1, 1, :, 256:384]], axis=0)
            both = mm(wide[...], jnp.concatenate([left, right], axis=1))
            parts[0, :, 256:384] = both[:, :128]
            parts[1, :, 256:384] = both[:, 128:]

        def turn(i, j):
            at = (i * 3 + j) * 384
            mid_t[at : at + 384] = mid[2, i, j * 384 : (j + 1) * 384].T

        most, rest = slice(0, 256), slice(256, 384)
        products = steps(product, (0, most), (1, most)) + steps(double, ()) + steps(product, (2, most), (2, rest))
        one = picker(cols, o)
        others = steps(turn, *[(i, j) for i in range(3) for j in range(3)])
        others += turning(back_odd, back_even, fwd)
        others += steps(placing(info, order, sel, count, width, tokens), *[(t,) for t in range(count)])
        others += steps(one, (reward, rows - 1, own, 0), (reward, rows, own, 1))
        weave(others, products)
        for k in range(rows + 4):
            total = jnp.zeros((cols, 384), F32)
            for i in range(3):
                r = k - 3 + i
                if 0 <= r < rows:
                    total = total + parts[i, r * cols : (r + 1) * cols]
            acc[k] = total
        for send, last in ((send_even, 1 - info[0]), (send_odd, info[0])):
            for k in range(3):
                send[k * cols : (k + 1) * cols] = acc[1 + last * 3 + k].astype(BF16)

    return body


def current_body(rows, cols, chan):
    per = chan * rows
    base = 3 * cols

    def body(info, latent, cached, got_even, got_odd, w_in, mid, half_gain, hidden, conv, lat, tall, wide, w_order, plain):
        even = info[0] == 0
        lat[...] = jnp.zeros_like(lat)

        def fill(first_row, got, ok):
            scale = ok.astype(F32)
            for t in range(3):
                x = got[base : base + per, t * 128 : t * 128 + 128].astype(F32) * scale
                y = got[base + per : base + 2 * per, t * 128 : t * 128 + cols - 128].astype(F32) * scale
                for r in range(rows):
                    at = pl.ds((first_row + r) * 3 * chan + t * chan, chan)
                    lat[at, 0:128] = x[r * chan : (r + 1) * chan]
                    lat[at, 128:cols] = y[r * chan : (r + 1) * chan]

        @pl.when(even)
        def _():
            fill(0, got_odd, info[1])
            fill(2 * rows, got_even, info[2])

        @pl.when(jnp.logical_not(even))
        def _():
            fill(0, got_even, info[1])
            fill(2 * rows, got_odd, info[2])

        for t in range(3):
            for r in range(rows):
                at = pl.ds((rows + r) * 3 * chan + t * chan, chan)
                lat[at, 0:cols] = (cached[t, r] if t < 2 else latent[r]).astype(F32)

        for r in range(3 * rows):
            for t in range(3):
                x = lat[pl.ds((r * 3 + t) * chan, chan), :]
                at = t * 3 * chan
                tall[r, at : at + chan] = pltpu.roll(x, 1, 1).astype(BF16)
                tall[r, at + chan : at + 2 * chan] = x.astype(BF16)
                tall[r, at + 2 * chan : at + 3 * chan] = pltpu.roll(x, 255, 1).astype(BF16)
        for i in range(3):
            for t in range(3):
                at = (i * 3 + t) * 3 * chan
                w_order[at : at + 3 * chan] = w_in[t, i]

        def hidden_row(k):
            lhs = tall[k : k + 3].reshape(27 * chan, 256)[:, 0:cols]
            h = lax.dot_general(lhs, w_order[...], (((0,), (0,)), ((), ())), preferred_element_type=F32)
            plain[k % 2] = h
            for c in range(0, cols, CHUNK):
                at = slice(c, c + CHUNK)
                v = plain[k % 2, at].astype(BF16)
                hidden[k, at] = v
                v = v.astype(F32)
                inv = lax.rsqrt(jnp.mean(v * v, axis=1, keepdims=True) + EPS)
                half = v * inv * half_gain[...]
                act = half * (jnp.tanh(half) + 1.0)
                if k < 3:
                    act = act * flag(info, 1)
                if k >= rows + 3:
                    act = act * flag(info, 2)
                plain[k % 2, at] = act
            for lanes in range(0, 384, 128):
                beside(wide.at[k], 0, lanes, plain[k % 2, :, lanes : lanes + 128], False)

        def conv_rows(p, number):
            lhs = [wide[p + i : p + i + number].reshape(number * cols, 1152) for i in range(3)]
            total = mm(jnp.concatenate(lhs, axis=1), mid[2, :, :, 0:256].reshape(3456, 256))
            conv[p : p + number, :, 0:256] = total.reshape(number, cols, 256)

        for k in range(4):
            hidden_row(k)
        for p in range(0, rows + 4, 2):
            conv_rows(p, 2)
            for k in (p + 4, p + 5):
                if k < rows + 6:
                    hidden_row(k)
        both = mm(
            wide[0 : rows + 5].reshape((rows + 5) * cols, 1152),
            jnp.concatenate([mid[2, 0, :, 256:384], mid[2, 1, :, 256:384]], axis=1),
        )
        rest = mm(wide[2 : rows + 6].reshape((rows + 4) * cols, 1152), mid[2, 2, :, 256:384])
        for p in range(rows + 4):
            at, after = slice(p * cols, (p + 1) * cols), slice((p + 1) * cols, (p + 2) * cols)
            conv[p, :, 256:384] = both[at, :128] + both[after, 128:] + rest[at]

    return body


def pulled(s, half_gain, grad):
    h = s * half_gain
    t = jnp.tanh(h)
    return (grad * half_gain) * ((1.0 + t) * (1.0 + h * (1.0 - t)))


def back_body(rows, cols, chan, count, o):
    size = rows * cols
    width = 2 * cols // count

    def body(
        info, hidden, conv, acc, got_even, got_odd, packed_even, packed_odd, own, own_mid, fwd, back_odd, back_even, mid_t, w_in, half_gain,
        half_out, payload, reward, edge, p0, p1, g_odd, g_even, wide, t_odd, t_even, back, act_grad, hid, tmp_odd, tmp_even, lines,
    ):
        even = info[0] == 0
        top, bottom = flag(info, 1), flag(info, 2)

        def take(got, packed, before):
            ok = top if before else bottom
            place = 0 if before else rows + 1
            for k in range(3):
                at = slice(k * cols, (k + 1) * cols)
                edge[place + k] = got[at].astype(F32) * ok
                reward[k if before else 2 * rows + 3 + k] = (packed[at].astype(F32) * ok).astype(BF16)

        @pl.when(even)
        def _():
            take(got_odd, packed_odd, True)
            take(got_even, packed_even, False)

        @pl.when(jnp.logical_not(even))
        def _():
            take(got_even, packed_even, True)
            take(got_odd, packed_odd, False)

        reward[3:6] = own[0:3]
        reward[6 : 2 * rows] = own_mid[...]
        reward[2 * rows : 2 * rows + 3] = own[3:6]

        def inside(x, k, first, last):
            return x * top if k < first else x * bottom if k >= last else x

        def state_row(k):
            for lanes in range(0, 384, 128):
                at = slice(lanes, lanes + 128)
                x = hidden[k + 1, :, at].astype(F32) + conv[k, :, at]
                if 1 <= k <= rows + 2:
                    x = x + acc[k, :, at]
                if k < 3 or k > rows:
                    x = x + edge[k, :, at]
                beside(wide.at[k], 0, lanes, inside(x, k, 2, rows + 2), False)

        def up_rows(first, last, b, n):
            count = last - first
            x = wide[first:last, :, b * 384 : b * 384 + 768].reshape(count * cols, 768)
            lanes = slice(n * 256, n * 256 + 256)
            (p0, p1)[b][first:last, :, lanes] = mm(x, fwd[b, :, lanes]).reshape(count, cols, 256)

        def down_rows(first, last, odd, n):
            count = last - first
            g, kernel, t = (g_odd, back_odd, t_odd) if odd else (g_even, back_even, t_even)
            lanes = slice(n * 256, n * 256 + 256)
            x = g[first:last].reshape(count * cols, 768)
            t[first:last, :, lanes] = mm(x, kernel[:, lanes]).reshape(count, cols, 256)

        low = lax.broadcasted_iota(jnp.int32, (CHUNK, 128), 1) < 64
        tall_low = lax.broadcasted_iota(jnp.int32, (cols, 128), 1) < 64
        gains = [half_out[:, 0:128], half_out[:, 128:256]]

        def pull(v0, v1, vm, r, zero_low):
            mine = low if zero_low else jnp.logical_not(low)
            def both(a0, a1, am):
                s0 = jnp.sum(a0 + jnp.where(mine, am, 0.0), axis=1, keepdims=True)
                s1 = jnp.sum(a1 + jnp.where(mine, 0.0, am), axis=1, keepdims=True)
                return s0 * (1.0 / o), s1 * (1.0 / o)

            q0, q1 = both(v0 * v0, v1 * v1, vm * vm)
            i0, i1 = lax.rsqrt(q0 + EPS), lax.rsqrt(q1 + EPS)
            im = jnp.where(mine, i0, i1)
            out = []
            for v, i, g, k in ((v0, i0, gains[0], 0), (v1, i1, gains[0], 1), (vm, im, gains[1], 2)):
                s = v * i
                out.append((s, pulled(s, g, r[:, k * 128 : k * 128 + 128].astype(F32))))
            m0, m1 = both(*(s * d for s, d in out))
            mx = jnp.where(mine, m0, m1)
            return [i * (d - s * m) for (s, d), i, m in zip(out, (i0, i1, im), (m0, m1, mx))]

        def pull_row(k, odd):
            target, tmp = (g_odd, tmp_odd) if odd else (g_even, tmp_even)
            for c in range(0, cols, CHUNK):
                at = slice(c, c + CHUNK)
                if odd:
                    v0 = p0[k, at, 256:384] + p0[k + 1, at, 0:128]
                    v1 = p1[k, at, 256:384] + p1[k + 1, at, 0:128]
                    m0 = p0[k, at, 640:768] + p0[k + 1, at, 512:640]
                    m1 = p1[k, at, 640:768] + p1[k + 1, at, 512:640]
                else:
                    v0 = p0[k + 1, at, 128:256] + p0[k, at, 384:512]
                    v1 = p1[k + 1, at, 128:256] + p1[k, at, 384:512]
                    m0 = p1[k + 1, at, 512:640] + p1[k, at, 640:768]
                    m1 = p0[k + 1, at, 512:640] + p0[k, at, 640:768]
                out = pull(v0, v1, jnp.where(low, m0, m1), reward[2 * k + (0 if odd else 1), at], odd)
                for n, value in enumerate(out):
                    lanes = slice(n * 128, n * 128 + 128)
                    target[k, at, lanes] = value.astype(BF16)
                    tmp[k % 2, at, lanes] = value
            target[k, :, 384:512] = from_right(tmp[k % 2, :, 0:128]).astype(BF16)
            target[k, :, 512:640] = from_left(tmp[k % 2, :, 128:256]).astype(BF16)
            x = tmp[k % 2, :, 256:384]
            sides = (from_right(x), from_left(x)) if odd else (from_left(x), from_right(x))
            target[k, :, 640:768] = jnp.where(tall_low, *sides).astype(BF16)

        def block_row(k):
            for lanes in range(0, 384, 128):
                at, far = slice(lanes, lanes + 128), slice(lanes + 384, lanes + 512)
                x = t_odd[k + 1, :, at] + t_odd[k, :, far] + t_even[k, :, at] + t_even[k + 1, :, far]
                beside(back.at[k], 0, lanes, inside(x, k, 1, rows + 1), True)

        def hidden_pull(k):
            for c in range(0, cols, CHUNK):
                at = slice(c, c + CHUNK)
                v = hidden[k + 3, at].astype(F32)
                inv = lax.rsqrt(jnp.mean(v * v, axis=1, keepdims=True) + EPS)
                s = v * inv
                d = pulled(s, half_gain[...], act_grad[k, at])
                dv = inv * (d - s * jnp.mean(d * s, axis=1, keepdims=True))
                hid[k, at] = (back[k + 1, at, 384:768].astype(F32) + dv).astype(BF16)

        fine = rows + 3
        for k in range(rows + 4):
            state_row(k)
        for b in range(2):
            up_rows(1, rows + 4, b, 0)
            up_rows(0, rows + 3, b, 1)
            up_rows(0, rows + 4, b, 2)
        for k in range(fine):
            pull_row(k, True)
            pull_row(k, False)
        for odd in (True, False):
            down_rows(1 if odd else 0, fine if odd else fine - 1, odd, 0)
            down_rows(0, fine, odd, 1)
            down_rows(0 if odd else 1, fine - 1 if odd else fine, odd, 2)
        for k in range(rows + 2):
            block_row(k)
        lhs = [back[2 - i : 2 - i + rows].reshape(size, 1152) for i in range(3)]
        act_grad[:, :, 0:256] = mm(jnp.concatenate(lhs, axis=1), mid_t[:, 0:256]).reshape(rows, cols, 256)
        both = mm(
            back[1 : rows + 2].reshape((rows + 1) * cols, 1152),
            jnp.concatenate([mid_t[1152:2304, 256:384], mid_t[0:1152, 256:384]], axis=1),
        )
        rest = mm(back[0:rows].reshape(size, 1152), mid_t[2304:3456, 256:384])
        for p in range(rows):
            at, after = slice(p * cols, (p + 1) * cols), slice((p + 1) * cols, (p + 2) * cols)
            act_grad[p, :, 256:384] = both[at, :128] + both[after, 128:] + rest[at]
        for k in range(rows):
            hidden_pull(k)

        z = mm_t(w_in[...], hid[...].reshape(size, 384))
        place = lax.broadcasted_iota(jnp.int32, (chan, size), 1)
        col = lax.rem(place, cols)
        sums = []
        for i in range(3):
            z0, z1, z2 = (z[(i * 3 + j) * chan : (i * 3 + j + 1) * chan] for j in range(3))
            left = jnp.where(col == cols - 1, 0.0, pltpu.roll(z0, size - 1, 1))
            right = jnp.where(col == 0, 0.0, pltpu.roll(z2, 1, 1))
            sums.append(left + z1 + right)
        inner = sums[1]
        inner = inner + jnp.where(place < size - cols, pltpu.roll(sums[0], size - cols, 1), 0.0)
        inner = inner + jnp.where(place >= cols, pltpu.roll(sums[2], cols, 1), 0.0)
        lines[0:chan] = inner
        lines[chan : 2 * chan] = sums[0]
        lines[2 * chan : 3 * chan] = sums[2]
        per_row = count // 2
        for u in range(count):
            pair, piece = u // per_row, u % per_row
            parts = []
            for a in range(2):
                at = (2 * pair + a) * cols + piece * width
                parts.append(lines[0:chan, at : at + width])
            at = piece * width + (0 if pair else (rows - 1) * cols)
            first = chan if pair else 2 * chan
            parts.append(lines[first : first + chan, at : at + width])
            parts.append(jnp.zeros((chan, 128 - 3 * width), F32))
            payload[u] = jnp.concatenate(parts, axis=1).astype(BF16)

    return body


def placing(info, order, sel, count, width, tokens):
    piece = width // 2
    pair = info[3]
    lane = lax.broadcasted_iota(jnp.int32, (128, 4 * tokens), 0)
    column = lax.broadcasted_iota(jnp.int32, (128, 4 * tokens), 1)
    group = (lane >= width).astype(jnp.int32) + (lane >= 2 * width).astype(jnp.int32)
    w = lane - group * width
    part = jnp.where(group == 2, pair, group)
    fixed = (2 * part + (w & 1)) * tokens + (w >> 1) - column
    fixed = jnp.where(lane < 3 * width, fixed, -99999)

    def one(t):
        step = t + 1 - 2 * pair
        valid = jnp.logical_and(step >= 0, step < count)
        beside = jnp.where(valid, piece * order[jnp.clip(step, 0, count - 1)], -9999)
        begin = jnp.where(group == 2, beside, piece * order[t])
        sel[t // 2, t % 2 * 128 : t % 2 * 128 + 128] = (fixed + begin == 0).astype(F32).astype(BF16)

    return one


def place_body(count, chan, tokens):
    def body(sel, got, out):
        total = None
        for t in range(count // 2):
            x = mm(jnp.concatenate([got[2 * t], got[2 * t + 1]], axis=1), sel[t])
            total = x if total is None else total + x
        for k in range(4):
            out[k * chan : (k + 1) * chan] = total[:, k * tokens : (k + 1) * tokens]

    return body


def swaps(count):
    within = [(i, i ^ 1) for i in range(count)]
    across = [(0, 0), (count - 1, count - 1)]
    for i in range(1, count - 1, 2):
        across += [(i, i + 1), (i + 1, i)]
    return within, sorted(across)


def shards(
    latent, cached_latent, cached_features, reward_grad, conv_in_weight, conv_mid_weight, conv_up_weight, norm_gain, out_gain, shard_order
):
    count = lax.axis_size("tile")
    rows, cols, chan = latent.shape
    mid_chan = norm_gain.shape[0]
    o = out_gain.shape[0]
    tile = lax.axis_index("tile")
    info = jnp.stack(
        [tile % 2, (tile > 0).astype(jnp.int32), (tile < count - 1).astype(jnp.int32), (tile >= count // 2).astype(jnp.int32)]
    ).astype(jnp.int32)
    lat = jnp.transpose(latent, (0, 2, 1))
    lat_cached = jnp.transpose(cached_latent, (0, 1, 3, 2))
    reward_t = jnp.transpose(reward_grad, (0, 2, 1))
    up_t = jnp.transpose(conv_up_weight, (0, 1, 3, 2))
    mid = conv_mid_weight.reshape(3, 3, 3 * mid_chan, mid_chan)
    w_in = conv_in_weight.reshape(3, 3, 3 * chan, mid_chan)
    gain = 0.5 * norm_gain.reshape(1, mid_chan)
    gain_out = 0.5 * jnp.concatenate([out_gain, out_gain[128:]]).reshape(1, 256)
    within, across = swaps(count)
    size = rows * cols
    edge_rows = 3 * cols + 2 * chan * rows

    info, back_odd, back_even = call(
        taps_body,
        [((4,), jnp.int32), ((768, 768), BF16), ((768, 768), BF16)],
        1, 1, [], 1e10, 8, 1,
    )(info, up_t)

    own, send_even, send_odd = call(
        pack_body(rows, cols, o, chan),
        [((6, cols, 384), BF16), ((edge_rows, 384), BF16), ((edge_rows, 384), BF16)],
        1, 3, [], 1e10, 8,
    )(info, reward_t, lat, lat_cached)
    packed_even = lax.ppermute(send_even, "tile", within)
    packed_odd = lax.ppermute(send_odd, "tile", across)

    width = 2 * cols // count
    tokens = size // 4
    acc, part_even, part_odd, mid_t, sel, fwd, own_mid = call(
        cached_body(rows, cols, count, width, tokens, o),
        [
            ((rows + 4, cols, 384), F32), ((3 * cols, 384), BF16), ((3 * cols, 384), BF16), ((3456, 384), BF16),
            ((count // 2, 256, 4 * tokens), BF16), ((2, 768, 768), BF16), ((2, cols, 384), BF16),
        ],
        2, 5, [pltpu.VMEM((size, 2304), BF16), pltpu.VMEM((3, size, 384), F32)], 4e9, 14,
    )(info, shard_order, cached_features, mid, back_odd, back_even, reward_t)
    got_even = lax.ppermute(part_even, "tile", within)
    got_odd = lax.ppermute(part_odd, "tile", across)

    hidden, conv = call(
        current_body(rows, cols, chan),
        [((rows + 6, cols, 384), BF16), ((rows + 4, cols, 384), F32)],
        1, 7,
        [
            pltpu.VMEM((9 * rows * chan, 256), F32),
            pltpu.VMEM((3 * rows, 9 * chan, 256), BF16),
            pltpu.VMEM((rows + 6, cols, 1152), BF16),
            pltpu.VMEM((27 * chan, 384), BF16),
            pltpu.VMEM((2, cols, 384), F32),
        ],
        5e9, 14,
    )(info, lat, lat_cached, packed_even, packed_odd, w_in, mid, gain)

    (payload,) = call(
        back_body(rows, cols, chan, count, o),
        [((count, chan, 128), BF16)],
        1, 16,
        [
            pltpu.VMEM((2 * rows + 6, cols, 384), BF16),
            pltpu.VMEM((rows + 4, cols, 384), F32),
            pltpu.VMEM((rows + 4, cols, 768), F32),
            pltpu.VMEM((rows + 4, cols, 768), F32),
            pltpu.VMEM((rows + 3, cols, 768), BF16),
            pltpu.VMEM((rows + 3, cols, 768), BF16),
            pltpu.VMEM((rows + 4, cols, 1152), BF16),
            pltpu.VMEM((rows + 3, cols, 768), F32),
            pltpu.VMEM((rows + 3, cols, 768), F32),
            pltpu.VMEM((rows + 2, cols, 1152), BF16),
            pltpu.VMEM((rows, cols, 384), F32),
            pltpu.VMEM((rows, cols, 384), BF16),
            pltpu.VMEM((2, cols, 384), F32),
            pltpu.VMEM((2, cols, 384), F32),
            pltpu.VMEM((3 * chan, size), F32),
        ],
        8e9, 34,
    )(
        info, hidden, conv, acc, got_even, got_odd, packed_even, packed_odd, own, own_mid, fwd, back_odd, back_even, mid_t,
        w_in[2].reshape(9 * chan, mid_chan), gain, gain_out,
    )
    received = lax.all_to_all(payload, "tile", split_axis=0, concat_axis=0, tiled=True)
    (placed,) = call(place_body(count, chan, tokens), [((4 * chan, tokens), F32)], 0, 2, [], 1e7, 8)(sel, received)
    return placed.T


def solution(mesh):
    return jax.shard_map(
        shards,
        mesh=mesh,
        in_specs=(
            P(("prompt", "tile"), None, None),
            P(None, ("prompt", "tile"), None, None),
            P(None, ("prompt", "tile"), None, None),
            P(("prompt", "tile"), None, None),
            P(),
            P(),
            P(),
            P(),
            P(),
            P("prompt"),
        ),
        out_specs=P(("prompt", "tile"), None),
        check_vma=False,
    )
```

```python
import jax
import jax.numpy as jnp
from jax import lax
from jax.experimental import pallas as pl
from jax.experimental.pallas import tpu as pltpu
from jax.sharding import PartitionSpec as P

EPS = 1e-06
F32 = jnp.float32
BF16 = jnp.bfloat16
VM = pl.BlockSpec(memory_space=pltpu.VMEM)
SM = pl.BlockSpec(memory_space=pltpu.SMEM)


def weave(*groups):
    total = max(len(g) for g in groups)
    done = [0] * len(groups)
    for k in range(total):
        for n, g in enumerate(groups):
            while done[n] * total < (k + 1) * len(g):
                g[done[n]]()
                done[n] += 1


def steps(f, *keys):
    return [lambda key=key: f(*key) for key in keys]


def call(body, outs, n_smem, n_vmem, scratch, flops, limit, smem_outs=0):
    specs = [SM] * n_smem + [VM] * n_vmem
    return pl.pallas_call(
        body,
        out_shape=[jax.ShapeDtypeStruct(s, d) for s, d in outs],
        in_specs=specs,
        out_specs=[SM] * smem_outs + [VM] * (len(outs) - smem_outs),
        scratch_shapes=scratch,
        cost_estimate=pl.CostEstimate(flops=int(flops), bytes_accessed=2**20, transcendentals=0),
        compiler_params=pltpu.CompilerParams(vmem_limit_bytes=limit << 20),
    )


def mm(a, b):
    return jnp.dot(a, b, preferred_element_type=F32)


def mm_t(a, b):
    return lax.dot_general(a, b, (((1,), (1,)), ((), ())), preferred_element_type=F32)


def flag(info, k):
    return info[k].astype(F32)


def from_left(x):
    moved = pltpu.roll(x, 1, 0)
    first = lax.broadcasted_iota(jnp.int32, (8, x.shape[1]), 0) == 0
    return jnp.concatenate([jnp.where(first, 0.0, moved[:8]), moved[8:]], axis=0)


def from_right(x):
    size = x.shape[0]
    moved = pltpu.roll(x, size - 1, 0)
    last = lax.broadcasted_iota(jnp.int32, (8, x.shape[1]), 0) == 7
    return jnp.concatenate([moved[: size - 8], jnp.where(last, 0.0, moved[size - 8 :])], axis=0)


def beside(target, base, lanes, x, ahead):
    sides = (from_right, from_left) if ahead else (from_left, from_right)
    for group, value in enumerate((sides[0](x), x, sides[1](x))):
        at = base + group * 384 + lanes
        target[:, at : at + 128] = value.astype(BF16)


CHUNK = 32


def picker(cols, o):
    half = o - 128
    x_index = lax.broadcasted_iota(jnp.int32, (cols, 2 * cols), 1)
    w_index = lax.broadcasted_iota(jnp.int32, (cols, 2 * cols), 0)
    pick = [(x_index == 2 * w_index + b).astype(F32).astype(BF16) for b in (0, 1)]
    zeros = jnp.zeros((128 - half, 2 * cols), BF16)

    def one(reward, f, own, k):
        r = reward[f]
        first, rest = r[:128], r[128:]
        low = jnp.concatenate([first, rest, zeros], axis=0)
        high = jnp.concatenate([first, zeros, rest], axis=0)
        sides = (low, high) if f % 2 else (high, low)
        d0, d1 = mm_t(pick[0], sides[0]), mm_t(pick[1], sides[1])
        own[k, :, 0:128] = d0[:, :128].astype(BF16)
        own[k, :, 128:256] = d1[:, :128].astype(BF16)
        own[k, :, 256:384] = (d0[:, 128:] + d1[:, 128:]).astype(BF16)

    return one


def pack_body(rows, cols, o, chan):
    def body(info, reward, latent, cached, own, send_even, send_odd):
        one = picker(cols, o)
        for k in range(6):
            one(reward, k if k < 3 else 2 * rows - 6 + k, own, k)
        base = 3 * cols
        per = chan * rows
        for send, last in ((send_even, 1 - info[0]), (send_odd, info[0])):
            begin = last * 3
            for k in range(3):
                send[k * cols : (k + 1) * cols] = own[begin + k]
            for t in range(3):
                src = cached[t] if t < 2 else latent[...]
                lat = src.reshape(per, cols)
                send[base : base + per, t * 128 : t * 128 + 128] = lat[:, :128]
                send[base + per : base + 2 * per, t * 128 : t * 128 + cols - 128] = lat[:, 128:]

    return body


def home(targets, q, p, tile):
    block, second = ((1, 1), (0, 0), (0, 1), (1, 0))[p]
    target, side = targets[q]
    if tile < 2:
        row = block * 384 + second * 128 + tile * 64
    else:
        row = block * 384 + 256 + 64 * (second if q % 2 == 0 else 1 - second)
    return target, row, side * 384


def turning(back_odd, back_even, fwd):
    targets = ((back_odd, 1), (back_even, 0), (back_odd, 0), (back_even, 1))

    def tap_tile(q, p, tile, lanes):
        target, row, side = home(targets, q, p, tile)
        return target[row : row + 64, side + lanes : side + lanes + 128]

    def one(b, side, lanes):
        p = ((3, 1), (2, 0))[b][side]
        at = slice(side * 384 + lanes, side * 384 + lanes + 128)
        for q in range(4):
            both = jnp.concatenate([tap_tile(q, p, 0, lanes), tap_tile(q, p, 1, lanes)], axis=0)
            fwd[b, at, q * 128 : q * 128 + 128] = both.T
        for half in range(2):
            pair = (2 * half, 2 * half + 1) if b == 0 else (2 * half + 1, 2 * half)
            both = jnp.concatenate([tap_tile(q, p, 2, lanes) for q in pair], axis=0)
            fwd[b, at, 512 + half * 128 : 640 + half * 128] = both.T

    return steps(one, *[(b, side, lanes) for b in range(2) for side in range(2) for lanes in range(0, 384, 128)])


def taps_body(info, up, info_out, back_odd, back_even):
    for k in range(4):
        info_out[k] = info[k]

    parts = ((2,), (1, 2), (0, 1), (0,))
    targets = ((back_odd, 1), (back_even, 0), (back_odd, 0), (back_even, 1))

    for tile in range(3):
        for lanes in range(0, 384, 128):
            w = [[up[i, j, tile * 64 : tile * 64 + 64, lanes : lanes + 128].astype(F32) for j in range(3)] for i in range(3)]
            for q in range(4):
                c = [w[parts[q][0]][j] + w[parts[q][1]][j] if len(parts[q]) > 1 else w[parts[q][0]][j] for j in range(3)]
                for p, tap in enumerate((c[2], c[1] + c[2], c[0] + c[1], c[0])):
                    target, row, side = home(targets, q, p, tile)
                    target[row : row + 64, side + lanes : side + lanes + 128] = tap.astype(BF16)


def cached_body(rows, cols, count, width, tokens, o):
    size = rows * cols

    def body(
        info, order, features, mid, back_odd, back_even, reward, acc, send_even, send_odd, mid_t, sel, fwd, own, wide, parts
    ):
        for t in range(2):
            for r in range(rows):
                for lanes in range(0, 384, 128):
                    x = features[t, r, :, lanes : lanes + 128].astype(F32)
                    beside(wide.at[r * cols : (r + 1) * cols], t * 1152, lanes, x, False)
        def product(i, lanes):
            parts[i, :, lanes] = mm(wide[...], jnp.concatenate([mid[0, i, :, lanes], mid[1, i, :, lanes]], axis=0))

        def double():
            left = jnp.concatenate([mid[0, 0, :, 256:384], mid[1, 0, :, 256:384]], axis=0)
            right = jnp.concatenate([mid[0, 1, :, 256:384], mid[1, 1, :, 256:384]], axis=0)
            both = mm(wide[...], jnp.concatenate([left, right], axis=1))
            parts[0, :, 256:384] = both[:, :128]
            parts[1, :, 256:384] = both[:, 128:]

        def turn(i, j):
            at = (i * 3 + j) * 384
            mid_t[at : at + 384] = mid[2, i, j * 384 : (j + 1) * 384].T

        most, rest = slice(0, 256), slice(256, 384)
        products = steps(product, (0, most), (1, most)) + steps(double, ()) + steps(product, (2, most), (2, rest))
        one = picker(cols, o)
        others = steps(turn, *[(i, j) for i in range(3) for j in range(3)])
        others += turning(back_odd, back_even, fwd)
        others += steps(placing(info, order, sel, count, width, tokens), *[(t,) for t in range(count)])
        others += steps(one, (reward, rows - 1, own, 0), (reward, rows, own, 1))
        weave(others, products)
        for k in range(rows + 4):
            total = jnp.zeros((cols, 384), F32)
            for i in range(3):
                r = k - 3 + i
                if 0 <= r < rows:
                    total = total + parts[i, r * cols : (r + 1) * cols]
            acc[k] = total
        for send, last in ((send_even, 1 - info[0]), (send_odd, info[0])):
            for k in range(3):
                send[k * cols : (k + 1) * cols] = acc[1 + last * 3 + k].astype(BF16)

    return body


def current_body(rows, cols, chan):
    per = chan * rows
    base = 3 * cols

    def body(info, latent, cached, got_even, got_odd, w_in, mid, half_gain, hidden, conv, lat, tall, wide, w_order, plain):
        even = info[0] == 0
        lat[...] = jnp.zeros_like(lat)

        def fill(first_row, got, ok):
            scale = ok.astype(F32)
            for t in range(3):
                x = got[base : base + per, t * 128 : t * 128 + 128].astype(F32) * scale
                y = got[base + per : base + 2 * per, t * 128 : t * 128 + cols - 128].astype(F32) * scale
                for r in range(rows):
                    at = pl.ds((first_row + r) * 3 * chan + t * chan, chan)
                    lat[at, 0:128] = x[r * chan : (r + 1) * chan]
                    lat[at, 128:cols] = y[r * chan : (r + 1) * chan]

        @pl.when(even)
        def _():
            fill(0, got_odd, info[1])
            fill(2 * rows, got_even, info[2])

        @pl.when(jnp.logical_not(even))
        def _():
            fill(0, got_even, info[1])
            fill(2 * rows, got_odd, info[2])

        for t in range(3):
            for r in range(rows):
                at = pl.ds((rows + r) * 3 * chan + t * chan, chan)
                lat[at, 0:cols] = (cached[t, r] if t < 2 else latent[r]).astype(F32)

        for r in range(3 * rows):
            for t in range(3):
                x = lat[pl.ds((r * 3 + t) * chan, chan), :]
                at = t * 3 * chan
                tall[r, at : at + chan] = pltpu.roll(x, 1, 1).astype(BF16)
                tall[r, at + chan : at + 2 * chan] = x.astype(BF16)
                tall[r, at + 2 * chan : at + 3 * chan] = pltpu.roll(x, 255, 1).astype(BF16)
        for i in range(3):
            for t in range(3):
                at = (i * 3 + t) * 3 * chan
                w_order[at : at + 3 * chan] = w_in[t, i]

        def hidden_row(k):
            lhs = tall[k : k + 3].reshape(27 * chan, 256)[:, 0:cols]
            h = lax.dot_general(lhs, w_order[...], (((0,), (0,)), ((), ())), preferred_element_type=F32)
            plain[k % 2] = h
            for c in range(0, cols, CHUNK):
                at = slice(c, c + CHUNK)
                v = plain[k % 2, at].astype(BF16)
                hidden[k, at] = v
                v = v.astype(F32)
                inv = lax.rsqrt(jnp.mean(v * v, axis=1, keepdims=True) + EPS)
                half = v * inv * half_gain[...]
                act = half * (jnp.tanh(half) + 1.0)
                if k < 3:
                    act = act * flag(info, 1)
                if k >= rows + 3:
                    act = act * flag(info, 2)
                plain[k % 2, at] = act
            for lanes in range(0, 384, 128):
                beside(wide.at[k], 0, lanes, plain[k % 2, :, lanes : lanes + 128], False)

        def conv_rows(p, number):
            lhs = [wide[p + i : p + i + number].reshape(number * cols, 1152) for i in range(3)]
            total = mm(jnp.concatenate(lhs, axis=1), mid[2, :, :, 0:256].reshape(3456, 256))
            conv[p : p + number, :, 0:256] = total.reshape(number, cols, 256)

        for k in range(4):
            hidden_row(k)
        for p in range(0, rows + 4, 2):
            conv_rows(p, 2)
            for k in (p + 4, p + 5):
                if k < rows + 6:
                    hidden_row(k)
        both = mm(
            wide[0 : rows + 5].reshape((rows + 5) * cols, 1152),
            jnp.concatenate([mid[2, 0, :, 256:384], mid[2, 1, :, 256:384]], axis=1),
        )
        rest = mm(wide[2 : rows + 6].reshape((rows + 4) * cols, 1152), mid[2, 2, :, 256:384])
        for p in range(rows + 4):
            at, after = slice(p * cols, (p + 1) * cols), slice((p + 1) * cols, (p + 2) * cols)
            conv[p, :, 256:384] = both[at, :128] + both[after, 128:] + rest[at]

    return body


def pulled(s, half_gain, grad):
    h = s * half_gain
    t = jnp.tanh(h)
    return (grad * half_gain) * ((1.0 + t) * (1.0 + h * (1.0 - t)))


def back_body(rows, cols, chan, count, o):
    size = rows * cols
    width = 2 * cols // count

    def body(
        info, hidden, conv, acc, got_even, got_odd, packed_even, packed_odd, own, own_mid, fwd, back_odd, back_even, mid_t, w_in, half_gain,
        half_out, payload, reward, edge, p0, p1, g_odd, g_even, wide, t_odd, t_even, main, back, act_grad, hid, tmp_odd, tmp_even,
        lines,
    ):
        even = info[0] == 0
        top, bottom = flag(info, 1), flag(info, 2)

        def take(got, packed, before):
            ok = top if before else bottom
            place = 0 if before else rows + 1
            for k in range(3):
                at = slice(k * cols, (k + 1) * cols)
                edge[place + k] = got[at].astype(F32) * ok
                reward[k if before else 2 * rows + 3 + k] = (packed[at].astype(F32) * ok).astype(BF16)

        @pl.when(even)
        def _():
            take(got_odd, packed_odd, True)
            take(got_even, packed_even, False)

        @pl.when(jnp.logical_not(even))
        def _():
            take(got_even, packed_even, True)
            take(got_odd, packed_odd, False)

        reward[3:6] = own[0:3]
        reward[6 : 2 * rows] = own_mid[...]
        reward[2 * rows : 2 * rows + 3] = own[3:6]

        def inside(x, k, first, last):
            return x * top if k < first else x * bottom if k >= last else x

        def state_row(k):
            for lanes in range(0, 384, 128):
                at = slice(lanes, lanes + 128)
                x = hidden[k + 1, :, at].astype(F32) + conv[k, :, at]
                if 1 <= k <= rows + 2:
                    x = x + acc[k, :, at]
                if k < 3 or k > rows:
                    x = x + edge[k, :, at]
                beside(wide.at[k], 0, lanes, inside(x, k, 2, rows + 2), False)

        def up_rows(first, last, b, n):
            count = last - first
            x = wide[first:last, :, b * 384 : b * 384 + 768].reshape(count * cols, 768)
            lanes = slice(n * 256, n * 256 + 256)
            (p0, p1)[b][first:last, :, lanes] = mm(x, fwd[b, :, lanes]).reshape(count, cols, 256)

        low = lax.broadcasted_iota(jnp.int32, (CHUNK, 128), 1) < 64
        tall_low = lax.broadcasted_iota(jnp.int32, (cols, 128), 1) < 64
        gains = [half_out[:, 0:128], half_out[:, 128:256]]

        def pull(v0, v1, vm, r, zero_low):
            mine = low if zero_low else jnp.logical_not(low)
            def both(a0, a1, am):
                s0 = jnp.sum(a0 + jnp.where(mine, am, 0.0), axis=1, keepdims=True)
                s1 = jnp.sum(a1 + jnp.where(mine, 0.0, am), axis=1, keepdims=True)
                return s0 * (1.0 / o), s1 * (1.0 / o)

            q0, q1 = both(v0 * v0, v1 * v1, vm * vm)
            i0, i1 = lax.rsqrt(q0 + EPS), lax.rsqrt(q1 + EPS)
            im = jnp.where(mine, i0, i1)
            out = []
            for v, i, g, k in ((v0, i0, gains[0], 0), (v1, i1, gains[0], 1), (vm, im, gains[1], 2)):
                s = v * i
                out.append((s, pulled(s, g, r[:, k * 128 : k * 128 + 128].astype(F32))))
            m0, m1 = both(*(s * d for s, d in out))
            mx = jnp.where(mine, m0, m1)
            return [i * (d - s * m) for (s, d), i, m in zip(out, (i0, i1, im), (m0, m1, mx))]

        def pull_row(k, odd):
            target, tmp = (g_odd, tmp_odd) if odd else (g_even, tmp_even)
            for c in range(0, cols, CHUNK):
                at = slice(c, c + CHUNK)
                if odd:
                    v0 = p0[k, at, 256:384] + p0[k + 1, at, 0:128]
                    v1 = p1[k, at, 256:384] + p1[k + 1, at, 0:128]
                    m0 = p0[k, at, 640:768] + p0[k + 1, at, 512:640]
                    m1 = p1[k, at, 640:768] + p1[k + 1, at, 512:640]
                else:
                    v0 = p0[k + 1, at, 128:256] + p0[k, at, 384:512]
                    v1 = p1[k + 1, at, 128:256] + p1[k, at, 384:512]
                    m0 = p1[k + 1, at, 512:640] + p1[k, at, 640:768]
                    m1 = p0[k + 1, at, 512:640] + p0[k, at, 640:768]
                out = pull(v0, v1, jnp.where(low, m0, m1), reward[2 * k + (0 if odd else 1), at], odd)
                for n, value in enumerate(out):
                    lanes = slice(n * 128, n * 128 + 128)
                    target[k, at, lanes] = value.astype(BF16)
                    tmp[k % 2, at, lanes] = value
            target[k, :, 384:512] = from_right(tmp[k % 2, :, 0:128]).astype(BF16)
            target[k, :, 512:640] = from_left(tmp[k % 2, :, 128:256]).astype(BF16)
            x = tmp[k % 2, :, 256:384]
            sides = (from_right(x), from_left(x)) if odd else (from_left(x), from_right(x))
            target[k, :, 640:768] = jnp.where(tall_low, *sides).astype(BF16)

        def block_row(k):
            for lanes in range(0, 384, 128):
                if lanes < 256:
                    x = main[k, :, lanes : lanes + 128]
                else:
                    x = t_odd[k + 1, :, 0:128] + t_odd[k, :, 128:256] + t_even[k, :, 0:128] + t_even[k + 1, :, 128:256]
                beside(back.at[k], 0, lanes, inside(x, k, 1, rows + 1), True)

        def hidden_pull(k):
            for c in range(0, cols, CHUNK):
                at = slice(c, c + CHUNK)
                v = hidden[k + 3, at].astype(F32)
                inv = lax.rsqrt(jnp.mean(v * v, axis=1, keepdims=True) + EPS)
                s = v * inv
                d = pulled(s, half_gain[...], act_grad[k, at])
                dv = inv * (d - s * jnp.mean(d * s, axis=1, keepdims=True))
                hid[k, at] = (back[k + 1, at, 384:768].astype(F32) + dv).astype(BF16)

        fine = rows + 3
        for k in range(rows + 4):
            state_row(k)
        for b in range(2):
            up_rows(1, rows + 4, b, 0)
            up_rows(0, rows + 3, b, 1)
            up_rows(0, rows + 4, b, 2)
        for k in range(fine):
            pull_row(k, True)
            pull_row(k, False)
        number = rows + 2
        lhs = [x.reshape(number * cols, 768) for x in (g_odd[1:fine], g_odd[0:number], g_even[0:number], g_even[1:fine])]
        rhs = [back_odd[:, 0:256], back_odd[:, 384:640], back_even[:, 0:256], back_even[:, 384:640]]
        main[...] = mm(jnp.concatenate(lhs, axis=1), jnp.concatenate(rhs, axis=0)).reshape(number, cols, 256)
        for g, kernel, t in ((g_odd, back_odd, t_odd), (g_even, back_even, t_even)):
            pair = jnp.concatenate([kernel[:, 256:384], kernel[:, 640:768]], axis=1)
            t[...] = mm(g[...].reshape(fine * cols, 768), pair).reshape(fine, cols, 256)
        for k in range(rows + 2):
            block_row(k)
        lhs = [back[2 - i : 2 - i + rows].reshape(size, 1152) for i in range(3)]
        act_grad[:, :, 0:256] = mm(jnp.concatenate(lhs, axis=1), mid_t[:, 0:256]).reshape(rows, cols, 256)
        both = mm(
            back[1 : rows + 2].reshape((rows + 1) * cols, 1152),
            jnp.concatenate([mid_t[1152:2304, 256:384], mid_t[0:1152, 256:384]], axis=1),
        )
        rest = mm(back[0:rows].reshape(size, 1152), mid_t[2304:3456, 256:384])
        for p in range(rows):
            at, after = slice(p * cols, (p + 1) * cols), slice((p + 1) * cols, (p + 2) * cols)
            act_grad[p, :, 256:384] = both[at, :128] + both[after, 128:] + rest[at]
        for k in range(rows):
            hidden_pull(k)

        z = mm_t(w_in[...], hid[...].reshape(size, 384))
        place = lax.broadcasted_iota(jnp.int32, (chan, size), 1)
        col = lax.rem(place, cols)
        sums = []
        for i in range(3):
            z0, z1, z2 = (z[(i * 3 + j) * chan : (i * 3 + j + 1) * chan] for j in range(3))
            left = jnp.where(col == cols - 1, 0.0, pltpu.roll(z0, size - 1, 1))
            right = jnp.where(col == 0, 0.0, pltpu.roll(z2, 1, 1))
            sums.append(left + z1 + right)
        inner = sums[1]
        inner = inner + jnp.where(place < size - cols, pltpu.roll(sums[0], size - cols, 1), 0.0)
        inner = inner + jnp.where(place >= cols, pltpu.roll(sums[2], cols, 1), 0.0)
        lines[0:chan] = inner
        lines[chan : 2 * chan] = sums[0]
        lines[2 * chan : 3 * chan] = sums[2]
        per_row = count // 2
        for u in range(count):
            pair, piece = u // per_row, u % per_row
            parts = []
            for a in range(2):
                at = (2 * pair + a) * cols + piece * width
                parts.append(lines[0:chan, at : at + width])
            at = piece * width + (0 if pair else (rows - 1) * cols)
            first = chan if pair else 2 * chan
            parts.append(lines[first : first + chan, at : at + width])
            parts.append(jnp.zeros((chan, 128 - 3 * width), F32))
            payload[u] = jnp.concatenate(parts, axis=1).astype(BF16)

    return body


def placing(info, order, sel, count, width, tokens):
    piece = width // 2
    pair = info[3]
    lane = lax.broadcasted_iota(jnp.int32, (128, 4 * tokens), 0)
    column = lax.broadcasted_iota(jnp.int32, (128, 4 * tokens), 1)
    group = (lane >= width).astype(jnp.int32) + (lane >= 2 * width).astype(jnp.int32)
    w = lane - group * width
    part = jnp.where(group == 2, pair, group)
    fixed = (2 * part + (w & 1)) * tokens + (w >> 1) - column
    fixed = jnp.where(lane < 3 * width, fixed, -99999)

    def one(t):
        step = t + 1 - 2 * pair
        valid = jnp.logical_and(step >= 0, step < count)
        beside = jnp.where(valid, piece * order[jnp.clip(step, 0, count - 1)], -9999)
        begin = jnp.where(group == 2, beside, piece * order[t])
        sel[t // 2, t % 2 * 128 : t % 2 * 128 + 128] = (fixed + begin == 0).astype(F32).astype(BF16)

    return one


def place_body(count, chan, tokens):
    def body(sel, got, out):
        total = None
        for t in range(count // 2):
            x = mm(jnp.concatenate([got[2 * t], got[2 * t + 1]], axis=1), sel[t])
            total = x if total is None else total + x
        for k in range(4):
            out[k * chan : (k + 1) * chan] = total[:, k * tokens : (k + 1) * tokens]

    return body


def swaps(count):
    within = [(i, i ^ 1) for i in range(count)]
    across = [(0, 0), (count - 1, count - 1)]
    for i in range(1, count - 1, 2):
        across += [(i, i + 1), (i + 1, i)]
    return within, sorted(across)


def shards(
    latent, cached_latent, cached_features, reward_grad, conv_in_weight, conv_mid_weight, conv_up_weight, norm_gain, out_gain, shard_order
):
    count = lax.axis_size("tile")
    rows, cols, chan = latent.shape
    mid_chan = norm_gain.shape[0]
    o = out_gain.shape[0]
    tile = lax.axis_index("tile")
    info = jnp.stack(
        [tile % 2, (tile > 0).astype(jnp.int32), (tile < count - 1).astype(jnp.int32), (tile >= count // 2).astype(jnp.int32)]
    ).astype(jnp.int32)
    lat = jnp.transpose(latent, (0, 2, 1))
    lat_cached = jnp.transpose(cached_latent, (0, 1, 3, 2))
    reward_t = jnp.transpose(reward_grad, (0, 2, 1))
    up_t = jnp.transpose(conv_up_weight, (0, 1, 3, 2))
    mid = conv_mid_weight.reshape(3, 3, 3 * mid_chan, mid_chan)
    w_in = conv_in_weight.reshape(3, 3, 3 * chan, mid_chan)
    gain = 0.5 * norm_gain.reshape(1, mid_chan)
    gain_out = 0.5 * jnp.concatenate([out_gain, out_gain[128:]]).reshape(1, 256)
    within, across = swaps(count)
    size = rows * cols
    edge_rows = 3 * cols + 2 * chan * rows

    info, back_odd, back_even = call(
        taps_body,
        [((4,), jnp.int32), ((768, 768), BF16), ((768, 768), BF16)],
        1, 1, [], 1e10, 8, 1,
    )(info, up_t)

    own, send_even, send_odd = call(
        pack_body(rows, cols, o, chan),
        [((6, cols, 384), BF16), ((edge_rows, 384), BF16), ((edge_rows, 384), BF16)],
        1, 3, [], 1e10, 8,
    )(info, reward_t, lat, lat_cached)
    packed_even = lax.ppermute(send_even, "tile", within)
    packed_odd = lax.ppermute(send_odd, "tile", across)

    width = 2 * cols // count
    tokens = size // 4
    acc, part_even, part_odd, mid_t, sel, fwd, own_mid = call(
        cached_body(rows, cols, count, width, tokens, o),
        [
            ((rows + 4, cols, 384), F32), ((3 * cols, 384), BF16), ((3 * cols, 384), BF16), ((3456, 384), BF16),
            ((count // 2, 256, 4 * tokens), BF16), ((2, 768, 768), BF16), ((2, cols, 384), BF16),
        ],
        2, 5, [pltpu.VMEM((size, 2304), BF16), pltpu.VMEM((3, size, 384), F32)], 4e9, 14,
    )(info, shard_order, cached_features, mid, back_odd, back_even, reward_t)
    got_even = lax.ppermute(part_even, "tile", within)
    got_odd = lax.ppermute(part_odd, "tile", across)

    hidden, conv = call(
        current_body(rows, cols, chan),
        [((rows + 6, cols, 384), BF16), ((rows + 4, cols, 384), F32)],
        1, 7,
        [
            pltpu.VMEM((9 * rows * chan, 256), F32),
            pltpu.VMEM((3 * rows, 9 * chan, 256), BF16),
            pltpu.VMEM((rows + 6, cols, 1152), BF16),
            pltpu.VMEM((27 * chan, 384), BF16),
            pltpu.VMEM((2, cols, 384), F32),
        ],
        5e9, 14,
    )(info, lat, lat_cached, packed_even, packed_odd, w_in, mid, gain)

    (payload,) = call(
        back_body(rows, cols, chan, count, o),
        [((count, chan, 128), BF16)],
        1, 16,
        [
            pltpu.VMEM((2 * rows + 6, cols, 384), BF16),
            pltpu.VMEM((rows + 4, cols, 384), F32),
            pltpu.VMEM((rows + 4, cols, 768), F32),
            pltpu.VMEM((rows + 4, cols, 768), F32),
            pltpu.VMEM((rows + 3, cols, 768), BF16),
            pltpu.VMEM((rows + 3, cols, 768), BF16),
            pltpu.VMEM((rows + 4, cols, 1152), BF16),
            pltpu.VMEM((rows + 3, cols, 256), F32),
            pltpu.VMEM((rows + 3, cols, 256), F32),
            pltpu.VMEM((rows + 2, cols, 256), F32),
            pltpu.VMEM((rows + 2, cols, 1152), BF16),
            pltpu.VMEM((rows, cols, 384), F32),
            pltpu.VMEM((rows, cols, 384), BF16),
            pltpu.VMEM((2, cols, 384), F32),
            pltpu.VMEM((2, cols, 384), F32),
            pltpu.VMEM((3 * chan, size), F32),
        ],
        8e9, 34,
    )(
        info, hidden, conv, acc, got_even, got_odd, packed_even, packed_odd, own, own_mid, fwd, back_odd, back_even, mid_t,
        w_in[2].reshape(9 * chan, mid_chan), gain, gain_out,
    )
    received = lax.all_to_all(payload, "tile", split_axis=0, concat_axis=0, tiled=True)
    (placed,) = call(place_body(count, chan, tokens), [((4 * chan, tokens), F32)], 0, 2, [], 1e7, 8)(sel, received)
    return placed.T


def solution(mesh):
    return jax.shard_map(
        shards,
        mesh=mesh,
        in_specs=(
            P(("prompt", "tile"), None, None),
            P(None, ("prompt", "tile"), None, None),
            P(None, ("prompt", "tile"), None, None),
            P(("prompt", "tile"), None, None),
            P(),
            P(),
            P(),
            P(),
            P(),
            P("prompt"),
        ),
        out_specs=P(("prompt", "tile"), None),
        check_vma=False,
    )
```

```python
import jax
import jax.numpy as jnp
from jax import lax
from jax.experimental import pallas as pl
from jax.experimental.pallas import tpu as pltpu
from jax.sharding import PartitionSpec as P

EPS = 1e-06
F32 = jnp.float32
BF16 = jnp.bfloat16
VM = pl.BlockSpec(memory_space=pltpu.VMEM)
SM = pl.BlockSpec(memory_space=pltpu.SMEM)


def weave(*groups):
    total = max(len(g) for g in groups)
    done = [0] * len(groups)
    for k in range(total):
        for n, g in enumerate(groups):
            while done[n] * total < (k + 1) * len(g):
                g[done[n]]()
                done[n] += 1


def steps(f, *keys):
    return [lambda key=key: f(*key) for key in keys]


def call(body, outs, n_smem, n_vmem, scratch, flops, limit, smem_outs=0):
    specs = [SM] * n_smem + [VM] * n_vmem
    return pl.pallas_call(
        body,
        out_shape=[jax.ShapeDtypeStruct(s, d) for s, d in outs],
        in_specs=specs,
        out_specs=[SM] * smem_outs + [VM] * (len(outs) - smem_outs),
        scratch_shapes=scratch,
        cost_estimate=pl.CostEstimate(flops=int(flops), bytes_accessed=2**20, transcendentals=0),
        compiler_params=pltpu.CompilerParams(vmem_limit_bytes=limit << 20),
    )


def mm(a, b):
    return jnp.dot(a, b, preferred_element_type=F32)


def mm_t(a, b):
    return lax.dot_general(a, b, (((1,), (1,)), ((), ())), preferred_element_type=F32)


def flag(info, k):
    return info[k].astype(F32)


def from_left(x):
    moved = pltpu.roll(x, 1, 0)
    first = lax.broadcasted_iota(jnp.int32, (8, x.shape[1]), 0) == 0
    return jnp.concatenate([jnp.where(first, 0.0, moved[:8]), moved[8:]], axis=0)


def from_right(x):
    size = x.shape[0]
    moved = pltpu.roll(x, size - 1, 0)
    last = lax.broadcasted_iota(jnp.int32, (8, x.shape[1]), 0) == 7
    return jnp.concatenate([moved[: size - 8], jnp.where(last, 0.0, moved[size - 8 :])], axis=0)


def beside(target, base, lanes, x, ahead):
    sides = (from_right, from_left) if ahead else (from_left, from_right)
    for group, value in enumerate((sides[0](x), x, sides[1](x))):
        at = base + group * 384 + lanes
        target[:, at : at + 128] = value.astype(BF16)


CHUNK = 32


def picker(cols, o):
    half = o - 128
    x_index = lax.broadcasted_iota(jnp.int32, (cols, 2 * cols), 1)
    w_index = lax.broadcasted_iota(jnp.int32, (cols, 2 * cols), 0)
    pick = [(x_index == 2 * w_index + b).astype(F32).astype(BF16) for b in (0, 1)]
    zeros = jnp.zeros((128 - half, 2 * cols), BF16)

    def one(reward, f, own, k):
        r = reward[f]
        first, rest = r[:128], r[128:]
        low = jnp.concatenate([first, rest, zeros], axis=0)
        high = jnp.concatenate([first, zeros, rest], axis=0)
        sides = (low, high) if f % 2 else (high, low)
        d0, d1 = mm_t(pick[0], sides[0]), mm_t(pick[1], sides[1])
        own[k, :, 0:128] = d0[:, :128].astype(BF16)
        own[k, :, 128:256] = d1[:, :128].astype(BF16)
        own[k, :, 256:384] = (d0[:, 128:] + d1[:, 128:]).astype(BF16)

    return one


def pack_body(rows, cols, o, chan):
    def body(info, reward, latent, cached, own, send_even, send_odd):
        one = picker(cols, o)
        for k in range(6):
            one(reward, k if k < 3 else 2 * rows - 6 + k, own, k)
        base = 3 * cols
        per = chan * rows
        for send, last in ((send_even, 1 - info[0]), (send_odd, info[0])):
            begin = last * 3
            for k in range(3):
                send[k * cols : (k + 1) * cols] = own[begin + k]
            for t in range(3):
                src = cached[t] if t < 2 else latent[...]
                lat = src.reshape(per, cols)
                send[base : base + per, t * 128 : t * 128 + 128] = lat[:, :128]
                send[base + per : base + 2 * per, t * 128 : t * 128 + cols - 128] = lat[:, 128:]

    return body


def home(targets, q, p, tile):
    block, second = ((1, 1), (0, 0), (0, 1), (1, 0))[p]
    target, side = targets[q]
    if tile < 2:
        row = block * 384 + second * 128 + tile * 64
    else:
        row = block * 384 + 256 + 64 * (second if q % 2 == 0 else 1 - second)
    return target, row, side * 384


def turning(back_odd, back_even, fwd):
    targets = ((back_odd, 1), (back_even, 0), (back_odd, 0), (back_even, 1))

    def tap_tile(q, p, tile, lanes):
        target, row, side = home(targets, q, p, tile)
        return target[row : row + 64, side + lanes : side + lanes + 128]

    def one(b, side, lanes):
        p = ((3, 1), (2, 0))[b][side]
        at = slice(side * 384 + lanes, side * 384 + lanes + 128)
        for q in range(4):
            both = jnp.concatenate([tap_tile(q, p, 0, lanes), tap_tile(q, p, 1, lanes)], axis=0)
            fwd[b, at, q * 128 : q * 128 + 128] = both.T
        for half in range(2):
            pair = (2 * half, 2 * half + 1) if b == 0 else (2 * half + 1, 2 * half)
            both = jnp.concatenate([tap_tile(q, p, 2, lanes) for q in pair], axis=0)
            fwd[b, at, 512 + half * 128 : 640 + half * 128] = both.T

    return steps(one, *[(b, side, lanes) for b in range(2) for side in range(2) for lanes in range(0, 384, 128)])


def taps_body(info, up, info_out, back_odd, back_even):
    for k in range(4):
        info_out[k] = info[k]

    parts = ((2,), (1, 2), (0, 1), (0,))
    targets = ((back_odd, 1), (back_even, 0), (back_odd, 0), (back_even, 1))

    for tile in range(3):
        for lanes in range(0, 384, 128):
            w = [[up[i, j, tile * 64 : tile * 64 + 64, lanes : lanes + 128].astype(F32) for j in range(3)] for i in range(3)]
            for q in range(4):
                c = [w[parts[q][0]][j] + w[parts[q][1]][j] if len(parts[q]) > 1 else w[parts[q][0]][j] for j in range(3)]
                for p, tap in enumerate((c[2], c[1] + c[2], c[0] + c[1], c[0])):
                    target, row, side = home(targets, q, p, tile)
                    target[row : row + 64, side + lanes : side + lanes + 128] = tap.astype(BF16)


def cached_body(rows, cols, count, width, tokens, o):
    size = rows * cols

    def body(
        info, order, features, mid, back_odd, back_even, reward, acc, send_even, send_odd, mid_t, sel, fwd, own, wide, parts
    ):
        for t in range(2):
            for r in range(rows):
                for lanes in range(0, 384, 128):
                    x = features[t, r, :, lanes : lanes + 128].astype(F32)
                    beside(wide.at[r * cols : (r + 1) * cols], t * 1152, lanes, x, False)
        def product(r, i, lanes):
            at = slice(r * cols, (r + 1) * cols)
            parts[i, at, lanes] = mm(wide[at], jnp.concatenate([mid[0, i, :, lanes], mid[1, i, :, lanes]], axis=0))

        def double(r):
            at = slice(r * cols, (r + 1) * cols)
            left = jnp.concatenate([mid[0, 0, :, 256:384], mid[1, 0, :, 256:384]], axis=0)
            right = jnp.concatenate([mid[0, 1, :, 256:384], mid[1, 1, :, 256:384]], axis=0)
            both = mm(wide[at], jnp.concatenate([left, right], axis=1))
            parts[0, at, 256:384] = both[:, :128]
            parts[1, at, 256:384] = both[:, 128:]

        def turn(i, j):
            at = (i * 3 + j) * 384
            mid_t[at : at + 384] = mid[2, i, j * 384 : (j + 1) * 384].T

        most, rest = slice(0, 256), slice(256, 384)
        products = []
        for r in range(rows):
            products += steps(product, (r, 0, most), (r, 1, most)) + steps(double, (r,))
            products += steps(product, (r, 2, most), (r, 2, rest))
        one = picker(cols, o)
        others = steps(turn, *[(i, j) for i in range(3) for j in range(3)])
        others += turning(back_odd, back_even, fwd)
        others += steps(placing(info, order, sel, count, width, tokens), *[(t,) for t in range(count)])
        others += steps(one, (reward, rows - 1, own, 0), (reward, rows, own, 1))
        weave(others, products)
        for k in range(rows + 4):
            total = jnp.zeros((cols, 384), F32)
            for i in range(3):
                r = k - 3 + i
                if 0 <= r < rows:
                    total = total + parts[i, r * cols : (r + 1) * cols]
            acc[k] = total
        for send, last in ((send_even, 1 - info[0]), (send_odd, info[0])):
            for k in range(3):
                send[k * cols : (k + 1) * cols] = acc[1 + last * 3 + k].astype(BF16)

    return body


def current_body(rows, cols, chan):
    per = chan * rows
    base = 3 * cols

    def body(info, latent, cached, got_even, got_odd, w_in, mid, half_gain, hidden, conv, lat, tall, wide, w_order, plain):
        even = info[0] == 0
        lat[...] = jnp.zeros_like(lat)

        def fill(first_row, got, ok):
            scale = ok.astype(F32)
            for t in range(3):
                x = got[base : base + per, t * 128 : t * 128 + 128].astype(F32) * scale
                y = got[base + per : base + 2 * per, t * 128 : t * 128 + cols - 128].astype(F32) * scale
                for r in range(rows):
                    at = pl.ds((first_row + r) * 3 * chan + t * chan, chan)
                    lat[at, 0:128] = x[r * chan : (r + 1) * chan]
                    lat[at, 128:cols] = y[r * chan : (r + 1) * chan]

        @pl.when(even)
        def _():
            fill(0, got_odd, info[1])
            fill(2 * rows, got_even, info[2])

        @pl.when(jnp.logical_not(even))
        def _():
            fill(0, got_even, info[1])
            fill(2 * rows, got_odd, info[2])

        for t in range(3):
            for r in range(rows):
                at = pl.ds((rows + r) * 3 * chan + t * chan, chan)
                lat[at, 0:cols] = (cached[t, r] if t < 2 else latent[r]).astype(F32)

        for r in range(3 * rows):
            for t in range(3):
                x = lat[pl.ds((r * 3 + t) * chan, chan), :]
                at = t * 3 * chan
                tall[r, at : at + chan] = pltpu.roll(x, 1, 1).astype(BF16)
                tall[r, at + chan : at + 2 * chan] = x.astype(BF16)
                tall[r, at + 2 * chan : at + 3 * chan] = pltpu.roll(x, 255, 1).astype(BF16)
        for i in range(3):
            for t in range(3):
                at = (i * 3 + t) * 3 * chan
                w_order[at : at + 3 * chan] = w_in[t, i]

        def hidden_row(k):
            lhs = tall[k : k + 3].reshape(27 * chan, 256)[:, 0:cols]
            h = lax.dot_general(lhs, w_order[...], (((0,), (0,)), ((), ())), preferred_element_type=F32)
            plain[k % 2] = h
            for c in range(0, cols, CHUNK):
                at = slice(c, c + CHUNK)
                v = plain[k % 2, at].astype(BF16)
                hidden[k, at] = v
                v = v.astype(F32)
                inv = lax.rsqrt(jnp.mean(v * v, axis=1, keepdims=True) + EPS)
                half = v * inv * half_gain[...]
                act = half * (jnp.tanh(half) + 1.0)
                if k < 3:
                    act = act * flag(info, 1)
                if k >= rows + 3:
                    act = act * flag(info, 2)
                plain[k % 2, at] = act
            for lanes in range(0, 384, 128):
                beside(wide.at[k], 0, lanes, plain[k % 2, :, lanes : lanes + 128], False)

        def conv_rows(p, number):
            lhs = [wide[p + i : p + i + number].reshape(number * cols, 1152) for i in range(3)]
            total = mm(jnp.concatenate(lhs, axis=1), mid[2, :, :, 0:256].reshape(3456, 256))
            conv[p : p + number, :, 0:256] = total.reshape(number, cols, 256)

        for k in range(4):
            hidden_row(k)
        for p in range(0, rows + 4, 2):
            for k in (p, p + 1):
                conv_rows(k, 1)
                if k + 4 < rows + 6:
                    hidden_row(k + 4)
        both = mm(
            wide[0 : rows + 5].reshape((rows + 5) * cols, 1152),
            jnp.concatenate([mid[2, 0, :, 256:384], mid[2, 1, :, 256:384]], axis=1),
        )
        rest = mm(wide[2 : rows + 6].reshape((rows + 4) * cols, 1152), mid[2, 2, :, 256:384])
        for p in range(rows + 4):
            at, after = slice(p * cols, (p + 1) * cols), slice((p + 1) * cols, (p + 2) * cols)
            conv[p, :, 256:384] = both[at, :128] + both[after, 128:] + rest[at]

    return body


def pulled(s, half_gain, grad):
    h = s * half_gain
    t = jnp.tanh(h)
    return (grad * half_gain) * ((1.0 + t) * (1.0 + h * (1.0 - t)))


def back_body(rows, cols, chan, count, o):
    size = rows * cols
    width = 2 * cols // count

    def body(
        info, hidden, conv, acc, got_even, got_odd, packed_even, packed_odd, own, own_mid, fwd, back_odd, back_even, mid_t, w_in, half_gain,
        half_out, payload, reward, edge, p0, p1, g_odd, g_even, wide, t_odd, t_even, back, act_grad, hid, tmp_odd, tmp_even, lines,
    ):
        even = info[0] == 0
        top, bottom = flag(info, 1), flag(info, 2)

        def take(got, packed, before):
            ok = top if before else bottom
            place = 0 if before else rows + 1
            for k in range(3):
                at = slice(k * cols, (k + 1) * cols)
                edge[place + k] = got[at].astype(F32) * ok
                reward[k if before else 2 * rows + 3 + k] = (packed[at].astype(F32) * ok).astype(BF16)

        @pl.when(even)
        def _():
            take(got_odd, packed_odd, True)
            take(got_even, packed_even, False)

        @pl.when(jnp.logical_not(even))
        def _():
            take(got_even, packed_even, True)
            take(got_odd, packed_odd, False)

        reward[3:6] = own[0:3]
        reward[6 : 2 * rows] = own_mid[...]
        reward[2 * rows : 2 * rows + 3] = own[3:6]

        def inside(x, k, first, last):
            return x * top if k < first else x * bottom if k >= last else x

        def state_row(k):
            for lanes in range(0, 384, 128):
                at = slice(lanes, lanes + 128)
                x = hidden[k + 1, :, at].astype(F32) + conv[k, :, at]
                if 1 <= k <= rows + 2:
                    x = x + acc[k, :, at]
                if k < 3 or k > rows:
                    x = x + edge[k, :, at]
                beside(wide.at[k], 0, lanes, inside(x, k, 2, rows + 2), False)

        def up_rows(first, last, b, n):
            count = last - first
            x = wide[first:last, :, b * 384 : b * 384 + 768].reshape(count * cols, 768)
            lanes = slice(n * 256, n * 256 + 256)
            (p0, p1)[b][first:last, :, lanes] = mm(x, fwd[b, :, lanes]).reshape(count, cols, 256)

        def down_rows(first, last, odd, n):
            count = last - first
            g, kernel, t = (g_odd, back_odd, t_odd) if odd else (g_even, back_even, t_even)
            lanes = slice(n * 256, n * 256 + 256)
            x = g[first:last].reshape(count * cols, 768)
            t[first:last, :, lanes] = mm(x, kernel[:, lanes]).reshape(count, cols, 256)

        low = lax.broadcasted_iota(jnp.int32, (CHUNK, 128), 1) < 64
        tall_low = lax.broadcasted_iota(jnp.int32, (cols, 128), 1) < 64
        gains = [half_out[:, 0:128], half_out[:, 128:256]]

        def pull(v0, v1, vm, r, zero_low):
            mine = low if zero_low else jnp.logical_not(low)
            def both(a0, a1, am):
                s0 = jnp.sum(a0 + jnp.where(mine, am, 0.0), axis=1, keepdims=True)
                s1 = jnp.sum(a1 + jnp.where(mine, 0.0, am), axis=1, keepdims=True)
                return s0 * (1.0 / o), s1 * (1.0 / o)

            q0, q1 = both(v0 * v0, v1 * v1, vm * vm)
            i0, i1 = lax.rsqrt(q0 + EPS), lax.rsqrt(q1 + EPS)
            im = jnp.where(mine, i0, i1)
            out = []
            for v, i, g, k in ((v0, i0, gains[0], 0), (v1, i1, gains[0], 1), (vm, im, gains[1], 2)):
                s = v * i
                out.append((s, pulled(s, g, r[:, k * 128 : k * 128 + 128].astype(F32))))
            m0, m1 = both(*(s * d for s, d in out))
            mx = jnp.where(mine, m0, m1)
            return [i * (d - s * m) for (s, d), i, m in zip(out, (i0, i1, im), (m0, m1, mx))]

        def pull_row(k, odd):
            target, tmp = (g_odd, tmp_odd) if odd else (g_even, tmp_even)
            for c in range(0, cols, CHUNK):
                at = slice(c, c + CHUNK)
                if odd:
                    v0 = p0[k, at, 256:384] + p0[k + 1, at, 0:128]
                    v1 = p1[k, at, 256:384] + p1[k + 1, at, 0:128]
                    m0 = p0[k, at, 640:768] + p0[k + 1, at, 512:640]
                    m1 = p1[k, at, 640:768] + p1[k + 1, at, 512:640]
                else:
                    v0 = p0[k + 1, at, 128:256] + p0[k, at, 384:512]
                    v1 = p1[k + 1, at, 128:256] + p1[k, at, 384:512]
                    m0 = p1[k + 1, at, 512:640] + p1[k, at, 640:768]
                    m1 = p0[k + 1, at, 512:640] + p0[k, at, 640:768]
                out = pull(v0, v1, jnp.where(low, m0, m1), reward[2 * k + (0 if odd else 1), at], odd)
                for n, value in enumerate(out):
                    lanes = slice(n * 128, n * 128 + 128)
                    target[k, at, lanes] = value.astype(BF16)
                    tmp[k % 2, at, lanes] = value
            target[k, :, 384:512] = from_right(tmp[k % 2, :, 0:128]).astype(BF16)
            target[k, :, 512:640] = from_left(tmp[k % 2, :, 128:256]).astype(BF16)
            x = tmp[k % 2, :, 256:384]
            sides = (from_right(x), from_left(x)) if odd else (from_left(x), from_right(x))
            target[k, :, 640:768] = jnp.where(tall_low, *sides).astype(BF16)

        def block_row(k):
            for lanes in range(0, 384, 128):
                at, far = slice(lanes, lanes + 128), slice(lanes + 384, lanes + 512)
                x = t_odd[k + 1, :, at] + t_odd[k, :, far] + t_even[k, :, at] + t_even[k + 1, :, far]
                beside(back.at[k], 0, lanes, inside(x, k, 1, rows + 1), True)

        def hidden_pull(k):
            for c in range(0, cols, CHUNK):
                at = slice(c, c + CHUNK)
                v = hidden[k + 3, at].astype(F32)
                inv = lax.rsqrt(jnp.mean(v * v, axis=1, keepdims=True) + EPS)
                s = v * inv
                d = pulled(s, half_gain[...], act_grad[k, at])
                dv = inv * (d - s * jnp.mean(d * s, axis=1, keepdims=True))
                hid[k, at] = (back[k + 1, at, 384:768].astype(F32) + dv).astype(BF16)

        fine = rows + 3
        for k in range(rows + 4):
            state_row(k)
        for b in range(2):
            up_rows(1, rows + 4, b, 0)
            up_rows(0, rows + 3, b, 1)
            up_rows(0, rows + 4, b, 2)
        for k in range(fine):
            pull_row(k, True)
            pull_row(k, False)
        for odd in (True, False):
            down_rows(1 if odd else 0, fine if odd else fine - 1, odd, 0)
            down_rows(0, fine, odd, 1)
            down_rows(0 if odd else 1, fine - 1 if odd else fine, odd, 2)
        for k in range(rows + 2):
            block_row(k)
        for p in range(rows):
            lhs = jnp.concatenate([back[p + 2], back[p + 1], back[p]], axis=1)
            act_grad[p, :, 0:256] = mm(lhs, mid_t[:, 0:256])
        both = mm(
            back[1 : rows + 2].reshape((rows + 1) * cols, 1152),
            jnp.concatenate([mid_t[1152:2304, 256:384], mid_t[0:1152, 256:384]], axis=1),
        )
        rest = mm(back[0:rows].reshape(size, 1152), mid_t[2304:3456, 256:384])
        for p in range(rows):
            at, after = slice(p * cols, (p + 1) * cols), slice((p + 1) * cols, (p + 2) * cols)
            act_grad[p, :, 256:384] = both[at, :128] + both[after, 128:] + rest[at]
        for k in range(rows):
            hidden_pull(k)

        z = mm_t(w_in[...], hid[...].reshape(size, 384))
        place = lax.broadcasted_iota(jnp.int32, (chan, size), 1)
        col = lax.rem(place, cols)
        sums = []
        for i in range(3):
            z0, z1, z2 = (z[(i * 3 + j) * chan : (i * 3 + j + 1) * chan] for j in range(3))
            left = jnp.where(col == cols - 1, 0.0, pltpu.roll(z0, size - 1, 1))
            right = jnp.where(col == 0, 0.0, pltpu.roll(z2, 1, 1))
            sums.append(left + z1 + right)
        inner = sums[1]
        inner = inner + jnp.where(place < size - cols, pltpu.roll(sums[0], size - cols, 1), 0.0)
        inner = inner + jnp.where(place >= cols, pltpu.roll(sums[2], cols, 1), 0.0)
        lines[0:chan] = inner
        lines[chan : 2 * chan] = sums[0]
        lines[2 * chan : 3 * chan] = sums[2]
        per_row = count // 2
        for u in range(count):
            pair, piece = u // per_row, u % per_row
            parts = []
            for a in range(2):
                at = (2 * pair + a) * cols + piece * width
                parts.append(lines[0:chan, at : at + width])
            at = piece * width + (0 if pair else (rows - 1) * cols)
            first = chan if pair else 2 * chan
            parts.append(lines[first : first + chan, at : at + width])
            parts.append(jnp.zeros((chan, 128 - 3 * width), F32))
            payload[u] = jnp.concatenate(parts, axis=1).astype(BF16)

    return body


def placing(info, order, sel, count, width, tokens):
    piece = width // 2
    pair = info[3]
    lane = lax.broadcasted_iota(jnp.int32, (128, 4 * tokens), 0)
    column = lax.broadcasted_iota(jnp.int32, (128, 4 * tokens), 1)
    group = (lane >= width).astype(jnp.int32) + (lane >= 2 * width).astype(jnp.int32)
    w = lane - group * width
    part = jnp.where(group == 2, pair, group)
    fixed = (2 * part + (w & 1)) * tokens + (w >> 1) - column
    fixed = jnp.where(lane < 3 * width, fixed, -99999)

    def one(t):
        step = t + 1 - 2 * pair
        valid = jnp.logical_and(step >= 0, step < count)
        beside = jnp.where(valid, piece * order[jnp.clip(step, 0, count - 1)], -9999)
        begin = jnp.where(group == 2, beside, piece * order[t])
        sel[t // 2, t % 2 * 128 : t % 2 * 128 + 128] = (fixed + begin == 0).astype(F32).astype(BF16)

    return one


def place_body(count, chan, tokens):
    def body(sel, got, out):
        total = None
        for t in range(count // 2):
            x = mm(jnp.concatenate([got[2 * t], got[2 * t + 1]], axis=1), sel[t])
            total = x if total is None else total + x
        for k in range(4):
            out[k * chan : (k + 1) * chan] = total[:, k * tokens : (k + 1) * tokens]

    return body


def swaps(count):
    within = [(i, i ^ 1) for i in range(count)]
    across = [(0, 0), (count - 1, count - 1)]
    for i in range(1, count - 1, 2):
        across += [(i, i + 1), (i + 1, i)]
    return within, sorted(across)


def shards(
    latent, cached_latent, cached_features, reward_grad, conv_in_weight, conv_mid_weight, conv_up_weight, norm_gain, out_gain, shard_order
):
    count = lax.axis_size("tile")
    rows, cols, chan = latent.shape
    mid_chan = norm_gain.shape[0]
    o = out_gain.shape[0]
    tile = lax.axis_index("tile")
    info = jnp.stack(
        [tile % 2, (tile > 0).astype(jnp.int32), (tile < count - 1).astype(jnp.int32), (tile >= count // 2).astype(jnp.int32)]
    ).astype(jnp.int32)
    lat = jnp.transpose(latent, (0, 2, 1))
    lat_cached = jnp.transpose(cached_latent, (0, 1, 3, 2))
    reward_t = jnp.transpose(reward_grad, (0, 2, 1))
    up_t = jnp.transpose(conv_up_weight, (0, 1, 3, 2))
    mid = conv_mid_weight.reshape(3, 3, 3 * mid_chan, mid_chan)
    w_in = conv_in_weight.reshape(3, 3, 3 * chan, mid_chan)
    gain = 0.5 * norm_gain.reshape(1, mid_chan)
    gain_out = 0.5 * jnp.concatenate([out_gain, out_gain[128:]]).reshape(1, 256)
    within, across = swaps(count)
    size = rows * cols
    edge_rows = 3 * cols + 2 * chan * rows

    info, back_odd, back_even = call(
        taps_body,
        [((4,), jnp.int32), ((768, 768), BF16), ((768, 768), BF16)],
        1, 1, [], 1e10, 8, 1,
    )(info, up_t)

    own, send_even, send_odd = call(
        pack_body(rows, cols, o, chan),
        [((6, cols, 384), BF16), ((edge_rows, 384), BF16), ((edge_rows, 384), BF16)],
        1, 3, [], 1e10, 8,
    )(info, reward_t, lat, lat_cached)
    packed_even = lax.ppermute(send_even, "tile", within)
    packed_odd = lax.ppermute(send_odd, "tile", across)

    width = 2 * cols // count
    tokens = size // 4
    acc, part_even, part_odd, mid_t, sel, fwd, own_mid = call(
        cached_body(rows, cols, count, width, tokens, o),
        [
            ((rows + 4, cols, 384), F32), ((3 * cols, 384), BF16), ((3 * cols, 384), BF16), ((3456, 384), BF16),
            ((count // 2, 256, 4 * tokens), BF16), ((2, 768, 768), BF16), ((2, cols, 384), BF16),
        ],
        2, 5, [pltpu.VMEM((size, 2304), BF16), pltpu.VMEM((3, size, 384), F32)], 4e9, 14,
    )(info, shard_order, cached_features, mid, back_odd, back_even, reward_t)
    got_even = lax.ppermute(part_even, "tile", within)
    got_odd = lax.ppermute(part_odd, "tile", across)

    hidden, conv = call(
        current_body(rows, cols, chan),
        [((rows + 6, cols, 384), BF16), ((rows + 4, cols, 384), F32)],
        1, 7,
        [
            pltpu.VMEM((9 * rows * chan, 256), F32),
            pltpu.VMEM((3 * rows, 9 * chan, 256), BF16),
            pltpu.VMEM((rows + 6, cols, 1152), BF16),
            pltpu.VMEM((27 * chan, 384), BF16),
            pltpu.VMEM((2, cols, 384), F32),
        ],
        5e9, 14,
    )(info, lat, lat_cached, packed_even, packed_odd, w_in, mid, gain)

    (payload,) = call(
        back_body(rows, cols, chan, count, o),
        [((count, chan, 128), BF16)],
        1, 16,
        [
            pltpu.VMEM((2 * rows + 6, cols, 384), BF16),
            pltpu.VMEM((rows + 4, cols, 384), F32),
            pltpu.VMEM((rows + 4, cols, 768), F32),
            pltpu.VMEM((rows + 4, cols, 768), F32),
            pltpu.VMEM((rows + 3, cols, 768), BF16),
            pltpu.VMEM((rows + 3, cols, 768), BF16),
            pltpu.VMEM((rows + 4, cols, 1152), BF16),
            pltpu.VMEM((rows + 3, cols, 768), F32),
            pltpu.VMEM((rows + 3, cols, 768), F32),
            pltpu.VMEM((rows + 2, cols, 1152), BF16),
            pltpu.VMEM((rows, cols, 384), F32),
            pltpu.VMEM((rows, cols, 384), BF16),
            pltpu.VMEM((2, cols, 384), F32),
            pltpu.VMEM((2, cols, 384), F32),
            pltpu.VMEM((3 * chan, size), F32),
        ],
        8e9, 34,
    )(
        info, hidden, conv, acc, got_even, got_odd, packed_even, packed_odd, own, own_mid, fwd, back_odd, back_even, mid_t,
        w_in[2].reshape(9 * chan, mid_chan), gain, gain_out,
    )
    received = lax.all_to_all(payload, "tile", split_axis=0, concat_axis=0, tiled=True)
    (placed,) = call(place_body(count, chan, tokens), [((4 * chan, tokens), F32)], 0, 2, [], 1e7, 8)(sel, received)
    return placed.T


def solution(mesh):
    return jax.shard_map(
        shards,
        mesh=mesh,
        in_specs=(
            P(("prompt", "tile"), None, None),
            P(None, ("prompt", "tile"), None, None),
            P(None, ("prompt", "tile"), None, None),
            P(("prompt", "tile"), None, None),
            P(),
            P(),
            P(),
            P(),
            P(),
            P("prompt"),
        ),
        out_specs=P(("prompt", "tile"), None),
        check_vma=False,
    )
```

```python
import jax
import jax.numpy as jnp
from jax import lax
from jax.experimental import pallas as pl
from jax.experimental.pallas import tpu as pltpu
from jax.sharding import PartitionSpec as P

EPS = 1e-06
F32 = jnp.float32
BF16 = jnp.bfloat16
VM = pl.BlockSpec(memory_space=pltpu.VMEM)
SM = pl.BlockSpec(memory_space=pltpu.SMEM)


def weave(*groups):
    total = max(len(g) for g in groups)
    done = [0] * len(groups)
    for k in range(total):
        for n, g in enumerate(groups):
            while done[n] * total < (k + 1) * len(g):
                g[done[n]]()
                done[n] += 1


def steps(f, *keys):
    return [lambda key=key: f(*key) for key in keys]


def call(body, outs, n_smem, n_vmem, scratch, flops, limit, smem_outs=0):
    specs = [SM] * n_smem + [VM] * n_vmem
    return pl.pallas_call(
        body,
        out_shape=[jax.ShapeDtypeStruct(s, d) for s, d in outs],
        in_specs=specs,
        out_specs=[SM] * smem_outs + [VM] * (len(outs) - smem_outs),
        scratch_shapes=scratch,
        cost_estimate=pl.CostEstimate(flops=int(flops), bytes_accessed=2**20, transcendentals=0),
        compiler_params=pltpu.CompilerParams(vmem_limit_bytes=limit << 20),
    )


def mm(a, b):
    return jnp.dot(a, b, preferred_element_type=F32)


def mm_t(a, b):
    return lax.dot_general(a, b, (((1,), (1,)), ((), ())), preferred_element_type=F32)


def flag(info, k):
    return info[k].astype(F32)


def from_left(x):
    moved = pltpu.roll(x, 1, 0)
    first = lax.broadcasted_iota(jnp.int32, (8, x.shape[1]), 0) == 0
    return jnp.concatenate([jnp.where(first, 0.0, moved[:8]), moved[8:]], axis=0)


def from_right(x):
    size = x.shape[0]
    moved = pltpu.roll(x, size - 1, 0)
    last = lax.broadcasted_iota(jnp.int32, (8, x.shape[1]), 0) == 7
    return jnp.concatenate([moved[: size - 8], jnp.where(last, 0.0, moved[size - 8 :])], axis=0)


def beside(target, base, lanes, x, ahead):
    sides = (from_right, from_left) if ahead else (from_left, from_right)
    for group, value in enumerate((sides[0](x), x, sides[1](x))):
        at = base + group * 384 + lanes
        target[:, at : at + 128] = value.astype(BF16)


CHUNK = 32


def picker(cols, o):
    half = o - 128
    x_index = lax.broadcasted_iota(jnp.int32, (cols, 2 * cols), 1)
    w_index = lax.broadcasted_iota(jnp.int32, (cols, 2 * cols), 0)
    pick = [(x_index == 2 * w_index + b).astype(F32).astype(BF16) for b in (0, 1)]
    zeros = jnp.zeros((128 - half, 2 * cols), BF16)

    def one(reward, f, own, k):
        r = reward[f]
        first, rest = r[:128], r[128:]
        low = jnp.concatenate([first, rest, zeros], axis=0)
        high = jnp.concatenate([first, zeros, rest], axis=0)
        sides = (low, high) if f % 2 else (high, low)
        d0, d1 = mm_t(pick[0], sides[0]), mm_t(pick[1], sides[1])
        own[k, :, 0:128] = d0[:, :128].astype(BF16)
        own[k, :, 128:256] = d1[:, :128].astype(BF16)
        own[k, :, 256:384] = (d0[:, 128:] + d1[:, 128:]).astype(BF16)

    return one


def pack_body(rows, cols, o, chan):
    def body(info, reward, latent, cached, own, send_even, send_odd):
        one = picker(cols, o)
        for k in range(6):
            one(reward, k if k < 3 else 2 * rows - 6 + k, own, k)
        base = 3 * cols
        per = chan * rows
        for send, last in ((send_even, 1 - info[0]), (send_odd, info[0])):
            begin = last * 3
            for k in range(3):
                send[k * cols : (k + 1) * cols] = own[begin + k]
            for t in range(3):
                src = cached[t] if t < 2 else latent[...]
                lat = src.reshape(per, cols)
                send[base : base + per, t * 128 : t * 128 + 128] = lat[:, :128]
                send[base + per : base + 2 * per, t * 128 : t * 128 + cols - 128] = lat[:, 128:]

    return body


def home(targets, q, p, tile):
    block, second = ((1, 1), (0, 0), (0, 1), (1, 0))[p]
    target, side = targets[q]
    if tile < 2:
        row = block * 384 + second * 128 + tile * 64
    else:
        row = block * 384 + 256 + 64 * (second if q % 2 == 0 else 1 - second)
    return target, row, side * 384


def turning(back_odd, back_even, fwd):
    targets = ((back_odd, 1), (back_even, 0), (back_odd, 0), (back_even, 1))

    def tap_tile(q, p, tile, lanes):
        target, row, side = home(targets, q, p, tile)
        return target[row : row + 64, side + lanes : side + lanes + 128]

    def one(b, side, lanes):
        p = ((3, 1), (2, 0))[b][side]
        at = slice(side * 384 + lanes, side * 384 + lanes + 128)
        for q in range(4):
            both = jnp.concatenate([tap_tile(q, p, 0, lanes), tap_tile(q, p, 1, lanes)], axis=0)
            fwd[b, at, q * 128 : q * 128 + 128] = both.T
        for half in range(2):
            pair = (2 * half, 2 * half + 1) if b == 0 else (2 * half + 1, 2 * half)
            both = jnp.concatenate([tap_tile(q, p, 2, lanes) for q in pair], axis=0)
            fwd[b, at, 512 + half * 128 : 640 + half * 128] = both.T

    return steps(one, *[(b, side, lanes) for b in range(2) for side in range(2) for lanes in range(0, 384, 128)])


def taps_body(info, up, info_out, back_odd, back_even):
    for k in range(4):
        info_out[k] = info[k]

    parts = ((2,), (1, 2), (0, 1), (0,))
    targets = ((back_odd, 1), (back_even, 0), (back_odd, 0), (back_even, 1))

    for tile in range(3):
        for lanes in range(0, 384, 128):
            w = [[up[i, j, tile * 64 : tile * 64 + 64, lanes : lanes + 128].astype(F32) for j in range(3)] for i in range(3)]
            for q in range(4):
                c = [w[parts[q][0]][j] + w[parts[q][1]][j] if len(parts[q]) > 1 else w[parts[q][0]][j] for j in range(3)]
                for p, tap in enumerate((c[2], c[1] + c[2], c[0] + c[1], c[0])):
                    target, row, side = home(targets, q, p, tile)
                    target[row : row + 64, side + lanes : side + lanes + 128] = tap.astype(BF16)


def cached_body(rows, cols, count, width, tokens, o):
    size = rows * cols

    def body(
        info, order, features, mid, back_odd, back_even, reward, acc, send_even, send_odd, mid_t, sel, fwd, own, wide, parts
    ):
        for t in range(2):
            for r in range(rows):
                for lanes in range(0, 384, 128):
                    x = features[t, r, :, lanes : lanes + 128].astype(F32)
                    beside(wide.at[r * cols : (r + 1) * cols], t * 1152, lanes, x, False)
        def product(i, lanes):
            parts[i, :, lanes] = mm(wide[...], jnp.concatenate([mid[0, i, :, lanes], mid[1, i, :, lanes]], axis=0))

        def double():
            left = jnp.concatenate([mid[0, 0, :, 256:384], mid[1, 0, :, 256:384]], axis=0)
            right = jnp.concatenate([mid[0, 1, :, 256:384], mid[1, 1, :, 256:384]], axis=0)
            both = mm(wide[...], jnp.concatenate([left, right], axis=1))
            parts[0, :, 256:384] = both[:, :128]
            parts[1, :, 256:384] = both[:, 128:]

        def turn(i, j):
            at = (i * 3 + j) * 384
            mid_t[at : at + 384] = mid[2, i, j * 384 : (j + 1) * 384].T

        most, rest = slice(0, 256), slice(256, 384)
        products = steps(product, (0, most), (1, most)) + steps(double, ()) + steps(product, (2, most), (2, rest))
        one = picker(cols, o)
        others = steps(turn, *[(i, j) for i in range(3) for j in range(3)])
        others += turning(back_odd, back_even, fwd)
        others += steps(placing(info, order, sel, count, width, tokens), *[(t,) for t in range(count)])
        others += steps(one, (reward, rows - 1, own, 0), (reward, rows, own, 1))
        weave(others, products)
        for k in range(rows + 4):
            total = jnp.zeros((cols, 384), F32)
            for i in range(3):
                r = k - 3 + i
                if 0 <= r < rows:
                    total = total + parts[i, r * cols : (r + 1) * cols]
            acc[k] = total
        for send, last in ((send_even, 1 - info[0]), (send_odd, info[0])):
            for k in range(3):
                send[k * cols : (k + 1) * cols] = acc[1 + last * 3 + k].astype(BF16)

    return body


def current_body(rows, cols, chan):
    per = chan * rows
    base = 3 * cols

    def body(info, latent, cached, got_even, got_odd, w_in, mid, half_gain, hidden, conv, lat, tall, wide, w_order, plain):
        even = info[0] == 0
        lat[...] = jnp.zeros_like(lat)

        def fill(first_row, got, ok):
            scale = ok.astype(F32)
            for t in range(3):
                x = got[base : base + per, t * 128 : t * 128 + 128].astype(F32) * scale
                y = got[base + per : base + 2 * per, t * 128 : t * 128 + cols - 128].astype(F32) * scale
                for r in range(rows):
                    at = pl.ds((first_row + r) * 3 * chan + t * chan, chan)
                    lat[at, 0:128] = x[r * chan : (r + 1) * chan]
                    lat[at, 128:cols] = y[r * chan : (r + 1) * chan]

        @pl.when(even)
        def _():
            fill(0, got_odd, info[1])
            fill(2 * rows, got_even, info[2])

        @pl.when(jnp.logical_not(even))
        def _():
            fill(0, got_even, info[1])
            fill(2 * rows, got_odd, info[2])

        for t in range(3):
            for r in range(rows):
                at = pl.ds((rows + r) * 3 * chan + t * chan, chan)
                lat[at, 0:cols] = (cached[t, r] if t < 2 else latent[r]).astype(F32)

        for r in range(3 * rows):
            for t in range(3):
                x = lat[pl.ds((r * 3 + t) * chan, chan), :]
                at = t * 3 * chan
                tall[r, at : at + chan] = pltpu.roll(x, 1, 1).astype(BF16)
                tall[r, at + chan : at + 2 * chan] = x.astype(BF16)
                tall[r, at + 2 * chan : at + 3 * chan] = pltpu.roll(x, 255, 1).astype(BF16)
        for i in range(3):
            for t in range(3):
                at = (i * 3 + t) * 3 * chan
                w_order[at : at + 3 * chan] = w_in[t, i]

        def hidden_row(k):
            lhs = tall[k : k + 3].reshape(27 * chan, 256)[:, 0:cols]
            h = lax.dot_general(lhs, w_order[...], (((0,), (0,)), ((), ())), preferred_element_type=F32)
            plain[k % 2] = h
            for c in range(0, cols, CHUNK):
                at = slice(c, c + CHUNK)
                v = plain[k % 2, at].astype(BF16)
                hidden[k, at] = v
                v = v.astype(F32)
                inv = lax.rsqrt(jnp.mean(v * v, axis=1, keepdims=True) + EPS)
                half = v * inv * half_gain[...]
                act = half * (jnp.tanh(half) + 1.0)
                if k < 3:
                    act = act * flag(info, 1)
                if k >= rows + 3:
                    act = act * flag(info, 2)
                plain[k % 2, at] = act
            for lanes in range(0, 384, 128):
                beside(wide.at[k], 0, lanes, plain[k % 2, :, lanes : lanes + 128], False)

        def conv_rows(p, number):
            lhs = [wide[p + i : p + i + number].reshape(number * cols, 1152) for i in range(3)]
            total = mm(jnp.concatenate(lhs, axis=1), mid[2, :, :, 0:256].reshape(3456, 256))
            conv[p : p + number, :, 0:256] = total.reshape(number, cols, 256)

        for k in range(4):
            hidden_row(k)
        for p in range(0, rows + 4, 2):
            conv_rows(p, 2)
            for k in (p + 4, p + 5):
                if k < rows + 6:
                    hidden_row(k)
        both = mm(
            wide[0 : rows + 5].reshape((rows + 5) * cols, 1152),
            jnp.concatenate([mid[2, 0, :, 256:384], mid[2, 1, :, 256:384]], axis=1),
        )
        rest = mm(wide[2 : rows + 6].reshape((rows + 4) * cols, 1152), mid[2, 2, :, 256:384])
        for p in range(rows + 4):
            at, after = slice(p * cols, (p + 1) * cols), slice((p + 1) * cols, (p + 2) * cols)
            conv[p, :, 256:384] = both[at, :128] + both[after, 128:] + rest[at]

    return body


def pulled(s, half_gain, grad):
    h = s * half_gain
    t = jnp.tanh(h)
    return (grad * half_gain) * ((1.0 + t) * (1.0 + h * (1.0 - t)))


def back_body(rows, cols, chan, count, o):
    size = rows * cols
    width = 2 * cols // count

    def body(
        info, hidden, conv, acc, got_even, got_odd, packed_even, packed_odd, own, own_mid, fwd, back_odd, back_even, mid_t, w_in, half_gain,
        half_out, payload, reward, edge, p0, p1, g_odd, g_even, wide, t_odd, t_even, back, act_grad, hid, tmp_odd, tmp_even, lines,
    ):
        even = info[0] == 0
        top, bottom = flag(info, 1), flag(info, 2)

        def take(got, packed, before):
            ok = top if before else bottom
            place = 0 if before else rows + 1
            for k in range(3):
                at = slice(k * cols, (k + 1) * cols)
                edge[place + k] = got[at].astype(F32) * ok
                reward[k if before else 2 * rows + 3 + k] = (packed[at].astype(F32) * ok).astype(BF16)

        @pl.when(even)
        def _():
            take(got_odd, packed_odd, True)
            take(got_even, packed_even, False)

        @pl.when(jnp.logical_not(even))
        def _():
            take(got_even, packed_even, True)
            take(got_odd, packed_odd, False)

        reward[3:6] = own[0:3]
        reward[6 : 2 * rows] = own_mid[...]
        reward[2 * rows : 2 * rows + 3] = own[3:6]

        def inside(x, k, first, last):
            return x * top if k < first else x * bottom if k >= last else x

        def state_row(k):
            for lanes in range(0, 384, 128):
                at = slice(lanes, lanes + 128)
                x = hidden[k + 1, :, at].astype(F32) + conv[k, :, at]
                if 1 <= k <= rows + 2:
                    x = x + acc[k, :, at]
                if k < 3 or k > rows:
                    x = x + edge[k, :, at]
                beside(wide.at[k], 0, lanes, inside(x, k, 2, rows + 2), False)

        def up_rows(first, last, b, n):
            count = last - first
            x = wide[first:last, :, b * 384 : b * 384 + 768].reshape(count * cols, 768)
            lanes = slice(n * 256, n * 256 + 256)
            (p0, p1)[b][first:last, :, lanes] = mm(x, fwd[b, :, lanes]).reshape(count, cols, 256)

        def down_rows(first, last, odd, n):
            count = last - first
            g, kernel, t = (g_odd, back_odd, t_odd) if odd else (g_even, back_even, t_even)
            lanes = slice(n * 256, n * 256 + 256)
            x = g[first:last].reshape(count * cols, 768)
            t[first:last, :, lanes] = mm(x, kernel[:, lanes]).reshape(count, cols, 256)

        low = lax.broadcasted_iota(jnp.int32, (CHUNK, 128), 1) < 64
        tall_low = lax.broadcasted_iota(jnp.int32, (cols, 128), 1) < 64
        gains = [half_out[:, 0:128], half_out[:, 128:256]]

        def pull(v0, v1, vm, r, zero_low):
            mine = low if zero_low else jnp.logical_not(low)
            def both(a0, a1, am):
                s0 = jnp.sum(a0 + jnp.where(mine, am, 0.0), axis=1, keepdims=True)
                s1 = jnp.sum(a1 + jnp.where(mine, 0.0, am), axis=1, keepdims=True)
                return s0 * (1.0 / o), s1 * (1.0 / o)

            q0, q1 = both(v0 * v0, v1 * v1, vm * vm)
            i0, i1 = lax.rsqrt(q0 + EPS), lax.rsqrt(q1 + EPS)
            im = jnp.where(mine, i0, i1)
            out = []
            for v, i, g, k in ((v0, i0, gains[0], 0), (v1, i1, gains[0], 1), (vm, im, gains[1], 2)):
                s = v * i
                out.append((s, pulled(s, g, r[:, k * 128 : k * 128 + 128].astype(F32))))
            m0, m1 = both(*(s * d for s, d in out))
            mx = jnp.where(mine, m0, m1)
            return [i * (d - s * m) for (s, d), i, m in zip(out, (i0, i1, im), (m0, m1, mx))]

        def pull_row(k, odd):
            target, tmp = (g_odd, tmp_odd) if odd else (g_even, tmp_even)
            for c in range(0, cols, CHUNK):
                at = slice(c, c + CHUNK)
                if odd:
                    v0 = p0[k, at, 256:384] + p0[k + 1, at, 0:128]
                    v1 = p1[k, at, 256:384] + p1[k + 1, at, 0:128]
                    m0 = p0[k, at, 640:768] + p0[k + 1, at, 512:640]
                    m1 = p1[k, at, 640:768] + p1[k + 1, at, 512:640]
                else:
                    v0 = p0[k + 1, at, 128:256] + p0[k, at, 384:512]
                    v1 = p1[k + 1, at, 128:256] + p1[k, at, 384:512]
                    m0 = p1[k + 1, at, 512:640] + p1[k, at, 640:768]
                    m1 = p0[k + 1, at, 512:640] + p0[k, at, 640:768]
                out = pull(v0, v1, jnp.where(low, m0, m1), reward[2 * k + (0 if odd else 1), at], odd)
                for n, value in enumerate(out):
                    lanes = slice(n * 128, n * 128 + 128)
                    target[k, at, lanes] = value.astype(BF16)
                    tmp[k % 2, at, lanes] = value
            target[k, :, 384:512] = from_right(tmp[k % 2, :, 0:128]).astype(BF16)
            target[k, :, 512:640] = from_left(tmp[k % 2, :, 128:256]).astype(BF16)
            x = tmp[k % 2, :, 256:384]
            sides = (from_right(x), from_left(x)) if odd else (from_left(x), from_right(x))
            target[k, :, 640:768] = jnp.where(tall_low, *sides).astype(BF16)

        def block_row(k):
            for lanes in range(0, 384, 128):
                at, far = slice(lanes, lanes + 128), slice(lanes + 384, lanes + 512)
                x = t_odd[k + 1, :, at] + t_odd[k, :, far] + t_even[k, :, at] + t_even[k + 1, :, far]
                beside(back.at[k], 0, lanes, inside(x, k, 1, rows + 1), True)

        def hidden_pull(k):
            for c in range(0, cols, CHUNK):
                at = slice(c, c + CHUNK)
                v = hidden[k + 3, at].astype(F32)
                inv = lax.rsqrt(jnp.mean(v * v, axis=1, keepdims=True) + EPS)
                s = v * inv
                d = pulled(s, half_gain[...], act_grad[k, at])
                dv = inv * (d - s * jnp.mean(d * s, axis=1, keepdims=True))
                hid[k, at] = (back[k + 1, at, 384:768].astype(F32) + dv).astype(BF16)

        fine = rows + 3
        def ups(first, last):
            for b in range(2):
                up_rows(max(first, 1), last, b, 0)
                up_rows(first, min(last, rows + 3), b, 1)
                up_rows(first, last, b, 2)

        def downs(first, last):
            for odd in (True, False):
                down_rows(max(first, 1) if odd else first, last if odd else min(last, fine - 1), odd, 0)
                down_rows(first, last, odd, 1)
                down_rows(first if odd else max(first, 1), min(last, fine - 1) if odd else last, odd, 2)

        def states(first, last):
            for k in range(first, last):
                state_row(k)

        def pulls(first, last):
            for k in range(first, last):
                pull_row(k, True)
                pull_row(k, False)

        states(0, rows)
        ups(0, 2)
        states(rows, rows + 2)
        ups(2, rows)
        states(rows + 2, rows + 4)
        ups(rows, rows + 2)
        pulls(0, 2)
        ups(rows + 2, rows + 4)
        pulls(2, rows)
        downs(0, 2)
        pulls(rows, rows + 2)
        downs(2, rows)
        pulls(rows + 2, fine)
        downs(rows, fine)
        for k in range(rows + 2):
            block_row(k)
        lhs = [back[2 - i : 2 - i + rows].reshape(size, 1152) for i in range(3)]
        act_grad[:, :, 0:256] = mm(jnp.concatenate(lhs, axis=1), mid_t[:, 0:256]).reshape(rows, cols, 256)
        both = mm(
            back[1 : rows + 2].reshape((rows + 1) * cols, 1152),
            jnp.concatenate([mid_t[1152:2304, 256:384], mid_t[0:1152, 256:384]], axis=1),
        )
        rest = mm(back[0:rows].reshape(size, 1152), mid_t[2304:3456, 256:384])
        for p in range(rows):
            at, after = slice(p * cols, (p + 1) * cols), slice((p + 1) * cols, (p + 2) * cols)
            act_grad[p, :, 256:384] = both[at, :128] + both[after, 128:] + rest[at]
        for k in range(rows):
            hidden_pull(k)

        z = mm_t(w_in[...], hid[...].reshape(size, 384))
        place = lax.broadcasted_iota(jnp.int32, (chan, size), 1)
        col = lax.rem(place, cols)
        sums = []
        for i in range(3):
            z0, z1, z2 = (z[(i * 3 + j) * chan : (i * 3 + j + 1) * chan] for j in range(3))
            left = jnp.where(col == cols - 1, 0.0, pltpu.roll(z0, size - 1, 1))
            right = jnp.where(col == 0, 0.0, pltpu.roll(z2, 1, 1))
            sums.append(left + z1 + right)
        inner = sums[1]
        inner = inner + jnp.where(place < size - cols, pltpu.roll(sums[0], size - cols, 1), 0.0)
        inner = inner + jnp.where(place >= cols, pltpu.roll(sums[2], cols, 1), 0.0)
        lines[0:chan] = inner
        lines[chan : 2 * chan] = sums[0]
        lines[2 * chan : 3 * chan] = sums[2]
        per_row = count // 2
        for u in range(count):
            pair, piece = u // per_row, u % per_row
            parts = []
            for a in range(2):
                at = (2 * pair + a) * cols + piece * width
                parts.append(lines[0:chan, at : at + width])
            at = piece * width + (0 if pair else (rows - 1) * cols)
            first = chan if pair else 2 * chan
            parts.append(lines[first : first + chan, at : at + width])
            parts.append(jnp.zeros((chan, 128 - 3 * width), F32))
            payload[u] = jnp.concatenate(parts, axis=1).astype(BF16)

    return body


def placing(info, order, sel, count, width, tokens):
    piece = width // 2
    pair = info[3]
    lane = lax.broadcasted_iota(jnp.int32, (128, 4 * tokens), 0)
    column = lax.broadcasted_iota(jnp.int32, (128, 4 * tokens), 1)
    group = (lane >= width).astype(jnp.int32) + (lane >= 2 * width).astype(jnp.int32)
    w = lane - group * width
    part = jnp.where(group == 2, pair, group)
    fixed = (2 * part + (w & 1)) * tokens + (w >> 1) - column
    fixed = jnp.where(lane < 3 * width, fixed, -99999)

    def one(t):
        step = t + 1 - 2 * pair
        valid = jnp.logical_and(step >= 0, step < count)
        beside = jnp.where(valid, piece * order[jnp.clip(step, 0, count - 1)], -9999)
        begin = jnp.where(group == 2, beside, piece * order[t])
        sel[t // 2, t % 2 * 128 : t % 2 * 128 + 128] = (fixed + begin == 0).astype(F32).astype(BF16)

    return one


def place_body(count, chan, tokens):
    def body(sel, got, out):
        total = None
        for t in range(count // 2):
            x = mm(jnp.concatenate([got[2 * t], got[2 * t + 1]], axis=1), sel[t])
            total = x if total is None else total + x
        for k in range(4):
            out[k * chan : (k + 1) * chan] = total[:, k * tokens : (k + 1) * tokens]

    return body


def swaps(count):
    within = [(i, i ^ 1) for i in range(count)]
    across = [(0, 0), (count - 1, count - 1)]
    for i in range(1, count - 1, 2):
        across += [(i, i + 1), (i + 1, i)]
    return within, sorted(across)


def shards(
    latent, cached_latent, cached_features, reward_grad, conv_in_weight, conv_mid_weight, conv_up_weight, norm_gain, out_gain, shard_order
):
    count = lax.axis_size("tile")
    rows, cols, chan = latent.shape
    mid_chan = norm_gain.shape[0]
    o = out_gain.shape[0]
    tile = lax.axis_index("tile")
    info = jnp.stack(
        [tile % 2, (tile > 0).astype(jnp.int32), (tile < count - 1).astype(jnp.int32), (tile >= count // 2).astype(jnp.int32)]
    ).astype(jnp.int32)
    lat = jnp.transpose(latent, (0, 2, 1))
    lat_cached = jnp.transpose(cached_latent, (0, 1, 3, 2))
    reward_t = jnp.transpose(reward_grad, (0, 2, 1))
    up_t = jnp.transpose(conv_up_weight, (0, 1, 3, 2))
    mid = conv_mid_weight.reshape(3, 3, 3 * mid_chan, mid_chan)
    w_in = conv_in_weight.reshape(3, 3, 3 * chan, mid_chan)
    gain = 0.5 * norm_gain.reshape(1, mid_chan)
    gain_out = 0.5 * jnp.concatenate([out_gain, out_gain[128:]]).reshape(1, 256)
    within, across = swaps(count)
    size = rows * cols
    edge_rows = 3 * cols + 2 * chan * rows

    info, back_odd, back_even = call(
        taps_body,
        [((4,), jnp.int32), ((768, 768), BF16), ((768, 768), BF16)],
        1, 1, [], 1e10, 8, 1,
    )(info, up_t)

    own, send_even, send_odd = call(
        pack_body(rows, cols, o, chan),
        [((6, cols, 384), BF16), ((edge_rows, 384), BF16), ((edge_rows, 384), BF16)],
        1, 3, [], 1e10, 8,
    )(info, reward_t, lat, lat_cached)
    packed_even = lax.ppermute(send_even, "tile", within)
    packed_odd = lax.ppermute(send_odd, "tile", across)

    width = 2 * cols // count
    tokens = size // 4
    acc, part_even, part_odd, mid_t, sel, fwd, own_mid = call(
        cached_body(rows, cols, count, width, tokens, o),
        [
            ((rows + 4, cols, 384), F32), ((3 * cols, 384), BF16), ((3 * cols, 384), BF16), ((3456, 384), BF16),
            ((count // 2, 256, 4 * tokens), BF16), ((2, 768, 768), BF16), ((2, cols, 384), BF16),
        ],
        2, 5, [pltpu.VMEM((size, 2304), BF16), pltpu.VMEM((3, size, 384), F32)], 4e9, 14,
    )(info, shard_order, cached_features, mid, back_odd, back_even, reward_t)
    got_even = lax.ppermute(part_even, "tile", within)
    got_odd = lax.ppermute(part_odd, "tile", across)

    hidden, conv = call(
        current_body(rows, cols, chan),
        [((rows + 6, cols, 384), BF16), ((rows + 4, cols, 384), F32)],
        1, 7,
        [
            pltpu.VMEM((9 * rows * chan, 256), F32),
            pltpu.VMEM((3 * rows, 9 * chan, 256), BF16),
            pltpu.VMEM((rows + 6, cols, 1152), BF16),
            pltpu.VMEM((27 * chan, 384), BF16),
            pltpu.VMEM((2, cols, 384), F32),
        ],
        5e9, 14,
    )(info, lat, lat_cached, packed_even, packed_odd, w_in, mid, gain)

    (payload,) = call(
        back_body(rows, cols, chan, count, o),
        [((count, chan, 128), BF16)],
        1, 16,
        [
            pltpu.VMEM((2 * rows + 6, cols, 384), BF16),
            pltpu.VMEM((rows + 4, cols, 384), F32),
            pltpu.VMEM((rows + 4, cols, 768), F32),
            pltpu.VMEM((rows + 4, cols, 768), F32),
            pltpu.VMEM((rows + 3, cols, 768), BF16),
            pltpu.VMEM((rows + 3, cols, 768), BF16),
            pltpu.VMEM((rows + 4, cols, 1152), BF16),
            pltpu.VMEM((rows + 3, cols, 768), F32),
            pltpu.VMEM((rows + 3, cols, 768), F32),
            pltpu.VMEM((rows + 2, cols, 1152), BF16),
            pltpu.VMEM((rows, cols, 384), F32),
            pltpu.VMEM((rows, cols, 384), BF16),
            pltpu.VMEM((2, cols, 384), F32),
            pltpu.VMEM((2, cols, 384), F32),
            pltpu.VMEM((3 * chan, size), F32),
        ],
        8e9, 34,
    )(
        info, hidden, conv, acc, got_even, got_odd, packed_even, packed_odd, own, own_mid, fwd, back_odd, back_even, mid_t,
        w_in[2].reshape(9 * chan, mid_chan), gain, gain_out,
    )
    received = lax.all_to_all(payload, "tile", split_axis=0, concat_axis=0, tiled=True)
    (placed,) = call(place_body(count, chan, tokens), [((4 * chan, tokens), F32)], 0, 2, [], 1e7, 8)(sel, received)
    return placed.T


def solution(mesh):
    return jax.shard_map(
        shards,
        mesh=mesh,
        in_specs=(
            P(("prompt", "tile"), None, None),
            P(None, ("prompt", "tile"), None, None),
            P(None, ("prompt", "tile"), None, None),
            P(("prompt", "tile"), None, None),
            P(),
            P(),
            P(),
            P(),
            P(),
            P("prompt"),
        ),
        out_specs=P(("prompt", "tile"), None),
        check_vma=False,
    )
```

```python
import jax
import jax.numpy as jnp
from jax import lax
from jax.experimental import pallas as pl
from jax.experimental.pallas import tpu as pltpu
from jax.sharding import PartitionSpec as P

EPS = 1e-06
F32 = jnp.float32
BF16 = jnp.bfloat16
VM = pl.BlockSpec(memory_space=pltpu.VMEM)
SM = pl.BlockSpec(memory_space=pltpu.SMEM)


def weave(*groups):
    total = max(len(g) for g in groups)
    done = [0] * len(groups)
    for k in range(total):
        for n, g in enumerate(groups):
            while done[n] * total < (k + 1) * len(g):
                g[done[n]]()
                done[n] += 1


def steps(f, *keys):
    return [lambda key=key: f(*key) for key in keys]


def call(body, outs, n_smem, n_vmem, scratch, flops, limit, smem_outs=0):
    specs = [SM] * n_smem + [VM] * n_vmem
    return pl.pallas_call(
        body,
        out_shape=[jax.ShapeDtypeStruct(s, d) for s, d in outs],
        in_specs=specs,
        out_specs=[SM] * smem_outs + [VM] * (len(outs) - smem_outs),
        scratch_shapes=scratch,
        cost_estimate=pl.CostEstimate(flops=int(flops), bytes_accessed=2**20, transcendentals=0),
        compiler_params=pltpu.CompilerParams(vmem_limit_bytes=limit << 20),
    )


def mm(a, b):
    return jnp.dot(a, b, preferred_element_type=F32)


def mm_t(a, b):
    return lax.dot_general(a, b, (((1,), (1,)), ((), ())), preferred_element_type=F32)


def flag(info, k):
    return info[k].astype(F32)


def from_left(x):
    moved = pltpu.roll(x, 1, 0)
    first = lax.broadcasted_iota(jnp.int32, (8, x.shape[1]), 0) == 0
    return jnp.concatenate([jnp.where(first, 0.0, moved[:8]), moved[8:]], axis=0)


def from_right(x):
    size = x.shape[0]
    moved = pltpu.roll(x, size - 1, 0)
    last = lax.broadcasted_iota(jnp.int32, (8, x.shape[1]), 0) == 7
    return jnp.concatenate([moved[: size - 8], jnp.where(last, 0.0, moved[size - 8 :])], axis=0)


def beside(target, base, lanes, x, ahead):
    sides = (from_right, from_left) if ahead else (from_left, from_right)
    for group, value in enumerate((sides[0](x), x, sides[1](x))):
        at = base + group * 384 + lanes
        target[:, at : at + 128] = value.astype(BF16)


CHUNK = 32


def picker(cols, o):
    half = o - 128
    x_index = lax.broadcasted_iota(jnp.int32, (cols, 2 * cols), 1)
    w_index = lax.broadcasted_iota(jnp.int32, (cols, 2 * cols), 0)
    pick = [(x_index == 2 * w_index + b).astype(F32).astype(BF16) for b in (0, 1)]
    zeros = jnp.zeros((128 - half, 2 * cols), BF16)

    def one(reward, f, own, k):
        r = reward[f]
        first, rest = r[:128], r[128:]
        low = jnp.concatenate([first, rest, zeros], axis=0)
        high = jnp.concatenate([first, zeros, rest], axis=0)
        sides = (low, high) if f % 2 else (high, low)
        d0, d1 = mm_t(pick[0], sides[0]), mm_t(pick[1], sides[1])
        own[k, :, 0:128] = d0[:, :128].astype(BF16)
        own[k, :, 128:256] = d1[:, :128].astype(BF16)
        own[k, :, 256:384] = (d0[:, 128:] + d1[:, 128:]).astype(BF16)

    return one


def pack_body(rows, cols, o, chan):
    def body(info, reward, latent, cached, own, send_even, send_odd):
        one = picker(cols, o)
        for k in range(6):
            one(reward, k if k < 3 else 2 * rows - 6 + k, own, k)
        base = 3 * cols
        per = chan * rows
        for send, last in ((send_even, 1 - info[0]), (send_odd, info[0])):
            begin = last * 3
            for k in range(3):
                send[k * cols : (k + 1) * cols] = own[begin + k]
            for t in range(3):
                src = cached[t] if t < 2 else latent[...]
                lat = src.reshape(per, cols)
                send[base : base + per, t * 128 : t * 128 + 128] = lat[:, :128]
                send[base + per : base + 2 * per, t * 128 : t * 128 + cols - 128] = lat[:, 128:]

    return body


def home(targets, q, p, tile):
    block, second = ((1, 1), (0, 0), (0, 1), (1, 0))[p]
    target, side = targets[q]
    if tile < 2:
        row = block * 384 + second * 128 + tile * 64
    else:
        row = block * 384 + 256 + 64 * (second if q % 2 == 0 else 1 - second)
    return target, row, side * 384


def turning(back_odd, back_even, fwd):
    targets = ((back_odd, 1), (back_even, 0), (back_odd, 0), (back_even, 1))

    def tap_tile(q, p, tile, lanes):
        target, row, side = home(targets, q, p, tile)
        return target[row : row + 64, side + lanes : side + lanes + 128]

    def one(b, side, lanes):
        p = ((3, 1), (2, 0))[b][side]
        at = slice(side * 384 + lanes, side * 384 + lanes + 128)
        for q in range(4):
            both = jnp.concatenate([tap_tile(q, p, 0, lanes), tap_tile(q, p, 1, lanes)], axis=0)
            fwd[b, at, q * 128 : q * 128 + 128] = both.T
        for half in range(2):
            pair = (2 * half, 2 * half + 1) if b == 0 else (2 * half + 1, 2 * half)
            both = jnp.concatenate([tap_tile(q, p, 2, lanes) for q in pair], axis=0)
            fwd[b, at, 512 + half * 128 : 640 + half * 128] = both.T

    return steps(one, *[(b, side, lanes) for b in range(2) for side in range(2) for lanes in range(0, 384, 128)])


def taps_body(info, up, info_out, back_odd, back_even):
    for k in range(4):
        info_out[k] = info[k]

    parts = ((2,), (1, 2), (0, 1), (0,))
    targets = ((back_odd, 1), (back_even, 0), (back_odd, 0), (back_even, 1))

    for tile in range(3):
        for lanes in range(0, 384, 128):
            w = [[up[i, j, tile * 64 : tile * 64 + 64, lanes : lanes + 128].astype(F32) for j in range(3)] for i in range(3)]
            for q in range(4):
                c = [w[parts[q][0]][j] + w[parts[q][1]][j] if len(parts[q]) > 1 else w[parts[q][0]][j] for j in range(3)]
                for p, tap in enumerate((c[2], c[1] + c[2], c[0] + c[1], c[0])):
                    target, row, side = home(targets, q, p, tile)
                    target[row : row + 64, side + lanes : side + lanes + 128] = tap.astype(BF16)


def cached_body(rows, cols, count, width, tokens, o):
    size = rows * cols

    def body(
        info, order, features, mid, back_odd, back_even, reward, acc, send_even, send_odd, mid_t, sel, fwd, own, wide, parts
    ):
        for t in range(2):
            for r in range(rows):
                for lanes in range(0, 384, 128):
                    x = features[t, r, :, lanes : lanes + 128].astype(F32)
                    beside(wide.at[r * cols : (r + 1) * cols], t * 1152, lanes, x, False)
        def product(i, lanes):
            parts[i, :, lanes] = mm(wide[...], jnp.concatenate([mid[0, i, :, lanes], mid[1, i, :, lanes]], axis=0))

        def double():
            left = jnp.concatenate([mid[0, 0, :, 256:384], mid[1, 0, :, 256:384]], axis=0)
            right = jnp.concatenate([mid[0, 1, :, 256:384], mid[1, 1, :, 256:384]], axis=0)
            both = mm(wide[...], jnp.concatenate([left, right], axis=1))
            parts[0, :, 256:384] = both[:, :128]
            parts[1, :, 256:384] = both[:, 128:]

        def turn(i, j):
            at = (i * 3 + j) * 384
            mid_t[at : at + 384] = mid[2, i, j * 384 : (j + 1) * 384].T

        most, rest = slice(0, 256), slice(256, 384)
        products = steps(product, (0, most), (1, most)) + steps(double, ()) + steps(product, (2, most), (2, rest))
        one = picker(cols, o)
        others = steps(turn, *[(i, j) for i in range(3) for j in range(3)])
        others += turning(back_odd, back_even, fwd)
        others += steps(placing(info, order, sel, count, width, tokens), *[(t,) for t in range(count)])
        others += steps(one, (reward, rows - 1, own, 0), (reward, rows, own, 1))
        weave(others, products)
        for k in range(rows + 4):
            total = jnp.zeros((cols, 384), F32)
            for i in range(3):
                r = k - 3 + i
                if 0 <= r < rows:
                    total = total + parts[i, r * cols : (r + 1) * cols]
            acc[k] = total
        for send, last in ((send_even, 1 - info[0]), (send_odd, info[0])):
            for k in range(3):
                send[k * cols : (k + 1) * cols] = acc[1 + last * 3 + k].astype(BF16)

    return body


def current_body(rows, cols, chan):
    per = chan * rows
    base = 3 * cols

    def body(info, latent, cached, got_even, got_odd, w_in, mid, half_gain, hidden, conv, lat, tall, wide, w_order, plain):
        even = info[0] == 0
        lat[...] = jnp.zeros_like(lat)

        def fill(first_row, got, ok):
            scale = ok.astype(F32)
            for t in range(3):
                x = got[base : base + per, t * 128 : t * 128 + 128].astype(F32) * scale
                y = got[base + per : base + 2 * per, t * 128 : t * 128 + cols - 128].astype(F32) * scale
                for r in range(rows):
                    at = pl.ds((first_row + r) * 3 * chan + t * chan, chan)
                    lat[at, 0:128] = x[r * chan : (r + 1) * chan]
                    lat[at, 128:cols] = y[r * chan : (r + 1) * chan]

        @pl.when(even)
        def _():
            fill(0, got_odd, info[1])
            fill(2 * rows, got_even, info[2])

        @pl.when(jnp.logical_not(even))
        def _():
            fill(0, got_even, info[1])
            fill(2 * rows, got_odd, info[2])

        for t in range(3):
            for r in range(rows):
                at = pl.ds((rows + r) * 3 * chan + t * chan, chan)
                lat[at, 0:cols] = (cached[t, r] if t < 2 else latent[r]).astype(F32)

        for r in range(3 * rows):
            for t in range(3):
                x = lat[pl.ds((r * 3 + t) * chan, chan), :]
                at = t * 3 * chan
                tall[r, at : at + chan] = pltpu.roll(x, 1, 1).astype(BF16)
                tall[r, at + chan : at + 2 * chan] = x.astype(BF16)
                tall[r, at + 2 * chan : at + 3 * chan] = pltpu.roll(x, 255, 1).astype(BF16)
        for i in range(3):
            for t in range(3):
                at = (i * 3 + t) * 3 * chan
                w_order[at : at + 3 * chan] = w_in[t, i]

        def hidden_row(k):
            lhs = tall[k : k + 3].reshape(27 * chan, 256)[:, 0:cols]
            h = lax.dot_general(lhs, w_order[...], (((0,), (0,)), ((), ())), preferred_element_type=F32)
            plain[k % 2] = h
            for c in range(0, cols, CHUNK):
                at = slice(c, c + CHUNK)
                v = plain[k % 2, at].astype(BF16)
                hidden[k, at] = v
                v = v.astype(F32)
                inv = lax.rsqrt(jnp.mean(v * v, axis=1, keepdims=True) + EPS)
                half = v * inv * half_gain[...]
                act = half * (jnp.tanh(half) + 1.0)
                if k < 3:
                    act = act * flag(info, 1)
                if k >= rows + 3:
                    act = act * flag(info, 2)
                plain[k % 2, at] = act
            for lanes in range(0, 384, 128):
                beside(wide.at[k], 0, lanes, plain[k % 2, :, lanes : lanes + 128], False)

        def conv_rows(p, number):
            lhs = [wide[p + i : p + i + number].reshape(number * cols, 1152) for i in range(3)]
            total = mm(jnp.concatenate(lhs, axis=1), mid[2, :, :, 0:256].reshape(3456, 256))
            conv[p : p + number, :, 0:256] = total.reshape(number, cols, 256)

        for k in range(4):
            hidden_row(k)
        for p in range(0, rows + 4, 2):
            conv_rows(p, 2)
            for k in (p + 4, p + 5):
                if k < rows + 6:
                    hidden_row(k)
        both = mm(
            wide[0 : rows + 5].reshape((rows + 5) * cols, 1152),
            jnp.concatenate([mid[2, 0, :, 256:384], mid[2, 1, :, 256:384]], axis=1),
        )
        rest = mm(wide[2 : rows + 6].reshape((rows + 4) * cols, 1152), mid[2, 2, :, 256:384])
        for p in range(rows + 4):
            at, after = slice(p * cols, (p + 1) * cols), slice((p + 1) * cols, (p + 2) * cols)
            conv[p, :, 256:384] = both[at, :128] + both[after, 128:] + rest[at]

    return body


def pulled(s, half_gain, grad):
    h = s * half_gain
    t = jnp.tanh(h)
    return (grad * half_gain) * ((1.0 + t) * (1.0 + h * (1.0 - t)))


def back_body(rows, cols, chan, count, o):
    size = rows * cols
    width = 2 * cols // count

    def body(
        info, hidden, conv, acc, got_even, got_odd, packed_even, packed_odd, own, own_mid, fwd, back_odd, back_even, mid_t, w_in, half_gain,
        half_out, payload, reward, edge, p0, p1, g_odd, g_even, wide, t_odd, t_even, back, act_grad, hid, tmp_odd, tmp_even, lines,
    ):
        even = info[0] == 0
        top, bottom = flag(info, 1), flag(info, 2)

        def take(got, packed, before):
            ok = top if before else bottom
            place = 0 if before else rows + 1
            for k in range(3):
                at = slice(k * cols, (k + 1) * cols)
                edge[place + k] = got[at].astype(F32) * ok
                reward[k if before else 2 * rows + 3 + k] = (packed[at].astype(F32) * ok).astype(BF16)

        @pl.when(even)
        def _():
            take(got_odd, packed_odd, True)
            take(got_even, packed_even, False)

        @pl.when(jnp.logical_not(even))
        def _():
            take(got_even, packed_even, True)
            take(got_odd, packed_odd, False)

        reward[3:6] = own[0:3]
        reward[6 : 2 * rows] = own_mid[...]
        reward[2 * rows : 2 * rows + 3] = own[3:6]

        def inside(x, k, first, last):
            return x * top if k < first else x * bottom if k >= last else x

        def state_row(k):
            for lanes in range(0, 384, 128):
                at = slice(lanes, lanes + 128)
                x = hidden[k + 1, :, at].astype(F32) + conv[k, :, at]
                if 1 <= k <= rows + 2:
                    x = x + acc[k, :, at]
                if k < 3 or k > rows:
                    x = x + edge[k, :, at]
                beside(wide.at[k], 0, lanes, inside(x, k, 2, rows + 2), False)

        def up_rows(first, last, b, n):
            count = last - first
            x = wide[first:last, :, b * 384 : b * 384 + 768].reshape(count * cols, 768)
            lanes = slice(n * 256, n * 256 + 256)
            (p0, p1)[b][first:last, :, lanes] = mm(x, fwd[b, :, lanes]).reshape(count, cols, 256)

        def down_rows(first, last, odd, n):
            count = last - first
            g, kernel, t = (g_odd, back_odd, t_odd) if odd else (g_even, back_even, t_even)
            lanes = slice(n * 256, n * 256 + 256)
            x = g[first:last].reshape(count * cols, 768)
            t[first:last, :, lanes] = mm(x, kernel[:, lanes]).reshape(count, cols, 256)

        low = lax.broadcasted_iota(jnp.int32, (CHUNK, 128), 1) < 64
        tall_low = lax.broadcasted_iota(jnp.int32, (cols, 128), 1) < 64
        gains = [half_out[:, 0:128], half_out[:, 128:256]]

        def pull(v0, v1, vm, r, zero_low):
            mine = low if zero_low else jnp.logical_not(low)
            def both(a0, a1, am):
                s0 = jnp.sum(a0 + jnp.where(mine, am, 0.0), axis=1, keepdims=True)
                s1 = jnp.sum(a1 + jnp.where(mine, 0.0, am), axis=1, keepdims=True)
                return s0 * (1.0 / o), s1 * (1.0 / o)

            q0, q1 = both(v0 * v0, v1 * v1, vm * vm)
            i0, i1 = lax.rsqrt(q0 + EPS), lax.rsqrt(q1 + EPS)
            im = jnp.where(mine, i0, i1)
            out = []
            for v, i, g, k in ((v0, i0, gains[0], 0), (v1, i1, gains[0], 1), (vm, im, gains[1], 2)):
                s = v * i
                out.append((s, pulled(s, g, r[:, k * 128 : k * 128 + 128].astype(F32))))
            m0, m1 = both(*(s * d for s, d in out))
            mx = jnp.where(mine, m0, m1)
            return [i * (d - s * m) for (s, d), i, m in zip(out, (i0, i1, im), (m0, m1, mx))]

        def pull_row(k, odd):
            target, tmp = (g_odd, tmp_odd) if odd else (g_even, tmp_even)
            for c in range(0, cols, CHUNK):
                at = slice(c, c + CHUNK)
                if odd:
                    v0 = p0[k, at, 256:384] + p0[k + 1, at, 0:128]
                    v1 = p1[k, at, 256:384] + p1[k + 1, at, 0:128]
                    m0 = p0[k, at, 640:768] + p0[k + 1, at, 512:640]
                    m1 = p1[k, at, 640:768] + p1[k + 1, at, 512:640]
                else:
                    v0 = p0[k + 1, at, 128:256] + p0[k, at, 384:512]
                    v1 = p1[k + 1, at, 128:256] + p1[k, at, 384:512]
                    m0 = p1[k + 1, at, 512:640] + p1[k, at, 640:768]
                    m1 = p0[k + 1, at, 512:640] + p0[k, at, 640:768]
                out = pull(v0, v1, jnp.where(low, m0, m1), reward[2 * k + (0 if odd else 1), at], odd)
                for n, value in enumerate(out):
                    lanes = slice(n * 128, n * 128 + 128)
                    target[k, at, lanes] = value.astype(BF16)
                    tmp[k % 2, at, lanes] = value
            target[k, :, 384:512] = from_right(tmp[k % 2, :, 0:128]).astype(BF16)
            target[k, :, 512:640] = from_left(tmp[k % 2, :, 128:256]).astype(BF16)
            x = tmp[k % 2, :, 256:384]
            sides = (from_right(x), from_left(x)) if odd else (from_left(x), from_right(x))
            target[k, :, 640:768] = jnp.where(tall_low, *sides).astype(BF16)

        def block_row(k):
            for lanes in range(0, 384, 128):
                at, far = slice(lanes, lanes + 128), slice(lanes + 384, lanes + 512)
                x = t_odd[k + 1, :, at] + t_odd[k, :, far] + t_even[k, :, at] + t_even[k + 1, :, far]
                beside(back.at[k], 0, lanes, inside(x, k, 1, rows + 1), True)

        def hidden_pull(k):
            for c in range(0, cols, CHUNK):
                at = slice(c, c + CHUNK)
                v = hidden[k + 3, at].astype(F32)
                inv = lax.rsqrt(jnp.mean(v * v, axis=1, keepdims=True) + EPS)
                s = v * inv
                d = pulled(s, half_gain[...], act_grad[k, at])
                dv = inv * (d - s * jnp.mean(d * s, axis=1, keepdims=True))
                hid[k, at] = (back[k + 1, at, 384:768].astype(F32) + dv).astype(BF16)

        fine = rows + 3
        def ups(first, last):
            for b in range(2):
                up_rows(max(first, 1), last, b, 0)
                up_rows(first, min(last, rows + 3), b, 1)
                up_rows(first, last, b, 2)

        def downs(first, last):
            for odd in (True, False):
                down_rows(max(first, 1) if odd else first, last if odd else min(last, fine - 1), odd, 0)
                down_rows(first, last, odd, 1)
                down_rows(first if odd else max(first, 1), min(last, fine - 1) if odd else last, odd, 2)

        def states(first, last):
            for k in range(first, last):
                state_row(k)

        def pulls(first, last):
            for k in range(first, last):
                pull_row(k, True)
                pull_row(k, False)

        def blocks(first, last):
            for k in range(first, last):
                block_row(k)

        def mid_rows(p, number):
            lhs = [back[p + 2 - i : p + 2 - i + number].reshape(number * cols, 1152) for i in range(3)]
            total = mm(jnp.concatenate(lhs, axis=1), mid_t[:, 0:256])
            act_grad[p : p + number, :, 0:256] = total.reshape(number, cols, 256)

        states(0, rows)
        ups(0, 2)
        states(rows, rows + 2)
        ups(2, rows)
        states(rows + 2, rows + 4)
        ups(rows, rows + 2)
        pulls(0, 2)
        ups(rows + 2, rows + 4)
        pulls(2, rows)
        downs(0, 2)
        pulls(rows, rows + 2)
        downs(2, rows)
        pulls(rows + 2, fine)
        blocks(0, rows - 1)
        downs(rows, fine)
        blocks(rows - 1, rows)
        mid_rows(0, 2)
        blocks(rows, rows + 2)
        mid_rows(2, rows - 2)
        both = mm(
            back[1 : rows + 2].reshape((rows + 1) * cols, 1152),
            jnp.concatenate([mid_t[1152:2304, 256:384], mid_t[0:1152, 256:384]], axis=1),
        )
        rest = mm(back[0:rows].reshape(size, 1152), mid_t[2304:3456, 256:384])
        for p in range(rows):
            at, after = slice(p * cols, (p + 1) * cols), slice((p + 1) * cols, (p + 2) * cols)
            act_grad[p, :, 256:384] = both[at, :128] + both[after, 128:] + rest[at]
        for k in range(rows):
            hidden_pull(k)

        z = mm_t(w_in[...], hid[...].reshape(size, 384))
        place = lax.broadcasted_iota(jnp.int32, (chan, size), 1)
        col = lax.rem(place, cols)
        sums = []
        for i in range(3):
            z0, z1, z2 = (z[(i * 3 + j) * chan : (i * 3 + j + 1) * chan] for j in range(3))
            left = jnp.where(col == cols - 1, 0.0, pltpu.roll(z0, size - 1, 1))
            right = jnp.where(col == 0, 0.0, pltpu.roll(z2, 1, 1))
            sums.append(left + z1 + right)
        inner = sums[1]
        inner = inner + jnp.where(place < size - cols, pltpu.roll(sums[0], size - cols, 1), 0.0)
        inner = inner + jnp.where(place >= cols, pltpu.roll(sums[2], cols, 1), 0.0)
        lines[0:chan] = inner
        lines[chan : 2 * chan] = sums[0]
        lines[2 * chan : 3 * chan] = sums[2]
        per_row = count // 2
        for u in range(count):
            pair, piece = u // per_row, u % per_row
            parts = []
            for a in range(2):
                at = (2 * pair + a) * cols + piece * width
                parts.append(lines[0:chan, at : at + width])
            at = piece * width + (0 if pair else (rows - 1) * cols)
            first = chan if pair else 2 * chan
            parts.append(lines[first : first + chan, at : at + width])
            parts.append(jnp.zeros((chan, 128 - 3 * width), F32))
            payload[u] = jnp.concatenate(parts, axis=1).astype(BF16)

    return body


def placing(info, order, sel, count, width, tokens):
    piece = width // 2
    pair = info[3]
    lane = lax.broadcasted_iota(jnp.int32, (128, 4 * tokens), 0)
    column = lax.broadcasted_iota(jnp.int32, (128, 4 * tokens), 1)
    group = (lane >= width).astype(jnp.int32) + (lane >= 2 * width).astype(jnp.int32)
    w = lane - group * width
    part = jnp.where(group == 2, pair, group)
    fixed = (2 * part + (w & 1)) * tokens + (w >> 1) - column
    fixed = jnp.where(lane < 3 * width, fixed, -99999)

    def one(t):
        step = t + 1 - 2 * pair
        valid = jnp.logical_and(step >= 0, step < count)
        beside = jnp.where(valid, piece * order[jnp.clip(step, 0, count - 1)], -9999)
        begin = jnp.where(group == 2, beside, piece * order[t])
        sel[t // 2, t % 2 * 128 : t % 2 * 128 + 128] = (fixed + begin == 0).astype(F32).astype(BF16)

    return one


def place_body(count, chan, tokens):
    def body(sel, got, out):
        total = None
        for t in range(count // 2):
            x = mm(jnp.concatenate([got[2 * t], got[2 * t + 1]], axis=1), sel[t])
            total = x if total is None else total + x
        for k in range(4):
            out[k * chan : (k + 1) * chan] = total[:, k * tokens : (k + 1) * tokens]

    return body


def swaps(count):
    within = [(i, i ^ 1) for i in range(count)]
    across = [(0, 0), (count - 1, count - 1)]
    for i in range(1, count - 1, 2):
        across += [(i, i + 1), (i + 1, i)]
    return within, sorted(across)


def shards(
    latent, cached_latent, cached_features, reward_grad, conv_in_weight, conv_mid_weight, conv_up_weight, norm_gain, out_gain, shard_order
):
    count = lax.axis_size("tile")
    rows, cols, chan = latent.shape
    mid_chan = norm_gain.shape[0]
    o = out_gain.shape[0]
    tile = lax.axis_index("tile")
    info = jnp.stack(
        [tile % 2, (tile > 0).astype(jnp.int32), (tile < count - 1).astype(jnp.int32), (tile >= count // 2).astype(jnp.int32)]
    ).astype(jnp.int32)
    lat = jnp.transpose(latent, (0, 2, 1))
    lat_cached = jnp.transpose(cached_latent, (0, 1, 3, 2))
    reward_t = jnp.transpose(reward_grad, (0, 2, 1))
    up_t = jnp.transpose(conv_up_weight, (0, 1, 3, 2))
    mid = conv_mid_weight.reshape(3, 3, 3 * mid_chan, mid_chan)
    w_in = conv_in_weight.reshape(3, 3, 3 * chan, mid_chan)
    gain = 0.5 * norm_gain.reshape(1, mid_chan)
    gain_out = 0.5 * jnp.concatenate([out_gain, out_gain[128:]]).reshape(1, 256)
    within, across = swaps(count)
    size = rows * cols
    edge_rows = 3 * cols + 2 * chan * rows

    info, back_odd, back_even = call(
        taps_body,
        [((4,), jnp.int32), ((768, 768), BF16), ((768, 768), BF16)],
        1, 1, [], 1e10, 8, 1,
    )(info, up_t)

    own, send_even, send_odd = call(
        pack_body(rows, cols, o, chan),
        [((6, cols, 384), BF16), ((edge_rows, 384), BF16), ((edge_rows, 384), BF16)],
        1, 3, [], 1e10, 8,
    )(info, reward_t, lat, lat_cached)
    packed_even = lax.ppermute(send_even, "tile", within)
    packed_odd = lax.ppermute(send_odd, "tile", across)

    width = 2 * cols // count
    tokens = size // 4
    acc, part_even, part_odd, mid_t, sel, fwd, own_mid = call(
        cached_body(rows, cols, count, width, tokens, o),
        [
            ((rows + 4, cols, 384), F32), ((3 * cols, 384), BF16), ((3 * cols, 384), BF16), ((3456, 384), BF16),
            ((count // 2, 256, 4 * tokens), BF16), ((2, 768, 768), BF16), ((2, cols, 384), BF16),
        ],
        2, 5, [pltpu.VMEM((size, 2304), BF16), pltpu.VMEM((3, size, 384), F32)], 4e9, 14,
    )(info, shard_order, cached_features, mid, back_odd, back_even, reward_t)
    got_even = lax.ppermute(part_even, "tile", within)
    got_odd = lax.ppermute(part_odd, "tile", across)

    hidden, conv = call(
        current_body(rows, cols, chan),
        [((rows + 6, cols, 384), BF16), ((rows + 4, cols, 384), F32)],
        1, 7,
        [
            pltpu.VMEM((9 * rows * chan, 256), F32),
            pltpu.VMEM((3 * rows, 9 * chan, 256), BF16),
            pltpu.VMEM((rows + 6, cols, 1152), BF16),
            pltpu.VMEM((27 * chan, 384), BF16),
            pltpu.VMEM((2, cols, 384), F32),
        ],
        5e9, 14,
    )(info, lat, lat_cached, packed_even, packed_odd, w_in, mid, gain)

    (payload,) = call(
        back_body(rows, cols, chan, count, o),
        [((count, chan, 128), BF16)],
        1, 16,
        [
            pltpu.VMEM((2 * rows + 6, cols, 384), BF16),
            pltpu.VMEM((rows + 4, cols, 384), F32),
            pltpu.VMEM((rows + 4, cols, 768), F32),
            pltpu.VMEM((rows + 4, cols, 768), F32),
            pltpu.VMEM((rows + 3, cols, 768), BF16),
            pltpu.VMEM((rows + 3, cols, 768), BF16),
            pltpu.VMEM((rows + 4, cols, 1152), BF16),
            pltpu.VMEM((rows + 3, cols, 768), F32),
            pltpu.VMEM((rows + 3, cols, 768), F32),
            pltpu.VMEM((rows + 2, cols, 1152), BF16),
            pltpu.VMEM((rows, cols, 384), F32),
            pltpu.VMEM((rows, cols, 384), BF16),
            pltpu.VMEM((2, cols, 384), F32),
            pltpu.VMEM((2, cols, 384), F32),
            pltpu.VMEM((3 * chan, size), F32),
        ],
        8e9, 34,
    )(
        info, hidden, conv, acc, got_even, got_odd, packed_even, packed_odd, own, own_mid, fwd, back_odd, back_even, mid_t,
        w_in[2].reshape(9 * chan, mid_chan), gain, gain_out,
    )
    received = lax.all_to_all(payload, "tile", split_axis=0, concat_axis=0, tiled=True)
    (placed,) = call(place_body(count, chan, tokens), [((4 * chan, tokens), F32)], 0, 2, [], 1e7, 8)(sel, received)
    return placed.T


def solution(mesh):
    return jax.shard_map(
        shards,
        mesh=mesh,
        in_specs=(
            P(("prompt", "tile"), None, None),
            P(None, ("prompt", "tile"), None, None),
            P(None, ("prompt", "tile"), None, None),
            P(("prompt", "tile"), None, None),
            P(),
            P(),
            P(),
            P(),
            P(),
            P("prompt"),
        ),
        out_specs=P(("prompt", "tile"), None),
        check_vma=False,
    )
```
